32 devices in a mesh: fsdp: 4 (over z), context: 4 (over x, core), tensor: 2 (over y).
Axes of the slice: x: 2, y: 2, z: 4, core: 2. Of those that a mesh axis runs over, the one named last changes fastest.
Arguments:
- tokens: bfloat16 [8, 2048, 2048], P('fsdp', ('context', 'tensor')), may hold values from -6 to 6
- segments: int32 [8, 2048], P('fsdp'), may hold values from 0 to 2, as said below
- forget: float32 [8], P('tensor'), may hold values from 0.0002 to 0.03
- ln1_gain: float32 [2048], replicated, may hold values from 0.1 to 1.9
- w_query: bfloat16 [2048, 2048], P('fsdp', 'tensor'), may hold values from -0.125 to 0.125
- w_key: bfloat16 [2048, 2048], P('fsdp', 'tensor'), may hold values from -0.125 to 0.125
- w_value: bfloat16 [2048, 4096], P('fsdp', 'tensor'), may hold values from -0.125 to 0.125
- w_gate: bfloat16 [2048, 4096], P('fsdp', 'tensor'), may hold values from -0.125 to 0.125
- norm_gain: float32 [4096], P('tensor'), may hold values from 0.1 to 1.9
- w_out: bfloat16 [4096, 2048], P('tensor', 'fsdp'), may hold values from -0.125 to 0.125
- ln2_gain: float32 [2048], replicated, may hold values from 0.1 to 1.9
- w_fc_gate: bfloat16 [2048, 4096], P('fsdp', 'tensor'), may hold values from -0.125 to 0.125
- w_fc_up: bfloat16 [2048, 4096], P('fsdp', 'tensor'), may hold values from -0.125 to 0.125
- w_fc_down: bfloat16 [4096, 2048], P('tensor', 'fsdp'), may hold values from -0.125 to 0.125
- cotangent: bfloat16 [8, 2048, 2048], P('fsdp', ('context', 'tensor')), may hold values from -6 to 6
Outputs:
- output: bfloat16 [8, 2048, 2048], P('fsdp', ('context', 'tensor'))
- grad_tokens: float32 [8, 2048, 2048], P('fsdp', ('context', 'tensor'))
- grad_ln1: float32 [2048], replicated
- grad_query: float32 [2048, 2048], P('fsdp', 'tensor')
- grad_key: float32 [2048, 2048], P('fsdp', 'tensor')
- grad_value: float32 [2048, 4096], P('fsdp', 'tensor')
- grad_gate: float32 [2048, 4096], P('fsdp', 'tensor')
- grad_norm: float32 [4096], P('tensor')
- grad_out: float32 [4096, 2048], P('tensor', 'fsdp')
- grad_ln2: float32 [2048], replicated
- grad_fc_gate: float32 [2048, 4096], P('fsdp', 'tensor')
- grad_fc_up: float32 [2048, 4096], P('fsdp', 'tensor')
- grad_fc_down: float32 [4096, 2048], P('tensor', 'fsdp')
The draws below stay inside these ranges and needn't reach their ends.
Inputs may be any that keep to these rules, and one draw needn't show every extreme that they name: `segments`: in every sequence the numbers start at 0, never fall, and rise by one at each of exactly two document starts; every document holds 204 tokens or more.
All inputs are finite; a program needn't handle non-finite values.
Results may differ from the reference program's by a relative error of at most 0.018.
Values may be sent and summed in bfloat16 or wider, within the bound.
No kernel may reach another device: no remote copies, remote signals or barrier semaphores. Data moves between devices by JAX's collectives and lax.ppermute only.
A program may use at most 232 MiB of HBM per device.

```python
import math
from functools import partial
import jax
import jax.numpy as jnp
from jax import lax

D = 2048
HEADS = 8
QK = 256
VH = 512
FF = 4096
LEN = 2048
SEQS = 2
VD = 4096
BATCH = 8
N_CONTEXT = 4


def draw_segments(key, part):
    key = jax.random.fold_in(key, 7)
    subkeys = jax.random.split(key, 6)
    shortest = LEN // 10
    piece_len = LEN // N_CONTEXT
    group_count = BATCH // SEQS
    chosen = jax.random.randint(subkeys[0], (group_count, 1), 0, SEQS)
    spanning = (jnp.arange(SEQS, dtype=jnp.int32)[None, :] == chosen).reshape(BATCH, 1)
    first_start = jax.random.randint(subkeys[1], (BATCH, 1), shortest, piece_len)
    last_start = jax.random.randint(subkeys[2], (BATCH, 1), LEN - piece_len + 1, LEN - shortest + 1)
    border = piece_len * jax.random.randint(subkeys[3], (BATCH, 1), 1, N_CONTEXT)
    left_room = border - 2 * shortest + 1
    right_room = LEN - border - 2 * shortest + 1
    coin = jax.random.randint(subkeys[4], (BATCH, 1), 0, 2)
    go_left = (coin == 0) & (left_room > 0) | (right_room <= 0)
    room = jnp.where(go_left, left_room, right_room)
    offset = jax.random.randint(subkeys[5], (BATCH, 1), 0, 1048576) % jnp.maximum(room, 1)
    other_start = jnp.where(go_left, shortest + offset, border + shortest + offset)
    lower = jnp.where(spanning, first_start, jnp.minimum(border, other_start))
    upper = jnp.where(spanning, last_start, jnp.maximum(border, other_start))
    places = jnp.arange(LEN, dtype=jnp.int32)[None, :]
    return (places >= lower).astype(jnp.int32) + (places >= upper).astype(jnp.int32)


def level_of(key, dims, shards, smallest, largest):
    factor_of = 1.0
    for axis_at, shards_of in shards:
        steps = jax.random.uniform(jax.random.fold_in(jax.random.fold_in(key, 6), axis_at), (shards_of,), jnp.float32, smallest / len(shards), largest / len(shards))
        factor_of = factor_of * jnp.repeat(jnp.exp(steps), dims[axis_at] // shards_of).reshape((-1,) + (1,) * (len(dims) - 1 - axis_at))
    return factor_of


def gaussian(rng, shape, width, reach, shards=(), kind=jnp.bfloat16):
    loudness = level_of(rng, shape, shards, -0.22, 0.18) if shards else 1.0
    drawn = jax.random.normal(rng, shape, jnp.float32) * width * loudness
    return jnp.minimum(jnp.maximum(drawn, -reach), reach).astype(kind)


def setup_inputs(seed: int = 0) -> dict:
    key_list = jax.random.split(jax.random.key(seed), 16)
    tokens = gaussian(key_list[0], (BATCH, LEN, D), 1.0, 6.0, ((0, 4), (1, 8)))
    segments = draw_segments(jax.random.fold_in(key_list[15], 71), 0)
    forget = jnp.clip(jnp.exp(math.log(0.03) - 5.0106353 * jax.random.uniform(key_list[2], (HEADS,), jnp.float32) ** level_of(key_list[2], (HEADS,), ((0, 2),), -0.2, 0.2)), 0.0002, 0.03)
    ln1_gain = jnp.clip(1.0 + 0.18 * jax.random.normal(key_list[3], (D,), jnp.float32), 0.1, 1.9)
    w_query = gaussian(key_list[4], (D, HEADS * QK), D ** -0.5, 0.125, ((0, 4), (1, 2)))
    w_key = gaussian(key_list[5], (D, HEADS * QK), D ** -0.5, 0.125, ((0, 4), (1, 2)))
    w_value = gaussian(key_list[6], (D, VD), D ** -0.5, 0.125, ((0, 4), (1, 2)))
    w_gate = gaussian(key_list[7], (D, VD), D ** -0.5, 0.125, ((0, 4), (1, 2)))
    norm_gain = jnp.clip(1.0 + 0.18 * jax.random.normal(key_list[8], (VD,), jnp.float32), 0.1, 1.9)
    w_out = gaussian(key_list[9], (VD, D), (VD // 2) ** -0.5, 0.125, ((0, 2), (1, 4)))
    ln2_gain = jnp.clip(1.0 + 0.18 * jax.random.normal(key_list[10], (D,), jnp.float32), 0.1, 1.9)
    w_fc_gate = gaussian(key_list[11], (D, FF), D ** -0.5, 0.125, ((0, 4), (1, 2)))
    w_fc_up = gaussian(key_list[12], (D, FF), D ** -0.5, 0.125, ((0, 4), (1, 2)))
    w_fc_down = gaussian(key_list[13], (FF, D), (FF // 2) ** -0.5, 0.125, ((0, 2), (1, 4)))
    cotangent = gaussian(key_list[14], (BATCH, LEN, D), 1.0, 6.0, ((0, 4), (1, 8)))
    return {"tokens": tokens, "segments": segments, "forget": forget, "ln1_gain": ln1_gain, "w_query": w_query, "w_key": w_key, "w_value": w_value, "w_gate": w_gate, "norm_gain": norm_gain, "w_out": w_out, "ln2_gain": ln2_gain, "w_fc_gate": w_fc_gate, "w_fc_up": w_fc_up, "w_fc_down": w_fc_down, "cotangent": cotangent}


@jax.custom_vjp
def low(v):
    return lax.optimization_barrier(v.astype(jnp.bfloat16)).astype(jnp.float32)

@jax.custom_vjp
def low_back(v):
    return v

def low_keep(v):
    return (low(v), None)

def low_pass(kept, grad):
    return (grad,)

def back_keep(v):
    return (v, None)

def back_low(kept, grad):
    return (low(grad),)
low.defvjp(low_keep, low_pass)
low_back.defvjp(back_keep, back_low)
precise = partial(jnp.einsum, precision=lax.Precision.HIGHEST)

def matmul(left, right):
    return jnp.dot(left, right, precision=lax.Precision.HIGHEST, preferred_element_type=jnp.float32)

def layer_norm(values, gain_vec, epsilon=1e-05):
    centred = values - lax.optimization_barrier(jnp.mean(values, axis=-1, keepdims=True))
    scale = lax.rsqrt(lax.optimization_barrier(jnp.mean(centred * centred, axis=-1, keepdims=True)) + epsilon)
    return centred * scale * gain_vec

def retention(query_s, keys_all, vals_all, seg_row, log_keep):
    block_len = min(512, LEN)
    count = LEN // block_len
    steps_idx = jnp.arange(block_len, dtype=jnp.float32)
    step_gap = jnp.maximum(steps_idx[:, None] - steps_idx[None, :], 0.0)
    causal = steps_idx[:, None] >= steps_idx[None, :]
    decay_tab = jnp.exp(step_gap[None] * log_keep[:, None, None])
    into_tab = jnp.exp((steps_idx[:, None] + 1.0) * log_keep[None, :])
    out_tab = jnp.exp((block_len - 1.0 - steps_idx)[:, None] * log_keep[None, :])
    whole_decay = jnp.exp(block_len * log_keep)

    def advance(carry, block):
        state, seg_prev = carry
        query_blk, keys_blk, vals_blk, seg_blk = block
        live_mask = (seg_blk == seg_prev).astype(jnp.float32)
        same_doc = (seg_blk[:, None] == seg_blk[None, :]) & causal
        weights_mask = jnp.where(same_doc[None], decay_tab, 0.0)
        scores = precise('thd,shd->hts', query_blk, keys_blk) * weights_mask
        inflow = live_mask[:, None] * into_tab
        outflow = (seg_blk == seg_blk[-1]).astype(jnp.float32)[:, None] * out_tab
        result = precise('hts,she->the', scores, vals_blk)
        result = result + inflow[:, :, None] * precise('thd,hde->the', query_blk, state)
        update = precise('shd,sh,she->hde', keys_blk, outflow, vals_blk)
        state_next = (live_mask[-1] * whole_decay)[:, None, None] * state + update
        return ((state_next, seg_blk[-1]), result)
    blocks = (query_s.reshape(count, block_len, HEADS, QK), keys_all.reshape(count, block_len, HEADS, QK), vals_all.reshape(count, block_len, HEADS, VH), seg_row.reshape(count, block_len))
    start = (jnp.zeros((HEADS, QK, VH), jnp.float32), seg_row[0])
    final, pieces = lax.scan(jax.checkpoint(advance), start, blocks)
    return pieces.reshape(LEN, HEADS, VH)

def forward_seq(x_row, seg_row, log_keep, params):
    ln1, w_q, w_k, w_v, w_g, gn_gain, w_o, ln2, w_one, w_three, w_two = params
    h_one = low(layer_norm(x_row, ln1))
    query = low_back(low(matmul(h_one, w_q)))
    keys = low_back(low(matmul(h_one, w_k)))
    values = low_back(low(matmul(h_one, w_v)))
    gate = low_back(matmul(h_one, w_g))
    retained = retention(query * 0.0625, keys, values, seg_row, log_keep)
    normed = layer_norm(retained, gn_gain.reshape(HEADS, VH), 0.01).reshape(LEN, VD)
    gated = low(jax.nn.silu(gate) * normed)
    branch = low_back(matmul(gated, w_o))
    middle = x_row + branch
    h_two = low(layer_norm(middle, ln2))
    fc_a = low_back(matmul(h_two, w_one))
    fc_b = low_back(matmul(h_two, w_three))
    hidden = low(jax.nn.silu(fc_a) * fc_b)
    return middle + matmul(hidden, w_two)

def reference(tokens, segments, forget, ln1_gain, w_query, w_key, w_value, w_gate, norm_gain, w_out, ln2_gain, w_fc_gate, w_fc_up, w_fc_down, cotangent):
    params = tuple((p.astype(jnp.float32) for p in (ln1_gain, w_query, w_key, w_value, w_gate, norm_gain, w_out, ln2_gain, w_fc_gate, w_fc_up, w_fc_down)))
    log_keep = jnp.log(1.0 - forget.astype(jnp.float32))

    def per_seq(totals, item):
        x_row, seg_row, cot_row = item

        def apply_block(x_in, *weights):
            return forward_seq(x_in, seg_row, log_keep, weights)
        out_row, pullback = jax.vjp(apply_block, x_row, *params)
        grads = pullback(cot_row)
        totals = tuple((a + g for a, g in zip(totals, grads[1:])))
        return (totals, (out_row.astype(jnp.bfloat16), grads[0]))
    start = tuple((jnp.zeros_like(p) for p in params))
    final, (outputs, grad_x) = lax.scan(per_seq, start, (tokens.astype(jnp.float32), segments, cotangent.astype(jnp.float32)))
    return (outputs, grad_x, final[0], final[1], final[2], final[3], final[4], final[5], final[6], final[7], final[8], final[9], final[10])
```

```python
from functools import partial
from types import SimpleNamespace

import jax
import jax.numpy as jnp
from jax import lax
from jax.experimental import pallas as pl
from jax.experimental.pallas import tpu as pltpu
from jax.sharding import PartitionSpec as P

FSDP, CONTEXT, TENSOR = "fsdp", "context", "tensor"

careful = partial(jnp.einsum, precision=lax.Precision.HIGH)


def entering(part, axis, combine, identity):
    place = lax.axis_index(axis)
    gathered = jax.tree.map(lambda a: lax.all_gather(a, axis), part)
    state = jax.tree.map(lambda a, e: jnp.zeros_like(a) + jnp.asarray(e, a.dtype), part, identity)

    def one(step, state):
        return combine(
            state, jax.tree.map(lambda a: lax.dynamic_index_in_dim(a, step, 0, False), gathered)
        )

    return lax.fori_loop(0, place, one, state)


def carried_in(value, axis, combine, identity):
    count, place = (lax.axis_size(axis), lax.axis_index(axis))
    everything = jax.tree.map(
        lambda part, kind: lax.all_gather(part.astype(kind), axis),
        value,
        jax.tree.map(lambda a: jnp.bfloat16 if a.dtype == jnp.float32 else a.dtype, value),
    )
    start = jax.tree.map(
        lambda part, zero: jnp.broadcast_to(jnp.asarray(zero, part.dtype), part.shape),
        value,
        identity,
    )

    def step(k, before):
        at = count - 1 - k
        reached = at > place
        new = combine(
            before, jax.tree.map(lambda part, own: part[at].astype(own.dtype), everything, value)
        )
        return jax.tree.map(lambda a, b: jnp.where(reached, a, b), new, before)

    return lax.fori_loop(0, count, step, start)


def norm_rows(values, gain_vec, epsilon=1e-05):
    centred = values - jnp.mean(values, axis=-1, keepdims=True)
    scale = lax.rsqrt(jnp.mean(centred * centred, axis=-1, keepdims=True) + epsilon)
    normed = centred * scale
    return (normed * gain_vec, normed, scale)


def norm_back(grad_in, normed, scale, gain_vec):
    d_normed = grad_in * gain_vec
    first_mean = jnp.mean(d_normed, axis=-1, keepdims=True)
    second_mean = jnp.mean(d_normed * normed, axis=-1, keepdims=True)
    return scale * (d_normed - first_mean - normed * second_mean)


def swish_slope(values):
    sigma = jax.nn.sigmoid(values)
    return sigma * (1.0 + values * (1.0 - sigma))


def compose(earlier, latter):
    return (earlier[0] * latter[0], latter[0][:, :, None, None] * earlier[1] + latter[1])


def share_gather(piece):
    return lax.all_gather(piece, TENSOR, axis=1, tiled=True)


def branch_sum(terms):
    return lax.psum_scatter(terms, TENSOR, scatter_dimension=1, tiled=True)


def input_sum(terms):
    return lax.psum_scatter(
        terms.astype(jnp.bfloat16), TENSOR, scatter_dimension=1, tiled=True
    ).astype(jnp.float32)


def mixer_fetch(w_query, w_key, w_value, w_gate, w_out):
    return (
        lax.all_gather(w_query, FSDP, axis=0, tiled=True),
        lax.all_gather(w_key, FSDP, axis=0, tiled=True),
        lax.all_gather(w_value, FSDP, axis=0, tiled=True),
        lax.all_gather(w_gate, FSDP, axis=0, tiled=True),
        lax.all_gather(w_out, FSDP, axis=1, tiled=True),
    )


def mlp_fetch(w_fc_gate, w_fc_up, w_fc_down):
    return (
        lax.all_gather(w_fc_gate, FSDP, axis=0, tiled=True),
        lax.all_gather(w_fc_up, FSDP, axis=0, tiled=True),
        lax.all_gather(w_fc_down, FSDP, axis=1, tiled=True),
    )


def product(form, left, right):
    return jnp.einsum(form, left, right, preferred_element_type=jnp.float32)


def general_body(
    tokens,
    segments,
    forget,
    ln1_gain,
    w_query,
    w_key,
    w_value,
    w_gate,
    norm_gain,
    w_out,
    ln2_gain,
    w_fc_gate,
    w_fc_up,
    w_fc_down,
    cotangent,
):
    heads_here = forget.shape[0]
    qk_width = w_query.shape[1] // heads_here
    v_width = w_value.shape[1] // heads_here
    v_local = heads_here * v_width
    gain_heads = norm_gain.reshape(heads_here, v_width)
    x_share = tokens.astype(jnp.float32)
    h1_share, ln1_normed, ln1_scale = norm_rows(x_share, ln1_gain)
    h_one = share_gather(h1_share.astype(jnp.bfloat16))
    wq_all, wk_all, wv_all, wg_all, wo_all = mixer_fetch(w_query, w_key, w_value, w_gate, w_out)
    seq_count, stretch_len = (h_one.shape[0], h_one.shape[1])
    query = product("btd,dq->btq", h_one, wq_all).astype(jnp.bfloat16)
    keys = product("btd,dq->btq", h_one, wk_all).astype(jnp.bfloat16)
    values = product("btd,dv->btv", h_one, wv_all).astype(jnp.bfloat16)
    gate_pre = product("btd,dv->btv", h_one, wg_all)
    query_heads = query.reshape(seq_count, stretch_len, heads_here, qk_width)
    keys_heads = keys.reshape(seq_count, stretch_len, heads_here, qk_width)
    query_full = query_heads.astype(jnp.float32) * 0.0625
    keys_full = keys_heads.astype(jnp.float32)
    values_full = values.astype(jnp.float32).reshape(seq_count, stretch_len, heads_here, v_width)
    log_keep = jnp.log(1.0 - forget)
    ctx_place = lax.axis_index(CONTEXT)
    seg_stretch = lax.dynamic_slice_in_dim(segments, ctx_place * stretch_len, stretch_len, 1)
    seg_prev = lax.dynamic_slice_in_dim(segments, jnp.maximum(ctx_place * stretch_len - 1, 0), 1, 1)
    live_mask = (seg_stretch == seg_prev).astype(jnp.float32)
    steps_idx = jnp.arange(stretch_len, dtype=jnp.float32)
    step_gap = jnp.maximum(steps_idx[:, None] - steps_idx[None, :], 0.0)
    causal = steps_idx[:, None] >= steps_idx[None, :]
    same_doc = (seg_stretch[:, :, None] == seg_stretch[:, None, :]) & causal[None]
    weights_mask = jnp.where(
        same_doc[:, None], jnp.exp(step_gap[None] * log_keep[:, None, None])[None], 0.0
    )
    inflow = live_mask[:, :, None] * jnp.exp((steps_idx[:, None] + 1.0) * log_keep[None, :])[None]
    outflow = (seg_stretch == seg_stretch[:, -1:]).astype(jnp.float32)[:, :, None] * jnp.exp(
        (stretch_len - 1.0 - steps_idx)[:, None] * log_keep[None, :]
    )[None]
    carry_decay = live_mask[:, -1:] * jnp.exp(stretch_len * log_keep)[None, :]
    update = careful("bshd,bsh,bshe->bhde", keys_full, outflow, values_full)
    identity = (jnp.ones_like(carry_decay), jnp.zeros_like(update))
    state_in = entering((carry_decay, update), CONTEXT, compose, identity)[1]
    scores = product("bthd,bshd->bhts", query_heads, keys_heads) * 0.0625 * weights_mask
    retained = careful("bhts,bshe->bthe", scores, values_full)
    retained = retained + inflow[..., None] * careful("bthd,bhde->bthe", query_full, state_in)
    normed_out, gn_normed, gn_scale = norm_rows(retained, gain_heads, 0.01)
    norm_flat = normed_out.reshape(seq_count, stretch_len, v_local)
    gate_act = jax.nn.silu(gate_pre)
    gated = (gate_act * norm_flat).astype(jnp.bfloat16)
    middle = x_share + branch_sum(product("btv,vd->btd", gated, wo_all))
    h2_share, ln2_normed, ln2_scale = norm_rows(middle, ln2_gain)
    h_two = share_gather(h2_share.astype(jnp.bfloat16))
    w1_all, w3_all, w2_all = mlp_fetch(w_fc_gate, w_fc_up, w_fc_down)
    fc_a = product("btd,df->btf", h_two, w1_all)
    fc_b = product("btd,df->btf", h_two, w3_all)
    silu_a = jax.nn.silu(fc_a)
    hidden = (silu_a * fc_b).astype(jnp.bfloat16)
    output = (middle + branch_sum(product("btf,fd->btd", hidden, w2_all))).astype(jnp.bfloat16)
    wq_all, wk_all, wv_all, wg_all, wo_all = mixer_fetch(w_query, w_key, w_value, w_gate, w_out)
    w1_all, w3_all, w2_all = mlp_fetch(w_fc_gate, w_fc_up, w_fc_down)
    cot_full = share_gather(cotangent)
    d_hidden = product("btd,fd->btf", cot_full, w2_all)
    g_down = product("btf,btd->fd", hidden, cot_full)
    d_fca = (d_hidden * fc_b * swish_slope(fc_a)).astype(jnp.bfloat16)
    d_fcb = (d_hidden * silu_a).astype(jnp.bfloat16)
    g_fc_gate = product("btd,btf->df", h_two, d_fca)
    g_fc_up = product("btd,btf->df", h_two, d_fcb)
    d_h2 = input_sum(product("btf,df->btd", d_fca, w1_all) + product("btf,df->btd", d_fcb, w3_all))
    d_middle = cotangent.astype(jnp.float32) + norm_back(d_h2, ln2_normed, ln2_scale, ln2_gain)
    g_ln2 = jnp.sum(d_h2 * ln2_normed, axis=(0, 1))
    d_branch = share_gather(d_middle.astype(jnp.bfloat16))
    d_gated = product("btd,vd->btv", d_branch, wo_all)
    g_out = product("btv,btd->vd", gated, d_branch)
    d_gate = (d_gated * norm_flat * swish_slope(gate_pre)).astype(jnp.bfloat16)
    d_normed = (d_gated * gate_act).reshape(seq_count, stretch_len, heads_here, v_width)
    g_norm = jnp.sum(d_normed * gn_normed, axis=(0, 1)).reshape(v_local)
    d_retained = norm_back(d_normed, gn_normed, gn_scale, gain_heads)
    d_scores = careful("bthe,bshe->bhts", d_retained, values_full) * weights_mask
    d_values = careful("bhts,bthe->bshe", scores, d_retained)
    d_query = careful("bhts,bshd->bthd", d_scores, keys_full)
    d_query = d_query + inflow[..., None] * careful("bthe,bhde->bthd", d_retained, state_in)
    d_keys = careful("bhts,bthd->bshd", d_scores, query_full)
    leaving = careful("bthd,bth,bthe->bhde", query_full, inflow, d_retained)
    state_grad = carried_in((carry_decay, leaving), CONTEXT, compose, identity)[1]
    d_keys = d_keys + outflow[..., None] * careful("bshe,bhde->bshd", values_full, state_grad)
    d_values = d_values + outflow[..., None] * careful("bshd,bhde->bshe", keys_full, state_grad)
    dq_low = (
        (d_query * 0.0625)
        .reshape(seq_count, stretch_len, heads_here * qk_width)
        .astype(jnp.bfloat16)
    )
    dk_low = d_keys.reshape(seq_count, stretch_len, heads_here * qk_width).astype(jnp.bfloat16)
    dv_low = d_values.reshape(seq_count, stretch_len, v_local).astype(jnp.bfloat16)
    g_query = product("btd,btq->dq", h_one, dq_low)
    g_key = product("btd,btq->dq", h_one, dk_low)
    g_value = product("btd,btv->dv", h_one, dv_low)
    g_gate = product("btd,btv->dv", h_one, d_gate)
    d_h1 = product("btq,dq->btd", dq_low, wq_all) + product("btq,dq->btd", dk_low, wk_all)
    d_h1 = d_h1 + product("btv,dv->btd", dv_low, wv_all) + product("btv,dv->btd", d_gate, wg_all)
    d_h1 = input_sum(d_h1)
    grad_tokens = d_middle + norm_back(d_h1, ln1_normed, ln1_scale, ln1_gain)
    g_ln1 = jnp.sum(d_h1 * ln1_normed, axis=(0, 1))
    tensor_place = lax.axis_index(TENSOR)
    norm_full = lax.dynamic_update_slice(
        jnp.zeros((v_local * lax.axis_size(TENSOR),), jnp.float32),
        g_norm,
        (tensor_place * v_local,),
    )
    g_ln1, g_ln2, norm_full = lax.psum((g_ln1, g_ln2, norm_full), (FSDP, CONTEXT, TENSOR))
    g_norm = lax.dynamic_slice_in_dim(norm_full, tensor_place * v_local, v_local)
    weight_grads = (g_query, g_key, g_value, g_gate, g_out, g_fc_gate, g_fc_up, g_down)
    summed = (
        lax.psum(weight_grads[0].astype(jnp.bfloat16), CONTEXT).astype(jnp.float32),
        lax.psum(weight_grads[1].astype(jnp.bfloat16), CONTEXT).astype(jnp.float32),
        lax.psum(weight_grads[2].astype(jnp.bfloat16), CONTEXT).astype(jnp.float32),
        lax.psum(weight_grads[3].astype(jnp.bfloat16), CONTEXT).astype(jnp.float32),
        lax.psum(weight_grads[4].astype(jnp.bfloat16), CONTEXT).astype(jnp.float32),
        lax.psum(weight_grads[5].astype(jnp.bfloat16), CONTEXT).astype(jnp.float32),
        lax.psum(weight_grads[6].astype(jnp.bfloat16), CONTEXT).astype(jnp.float32),
        lax.psum(weight_grads[7].astype(jnp.bfloat16), CONTEXT).astype(jnp.float32),
    )
    shards = (
        lax.psum_scatter(
            summed[0].astype(jnp.bfloat16), FSDP, scatter_dimension=0, tiled=True
        ).astype(jnp.float32),
        lax.psum_scatter(
            summed[1].astype(jnp.bfloat16), FSDP, scatter_dimension=0, tiled=True
        ).astype(jnp.float32),
        lax.psum_scatter(
            summed[2].astype(jnp.bfloat16), FSDP, scatter_dimension=0, tiled=True
        ).astype(jnp.float32),
        lax.psum_scatter(
            summed[3].astype(jnp.bfloat16), FSDP, scatter_dimension=0, tiled=True
        ).astype(jnp.float32),
        lax.psum_scatter(
            summed[4].astype(jnp.bfloat16), FSDP, scatter_dimension=1, tiled=True
        ).astype(jnp.float32),
        lax.psum_scatter(
            summed[5].astype(jnp.bfloat16), FSDP, scatter_dimension=0, tiled=True
        ).astype(jnp.float32),
        lax.psum_scatter(
            summed[6].astype(jnp.bfloat16), FSDP, scatter_dimension=0, tiled=True
        ).astype(jnp.float32),
        lax.psum_scatter(
            summed[7].astype(jnp.bfloat16), FSDP, scatter_dimension=1, tiled=True
        ).astype(jnp.float32),
    )
    return (
        output,
        grad_tokens,
        g_ln1,
        shards[0],
        shards[1],
        shards[2],
        shards[3],
        g_norm,
        shards[4],
        g_ln2,
        shards[5],
        shards[6],
        shards[7],
    )


F32 = jnp.float32
BF16 = jnp.bfloat16
BOTH_X = [(0, 2), (2, 0), (1, 3), (3, 1)]
UP_X = [(0, 2), (1, 3)]
DOWN_X = [(2, 0), (3, 1)]
CORES = [(0, 1), (1, 0), (2, 3), (3, 2)]
UP_Z = [[(0, 1), (1, 2), (2, 3)], [(1, 2), (2, 3)], [(2, 3)]]
SCALE = 0.0625
ROWS, GAINS, STATES = range(3)
DOWN_Z = [[(3, 2), (2, 1), (1, 0)], [(2, 1), (1, 0)], [(1, 0)]]


def over_x(value):
    return lax.ppermute(value, CONTEXT, BOTH_X)


def over_core(value):
    return lax.ppermute(value, CONTEXT, CORES)


def over_y(value):
    return lax.ppermute(value, TENSOR, [(0, 1), (1, 0)])


def tie(*values):
    return lax.optimization_barrier(values)


def butterfly(value, axis):
    size = lax.axis_size(axis)
    step = 1
    while step < size:
        value = value + lax.ppermute(value, axis, [(i, i ^ step) for i in range(size)])
        step *= 2
    return value


def quarter_of(weight, dim, index):
    size = weight.shape[dim] // 4
    return lax.dynamic_slice_in_dim(weight, index * size, size, dim)


def assemble_kernel(spot_ref, *refs):
    at = pl.program_id(0)
    for index, block in enumerate(refs[:8]):

        @pl.when(at == index)
        def _(block=block):
            refs[8][...] = block[...]


def assemble(blocks, spots, by_rows):
    size = blocks[0].shape[0]
    shape = (2 * size, 4 * size) if by_rows else (4 * size, 2 * size)

    def spot(at, spots_ref):
        z_from, x_from = spots_ref[at % 4], spots_ref[4 + at // 4]
        return (x_from, z_from) if by_rows else (z_from, x_from)

    return pl.pallas_call(
        assemble_kernel,
        out_shape=jax.ShapeDtypeStruct(shape, blocks[0].dtype),
        grid_spec=pltpu.PrefetchScalarGridSpec(
            num_scalar_prefetch=1,
            grid=(8,),
            in_specs=[pl.BlockSpec((size, size), lambda at, spots_ref: (0, 0))] * 8,
            out_specs=pl.BlockSpec((size, size), spot),
        ),
        compiler_params=pltpu.CompilerParams(vmem_limit_bytes=32 << 20),
        cost_estimate=pl.CostEstimate(flops=0, transcendentals=0, bytes_accessed=32 * size * size),
    )(spots, *blocks)


def nn(left, right):
    return lax.dot_general(left, right, (((1,), (0,)), ((), ())), preferred_element_type=F32)


def nt(left, right):
    return lax.dot_general(left, right, (((1,), (1,)), ((), ())), preferred_element_type=F32)


def tn(left, right):
    return lax.dot_general(left, right, (((0,), (0,)), ((), ())), preferred_element_type=F32)


def where_is(whole, chunk, piece_len):
    share_len = piece_len // 2
    spots = []
    for shape, dim in (((piece_len, 1), 0), ((1, piece_len), 1)):
        at = lax.broadcasted_iota(jnp.int32, shape, dim) + whole[2] * share_len
        spots.append(jnp.where(at >= piece_len, at - piece_len, at))
    start = whole[0] * (2 * piece_len) + chunk * piece_len
    return spots[0], spots[1], start


def document(whole, spot):
    seq = pl.program_id(0)
    first, second = whole[3 + 2 * seq], whole[4 + 2 * seq]
    return jnp.where(spot >= second, 2, jnp.where(spot >= first, 1, 0))


def fade(gap, log_keep):
    return jnp.exp(jnp.maximum(gap, 0).astype(F32) * log_keep)


def piece_terms(whole, log_keep, chunk, piece_len):
    rows, cols, start = where_is(whole, chunk, piece_len)
    doc_rows, doc_cols = document(whole, start + rows), document(whole, start + cols)
    before, last = document(whole, start - 1), document(whole, start + piece_len - 1)
    within = jnp.where(
        (rows >= cols) & (doc_rows == doc_cols), fade(rows - cols, log_keep) * SCALE, 0.0
    )
    inflow = jnp.where(doc_rows == before, fade(rows + 1, log_keep) * SCALE, 0.0)
    outflow = jnp.where(doc_rows == last, fade(piece_len - 1 - rows, log_keep), 0.0)
    whole_gap = jnp.full((1, 1), piece_len, jnp.int32)
    over = jnp.where(before == last, fade(whole_gap, log_keep), 0.0)
    return within, inflow, outflow, over


def piece_of(ref, whole, chunk):
    group = lax.rem(chunk + whole[1], 2) * 2
    value = ref[pl.ds(group, 2), 0]
    return value.reshape(value.shape[0] * value.shape[1], value.shape[2])


def put_piece(ref, whole, chunk, value):
    group = lax.rem(chunk + whole[1], 2) * 2
    ref[pl.ds(group, 2), 0] = value.astype(ref.dtype).reshape(2, value.shape[0] // 2, value.shape[1])


def split_kq(ref, whole, chunk):
    both = piece_of(ref, whole, chunk)
    width = both.shape[1] // 2
    return both[:, :width], both[:, width:]


def update_kernel(whole, keeps, kq_ref, v_ref, out_ref):
    log_keep = keeps[pl.program_id(1)]
    piece_len = 2 * kq_ref.shape[2]
    total = jnp.zeros(out_ref.shape[2:], F32)
    for chunk in range(2):
        rows, _, start = where_is(whole, chunk, piece_len)
        last = document(whole, whole[0] * (2 * piece_len) + 2 * piece_len - 1)
        gap = (2 - chunk) * piece_len - 1 - rows
        weight = jnp.where(document(whole, start + rows) == last, fade(gap, log_keep), 0.0)
        keys, _ = split_kq(kq_ref, whole, chunk)
        values = piece_of(v_ref, whole, chunk)
        total = total + tn((keys.astype(F32) * weight).astype(BF16), values)
    out_ref[0, 0] = total.astype(BF16)


def next_state(state, keys, values, outflow, over):
    return over * state + tn((keys.astype(F32) * outflow).astype(BF16), values)


def forward_kernel(
    whole, keeps, kq_ref, v_ref, gate_ref, state_ref, gain_ref, gated_ref, retained_ref
):
    log_keep = keeps[pl.program_id(1)]
    piece_len = 2 * kq_ref.shape[2]
    state = state_ref[0, 0].astype(F32)
    for chunk in range(2):
        within, inflow, outflow, over = piece_terms(whole, log_keep, chunk, piece_len)
        keys, query = split_kq(kq_ref, whole, chunk)
        values = piece_of(v_ref, whole, chunk)
        scores = (nt(query, keys) * within).astype(BF16)
        retained = nn(scores, values) + inflow * nn(query, state.astype(BF16))
        if chunk == 0:
            state = next_state(state, keys, values, outflow, over)
        put_piece(retained_ref, whole, chunk, retained)
        normed, _, _ = norm_rows(retained, gain_ref[0], 0.01)
        gate = piece_of(gate_ref, whole, chunk).astype(F32)
        put_piece(gated_ref, whole, chunk, gate * jax.nn.sigmoid(gate) * normed)


def norm_back_kernel(
    whole,
    keeps,
    d_gated_ref,
    gate_ref,
    retained_ref,
    kq_ref,
    gain_ref,
    d_gate_ref,
    d_retained_ref,
    d_gain_ref,
    leaving_ref,
):
    log_keep = keeps[pl.program_id(1)]
    piece_len = 2 * kq_ref.shape[2]
    total = jnp.zeros(leaving_ref.shape[2:], F32)
    gain = gain_ref[0]
    d_gain = jnp.zeros(gain.shape, F32)
    for chunk in range(2):
        rows, _, start = where_is(whole, chunk, piece_len)
        before = document(whole, whole[0] * (2 * piece_len) - 1)
        gap = chunk * piece_len + rows + 1
        weight = jnp.where(
            document(whole, start + rows) == before, fade(gap, log_keep) * SCALE, 0.0
        )
        _, query = split_kq(kq_ref, whole, chunk)
        retained = piece_of(retained_ref, whole, chunk).astype(F32)
        normed, unit, scale = norm_rows(retained, gain, 0.01)
        gate = piece_of(gate_ref, whole, chunk).astype(F32)
        d_gated = piece_of(d_gated_ref, whole, chunk).astype(F32)
        sigma = jax.nn.sigmoid(gate)
        put_piece(
            d_gate_ref, whole, chunk, d_gated * normed * sigma * (1.0 + gate * (1.0 - sigma))
        )
        d_normed = d_gated * gate * sigma
        d_gain = d_gain + jnp.sum(d_normed * unit, axis=0, keepdims=True)
        d_retained = norm_back(d_normed, unit, scale, gain)
        put_piece(d_retained_ref, whole, chunk, d_retained)
        total = total + tn(query, (d_retained * weight).astype(BF16))
    d_gain_ref[0, 0] = d_gain
    leaving_ref[0, 0] = total.astype(BF16)


def backward_kernel(
    whole, keeps, kq_ref, v_ref, d_retained_ref, state_ref, d_state_ref, d_kq_ref, d_v_ref
):
    log_keep = keeps[pl.program_id(1)]
    piece_len = 2 * kq_ref.shape[2]
    terms = [piece_terms(whole, log_keep, chunk, piece_len) for chunk in range(2)]
    state = state_ref[0, 0].astype(F32)
    keys, _ = split_kq(kq_ref, whole, 0)
    _, _, outflow, over = terms[0]
    states = [state, next_state(state, keys, piece_of(v_ref, whole, 0), outflow, over)]
    d_state = d_state_ref[0, 0].astype(F32)
    for chunk in (1, 0):
        within, inflow, outflow, over = terms[chunk]
        keys, query = split_kq(kq_ref, whole, chunk)
        values = piece_of(v_ref, whole, chunk)
        d_ret = piece_of(d_retained_ref, whole, chunk)
        state_low, d_state_low = states[chunk].astype(BF16), d_state.astype(BF16)
        scores = (nt(query, keys) * within).astype(BF16)
        d_scores = (nt(d_ret, values) * within).astype(BF16)
        d_values = tn(scores, d_ret) + outflow * nn(keys, d_state_low)
        put_piece(d_v_ref, whole, chunk, d_values)
        d_query = nn(d_scores, keys) + inflow * nt(d_ret, state_low)
        d_keys = tn(d_scores, query) + outflow * nt(values, d_state_low)
        put_piece(d_kq_ref, whole, chunk, jnp.concatenate([d_keys, d_query], axis=1))
        if chunk == 1:
            entering = tn(query, (d_ret.astype(F32) * inflow).astype(BF16))
            d_state = over * d_state + entering


def per_head(kernel, scalars, blocks, outs, flops):
    def spec(array, kind):
        if kind == ROWS:
            width = array.shape[3] // heads
            return pl.BlockSpec((4, 1, array.shape[2], width), lambda b, h, *_: (0, b, 0, h))
        if kind == GAINS:
            return pl.BlockSpec((1, *array.shape[1:]), lambda b, h, *_: (h, 0, 0))
        return pl.BlockSpec((1, 1, *array.shape[2:]), lambda b, h, *_: (b, h, 0, 0))

    heads = scalars[1].shape[0]
    seq_count = (scalars[0].shape[0] - 3) // 2
    moved = sum(a.size * a.dtype.itemsize for a, _ in (*blocks, *outs))
    return pl.pallas_call(
        kernel,
        out_shape=[a for a, _ in outs],
        grid_spec=pltpu.PrefetchScalarGridSpec(
            num_scalar_prefetch=2,
            grid=(seq_count, heads),
            in_specs=[spec(*block) for block in blocks],
            out_specs=[spec(*out) for out in outs],
        ),
        compiler_params=pltpu.CompilerParams(vmem_limit_bytes=56 << 20),
        cost_estimate=pl.CostEstimate(flops=flops, transcendentals=0, bytes_accessed=moved),
    )(*scalars, *(a for a, _ in blocks))


def both_quarters(mine, across, first, dim):
    return jnp.concatenate(
        [jnp.where(first, mine, across), jnp.where(first, across, mine)], axis=dim
    )


def paired_body(
    tokens,
    segments,
    forget,
    ln1_gain,
    w_query,
    w_key,
    w_value,
    w_gate,
    norm_gain,
    w_out,
    ln2_gain,
    w_fc_gate,
    w_fc_up,
    w_fc_down,
    cotangent,
):
    place = lax.axis_index(CONTEXT)
    x_at, core, y_at = place // 2, place % 2, lax.axis_index(TENSOR)
    z_at = lax.axis_index(FSDP)
    heads = forget.shape[0] // 2
    qk_width = w_query.shape[1] // forget.shape[0]
    v_width = w_value.shape[1] // forget.shape[0]
    width = tokens.shape[2]
    seq_count, share_len = tokens.shape[0], tokens.shape[1]
    share_rows = seq_count * share_len
    piece_len = 2 * share_len
    chip_len = 2 * piece_len
    v_half = heads * v_width
    forget_half = lax.dynamic_slice_in_dim(forget, core * heads, heads)
    gain_half = lax.dynamic_slice_in_dim(norm_gain, core * v_half, v_half)

    def part(array, first, last):
        return array[first * share_rows : last * share_rows]

    def unit(x_index):
        q = core * 2 + x_index
        key_query = [quarter_of(w_key, 1, q), quarter_of(w_query, 1, q)]
        return [
            jnp.concatenate(key_query, axis=1),
            quarter_of(w_value, 1, q),
            quarter_of(w_gate, 1, q),
            quarter_of(w_out, 0, q),
            quarter_of(w_fc_down, 0, q),
            quarter_of(w_fc_gate, 1, q),
            quarter_of(w_fc_up, 1, q),
        ]

    KQ, V, G, O, W2, W1, W3 = range(7)
    by_rows = [False, False, False, True, True, False, False]
    own, sibling = unit(x_at), unit(1 - x_at)
    z_last = lax.axis_size(FSDP) - 1
    s_one = jnp.where(z_at == 0, 1, z_at - 1)
    s_three = jnp.where(z_at == z_last, 0, jnp.where(z_at == 1, 2, z_last))
    spots = jnp.stack([z_at, s_one, z_at ^ 2, s_three, x_at, 1 - x_at]).astype(jnp.int32)
    slots = [[None] * 3 for _ in range(7)]
    across = [[None] * 3 for _ in range(7)]

    def weight(index):
        blocks = [own[index], *slots[index], sibling[index], *across[index]]
        return assemble(blocks, spots, by_rows[index])

    env = SimpleNamespace()
    firsts = jnp.sum((segments == 0).astype(jnp.int32), axis=1)
    seconds = jnp.sum((segments <= 1).astype(jnp.int32), axis=1)
    starts = jnp.stack([firsts, seconds], axis=1).reshape(-1)
    whole = jnp.concatenate([jnp.stack([x_at, core, y_at]).astype(jnp.int32), starts])
    scalars = (whole, jnp.log(1.0 - forget_half))
    gains = gain_half.reshape(heads, 1, v_width)
    state_type = jax.ShapeDtypeStruct((seq_count, heads, qk_width, v_width), BF16)
    rows_type = jax.ShapeDtypeStruct((4, seq_count, share_len, v_half), BF16)
    kq_type = jax.ShapeDtypeStruct((4, seq_count, share_len, 2 * heads * qk_width), BF16)
    gain_type = jax.ShapeDtypeStruct((seq_count, heads, 1, v_width), F32)
    pair_flops = seq_count * heads * chip_len * qk_width * v_width * 2

    def shaped(rows_in):
        return rows_in.reshape(4, seq_count, share_len, -1)

    def flat(rows_in):
        return rows_in.reshape(4 * share_rows, -1)

    x_share = tokens.reshape(share_rows, width).astype(F32)
    cot_share = cotangent.reshape(share_rows, width)

    def work_norm():
        h1, ln1_normed, ln1_scale = norm_rows(x_share, ln1_gain)
        env.ln1 = (ln1_normed, ln1_scale)
        env.h = h1.astype(BF16)
        env.hy = over_y(env.h)
        return ["h"]

    def work_core():
        env.hc, env.hcy = over_core(env.h), over_core(env.hy)
        env.cy = over_y(cot_share)
        return []

    def work_rows():
        env.h_one = jnp.concatenate([env.h, env.hy, env.hc, env.hcy], axis=0)
        env.wkq = weight(KQ)
        return ["h_one", "wkq"]

    def work_kq():
        env.kq = nn(env.h_one, env.wkq).astype(BF16)
        env.wv = weight(V)
        return ["kq", "wv"]

    def work_v():
        env.v = nn(env.h_one, env.wv).astype(BF16)
        return ["v"]

    def work_state():
        (update,) = per_head(
            update_kernel,
            scalars,
            [(shaped(env.kq), ROWS), (shaped(env.v), ROWS)],
            [(state_type, STATES)],
            pair_flops,
        )
        env.state = lax.ppermute(update, CONTEXT, UP_X)
        env.wg = weight(G)
        env.cc, env.ccy = over_core(cot_share), over_core(env.cy)
        return ["wg"]

    def work_gate():
        env.gate = nn(env.h_one, env.wg).astype(BF16)
        env.wo = weight(O)
        return ["gate", "wo"]

    def work_retained():
        gated, env.retained = per_head(
            forward_kernel,
            scalars,
            [
                (shaped(env.kq), ROWS),
                (shaped(env.v), ROWS),
                (shaped(env.gate), ROWS),
                (env.state, STATES),
                (gains, GAINS),
            ],
            [(rows_type, ROWS), (rows_type, ROWS)],
            5 * pair_flops,
        )
        env.gated = flat(gated)
        return ["gated", "retained"]

    def work_out_far():
        env.far = over_core(nn(part(env.gated, 2, 4), env.wo).astype(BF16))
        return []

    def work_out_near():
        far_other = env.far[share_rows:].astype(F32)
        near = nn(part(env.gated, 1, 2), env.wo) + far_other
        env.near = over_y(near.astype(BF16))
        own_sum = nn(part(env.gated, 0, 1), env.wo) + x_share
        env.own = own_sum + env.far[:share_rows].astype(F32)
        return ["own"]

    def work_cot():
        env.cot = jnp.concatenate([cot_share, env.cy, env.cc, env.ccy], axis=0)
        env.w2 = weight(W2)
        return ["cot", "w2"]

    def work_d_hidden():
        env.d_hidden = nt(env.cot, env.w2)
        return ["d_hidden"]

    def work_middle():
        env.middle = env.own + env.near.astype(F32)
        h2, ln2_normed, ln2_scale = norm_rows(env.middle, ln2_gain)
        env.ln2 = (ln2_normed, ln2_scale)
        env.h2 = h2.astype(BF16)
        env.h2y, env.h2c = over_y(env.h2), over_core(env.h2)
        env.w1 = weight(W1)
        return ["h2", "w1", "middle"]

    def work_h2():
        env.h2cy = over_core(env.h2y)
        env.w3 = weight(W3)
        return ["w3"]

    plan = {
        0: [work_norm],
        5: [work_core],
        6: [work_rows],
        7: [work_kq],
        8: [work_v],
        9: [work_state],
        13: [work_gate],
        14: [work_retained],
        15: [work_out_far],
        16: [work_out_near],
        18: [work_cot],
        19: [work_d_hidden],
        21: [work_middle],
        23: [work_h2],
    }
    up, down, keep_down, to_send = None, None, None, None
    for tick in range(24):
        index, hop = divmod(tick, 3)
        received = []
        if to_send is not None:
            which, slot, value = to_send
            slots[which][slot] = value
            across[which][slot] = over_x(value)
        sent = to_send
        to_send = None
        if index < 7:
            if hop == 0:
                up, down = own[index], own[index]
            up = lax.ppermute(up, FSDP, UP_Z[hop])
            down = lax.ppermute(down, FSDP, DOWN_Z[hop])
        names = []
        for work in plan.get(tick, []):
            names += work()
        held = [getattr(env, name) for name in names]
        if sent is not None:
            held.append(across[sent[0]][sent[1]])
        if index < 7:
            held += [up, down] + ([keep_down] if hop else [])
        elif not held:
            continue
        held = list(tie(*held, *own[index + 1 : index + 2]))
        if index + 1 < 7:
            own[index + 1] = held.pop()
        if index < 7:
            if hop:
                keep_down = held.pop()
            down, up = held.pop(), held.pop()
        if sent is not None:
            across[sent[0]][sent[1]] = held.pop()
        for name, value in zip(names, held, strict=True):
            setattr(env, name, value)
        if index < 7:
            if hop == 0:
                keep_down = down
                to_send = (index, 0, jnp.where(z_at > 0, up, down))
            elif hop == 1:
                to_send = (index, 1, jnp.where(z_at >= 2, up, down))
            else:
                middle_slot = jnp.where(z_at == 0, down, keep_down)
                to_send = (index, 2, jnp.where(z_at == z_last, up, middle_slot))

    h_one, gated, gate_pre = env.h_one, env.gated, env.gate
    wkq, wv, wg, wo, w1, w2, w3 = env.wkq, env.wv, env.wg, env.wo, env.w1, env.w2, env.w3
    cot_full, d_hidden, middle = env.cot, env.d_hidden, env.middle

    token = [h_one]

    def step(run, *args):
        *args, _ = tie(*args, token[0])
        out = run(*args)
        token[0] = out[0] if isinstance(out, tuple) else out
        return out

    def columns(array, index):
        size = array.shape[1] // 2
        return lax.dynamic_slice_in_dim(array, index * size, size, 1)

    def theirs(left, right, rows):
        if rows:
            return tn(columns(left, 1 - x_at), right).astype(BF16)
        return tn(left, columns(right, 1 - x_at)).astype(BF16)

    def ours(left, right, got, rows):
        if rows:
            total = tn(columns(left, x_at), right)
        else:
            total = tn(left, columns(right, x_at))
        total = (total + got.astype(F32)).astype(BF16)
        return total

    def scatter(total, rows):
        dim = int(rows)
        size = total.shape[dim] // (z_last + 1)
        count = z_last + 1

        def block(index):
            return lax.dynamic_slice_in_dim(total, index * size, size, dim)

        blocks = [block(z_at)]
        for hop in range(1, count):
            pairs = [(i, (i + hop) % count) for i in range(count)]
            blocks.append(lax.ppermute(block((z_at + hop) % count), FSDP, pairs))
        return blocks

    def gather_sum(*blocks):
        return sum(b.astype(F32) for b in blocks).astype(BF16)

    def finish(mine, rows):
        dim = 1 - int(rows)
        beside = over_x(mine)
        both = both_quarters(mine, beside, x_at == 0, dim)
        other = over_core(both)
        return both_quarters(both, other, core == 0, dim).astype(F32)

    def activate(h_two, d_hidden, w1, w3):
        fc_a, fc_b = nn(h_two, w1), nn(h_two, w3)
        silu_a = jax.nn.silu(fc_a)
        hidden = (silu_a * fc_b).astype(BF16)
        d_fca = (d_hidden * fc_b * swish_slope(fc_a)).astype(BF16)
        d_fcb = (d_hidden * silu_a).astype(BF16)
        return hidden, d_fca, d_fcb

    h_two = jnp.concatenate([env.h2, env.h2y, env.h2c, env.h2cy], axis=0)
    hidden, d_fca, d_fcb = step(activate, h_two, d_hidden, w1, w3)

    def d_h2_terms(a, b, d_fca, d_fcb):
        return nt(part(d_fca, a, b), w1) + nt(part(d_fcb, a, b), w3)

    far = step(lambda a, b: d_h2_terms(2, 4, a, b).astype(BF16), d_fca, d_fcb)
    far = over_core(far)
    down_theirs = step(partial(theirs, rows=True), hidden, cot_full)
    down_got = over_x(down_theirs)
    near = step(
        lambda a, b, c: (d_h2_terms(1, 2, a, b) + c[share_rows:].astype(F32)).astype(BF16),
        d_fca,
        d_fcb,
        far,
    )
    near = over_y(near)
    own_part = step(
        lambda a, b, c: d_h2_terms(0, 1, a, b) + c[:share_rows].astype(F32), d_fca, d_fcb, far
    )
    gate_theirs = step(partial(theirs, rows=False), h_two, d_fca)
    up_theirs = step(partial(theirs, rows=False), h_two, d_fcb)
    out_far = over_core(step(lambda a, b: nn(part(a, 2, 4), b).astype(BF16), hidden, w2))
    down_total = step(partial(ours, rows=True), hidden, cot_full, down_got)
    down_mine = scatter(down_total, True)
    gate_theirs, _ = tie(gate_theirs, down_got)
    gate_got = over_x(gate_theirs)

    def middle_back(own_part, near):
        d_h2 = own_part + near.astype(F32)
        ln2_normed, ln2_scale = env.ln2
        d_middle = cot_share.astype(F32) + norm_back(d_h2, ln2_normed, ln2_scale, ln2_gain)
        return d_middle.astype(BF16), d_middle, jnp.sum(d_h2 * ln2_normed, axis=0)

    d_mid_low, d_middle, g_ln2 = step(middle_back, own_part, near)
    d_mid_y, d_mid_c = over_y(d_mid_low), over_core(d_mid_low)
    gate_total = step(partial(ours, rows=False), h_two, d_fca, gate_got)
    gate_mine = scatter(gate_total, False)
    up_theirs, _ = tie(up_theirs, gate_got)
    up_got = over_x(up_theirs)
    d_mid_y, _ = tie(d_mid_y, gate_total)
    d_mid_cy = over_core(d_mid_y)

    def gate_back(share, y, c, cy):
        d_branch = jnp.concatenate([share, y, c, cy], axis=0)
        return nt(d_branch, wo).astype(BF16), d_branch

    d_gated, d_branch = step(gate_back, d_mid_low, d_mid_y, d_mid_c, d_mid_cy)
    kq, values, state_in = shaped(env.kq), shaped(env.v), env.state

    def retained_back(d_gated, kq):
        return per_head(
            norm_back_kernel,
            scalars,
            [
                (shaped(d_gated), ROWS),
                (shaped(gate_pre), ROWS),
                (env.retained, ROWS),
                (kq, ROWS),
                (gains, GAINS),
            ],
            [(rows_type, ROWS), (rows_type, ROWS), (gain_type, STATES), (state_type, STATES)],
            pair_flops,
        )

    d_gate, d_retained, g_norm, leaving = step(retained_back, d_gated, kq)
    d_gate = flat(d_gate)
    g_norm = jnp.sum(g_norm, axis=0).reshape(v_half)
    state_grad = lax.ppermute(leaving, CONTEXT, DOWN_X)
    up_total = step(partial(ours, rows=False), h_two, d_fcb, up_got)
    up_mine = scatter(up_total, False)
    down_mine = step(gather_sum, *down_mine)
    out_theirs = step(partial(theirs, rows=True), gated, d_branch)
    out_theirs, _ = tie(out_theirs, up_got)
    out_got = over_x(out_theirs)

    gg_theirs = step(partial(theirs, rows=False), h_one, d_gate)

    def pair_back(d_retained, state_grad):
        return per_head(
            backward_kernel,
            scalars,
            [
                (kq, ROWS),
                (values, ROWS),
                (d_retained, ROWS),
                (state_in, STATES),
                (state_grad, STATES),
            ],
            [(kq_type, ROWS), (rows_type, ROWS)],
            13 * pair_flops,
        )

    dkq_low, dv_low = step(pair_back, d_retained, state_grad)
    dkq_low, dv_low = flat(dkq_low), flat(dv_low)
    out_total = step(partial(ours, rows=True), gated, d_branch, out_got)
    out_mine = scatter(out_total, True)
    gate_mine = step(gather_sum, *gate_mine)
    gg_theirs, _ = tie(gg_theirs, out_got)
    gg_got = over_x(gg_theirs)

    def d_h1_terms(a, b, dkq, dv, dg):
        terms = nt(part(dkq, a, b), wkq)
        return terms + nt(part(dv, a, b), wv) + nt(part(dg, a, b), wg)

    far = step(lambda *d: d_h1_terms(2, 4, *d).astype(BF16), dkq_low, dv_low, d_gate)
    far = over_core(far)
    v_theirs = step(partial(theirs, rows=False), h_one, dv_low)
    near = step(
        lambda c, *d: (d_h1_terms(1, 2, *d) + c[share_rows:].astype(F32)).astype(BF16),
        far,
        dkq_low,
        dv_low,
        d_gate,
    )
    near = over_y(near)
    kq_theirs = step(partial(theirs, rows=False), h_one, dkq_low)
    gg_total = step(partial(ours, rows=False), h_one, d_gate, gg_got)
    gg_mine = scatter(gg_total, False)
    up_mine = step(gather_sum, *up_mine)
    v_theirs, _ = tie(v_theirs, gg_got)
    v_got = over_x(v_theirs)
    own_part = step(
        lambda c, *d: d_h1_terms(0, 1, *d) + c[:share_rows].astype(F32),
        far,
        dkq_low,
        dv_low,
        d_gate,
    )
    out_near = step(
        lambda a, b, c: (nn(part(a, 1, 2), b) + c[share_rows:].astype(F32)).astype(BF16),
        hidden,
        w2,
        out_far,
    )
    out_near, _ = tie(out_near, near)
    out_near = over_y(out_near)
    v_total = step(partial(ours, rows=False), h_one, dv_low, v_got)
    v_mine = scatter(v_total, False)
    out_mine = step(gather_sum, *out_mine)
    kq_theirs, _ = tie(kq_theirs, v_got)
    kq_got = over_x(kq_theirs)

    def tokens_back(own_part, near):
        d_h1 = own_part + near.astype(F32)
        ln1_normed, ln1_scale = env.ln1
        grad = d_middle + norm_back(d_h1, ln1_normed, ln1_scale, ln1_gain)
        return grad, jnp.sum(d_h1 * ln1_normed, axis=0)

    grad_tokens, g_ln1 = step(tokens_back, own_part, near)
    out_own = step(
        lambda a, b, c, d: nn(part(a, 0, 1), b) + c[:share_rows].astype(F32) + d,
        hidden,
        w2,
        out_far,
        middle,
    )
    kq_total = step(partial(ours, rows=False), h_one, dkq_low, kq_got)
    kq_mine = scatter(kq_total, False)
    gg_mine = step(gather_sum, *gg_mine)
    v_mine = step(gather_sum, *v_mine)
    kq_mine = step(gather_sum, *kq_mine)
    minis = down_mine, gate_mine, up_mine
    g_down, g_fc_gate, g_fc_up = finish(minis[0], True), finish(minis[1], False), finish(minis[2], False)
    g_out, g_gate, g_value = finish(out_mine, True), finish(gg_mine, False), finish(v_mine, False)
    g_kq = finish(kq_mine, False).reshape(w_key.shape[0], -1, 2, qk_width)
    g_key = g_kq[:, :, 0].reshape(w_key.shape)
    g_query = g_kq[:, :, 1].reshape(w_query.shape)
    output = (out_own + out_near.astype(F32)).astype(BF16)

    def all_sum(value):
        return butterfly(butterfly(butterfly(value, TENSOR), CONTEXT), FSDP)

    g_norm = g_norm + over_x(g_norm)
    g_norm = butterfly(g_norm, FSDP)
    g_norm = both_quarters(g_norm, over_core(g_norm), core == 0, 0)
    return (
        output.reshape(tokens.shape),
        grad_tokens.reshape(tokens.shape),
        all_sum(g_ln1),
        g_query,
        g_key,
        g_value,
        g_gate,
        g_norm,
        g_out,
        all_sum(g_ln2),
        g_fc_gate,
        g_fc_up,
        g_down,
    )


def body(tensor_size, *arrays):
    heads_here = arrays[2].shape[0]
    paired = tensor_size == 2 and heads_here % 2 == 0 and lax.axis_size(CONTEXT) == 4
    paired = paired and lax.axis_size(FSDP) == 4
    return (paired_body if paired else general_body)(*arrays)


def solution(mesh):
    in_specs = (
        P(FSDP, (CONTEXT, TENSOR), None),
        P(FSDP, None),
        P(TENSOR),
        P(),
        P(FSDP, TENSOR),
        P(FSDP, TENSOR),
        P(FSDP, TENSOR),
        P(FSDP, TENSOR),
        P(TENSOR),
        P(TENSOR, FSDP),
        P(),
        P(FSDP, TENSOR),
        P(FSDP, TENSOR),
        P(TENSOR, FSDP),
        P(FSDP, (CONTEXT, TENSOR), None),
    )
    out_specs = (
        P(FSDP, (CONTEXT, TENSOR), None),
        P(FSDP, (CONTEXT, TENSOR), None),
        P(),
        P(FSDP, TENSOR),
        P(FSDP, TENSOR),
        P(FSDP, TENSOR),
        P(FSDP, TENSOR),
        P(TENSOR),
        P(TENSOR, FSDP),
        P(),
        P(FSDP, TENSOR),
        P(FSDP, TENSOR),
        P(TENSOR, FSDP),
    )
    return jax.shard_map(partial(body, mesh.shape[TENSOR]), mesh=mesh, in_specs=in_specs, out_specs=out_specs, check_vma=False)
```

```python
from functools import partial
from types import SimpleNamespace

import jax
import jax.numpy as jnp
from jax import lax
from jax.experimental import pallas as pl
from jax.experimental.pallas import tpu as pltpu
from jax.sharding import PartitionSpec as P

FSDP, CONTEXT, TENSOR = "fsdp", "context", "tensor"

careful = partial(jnp.einsum, precision=lax.Precision.HIGH)


def entering(part, axis, combine, identity):
    place = lax.axis_index(axis)
    gathered = jax.tree.map(lambda a: lax.all_gather(a, axis), part)
    state = jax.tree.map(lambda a, e: jnp.zeros_like(a) + jnp.asarray(e, a.dtype), part, identity)

    def one(step, state):
        return combine(
            state, jax.tree.map(lambda a: lax.dynamic_index_in_dim(a, step, 0, False), gathered)
        )

    return lax.fori_loop(0, place, one, state)


def carried_in(value, axis, combine, identity):
    count, place = (lax.axis_size(axis), lax.axis_index(axis))
    everything = jax.tree.map(
        lambda part, kind: lax.all_gather(part.astype(kind), axis),
        value,
        jax.tree.map(lambda a: jnp.bfloat16 if a.dtype == jnp.float32 else a.dtype, value),
    )
    start = jax.tree.map(
        lambda part, zero: jnp.broadcast_to(jnp.asarray(zero, part.dtype), part.shape),
        value,
        identity,
    )

    def step(k, before):
        at = count - 1 - k
        reached = at > place
        new = combine(
            before, jax.tree.map(lambda part, own: part[at].astype(own.dtype), everything, value)
        )
        return jax.tree.map(lambda a, b: jnp.where(reached, a, b), new, before)

    return lax.fori_loop(0, count, step, start)


def norm_rows(values, gain_vec, epsilon=1e-05):
    centred = values - jnp.mean(values, axis=-1, keepdims=True)
    scale = lax.rsqrt(jnp.mean(centred * centred, axis=-1, keepdims=True) + epsilon)
    normed = centred * scale
    return (normed * gain_vec, normed, scale)


def norm_back(grad_in, normed, scale, gain_vec):
    d_normed = grad_in * gain_vec
    first_mean = jnp.mean(d_normed, axis=-1, keepdims=True)
    second_mean = jnp.mean(d_normed * normed, axis=-1, keepdims=True)
    return scale * (d_normed - first_mean - normed * second_mean)


def swish_slope(values):
    sigma = jax.nn.sigmoid(values)
    return sigma * (1.0 + values * (1.0 - sigma))


def compose(earlier, latter):
    return (earlier[0] * latter[0], latter[0][:, :, None, None] * earlier[1] + latter[1])


def share_gather(piece):
    return lax.all_gather(piece, TENSOR, axis=1, tiled=True)


def branch_sum(terms):
    return lax.psum_scatter(terms, TENSOR, scatter_dimension=1, tiled=True)


def input_sum(terms):
    return lax.psum_scatter(
        terms.astype(jnp.bfloat16), TENSOR, scatter_dimension=1, tiled=True
    ).astype(jnp.float32)


def mixer_fetch(w_query, w_key, w_value, w_gate, w_out):
    return (
        lax.all_gather(w_query, FSDP, axis=0, tiled=True),
        lax.all_gather(w_key, FSDP, axis=0, tiled=True),
        lax.all_gather(w_value, FSDP, axis=0, tiled=True),
        lax.all_gather(w_gate, FSDP, axis=0, tiled=True),
        lax.all_gather(w_out, FSDP, axis=1, tiled=True),
    )


def mlp_fetch(w_fc_gate, w_fc_up, w_fc_down):
    return (
        lax.all_gather(w_fc_gate, FSDP, axis=0, tiled=True),
        lax.all_gather(w_fc_up, FSDP, axis=0, tiled=True),
        lax.all_gather(w_fc_down, FSDP, axis=1, tiled=True),
    )


def product(form, left, right):
    return jnp.einsum(form, left, right, preferred_element_type=jnp.float32)


def general_body(
    tokens,
    segments,
    forget,
    ln1_gain,
    w_query,
    w_key,
    w_value,
    w_gate,
    norm_gain,
    w_out,
    ln2_gain,
    w_fc_gate,
    w_fc_up,
    w_fc_down,
    cotangent,
):
    heads_here = forget.shape[0]
    qk_width = w_query.shape[1] // heads_here
    v_width = w_value.shape[1] // heads_here
    v_local = heads_here * v_width
    gain_heads = norm_gain.reshape(heads_here, v_width)
    x_share = tokens.astype(jnp.float32)
    h1_share, ln1_normed, ln1_scale = norm_rows(x_share, ln1_gain)
    h_one = share_gather(h1_share.astype(jnp.bfloat16))
    wq_all, wk_all, wv_all, wg_all, wo_all = mixer_fetch(w_query, w_key, w_value, w_gate, w_out)
    seq_count, stretch_len = (h_one.shape[0], h_one.shape[1])
    query = product("btd,dq->btq", h_one, wq_all).astype(jnp.bfloat16)
    keys = product("btd,dq->btq", h_one, wk_all).astype(jnp.bfloat16)
    values = product("btd,dv->btv", h_one, wv_all).astype(jnp.bfloat16)
    gate_pre = product("btd,dv->btv", h_one, wg_all)
    query_heads = query.reshape(seq_count, stretch_len, heads_here, qk_width)
    keys_heads = keys.reshape(seq_count, stretch_len, heads_here, qk_width)
    query_full = query_heads.astype(jnp.float32) * 0.0625
    keys_full = keys_heads.astype(jnp.float32)
    values_full = values.astype(jnp.float32).reshape(seq_count, stretch_len, heads_here, v_width)
    log_keep = jnp.log(1.0 - forget)
    ctx_place = lax.axis_index(CONTEXT)
    seg_stretch = lax.dynamic_slice_in_dim(segments, ctx_place * stretch_len, stretch_len, 1)
    seg_prev = lax.dynamic_slice_in_dim(segments, jnp.maximum(ctx_place * stretch_len - 1, 0), 1, 1)
    live_mask = (seg_stretch == seg_prev).astype(jnp.float32)
    steps_idx = jnp.arange(stretch_len, dtype=jnp.float32)
    step_gap = jnp.maximum(steps_idx[:, None] - steps_idx[None, :], 0.0)
    causal = steps_idx[:, None] >= steps_idx[None, :]
    same_doc = (seg_stretch[:, :, None] == seg_stretch[:, None, :]) & causal[None]
    weights_mask = jnp.where(
        same_doc[:, None], jnp.exp(step_gap[None] * log_keep[:, None, None])[None], 0.0
    )
    inflow = live_mask[:, :, None] * jnp.exp((steps_idx[:, None] + 1.0) * log_keep[None, :])[None]
    outflow = (seg_stretch == seg_stretch[:, -1:]).astype(jnp.float32)[:, :, None] * jnp.exp(
        (stretch_len - 1.0 - steps_idx)[:, None] * log_keep[None, :]
    )[None]
    carry_decay = live_mask[:, -1:] * jnp.exp(stretch_len * log_keep)[None, :]
    update = careful("bshd,bsh,bshe->bhde", keys_full, outflow, values_full)
    identity = (jnp.ones_like(carry_decay), jnp.zeros_like(update))
    state_in = entering((carry_decay, update), CONTEXT, compose, identity)[1]
    scores = product("bthd,bshd->bhts", query_heads, keys_heads) * 0.0625 * weights_mask
    retained = careful("bhts,bshe->bthe", scores, values_full)
    retained = retained + inflow[..., None] * careful("bthd,bhde->bthe", query_full, state_in)
    normed_out, gn_normed, gn_scale = norm_rows(retained, gain_heads, 0.01)
    norm_flat = normed_out.reshape(seq_count, stretch_len, v_local)
    gate_act = jax.nn.silu(gate_pre)
    gated = (gate_act * norm_flat).astype(jnp.bfloat16)
    middle = x_share + branch_sum(product("btv,vd->btd", gated, wo_all))
    h2_share, ln2_normed, ln2_scale = norm_rows(middle, ln2_gain)
    h_two = share_gather(h2_share.astype(jnp.bfloat16))
    w1_all, w3_all, w2_all = mlp_fetch(w_fc_gate, w_fc_up, w_fc_down)
    fc_a = product("btd,df->btf", h_two, w1_all)
    fc_b = product("btd,df->btf", h_two, w3_all)
    silu_a = jax.nn.silu(fc_a)
    hidden = (silu_a * fc_b).astype(jnp.bfloat16)
    output = (middle + branch_sum(product("btf,fd->btd", hidden, w2_all))).astype(jnp.bfloat16)
    wq_all, wk_all, wv_all, wg_all, wo_all = mixer_fetch(w_query, w_key, w_value, w_gate, w_out)
    w1_all, w3_all, w2_all = mlp_fetch(w_fc_gate, w_fc_up, w_fc_down)
    cot_full = share_gather(cotangent)
    d_hidden = product("btd,fd->btf", cot_full, w2_all)
    g_down = product("btf,btd->fd", hidden, cot_full)
    d_fca = (d_hidden * fc_b * swish_slope(fc_a)).astype(jnp.bfloat16)
    d_fcb = (d_hidden * silu_a).astype(jnp.bfloat16)
    g_fc_gate = product("btd,btf->df", h_two, d_fca)
    g_fc_up = product("btd,btf->df", h_two, d_fcb)
    d_h2 = input_sum(product("btf,df->btd", d_fca, w1_all) + product("btf,df->btd", d_fcb, w3_all))
    d_middle = cotangent.astype(jnp.float32) + norm_back(d_h2, ln2_normed, ln2_scale, ln2_gain)
    g_ln2 = jnp.sum(d_h2 * ln2_normed, axis=(0, 1))
    d_branch = share_gather(d_middle.astype(jnp.bfloat16))
    d_gated = product("btd,vd->btv", d_branch, wo_all)
    g_out = product("btv,btd->vd", gated, d_branch)
    d_gate = (d_gated * norm_flat * swish_slope(gate_pre)).astype(jnp.bfloat16)
    d_normed = (d_gated * gate_act).reshape(seq_count, stretch_len, heads_here, v_width)
    g_norm = jnp.sum(d_normed * gn_normed, axis=(0, 1)).reshape(v_local)
    d_retained = norm_back(d_normed, gn_normed, gn_scale, gain_heads)
    d_scores = careful("bthe,bshe->bhts", d_retained, values_full) * weights_mask
    d_values = careful("bhts,bthe->bshe", scores, d_retained)
    d_query = careful("bhts,bshd->bthd", d_scores, keys_full)
    d_query = d_query + inflow[..., None] * careful("bthe,bhde->bthd", d_retained, state_in)
    d_keys = careful("bhts,bthd->bshd", d_scores, query_full)
    leaving = careful("bthd,bth,bthe->bhde", query_full, inflow, d_retained)
    state_grad = carried_in((carry_decay, leaving), CONTEXT, compose, identity)[1]
    d_keys = d_keys + outflow[..., None] * careful("bshe,bhde->bshd", values_full, state_grad)
    d_values = d_values + outflow[..., None] * careful("bshd,bhde->bshe", keys_full, state_grad)
    dq_low = (
        (d_query * 0.0625)
        .reshape(seq_count, stretch_len, heads_here * qk_width)
        .astype(jnp.bfloat16)
    )
    dk_low = d_keys.reshape(seq_count, stretch_len, heads_here * qk_width).astype(jnp.bfloat16)
    dv_low = d_values.reshape(seq_count, stretch_len, v_local).astype(jnp.bfloat16)
    g_query = product("btd,btq->dq", h_one, dq_low)
    g_key = product("btd,btq->dq", h_one, dk_low)
    g_value = product("btd,btv->dv", h_one, dv_low)
    g_gate = product("btd,btv->dv", h_one, d_gate)
    d_h1 = product("btq,dq->btd", dq_low, wq_all) + product("btq,dq->btd", dk_low, wk_all)
    d_h1 = d_h1 + product("btv,dv->btd", dv_low, wv_all) + product("btv,dv->btd", d_gate, wg_all)
    d_h1 = input_sum(d_h1)
    grad_tokens = d_middle + norm_back(d_h1, ln1_normed, ln1_scale, ln1_gain)
    g_ln1 = jnp.sum(d_h1 * ln1_normed, axis=(0, 1))
    tensor_place = lax.axis_index(TENSOR)
    norm_full = lax.dynamic_update_slice(
        jnp.zeros((v_local * lax.axis_size(TENSOR),), jnp.float32),
        g_norm,
        (tensor_place * v_local,),
    )
    g_ln1, g_ln2, norm_full = lax.psum((g_ln1, g_ln2, norm_full), (FSDP, CONTEXT, TENSOR))
    g_norm = lax.dynamic_slice_in_dim(norm_full, tensor_place * v_local, v_local)
    weight_grads = (g_query, g_key, g_value, g_gate, g_out, g_fc_gate, g_fc_up, g_down)
    summed = (
        lax.psum(weight_grads[0].astype(jnp.bfloat16), CONTEXT).astype(jnp.float32),
        lax.psum(weight_grads[1].astype(jnp.bfloat16), CONTEXT).astype(jnp.float32),
        lax.psum(weight_grads[2].astype(jnp.bfloat16), CONTEXT).astype(jnp.float32),
        lax.psum(weight_grads[3].astype(jnp.bfloat16), CONTEXT).astype(jnp.float32),
        lax.psum(weight_grads[4].astype(jnp.bfloat16), CONTEXT).astype(jnp.float32),
        lax.psum(weight_grads[5].astype(jnp.bfloat16), CONTEXT).astype(jnp.float32),
        lax.psum(weight_grads[6].astype(jnp.bfloat16), CONTEXT).astype(jnp.float32),
        lax.psum(weight_grads[7].astype(jnp.bfloat16), CONTEXT).astype(jnp.float32),
    )
    shards = (
        lax.psum_scatter(
            summed[0].astype(jnp.bfloat16), FSDP, scatter_dimension=0, tiled=True
        ).astype(jnp.float32),
        lax.psum_scatter(
            summed[1].astype(jnp.bfloat16), FSDP, scatter_dimension=0, tiled=True
        ).astype(jnp.float32),
        lax.psum_scatter(
            summed[2].astype(jnp.bfloat16), FSDP, scatter_dimension=0, tiled=True
        ).astype(jnp.float32),
        lax.psum_scatter(
            summed[3].astype(jnp.bfloat16), FSDP, scatter_dimension=0, tiled=True
        ).astype(jnp.float32),
        lax.psum_scatter(
            summed[4].astype(jnp.bfloat16), FSDP, scatter_dimension=1, tiled=True
        ).astype(jnp.float32),
        lax.psum_scatter(
            summed[5].astype(jnp.bfloat16), FSDP, scatter_dimension=0, tiled=True
        ).astype(jnp.float32),
        lax.psum_scatter(
            summed[6].astype(jnp.bfloat16), FSDP, scatter_dimension=0, tiled=True
        ).astype(jnp.float32),
        lax.psum_scatter(
            summed[7].astype(jnp.bfloat16), FSDP, scatter_dimension=1, tiled=True
        ).astype(jnp.float32),
    )
    return (
        output,
        grad_tokens,
        g_ln1,
        shards[0],
        shards[1],
        shards[2],
        shards[3],
        g_norm,
        shards[4],
        g_ln2,
        shards[5],
        shards[6],
        shards[7],
    )


F32 = jnp.float32
BF16 = jnp.bfloat16
BOTH_X = [(0, 2), (2, 0), (1, 3), (3, 1)]
UP_X = [(0, 2), (1, 3)]
DOWN_X = [(2, 0), (3, 1)]
CORES = [(0, 1), (1, 0), (2, 3), (3, 2)]
UP_Z = [[(0, 1), (1, 2), (2, 3)], [(1, 2), (2, 3)], [(2, 3)]]
SCALE = 0.0625
UP_SUM = [[(0, 1)], [(0, 1), (1, 2)], [(0, 1), (1, 2), (2, 3)]]
DOWN_SUM = [[(3, 2)], [(3, 2), (2, 1)], [(3, 2), (2, 1), (1, 0)]]
ROWS, GAINS, STATES = range(3)
DOWN_Z = [[(3, 2), (2, 1), (1, 0)], [(2, 1), (1, 0)], [(1, 0)]]


def over_x(value):
    return lax.ppermute(value, CONTEXT, BOTH_X)


def over_core(value):
    return lax.ppermute(value, CONTEXT, CORES)


def over_y(value):
    return lax.ppermute(value, TENSOR, [(0, 1), (1, 0)])


def tie(*values):
    return lax.optimization_barrier(values)


def butterfly(value, axis):
    size = lax.axis_size(axis)
    step = 1
    while step < size:
        value = value + lax.ppermute(value, axis, [(i, i ^ step) for i in range(size)])
        step *= 2
    return value


def quarter_of(weight, dim, index):
    size = weight.shape[dim] // 4
    return lax.dynamic_slice_in_dim(weight, index * size, size, dim)


def assemble_kernel(spot_ref, *refs):
    at = pl.program_id(0)
    for index, block in enumerate(refs[:8]):

        @pl.when(at == index)
        def _(block=block):
            refs[8][...] = block[...]


def assemble(blocks, spots, by_rows):
    size = blocks[0].shape[0]
    shape = (2 * size, 4 * size) if by_rows else (4 * size, 2 * size)

    def spot(at, spots_ref):
        z_from, x_from = spots_ref[at % 4], spots_ref[4 + at // 4]
        return (x_from, z_from) if by_rows else (z_from, x_from)

    return pl.pallas_call(
        assemble_kernel,
        out_shape=jax.ShapeDtypeStruct(shape, blocks[0].dtype),
        grid_spec=pltpu.PrefetchScalarGridSpec(
            num_scalar_prefetch=1,
            grid=(8,),
            in_specs=[pl.BlockSpec((size, size), lambda at, spots_ref: (0, 0))] * 8,
            out_specs=pl.BlockSpec((size, size), spot),
        ),
        compiler_params=pltpu.CompilerParams(vmem_limit_bytes=32 << 20),
        cost_estimate=pl.CostEstimate(flops=0, transcendentals=0, bytes_accessed=32 * size * size),
    )(spots, *blocks)


def nn(left, right):
    return lax.dot_general(left, right, (((1,), (0,)), ((), ())), preferred_element_type=F32)


def nt(left, right):
    return lax.dot_general(left, right, (((1,), (1,)), ((), ())), preferred_element_type=F32)


def tn(left, right):
    return lax.dot_general(left, right, (((0,), (0,)), ((), ())), preferred_element_type=F32)


def where_is(whole, chunk, piece_len):
    share_len = piece_len // 2
    spots = []
    for shape, dim in (((piece_len, 1), 0), ((1, piece_len), 1)):
        at = lax.broadcasted_iota(jnp.int32, shape, dim) + whole[2] * share_len
        spots.append(jnp.where(at >= piece_len, at - piece_len, at))
    start = whole[0] * (2 * piece_len) + chunk * piece_len
    return spots[0], spots[1], start


def document(whole, spot):
    seq = pl.program_id(0)
    first, second = whole[3 + 2 * seq], whole[4 + 2 * seq]
    return jnp.where(spot >= second, 2, jnp.where(spot >= first, 1, 0))


def fade(gap, log_keep):
    return jnp.exp(jnp.maximum(gap, 0).astype(F32) * log_keep)


def piece_terms(whole, log_keep, chunk, piece_len):
    rows, cols, start = where_is(whole, chunk, piece_len)
    doc_rows, doc_cols = document(whole, start + rows), document(whole, start + cols)
    before, last = document(whole, start - 1), document(whole, start + piece_len - 1)
    within = jnp.where(
        (rows >= cols) & (doc_rows == doc_cols), fade(rows - cols, log_keep) * SCALE, 0.0
    )
    inflow = jnp.where(doc_rows == before, fade(rows + 1, log_keep) * SCALE, 0.0)
    outflow = jnp.where(doc_rows == last, fade(piece_len - 1 - rows, log_keep), 0.0)
    whole_gap = jnp.full((1, 1), piece_len, jnp.int32)
    over = jnp.where(before == last, fade(whole_gap, log_keep), 0.0)
    return within, inflow, outflow, over


def piece_of(ref, whole, chunk):
    group = lax.rem(chunk + whole[1], 2) * 2
    value = ref[pl.ds(group, 2), 0]
    return value.reshape(value.shape[0] * value.shape[1], value.shape[2])


def put_piece(ref, whole, chunk, value):
    group = lax.rem(chunk + whole[1], 2) * 2
    ref[pl.ds(group, 2), 0] = value.astype(ref.dtype).reshape(2, value.shape[0] // 2, value.shape[1])


def split_kq(ref, whole, chunk):
    both = piece_of(ref, whole, chunk)
    width = both.shape[1] // 2
    return both[:, :width], both[:, width:]


def update_kernel(whole, keeps, kq_ref, v_ref, out_ref):
    log_keep = keeps[pl.program_id(1)]
    piece_len = 2 * kq_ref.shape[2]
    total = jnp.zeros(out_ref.shape[2:], F32)
    for chunk in range(2):
        rows, _, start = where_is(whole, chunk, piece_len)
        last = document(whole, whole[0] * (2 * piece_len) + 2 * piece_len - 1)
        gap = (2 - chunk) * piece_len - 1 - rows
        weight = jnp.where(document(whole, start + rows) == last, fade(gap, log_keep), 0.0)
        keys, _ = split_kq(kq_ref, whole, chunk)
        values = piece_of(v_ref, whole, chunk)
        total = total + tn((keys.astype(F32) * weight).astype(BF16), values)
    out_ref[0, 0] = total.astype(BF16)


def next_state(state, keys, values, outflow, over):
    return over * state + tn((keys.astype(F32) * outflow).astype(BF16), values)


def forward_kernel(
    whole, keeps, kq_ref, v_ref, gate_ref, state_ref, gain_ref, gated_ref, retained_ref
):
    log_keep = keeps[pl.program_id(1)]
    piece_len = 2 * kq_ref.shape[2]
    state = state_ref[0, 0].astype(F32)
    for chunk in range(2):
        within, inflow, outflow, over = piece_terms(whole, log_keep, chunk, piece_len)
        keys, query = split_kq(kq_ref, whole, chunk)
        values = piece_of(v_ref, whole, chunk)
        scores = (nt(query, keys) * within).astype(BF16)
        retained = nn(scores, values) + inflow * nn(query, state.astype(BF16))
        if chunk == 0:
            state = next_state(state, keys, values, outflow, over)
        put_piece(retained_ref, whole, chunk, retained)
        normed, _, _ = norm_rows(retained, gain_ref[0], 0.01)
        gate = piece_of(gate_ref, whole, chunk).astype(F32)
        put_piece(gated_ref, whole, chunk, gate * jax.nn.sigmoid(gate) * normed)


def norm_back_kernel(
    whole,
    keeps,
    d_gated_ref,
    gate_ref,
    retained_ref,
    kq_ref,
    gain_ref,
    d_gate_ref,
    d_retained_ref,
    d_gain_ref,
    leaving_ref,
):
    log_keep = keeps[pl.program_id(1)]
    piece_len = 2 * kq_ref.shape[2]
    total = jnp.zeros(leaving_ref.shape[2:], F32)
    gain = gain_ref[0]
    d_gain = jnp.zeros(gain.shape, F32)
    for chunk in range(2):
        rows, _, start = where_is(whole, chunk, piece_len)
        before = document(whole, whole[0] * (2 * piece_len) - 1)
        gap = chunk * piece_len + rows + 1
        weight = jnp.where(
            document(whole, start + rows) == before, fade(gap, log_keep) * SCALE, 0.0
        )
        _, query = split_kq(kq_ref, whole, chunk)
        retained = piece_of(retained_ref, whole, chunk).astype(F32)
        normed, unit, scale = norm_rows(retained, gain, 0.01)
        gate = piece_of(gate_ref, whole, chunk).astype(F32)
        d_gated = piece_of(d_gated_ref, whole, chunk).astype(F32)
        sigma = jax.nn.sigmoid(gate)
        put_piece(
            d_gate_ref, whole, chunk, d_gated * normed * sigma * (1.0 + gate * (1.0 - sigma))
        )
        d_normed = d_gated * gate * sigma
        d_gain = d_gain + jnp.sum(d_normed * unit, axis=0, keepdims=True)
        d_retained = norm_back(d_normed, unit, scale, gain)
        put_piece(d_retained_ref, whole, chunk, d_retained)
        total = total + tn(query, (d_retained * weight).astype(BF16))
    d_gain_ref[0, 0] = d_gain
    leaving_ref[0, 0] = total.astype(BF16)


def backward_kernel(
    whole, keeps, kq_ref, v_ref, d_retained_ref, state_ref, d_state_ref, d_kq_ref, d_v_ref
):
    log_keep = keeps[pl.program_id(1)]
    piece_len = 2 * kq_ref.shape[2]
    terms = [piece_terms(whole, log_keep, chunk, piece_len) for chunk in range(2)]
    state = state_ref[0, 0].astype(F32)
    keys, _ = split_kq(kq_ref, whole, 0)
    _, _, outflow, over = terms[0]
    states = [state, next_state(state, keys, piece_of(v_ref, whole, 0), outflow, over)]
    d_state = d_state_ref[0, 0].astype(F32)
    for chunk in (1, 0):
        within, inflow, outflow, over = terms[chunk]
        keys, query = split_kq(kq_ref, whole, chunk)
        values = piece_of(v_ref, whole, chunk)
        d_ret = piece_of(d_retained_ref, whole, chunk)
        state_low, d_state_low = states[chunk].astype(BF16), d_state.astype(BF16)
        scores = (nt(query, keys) * within).astype(BF16)
        d_scores = (nt(d_ret, values) * within).astype(BF16)
        d_values = tn(scores, d_ret) + outflow * nn(keys, d_state_low)
        put_piece(d_v_ref, whole, chunk, d_values)
        d_query = nn(d_scores, keys) + inflow * nt(d_ret, state_low)
        d_keys = tn(d_scores, query) + outflow * nt(values, d_state_low)
        put_piece(d_kq_ref, whole, chunk, jnp.concatenate([d_keys, d_query], axis=1))
        if chunk == 1:
            entering = tn(query, (d_ret.astype(F32) * inflow).astype(BF16))
            d_state = over * d_state + entering


def per_head(kernel, scalars, blocks, outs, flops):
    def spec(array, kind):
        if kind == ROWS:
            width = array.shape[3] // heads
            return pl.BlockSpec((4, 1, array.shape[2], width), lambda b, h, *_: (0, b, 0, h))
        if kind == GAINS:
            return pl.BlockSpec((1, *array.shape[1:]), lambda b, h, *_: (h, 0, 0))
        return pl.BlockSpec((1, 1, *array.shape[2:]), lambda b, h, *_: (b, h, 0, 0))

    heads = scalars[1].shape[0]
    seq_count = (scalars[0].shape[0] - 3) // 2
    moved = sum(a.size * a.dtype.itemsize for a, _ in (*blocks, *outs))
    return pl.pallas_call(
        kernel,
        out_shape=[a for a, _ in outs],
        grid_spec=pltpu.PrefetchScalarGridSpec(
            num_scalar_prefetch=2,
            grid=(seq_count, heads),
            in_specs=[spec(*block) for block in blocks],
            out_specs=[spec(*out) for out in outs],
        ),
        compiler_params=pltpu.CompilerParams(vmem_limit_bytes=56 << 20),
        cost_estimate=pl.CostEstimate(flops=flops, transcendentals=0, bytes_accessed=moved),
    )(*scalars, *(a for a, _ in blocks))


def both_quarters(mine, across, first, dim):
    return jnp.concatenate(
        [jnp.where(first, mine, across), jnp.where(first, across, mine)], axis=dim
    )


def paired_body(
    tokens,
    segments,
    forget,
    ln1_gain,
    w_query,
    w_key,
    w_value,
    w_gate,
    norm_gain,
    w_out,
    ln2_gain,
    w_fc_gate,
    w_fc_up,
    w_fc_down,
    cotangent,
):
    place = lax.axis_index(CONTEXT)
    x_at, core, y_at = place // 2, place % 2, lax.axis_index(TENSOR)
    z_at = lax.axis_index(FSDP)
    heads = forget.shape[0] // 2
    qk_width = w_query.shape[1] // forget.shape[0]
    v_width = w_value.shape[1] // forget.shape[0]
    width = tokens.shape[2]
    seq_count, share_len = tokens.shape[0], tokens.shape[1]
    share_rows = seq_count * share_len
    piece_len = 2 * share_len
    chip_len = 2 * piece_len
    v_half = heads * v_width
    forget_half = lax.dynamic_slice_in_dim(forget, core * heads, heads)
    gain_half = lax.dynamic_slice_in_dim(norm_gain, core * v_half, v_half)

    def part(array, first, last):
        return array[first * share_rows : last * share_rows]

    def unit(x_index):
        q = core * 2 + x_index
        key_query = [quarter_of(w_key, 1, q), quarter_of(w_query, 1, q)]
        return [
            jnp.concatenate(key_query, axis=1),
            quarter_of(w_value, 1, q),
            quarter_of(w_gate, 1, q),
            quarter_of(w_out, 0, q),
            quarter_of(w_fc_down, 0, q),
            quarter_of(w_fc_gate, 1, q),
            quarter_of(w_fc_up, 1, q),
        ]

    KQ, V, G, O, W2, W1, W3 = range(7)
    by_rows = [False, False, False, True, True, False, False]
    own, sibling = unit(x_at), unit(1 - x_at)
    z_last = lax.axis_size(FSDP) - 1
    s_one = jnp.where(z_at == 0, 1, z_at - 1)
    s_three = jnp.where(z_at == z_last, 0, jnp.where(z_at == 1, 2, z_last))
    spots = jnp.stack([z_at, s_one, z_at ^ 2, s_three, x_at, 1 - x_at]).astype(jnp.int32)
    slots = [[None] * 3 for _ in range(7)]
    across = [[None] * 3 for _ in range(7)]

    def weight(index):
        blocks = [own[index], *slots[index], sibling[index], *across[index]]
        return assemble(blocks, spots, by_rows[index])

    env = SimpleNamespace()
    firsts = jnp.sum((segments == 0).astype(jnp.int32), axis=1)
    seconds = jnp.sum((segments <= 1).astype(jnp.int32), axis=1)
    starts = jnp.stack([firsts, seconds], axis=1).reshape(-1)
    whole = jnp.concatenate([jnp.stack([x_at, core, y_at]).astype(jnp.int32), starts])
    scalars = (whole, jnp.log(1.0 - forget_half))
    gains = gain_half.reshape(heads, 1, v_width)
    state_type = jax.ShapeDtypeStruct((seq_count, heads, qk_width, v_width), BF16)
    rows_type = jax.ShapeDtypeStruct((4, seq_count, share_len, v_half), BF16)
    kq_type = jax.ShapeDtypeStruct((4, seq_count, share_len, 2 * heads * qk_width), BF16)
    gain_type = jax.ShapeDtypeStruct((seq_count, heads, 1, v_width), F32)
    pair_flops = seq_count * heads * chip_len * qk_width * v_width * 2

    def shaped(rows_in):
        return rows_in.reshape(4, seq_count, share_len, -1)

    def flat(rows_in):
        return rows_in.reshape(4 * share_rows, -1)

    x_share = tokens.reshape(share_rows, width).astype(F32)
    cot_share = cotangent.reshape(share_rows, width)

    def work_norm():
        h1, ln1_normed, ln1_scale = norm_rows(x_share, ln1_gain)
        env.ln1 = (ln1_normed, ln1_scale)
        env.h = h1.astype(BF16)
        env.hy = over_y(env.h)
        return [env.h]

    def work_core():
        env.hc, env.hcy = over_core(env.h), over_core(env.hy)
        env.cy = over_y(cot_share)
        return []

    def work_rows():
        env.h_one = jnp.concatenate([env.h, env.hy, env.hc, env.hcy], axis=0)
        return [env.h_one]

    def work_kq():
        env.wkq = weight(KQ)
        env.kq = nn(env.h_one, env.wkq).astype(BF16)
        return [env.kq]

    def work_v():
        env.wv = weight(V)
        env.v = nn(env.h_one, env.wv).astype(BF16)
        return [env.v]

    def work_state():
        (update,) = per_head(
            update_kernel,
            scalars,
            [(shaped(env.kq), ROWS), (shaped(env.v), ROWS)],
            [(state_type, STATES)],
            pair_flops,
        )
        env.state = lax.ppermute(update, CONTEXT, UP_X)
        env.cc, env.ccy = over_core(cot_share), over_core(env.cy)
        return [update]

    def work_gate():
        env.wg = weight(G)
        env.gate = nn(env.h_one, env.wg).astype(BF16)
        return [env.gate]

    def work_retained():
        gated, env.retained = per_head(
            forward_kernel,
            scalars,
            [
                (shaped(env.kq), ROWS),
                (shaped(env.v), ROWS),
                (shaped(env.gate), ROWS),
                (env.state, STATES),
                (gains, GAINS),
            ],
            [(rows_type, ROWS), (rows_type, ROWS)],
            5 * pair_flops,
        )
        env.gated = flat(gated)
        return [env.gated]

    def work_out_far():
        env.wo = weight(O)
        far = nn(part(env.gated, 2, 4), env.wo).astype(BF16)
        env.far_other, env.far_own = over_core(far[share_rows:]), over_core(far[:share_rows])
        return [far]

    def work_out_near():
        near = nn(part(env.gated, 1, 2), env.wo) + env.far_other.astype(F32)
        near = near.astype(BF16)
        env.near = over_y(near)
        return [near]

    def work_out_own():
        env.own = nn(part(env.gated, 0, 1), env.wo) + x_share + env.far_own.astype(F32)
        return [env.own]

    def work_cot():
        env.cot = jnp.concatenate([cot_share, env.cy, env.cc, env.ccy], axis=0)
        return [env.cot]

    def work_d_hidden():
        env.w2 = weight(W2)
        env.d_hidden = nt(env.cot, env.w2)
        return [env.d_hidden]

    def work_middle():
        env.middle = env.own + env.near.astype(F32)
        h2, ln2_normed, ln2_scale = norm_rows(env.middle, ln2_gain)
        env.ln2 = (ln2_normed, ln2_scale)
        env.h2 = h2.astype(BF16)
        env.h2y, env.h2c = over_y(env.h2), over_core(env.h2)
        return [env.h2]

    def work_up():
        env.w1 = weight(W1)
        return [env.w1]

    def work_h2():
        env.h2cy = over_core(env.h2y)
        env.w3 = weight(W3)
        return [env.w3]

    plan = {
        0: [work_norm],
        5: [work_core],
        7: [work_rows],
        8: [work_kq],
        9: [work_v],
        10: [work_state],
        14: [work_gate],
        15: [work_retained],
        16: [work_out_far],
        17: [work_out_near],
        18: [work_out_own],
        19: [work_cot],
        21: [work_middle],
        22: [work_d_hidden],
        23: [work_up],
        25: [work_h2],
    }
    order = []
    for group in ((KQ, V), (G, O), (W2, W1, W3)):
        order += [(index, hop) for hop in range(3) for index in group]
    ups, downs, kept = {}, {}, {}
    flying, to_send, sent = None, None, None
    for event in range(26):
        launched = order[event] if event < len(order) else None
        if launched:
            index, hop = launched
            from_up, from_down = (ups[index], downs[index]) if hop else (own[index], own[index])
            new_up = lax.ppermute(from_up, FSDP, UP_Z[hop])
            new_down = lax.ppermute(from_down, FSDP, DOWN_Z[hop])
        now_sent, to_send = to_send, None
        if now_sent:
            which, slot, value = now_sent
            slots[which][slot] = value
            across[which][slot] = over_x(value)
        held = []
        for work in plan.get(event, []):
            held += work()
        if flying:
            held += [flying[2], flying[3]]
        if sent:
            held.append(across[sent[0]][sent[1]])
        ahead = order[event + 1] if event + 1 < len(order) else None
        if ahead and ahead[1] and flying and flying[0] == ahead[0]:
            ahead = None
        keep = []
        if ahead and ahead[1] == 0:
            keep.append(own[ahead[0]])
        elif ahead:
            keep += [ups[ahead[0]], downs[ahead[0]]]
        next_works = plan.get(event + 1, [])
        if not (held and (keep or flying or sent or next_works)):
            sent, flying = now_sent, (*launched, new_up, new_down) if launched else None
            continue
        names = [n for n in ("h_one", "kq", "gate", "gated", "cot", "h2") if hasattr(env, n)]
        tied = list(tie(*[getattr(env, n) for n in names], *keep, *held))
        for n in names:
            setattr(env, n, tied.pop(0))
        if ahead and ahead[1] == 0:
            own[ahead[0]] = tied.pop(0)
        elif ahead:
            ups[ahead[0]], downs[ahead[0]] = tied.pop(0), tied.pop(0)
        if sent:
            across[sent[0]][sent[1]] = tied.pop()
        if flying:
            index, hop = flying[0], flying[1]
            downs[index], ups[index] = tied.pop(), tied.pop()
            if hop == 0:
                kept[index] = downs[index]
                to_send = (index, 0, jnp.where(z_at > 0, ups[index], downs[index]))
            elif hop == 1:
                to_send = (index, 1, jnp.where(z_at >= 2, ups[index], downs[index]))
            else:
                middle_slot = jnp.where(z_at == 0, downs[index], kept[index])
                to_send = (index, 2, jnp.where(z_at == z_last, ups[index], middle_slot))
        sent, flying = now_sent, (*launched, new_up, new_down) if launched else None

    h_one, gated, gate_pre = env.h_one, env.gated, env.gate
    wkq, wv, wg, wo, w1, w2, w3 = env.wkq, env.wv, env.wg, env.wo, env.w1, env.w2, env.w3
    cot_full, d_hidden, middle = env.cot, env.d_hidden, env.middle

    token = [h_one]

    def step(run, *args):
        *args, _ = tie(*args, token[0])
        out = run(*args)
        token[0] = out[0] if isinstance(out, (tuple, list)) else out
        return out

    def columns(array, index):
        size = array.shape[1] // 2
        return lax.dynamic_slice_in_dim(array, index * size, size, 1)

    def theirs(rows, left, right):
        if rows:
            return tn(columns(left, 1 - x_at), right).astype(BF16)
        return tn(left, columns(right, 1 - x_at)).astype(BF16)

    def ours(rows, left, right, got):
        if rows:
            total = tn(columns(left, x_at), right)
        else:
            total = tn(left, columns(right, x_at))
        return (total + got.astype(F32)).astype(BF16)

    def z_block(rows, total, offset):
        dim = int(rows)
        size = total.shape[dim] // (z_last + 1)
        at = jnp.clip(z_at + offset, 0, z_last)
        return lax.dynamic_slice_in_dim(total, at * size, size, dim).astype(F32)

    def hop_terms(rows, reach, total, *got):
        up, down = z_block(rows, total, reach), z_block(rows, total, -reach)
        if got:
            up, down = up + got[0].astype(F32), down + got[1].astype(F32)
        return up.astype(BF16), down.astype(BF16)

    def last_terms(rows, total, up, down):
        return (z_block(rows, total, 0) + up.astype(F32) + down.astype(F32)).astype(BF16)

    def along_z(rows, total):
        got = ()
        for hop in range(3):
            up, down = step(partial(hop_terms, rows, 3 - hop), total, *got)
            up = lax.ppermute(up, FSDP, UP_SUM[hop])
            down = lax.ppermute(down, FSDP, DOWN_SUM[hop])
            got = (up, down)
            yield None
        yield step(partial(last_terms, rows), total, *got)

    def x_first(rows, left, right):
        got = over_x(step(partial(theirs, rows), left, right))
        yield
        total = step(partial(ours, rows), left, right, got)
        for mine in along_z(rows, total):
            if mine is None:
                yield
        beside = over_x(mine)
        yield
        both = step(lambda a, b: both_quarters(a, b, x_at == 0, 1 - int(rows)), mine, beside)
        yield both, over_core(both)

    def z_first(rows, left, right):
        total = step(lambda a, b: tn(a, b).astype(BF16), left, right)
        for mine in along_z(rows, total):
            if mine is None:
                yield
        beside = over_x(mine)
        yield
        both = step(lambda a, b: (a.astype(F32) + b.astype(F32)).astype(BF16), mine, beside)
        yield both, over_core(both)

    def halves(pair):
        both, other = pair
        return jnp.where(core == 0, both, other), jnp.where(core == 0, other, both)

    def whole_shard(pair, rows):
        return jnp.concatenate(halves(pair), axis=1 - int(rows)).astype(F32)

    def activate(h_two, d_hidden, w1, w3):
        fc_a, fc_b = nn(h_two, w1), nn(h_two, w3)
        silu_a = jax.nn.silu(fc_a)
        hidden = (silu_a * fc_b).astype(BF16)
        d_fca = (d_hidden * fc_b * swish_slope(fc_a)).astype(BF16)
        d_fcb = (d_hidden * silu_a).astype(BF16)
        return hidden, d_fca, d_fcb

    h_two = jnp.concatenate([env.h2, env.h2y, env.h2c, env.h2cy], axis=0)
    hidden, d_fca, d_fcb = step(activate, h_two, d_hidden, w1, w3)

    def d_h2_terms(a, b, d_fca, d_fcb):
        return nt(part(d_fca, a, b), w1) + nt(part(d_fcb, a, b), w3)

    far = step(lambda a, b: d_h2_terms(2, 4, a, b).astype(BF16), d_fca, d_fcb)
    far_other, far_own = over_core(far[share_rows:]), over_core(far[:share_rows])
    down = z_first(True, hidden, cot_full)
    next(down)
    near = step(
        lambda a, b, c: (d_h2_terms(1, 2, a, b) + c.astype(F32)).astype(BF16),
        d_fca,
        d_fcb,
        far_other,
    )
    near = over_y(near)
    fc_gate = x_first(False, h_two, d_fca)
    next(fc_gate)
    own_part = step(lambda a, b, c: d_h2_terms(0, 1, a, b) + c.astype(F32), d_fca, d_fcb, far_own)
    next(down)
    fc_up = x_first(False, h_two, d_fcb)
    next(fc_up)
    out_far = step(lambda a, b: nn(part(a, 2, 4), b).astype(BF16), hidden, w2)
    next(down)
    out_far_other, out_far_own = over_core(out_far[share_rows:]), over_core(out_far[:share_rows])

    def middle_back(own_part, near):
        d_h2 = own_part + near.astype(F32)
        ln2_normed, ln2_scale = env.ln2
        d_middle = cot_share.astype(F32) + norm_back(d_h2, ln2_normed, ln2_scale, ln2_gain)
        return d_middle.astype(BF16), d_middle, jnp.sum(d_h2 * ln2_normed, axis=0)

    d_mid_low, d_middle, g_ln2 = step(middle_back, own_part, near)
    d_mid_y, d_mid_c = over_y(d_mid_low), over_core(d_mid_low)
    next(down)
    next(fc_gate)
    out_near = step(
        lambda a, b, c: (nn(part(a, 1, 2), b) + c.astype(F32)).astype(BF16),
        hidden,
        w2,
        out_far_other,
    )
    next(fc_gate)
    next(fc_up)
    d_mid_y, out_near = step(lambda a, b: (a, b), d_mid_y, out_near)
    d_mid_cy = over_core(d_mid_y)
    out_near = over_y(out_near)
    next(fc_gate)

    def gate_back(share, y, c, cy):
        d_branch = jnp.concatenate([share, y, c, cy], axis=0)
        return nt(d_branch, wo).astype(BF16), d_branch

    d_gated, d_branch = step(gate_back, d_mid_low, d_mid_y, d_mid_c, d_mid_cy)
    kq, values, state_in = shaped(env.kq), shaped(env.v), env.state

    def retained_back(d_gated, kq):
        return per_head(
            norm_back_kernel,
            scalars,
            [
                (shaped(d_gated), ROWS),
                (shaped(gate_pre), ROWS),
                (env.retained, ROWS),
                (kq, ROWS),
                (gains, GAINS),
            ],
            [(rows_type, ROWS), (rows_type, ROWS), (gain_type, STATES), (state_type, STATES)],
            pair_flops,
        )

    d_gate, d_retained, g_norm, leaving = step(retained_back, d_gated, kq)
    d_gate = flat(d_gate)
    g_norm = jnp.sum(g_norm, axis=0).reshape(v_half)
    state_grad = lax.ppermute(leaving, CONTEXT, DOWN_X)
    next(fc_gate)
    next(fc_up)
    out = z_first(True, gated, d_branch)
    next(out)
    gate = x_first(False, h_one, d_gate)
    next(gate)
    next(fc_up)

    def pair_back(d_retained, state_grad):
        return per_head(
            backward_kernel,
            scalars,
            [
                (kq, ROWS),
                (values, ROWS),
                (d_retained, ROWS),
                (state_in, STATES),
                (state_grad, STATES),
            ],
            [(kq_type, ROWS), (rows_type, ROWS)],
            13 * pair_flops,
        )

    dkq_low, dv_low = step(pair_back, d_retained, state_grad)
    dkq_low, dv_low = flat(dkq_low), flat(dv_low)
    next(out)
    value = x_first(False, h_one, dv_low)
    next(value)
    next(fc_up)
    key_query = x_first(False, h_one, dkq_low)
    next(key_query)
    next(out)

    def d_h1_terms(a, b, dkq, dv, dg):
        terms = nt(part(dkq, a, b), wkq)
        return terms + nt(part(dv, a, b), wv) + nt(part(dg, a, b), wg)

    far = step(lambda *d: d_h1_terms(2, 4, *d).astype(BF16), dkq_low, dv_low, d_gate)
    far_other, far_own = over_core(far[share_rows:]), over_core(far[:share_rows])
    next(out)
    next(gate)
    near = step(
        lambda c, *d: (d_h1_terms(1, 2, *d) + c.astype(F32)).astype(BF16),
        far_other,
        dkq_low,
        dv_low,
        d_gate,
    )
    near = over_y(near)
    next(gate)
    own_part = step(
        lambda c, *d: d_h1_terms(0, 1, *d) + c.astype(F32), far_own, dkq_low, dv_low, d_gate
    )
    next(gate)
    next(value)
    g_down = whole_shard(next(down), True)
    out_own = step(
        lambda a, b, c, d, e: (nn(part(a, 0, 1), b) + c.astype(F32) + d + e.astype(F32)).astype(BF16),
        hidden,
        w2,
        out_far_own,
        middle,
        out_near,
    )
    next(value)
    next(gate)
    next(key_query)
    g_fc_gate = whole_shard(next(fc_gate), False)
    next(value)
    next(key_query)

    def tokens_back(own_part, near):
        d_h1 = own_part + near.astype(F32)
        ln1_normed, ln1_scale = env.ln1
        grad = d_middle + norm_back(d_h1, ln1_normed, ln1_scale, ln1_gain)
        return grad, jnp.sum(d_h1 * ln1_normed, axis=0)

    grad_tokens, g_ln1 = step(tokens_back, own_part, near)
    next(value)
    next(key_query)
    g_out = whole_shard(next(out), True)
    g_fc_up = whole_shard(next(fc_up), False)
    next(key_query)
    g_gate = whole_shard(next(gate), False)
    g_value = whole_shard(next(value), False)
    first, second = halves(next(key_query))
    sides = [half[:, at : at + qk_width] for half in (first, second) for at in range(0, half.shape[1], qk_width)]
    g_key = jnp.concatenate(sides[0::2], axis=1).astype(F32)
    g_query = jnp.concatenate(sides[1::2], axis=1).astype(F32)
    output = out_own

    def all_sum(value):
        return butterfly(butterfly(butterfly(value, TENSOR), CONTEXT), FSDP)

    g_norm = g_norm + over_x(g_norm)
    g_norm = butterfly(g_norm, FSDP)
    g_norm = both_quarters(g_norm, over_core(g_norm), core == 0, 0)
    return (
        output.reshape(tokens.shape),
        grad_tokens.reshape(tokens.shape),
        all_sum(g_ln1),
        g_query,
        g_key,
        g_value,
        g_gate,
        g_norm,
        g_out,
        all_sum(g_ln2),
        g_fc_gate,
        g_fc_up,
        g_down,
    )


def body(tensor_size, *arrays):
    heads_here = arrays[2].shape[0]
    paired = tensor_size == 2 and heads_here % 2 == 0 and lax.axis_size(CONTEXT) == 4
    paired = paired and lax.axis_size(FSDP) == 4
    return (paired_body if paired else general_body)(*arrays)


def solution(mesh):
    in_specs = (
        P(FSDP, (CONTEXT, TENSOR), None),
        P(FSDP, None),
        P(TENSOR),
        P(),
        P(FSDP, TENSOR),
        P(FSDP, TENSOR),
        P(FSDP, TENSOR),
        P(FSDP, TENSOR),
        P(TENSOR),
        P(TENSOR, FSDP),
        P(),
        P(FSDP, TENSOR),
        P(FSDP, TENSOR),
        P(TENSOR, FSDP),
        P(FSDP, (CONTEXT, TENSOR), None),
    )
    out_specs = (
        P(FSDP, (CONTEXT, TENSOR), None),
        P(FSDP, (CONTEXT, TENSOR), None),
        P(),
        P(FSDP, TENSOR),
        P(FSDP, TENSOR),
        P(FSDP, TENSOR),
        P(FSDP, TENSOR),
        P(TENSOR),
        P(TENSOR, FSDP),
        P(),
        P(FSDP, TENSOR),
        P(FSDP, TENSOR),
        P(TENSOR, FSDP),
    )
    return jax.shard_map(partial(body, mesh.shape[TENSOR]), mesh=mesh, in_specs=in_specs, out_specs=out_specs, check_vma=False)
```

```python
from functools import partial
from types import SimpleNamespace

import jax
import jax.numpy as jnp
from jax import lax
from jax.experimental import pallas as pl
from jax.experimental.pallas import tpu as pltpu
from jax.sharding import PartitionSpec as P

FSDP, CONTEXT, TENSOR = "fsdp", "context", "tensor"

careful = partial(jnp.einsum, precision=lax.Precision.HIGH)


def entering(part, axis, combine, identity):
    place = lax.axis_index(axis)
    gathered = jax.tree.map(lambda a: lax.all_gather(a, axis), part)
    state = jax.tree.map(lambda a, e: jnp.zeros_like(a) + jnp.asarray(e, a.dtype), part, identity)

    def one(step, state):
        return combine(
            state, jax.tree.map(lambda a: lax.dynamic_index_in_dim(a, step, 0, False), gathered)
        )

    return lax.fori_loop(0, place, one, state)


def carried_in(value, axis, combine, identity):
    count, place = (lax.axis_size(axis), lax.axis_index(axis))
    everything = jax.tree.map(
        lambda part, kind: lax.all_gather(part.astype(kind), axis),
        value,
        jax.tree.map(lambda a: jnp.bfloat16 if a.dtype == jnp.float32 else a.dtype, value),
    )
    start = jax.tree.map(
        lambda part, zero: jnp.broadcast_to(jnp.asarray(zero, part.dtype), part.shape),
        value,
        identity,
    )

    def step(k, before):
        at = count - 1 - k
        reached = at > place
        new = combine(
            before, jax.tree.map(lambda part, own: part[at].astype(own.dtype), everything, value)
        )
        return jax.tree.map(lambda a, b: jnp.where(reached, a, b), new, before)

    return lax.fori_loop(0, count, step, start)


def norm_rows(values, gain_vec, epsilon=1e-05):
    centred = values - jnp.mean(values, axis=-1, keepdims=True)
    scale = lax.rsqrt(jnp.mean(centred * centred, axis=-1, keepdims=True) + epsilon)
    normed = centred * scale
    return (normed * gain_vec, normed, scale)


def norm_back(grad_in, normed, scale, gain_vec):
    d_normed = grad_in * gain_vec
    first_mean = jnp.mean(d_normed, axis=-1, keepdims=True)
    second_mean = jnp.mean(d_normed * normed, axis=-1, keepdims=True)
    return scale * (d_normed - first_mean - normed * second_mean)


def swish_slope(values):
    sigma = jax.nn.sigmoid(values)
    return sigma * (1.0 + values * (1.0 - sigma))


def compose(earlier, latter):
    return (earlier[0] * latter[0], latter[0][:, :, None, None] * earlier[1] + latter[1])


def share_gather(piece):
    return lax.all_gather(piece, TENSOR, axis=1, tiled=True)


def branch_sum(terms):
    return lax.psum_scatter(terms, TENSOR, scatter_dimension=1, tiled=True)


def input_sum(terms):
    return lax.psum_scatter(
        terms.astype(jnp.bfloat16), TENSOR, scatter_dimension=1, tiled=True
    ).astype(jnp.float32)


def mixer_fetch(w_query, w_key, w_value, w_gate, w_out):
    return (
        lax.all_gather(w_query, FSDP, axis=0, tiled=True),
        lax.all_gather(w_key, FSDP, axis=0, tiled=True),
        lax.all_gather(w_value, FSDP, axis=0, tiled=True),
        lax.all_gather(w_gate, FSDP, axis=0, tiled=True),
        lax.all_gather(w_out, FSDP, axis=1, tiled=True),
    )


def mlp_fetch(w_fc_gate, w_fc_up, w_fc_down):
    return (
        lax.all_gather(w_fc_gate, FSDP, axis=0, tiled=True),
        lax.all_gather(w_fc_up, FSDP, axis=0, tiled=True),
        lax.all_gather(w_fc_down, FSDP, axis=1, tiled=True),
    )


def product(form, left, right):
    return jnp.einsum(form, left, right, preferred_element_type=jnp.float32)


def general_body(
    tokens,
    segments,
    forget,
    ln1_gain,
    w_query,
    w_key,
    w_value,
    w_gate,
    norm_gain,
    w_out,
    ln2_gain,
    w_fc_gate,
    w_fc_up,
    w_fc_down,
    cotangent,
):
    heads_here = forget.shape[0]
    qk_width = w_query.shape[1] // heads_here
    v_width = w_value.shape[1] // heads_here
    v_local = heads_here * v_width
    gain_heads = norm_gain.reshape(heads_here, v_width)
    x_share = tokens.astype(jnp.float32)
    h1_share, ln1_normed, ln1_scale = norm_rows(x_share, ln1_gain)
    h_one = share_gather(h1_share.astype(jnp.bfloat16))
    wq_all, wk_all, wv_all, wg_all, wo_all = mixer_fetch(w_query, w_key, w_value, w_gate, w_out)
    seq_count, stretch_len = (h_one.shape[0], h_one.shape[1])
    query = product("btd,dq->btq", h_one, wq_all).astype(jnp.bfloat16)
    keys = product("btd,dq->btq", h_one, wk_all).astype(jnp.bfloat16)
    values = product("btd,dv->btv", h_one, wv_all).astype(jnp.bfloat16)
    gate_pre = product("btd,dv->btv", h_one, wg_all)
    query_heads = query.reshape(seq_count, stretch_len, heads_here, qk_width)
    keys_heads = keys.reshape(seq_count, stretch_len, heads_here, qk_width)
    query_full = query_heads.astype(jnp.float32) * 0.0625
    keys_full = keys_heads.astype(jnp.float32)
    values_full = values.astype(jnp.float32).reshape(seq_count, stretch_len, heads_here, v_width)
    log_keep = jnp.log(1.0 - forget)
    ctx_place = lax.axis_index(CONTEXT)
    seg_stretch = lax.dynamic_slice_in_dim(segments, ctx_place * stretch_len, stretch_len, 1)
    seg_prev = lax.dynamic_slice_in_dim(segments, jnp.maximum(ctx_place * stretch_len - 1, 0), 1, 1)
    live_mask = (seg_stretch == seg_prev).astype(jnp.float32)
    steps_idx = jnp.arange(stretch_len, dtype=jnp.float32)
    step_gap = jnp.maximum(steps_idx[:, None] - steps_idx[None, :], 0.0)
    causal = steps_idx[:, None] >= steps_idx[None, :]
    same_doc = (seg_stretch[:, :, None] == seg_stretch[:, None, :]) & causal[None]
    weights_mask = jnp.where(
        same_doc[:, None], jnp.exp(step_gap[None] * log_keep[:, None, None])[None], 0.0
    )
    inflow = live_mask[:, :, None] * jnp.exp((steps_idx[:, None] + 1.0) * log_keep[None, :])[None]
    outflow = (seg_stretch == seg_stretch[:, -1:]).astype(jnp.float32)[:, :, None] * jnp.exp(
        (stretch_len - 1.0 - steps_idx)[:, None] * log_keep[None, :]
    )[None]
    carry_decay = live_mask[:, -1:] * jnp.exp(stretch_len * log_keep)[None, :]
    update = careful("bshd,bsh,bshe->bhde", keys_full, outflow, values_full)
    identity = (jnp.ones_like(carry_decay), jnp.zeros_like(update))
    state_in = entering((carry_decay, update), CONTEXT, compose, identity)[1]
    scores = product("bthd,bshd->bhts", query_heads, keys_heads) * 0.0625 * weights_mask
    retained = careful("bhts,bshe->bthe", scores, values_full)
    retained = retained + inflow[..., None] * careful("bthd,bhde->bthe", query_full, state_in)
    normed_out, gn_normed, gn_scale = norm_rows(retained, gain_heads, 0.01)
    norm_flat = normed_out.reshape(seq_count, stretch_len, v_local)
    gate_act = jax.nn.silu(gate_pre)
    gated = (gate_act * norm_flat).astype(jnp.bfloat16)
    middle = x_share + branch_sum(product("btv,vd->btd", gated, wo_all))
    h2_share, ln2_normed, ln2_scale = norm_rows(middle, ln2_gain)
    h_two = share_gather(h2_share.astype(jnp.bfloat16))
    w1_all, w3_all, w2_all = mlp_fetch(w_fc_gate, w_fc_up, w_fc_down)
    fc_a = product("btd,df->btf", h_two, w1_all)
    fc_b = product("btd,df->btf", h_two, w3_all)
    silu_a = jax.nn.silu(fc_a)
    hidden = (silu_a * fc_b).astype(jnp.bfloat16)
    output = (middle + branch_sum(product("btf,fd->btd", hidden, w2_all))).astype(jnp.bfloat16)
    wq_all, wk_all, wv_all, wg_all, wo_all = mixer_fetch(w_query, w_key, w_value, w_gate, w_out)
    w1_all, w3_all, w2_all = mlp_fetch(w_fc_gate, w_fc_up, w_fc_down)
    cot_full = share_gather(cotangent)
    d_hidden = product("btd,fd->btf", cot_full, w2_all)
    g_down = product("btf,btd->fd", hidden, cot_full)
    d_fca = (d_hidden * fc_b * swish_slope(fc_a)).astype(jnp.bfloat16)
    d_fcb = (d_hidden * silu_a).astype(jnp.bfloat16)
    g_fc_gate = product("btd,btf->df", h_two, d_fca)
    g_fc_up = product("btd,btf->df", h_two, d_fcb)
    d_h2 = input_sum(product("btf,df->btd", d_fca, w1_all) + product("btf,df->btd", d_fcb, w3_all))
    d_middle = cotangent.astype(jnp.float32) + norm_back(d_h2, ln2_normed, ln2_scale, ln2_gain)
    g_ln2 = jnp.sum(d_h2 * ln2_normed, axis=(0, 1))
    d_branch = share_gather(d_middle.astype(jnp.bfloat16))
    d_gated = product("btd,vd->btv", d_branch, wo_all)
    g_out = product("btv,btd->vd", gated, d_branch)
    d_gate = (d_gated * norm_flat * swish_slope(gate_pre)).astype(jnp.bfloat16)
    d_normed = (d_gated * gate_act).reshape(seq_count, stretch_len, heads_here, v_width)
    g_norm = jnp.sum(d_normed * gn_normed, axis=(0, 1)).reshape(v_local)
    d_retained = norm_back(d_normed, gn_normed, gn_scale, gain_heads)
    d_scores = careful("bthe,bshe->bhts", d_retained, values_full) * weights_mask
    d_values = careful("bhts,bthe->bshe", scores, d_retained)
    d_query = careful("bhts,bshd->bthd", d_scores, keys_full)
    d_query = d_query + inflow[..., None] * careful("bthe,bhde->bthd", d_retained, state_in)
    d_keys = careful("bhts,bthd->bshd", d_scores, query_full)
    leaving = careful("bthd,bth,bthe->bhde", query_full, inflow, d_retained)
    state_grad = carried_in((carry_decay, leaving), CONTEXT, compose, identity)[1]
    d_keys = d_keys + outflow[..., None] * careful("bshe,bhde->bshd", values_full, state_grad)
    d_values = d_values + outflow[..., None] * careful("bshd,bhde->bshe", keys_full, state_grad)
    dq_low = (
        (d_query * 0.0625)
        .reshape(seq_count, stretch_len, heads_here * qk_width)
        .astype(jnp.bfloat16)
    )
    dk_low = d_keys.reshape(seq_count, stretch_len, heads_here * qk_width).astype(jnp.bfloat16)
    dv_low = d_values.reshape(seq_count, stretch_len, v_local).astype(jnp.bfloat16)
    g_query = product("btd,btq->dq", h_one, dq_low)
    g_key = product("btd,btq->dq", h_one, dk_low)
    g_value = product("btd,btv->dv", h_one, dv_low)
    g_gate = product("btd,btv->dv", h_one, d_gate)
    d_h1 = product("btq,dq->btd", dq_low, wq_all) + product("btq,dq->btd", dk_low, wk_all)
    d_h1 = d_h1 + product("btv,dv->btd", dv_low, wv_all) + product("btv,dv->btd", d_gate, wg_all)
    d_h1 = input_sum(d_h1)
    grad_tokens = d_middle + norm_back(d_h1, ln1_normed, ln1_scale, ln1_gain)
    g_ln1 = jnp.sum(d_h1 * ln1_normed, axis=(0, 1))
    tensor_place = lax.axis_index(TENSOR)
    norm_full = lax.dynamic_update_slice(
        jnp.zeros((v_local * lax.axis_size(TENSOR),), jnp.float32),
        g_norm,
        (tensor_place * v_local,),
    )
    g_ln1, g_ln2, norm_full = lax.psum((g_ln1, g_ln2, norm_full), (FSDP, CONTEXT, TENSOR))
    g_norm = lax.dynamic_slice_in_dim(norm_full, tensor_place * v_local, v_local)
    weight_grads = (g_query, g_key, g_value, g_gate, g_out, g_fc_gate, g_fc_up, g_down)
    summed = (
        lax.psum(weight_grads[0].astype(jnp.bfloat16), CONTEXT).astype(jnp.float32),
        lax.psum(weight_grads[1].astype(jnp.bfloat16), CONTEXT).astype(jnp.float32),
        lax.psum(weight_grads[2].astype(jnp.bfloat16), CONTEXT).astype(jnp.float32),
        lax.psum(weight_grads[3].astype(jnp.bfloat16), CONTEXT).astype(jnp.float32),
        lax.psum(weight_grads[4].astype(jnp.bfloat16), CONTEXT).astype(jnp.float32),
        lax.psum(weight_grads[5].astype(jnp.bfloat16), CONTEXT).astype(jnp.float32),
        lax.psum(weight_grads[6].astype(jnp.bfloat16), CONTEXT).astype(jnp.float32),
        lax.psum(weight_grads[7].astype(jnp.bfloat16), CONTEXT).astype(jnp.float32),
    )
    shards = (
        lax.psum_scatter(
            summed[0].astype(jnp.bfloat16), FSDP, scatter_dimension=0, tiled=True
        ).astype(jnp.float32),
        lax.psum_scatter(
            summed[1].astype(jnp.bfloat16), FSDP, scatter_dimension=0, tiled=True
        ).astype(jnp.float32),
        lax.psum_scatter(
            summed[2].astype(jnp.bfloat16), FSDP, scatter_dimension=0, tiled=True
        ).astype(jnp.float32),
        lax.psum_scatter(
            summed[3].astype(jnp.bfloat16), FSDP, scatter_dimension=0, tiled=True
        ).astype(jnp.float32),
        lax.psum_scatter(
            summed[4].astype(jnp.bfloat16), FSDP, scatter_dimension=1, tiled=True
        ).astype(jnp.float32),
        lax.psum_scatter(
            summed[5].astype(jnp.bfloat16), FSDP, scatter_dimension=0, tiled=True
        ).astype(jnp.float32),
        lax.psum_scatter(
            summed[6].astype(jnp.bfloat16), FSDP, scatter_dimension=0, tiled=True
        ).astype(jnp.float32),
        lax.psum_scatter(
            summed[7].astype(jnp.bfloat16), FSDP, scatter_dimension=1, tiled=True
        ).astype(jnp.float32),
    )
    return (
        output,
        grad_tokens,
        g_ln1,
        shards[0],
        shards[1],
        shards[2],
        shards[3],
        g_norm,
        shards[4],
        g_ln2,
        shards[5],
        shards[6],
        shards[7],
    )


F32 = jnp.float32
BF16 = jnp.bfloat16
BOTH_X = [(0, 2), (2, 0), (1, 3), (3, 1)]
UP_X = [(0, 2), (1, 3)]
DOWN_X = [(2, 0), (3, 1)]
CORES = [(0, 1), (1, 0), (2, 3), (3, 2)]
UP_Z = [[(0, 1), (1, 2), (2, 3)], [(1, 2), (2, 3)], [(2, 3)]]
SCALE = 0.0625
UP_SUM = [[(0, 1)], [(0, 1), (1, 2)], [(0, 1), (1, 2), (2, 3)]]
DOWN_SUM = [[(3, 2)], [(3, 2), (2, 1)], [(3, 2), (2, 1), (1, 0)]]
ROWS, GAINS, STATES = range(3)
DOWN_Z = [[(3, 2), (2, 1), (1, 0)], [(2, 1), (1, 0)], [(1, 0)]]


def over_x(value):
    return lax.ppermute(value, CONTEXT, BOTH_X)


def over_core(value):
    return lax.ppermute(value, CONTEXT, CORES)


def over_y(value):
    return lax.ppermute(value, TENSOR, [(0, 1), (1, 0)])


def tie(*values):
    return lax.optimization_barrier(values)


def butterfly(value, axis):
    size = lax.axis_size(axis)
    step = 1
    while step < size:
        value = value + lax.ppermute(value, axis, [(i, i ^ step) for i in range(size)])
        step *= 2
    return value


def quarter_of(weight, dim, index):
    size = weight.shape[dim] // 4
    return lax.dynamic_slice_in_dim(weight, index * size, size, dim)


def assemble_kernel(spot_ref, *refs):
    at = pl.program_id(0)
    for index, block in enumerate(refs[:8]):

        @pl.when(at == index)
        def _(block=block):
            refs[8][...] = block[...]


def assemble(blocks, spots, by_rows, size):
    shape = (2 * size, 4 * size) if by_rows else (4 * size, 2 * size)

    def spot(at, spots_ref):
        z_from, x_from = spots_ref[at % 4], spots_ref[4 + at // 4]
        return (x_from, z_from) if by_rows else (z_from, x_from)

    return pl.pallas_call(
        assemble_kernel,
        out_shape=jax.ShapeDtypeStruct(shape, BF16),
        grid_spec=pltpu.PrefetchScalarGridSpec(
            num_scalar_prefetch=1,
            grid=(8,),
            in_specs=[
                pl.BlockSpec((size, size), lambda at, spots_ref, row=row: (row, 0))
                for _, row in blocks
            ],
            out_specs=pl.BlockSpec((size, size), spot),
        ),
        compiler_params=pltpu.CompilerParams(vmem_limit_bytes=32 << 20),
        cost_estimate=pl.CostEstimate(flops=0, transcendentals=0, bytes_accessed=32 * size * size),
    )(spots, *(array for array, _ in blocks))


def sum_kernel(count, *refs):
    lefts, rights, extras, out_ref = refs[:count], refs[count : 2 * count], refs[2 * count : -1], refs[-1]
    total = nt(lefts[0][...], rights[0][...])
    for left, right in zip(lefts[1:], rights[1:]):
        total = total + nt(left[...], right[...])
    for extra in extras:
        total = total + extra[...].astype(F32)
    out_ref[...] = total.astype(out_ref.dtype)


def sum_of_products(lefts, rights, first, rows, extras, kind):
    width = rights[0].shape[0]
    block = min(512, rows)
    depth = sum(left.shape[1] for left in lefts)

    def rows_spec(columns, from_row):
        return pl.BlockSpec((block, columns), lambda n, m: (from_row // block + m, 0))

    def tile_spec(from_row):
        return pl.BlockSpec((block, block), lambda n, m: (from_row // block + m, n))

    return pl.pallas_call(
        partial(sum_kernel, len(lefts)),
        grid=(width // block, rows // block),
        out_shape=jax.ShapeDtypeStruct((rows, width), kind),
        in_specs=[rows_spec(left.shape[1], first) for left in lefts]
        + [pl.BlockSpec((block, right.shape[1]), lambda n, m: (n, 0)) for right in rights]
        + [tile_spec(from_row) for _, from_row in extras],
        out_specs=tile_spec(0),
        compiler_params=pltpu.CompilerParams(vmem_limit_bytes=56 << 20),
        cost_estimate=pl.CostEstimate(
            flops=2 * rows * width * depth,
            transcendentals=0,
            bytes_accessed=2 * (rows + width) * depth + 4 * rows * width,
        ),
    )(*lefts, *rights, *(array for array, _ in extras))


def nn(left, right):
    return lax.dot_general(left, right, (((1,), (0,)), ((), ())), preferred_element_type=F32)


def nt(left, right):
    return lax.dot_general(left, right, (((1,), (1,)), ((), ())), preferred_element_type=F32)


def tn(left, right):
    return lax.dot_general(left, right, (((0,), (0,)), ((), ())), preferred_element_type=F32)


def where_is(whole, chunk, piece_len):
    share_len = piece_len // 2
    spots = []
    for shape, dim in (((piece_len, 1), 0), ((1, piece_len), 1)):
        at = lax.broadcasted_iota(jnp.int32, shape, dim) + whole[2] * share_len
        spots.append(jnp.where(at >= piece_len, at - piece_len, at))
    start = whole[0] * (2 * piece_len) + chunk * piece_len
    return spots[0], spots[1], start


def document(whole, spot):
    seq = pl.program_id(0)
    first, second = whole[3 + 2 * seq], whole[4 + 2 * seq]
    return jnp.where(spot >= second, 2, jnp.where(spot >= first, 1, 0))


def fade(gap, log_keep):
    return jnp.exp(jnp.maximum(gap, 0).astype(F32) * log_keep)


def piece_terms(whole, log_keep, chunk, piece_len):
    rows, cols, start = where_is(whole, chunk, piece_len)
    doc_rows, doc_cols = document(whole, start + rows), document(whole, start + cols)
    before, last = document(whole, start - 1), document(whole, start + piece_len - 1)
    within = jnp.where(
        (rows >= cols) & (doc_rows == doc_cols), fade(rows - cols, log_keep) * SCALE, 0.0
    )
    inflow = jnp.where(doc_rows == before, fade(rows + 1, log_keep) * SCALE, 0.0)
    outflow = jnp.where(doc_rows == last, fade(piece_len - 1 - rows, log_keep), 0.0)
    whole_gap = jnp.full((1, 1), piece_len, jnp.int32)
    over = jnp.where(before == last, fade(whole_gap, log_keep), 0.0)
    return within, inflow, outflow, over


def piece_of(ref, whole, chunk):
    group = lax.rem(chunk + whole[1], 2) * 2
    value = ref[pl.ds(group, 2), 0]
    return value.reshape(value.shape[0] * value.shape[1], value.shape[2])


def put_piece(ref, whole, chunk, value):
    group = lax.rem(chunk + whole[1], 2) * 2
    ref[pl.ds(group, 2), 0] = value.astype(ref.dtype).reshape(2, value.shape[0] // 2, value.shape[1])


def split_kq(ref, whole, chunk):
    both = piece_of(ref, whole, chunk)
    width = both.shape[1] // 2
    return both[:, :width], both[:, width:]


def update_kernel(whole, keeps, kq_ref, v_ref, out_ref):
    log_keep = keeps[pl.program_id(1)]
    piece_len = 2 * kq_ref.shape[2]
    total = jnp.zeros(out_ref.shape[2:], F32)
    for chunk in range(2):
        rows, _, start = where_is(whole, chunk, piece_len)
        last = document(whole, whole[0] * (2 * piece_len) + 2 * piece_len - 1)
        gap = (2 - chunk) * piece_len - 1 - rows
        weight = jnp.where(document(whole, start + rows) == last, fade(gap, log_keep), 0.0)
        keys, _ = split_kq(kq_ref, whole, chunk)
        values = piece_of(v_ref, whole, chunk)
        total = total + tn((keys.astype(F32) * weight).astype(BF16), values)
    out_ref[0, 0] = total.astype(BF16)


def next_state(state, keys, values, outflow, over):
    return over * state + tn((keys.astype(F32) * outflow).astype(BF16), values)


def forward_kernel(
    whole, keeps, kq_ref, v_ref, gate_ref, state_ref, gain_ref, gated_ref, retained_ref
):
    log_keep = keeps[pl.program_id(1)]
    piece_len = 2 * kq_ref.shape[2]
    state = state_ref[0, 0].astype(F32)
    for chunk in range(2):
        within, inflow, outflow, over = piece_terms(whole, log_keep, chunk, piece_len)
        keys, query = split_kq(kq_ref, whole, chunk)
        values = piece_of(v_ref, whole, chunk)
        scores = (nt(query, keys) * within).astype(BF16)
        retained = nn(scores, values) + inflow * nn(query, state.astype(BF16))
        if chunk == 0:
            state = next_state(state, keys, values, outflow, over)
        put_piece(retained_ref, whole, chunk, retained)
        normed, _, _ = norm_rows(retained, gain_ref[0], 0.01)
        gate = piece_of(gate_ref, whole, chunk).astype(F32)
        put_piece(gated_ref, whole, chunk, gate * jax.nn.sigmoid(gate) * normed)


def norm_back_kernel(
    whole,
    keeps,
    d_gated_ref,
    gate_ref,
    retained_ref,
    kq_ref,
    gain_ref,
    d_gate_ref,
    d_retained_ref,
    d_gain_ref,
    leaving_ref,
):
    log_keep = keeps[pl.program_id(1)]
    piece_len = 2 * kq_ref.shape[2]
    total = jnp.zeros(leaving_ref.shape[2:], F32)
    gain = gain_ref[0]
    d_gain = jnp.zeros(gain.shape, F32)
    for chunk in range(2):
        rows, _, start = where_is(whole, chunk, piece_len)
        before = document(whole, whole[0] * (2 * piece_len) - 1)
        gap = chunk * piece_len + rows + 1
        weight = jnp.where(
            document(whole, start + rows) == before, fade(gap, log_keep) * SCALE, 0.0
        )
        _, query = split_kq(kq_ref, whole, chunk)
        retained = piece_of(retained_ref, whole, chunk).astype(F32)
        normed, unit, scale = norm_rows(retained, gain, 0.01)
        gate = piece_of(gate_ref, whole, chunk).astype(F32)
        d_gated = piece_of(d_gated_ref, whole, chunk).astype(F32)
        sigma = jax.nn.sigmoid(gate)
        put_piece(
            d_gate_ref, whole, chunk, d_gated * normed * sigma * (1.0 + gate * (1.0 - sigma))
        )
        d_normed = d_gated * gate * sigma
        d_gain = d_gain + jnp.sum(d_normed * unit, axis=0, keepdims=True)
        d_retained = norm_back(d_normed, unit, scale, gain)
        put_piece(d_retained_ref, whole, chunk, d_retained)
        total = total + tn(query, (d_retained * weight).astype(BF16))
    d_gain_ref[0, 0] = d_gain
    leaving_ref[0, 0] = total.astype(BF16)


def backward_kernel(
    whole, keeps, kq_ref, v_ref, d_retained_ref, state_ref, d_state_ref, d_kq_ref, d_v_ref
):
    log_keep = keeps[pl.program_id(1)]
    piece_len = 2 * kq_ref.shape[2]
    terms = [piece_terms(whole, log_keep, chunk, piece_len) for chunk in range(2)]
    state = state_ref[0, 0].astype(F32)
    keys, _ = split_kq(kq_ref, whole, 0)
    _, _, outflow, over = terms[0]
    states = [state, next_state(state, keys, piece_of(v_ref, whole, 0), outflow, over)]
    d_state = d_state_ref[0, 0].astype(F32)
    for chunk in (1, 0):
        within, inflow, outflow, over = terms[chunk]
        keys, query = split_kq(kq_ref, whole, chunk)
        values = piece_of(v_ref, whole, chunk)
        d_ret = piece_of(d_retained_ref, whole, chunk)
        state_low, d_state_low = states[chunk].astype(BF16), d_state.astype(BF16)
        scores = (nt(query, keys) * within).astype(BF16)
        d_scores = (nt(d_ret, values) * within).astype(BF16)
        d_values = tn(scores, d_ret) + outflow * nn(keys, d_state_low)
        put_piece(d_v_ref, whole, chunk, d_values)
        d_query = nn(d_scores, keys) + inflow * nt(d_ret, state_low)
        d_keys = tn(d_scores, query) + outflow * nt(values, d_state_low)
        put_piece(d_kq_ref, whole, chunk, jnp.concatenate([d_keys, d_query], axis=1))
        if chunk == 1:
            entering = tn(query, (d_ret.astype(F32) * inflow).astype(BF16))
            d_state = over * d_state + entering


def per_head(kernel, scalars, blocks, outs, flops):
    def spec(array, kind):
        if kind == ROWS:
            width = array.shape[3] // heads
            return pl.BlockSpec((4, 1, array.shape[2], width), lambda b, h, *_: (0, b, 0, h))
        if kind == GAINS:
            return pl.BlockSpec((1, *array.shape[1:]), lambda b, h, *_: (h, 0, 0))
        return pl.BlockSpec((1, 1, *array.shape[2:]), lambda b, h, *_: (b, h, 0, 0))

    heads = scalars[1].shape[0]
    seq_count = (scalars[0].shape[0] - 3) // 2
    moved = sum(a.size * a.dtype.itemsize for a, _ in (*blocks, *outs))
    return pl.pallas_call(
        kernel,
        out_shape=[a for a, _ in outs],
        grid_spec=pltpu.PrefetchScalarGridSpec(
            num_scalar_prefetch=2,
            grid=(seq_count, heads),
            in_specs=[spec(*block) for block in blocks],
            out_specs=[spec(*out) for out in outs],
        ),
        compiler_params=pltpu.CompilerParams(vmem_limit_bytes=56 << 20),
        cost_estimate=pl.CostEstimate(flops=flops, transcendentals=0, bytes_accessed=moved),
    )(*scalars, *(a for a, _ in blocks))


def both_quarters(mine, across, first, dim):
    return jnp.concatenate(
        [jnp.where(first, mine, across), jnp.where(first, across, mine)], axis=dim
    )


def paired_body(
    tokens,
    segments,
    forget,
    ln1_gain,
    w_query,
    w_key,
    w_value,
    w_gate,
    norm_gain,
    w_out,
    ln2_gain,
    w_fc_gate,
    w_fc_up,
    w_fc_down,
    cotangent,
):
    place = lax.axis_index(CONTEXT)
    x_at, core, y_at = place // 2, place % 2, lax.axis_index(TENSOR)
    z_at = lax.axis_index(FSDP)
    heads = forget.shape[0] // 2
    qk_width = w_query.shape[1] // forget.shape[0]
    v_width = w_value.shape[1] // forget.shape[0]
    width = tokens.shape[2]
    seq_count, share_len = tokens.shape[0], tokens.shape[1]
    share_rows = seq_count * share_len
    piece_len = 2 * share_len
    chip_len = 2 * piece_len
    v_half = heads * v_width
    forget_half = lax.dynamic_slice_in_dim(forget, core * heads, heads)
    gain_half = lax.dynamic_slice_in_dim(norm_gain, core * v_half, v_half)

    def part(array, first, last):
        return array[first * share_rows : last * share_rows]

    def unit(x_index):
        q = core * 2 + x_index
        key_query = [quarter_of(w_key, 1, q), quarter_of(w_query, 1, q)]
        return [
            jnp.concatenate(key_query, axis=1),
            quarter_of(w_value, 1, q),
            quarter_of(w_gate, 1, q),
            quarter_of(w_out, 0, q),
            quarter_of(w_fc_down, 0, q),
            quarter_of(w_fc_gate, 1, q),
            quarter_of(w_fc_up, 1, q),
        ]

    KQ, V, G, O, W2, W1, W3 = range(7)
    by_rows = [False, False, False, True, True, False, False]
    own, sibling = unit(x_at), unit(1 - x_at)
    size = own[0].shape[0]
    z_last = lax.axis_size(FSDP) - 1
    s_one = jnp.where(z_at == 0, 1, z_at - 1)
    s_three = jnp.where(z_at == z_last, 0, jnp.where(z_at == 1, 2, z_last))
    spots = jnp.stack([z_at, s_one, z_at ^ 2, s_three, x_at, 1 - x_at]).astype(jnp.int32)
    groups = [[KQ, V], [G, O], [W2, W1, W3]]
    slots, across = [[], [], []], [[], [], []]

    def weight(index):
        at, row = next((i, g.index(index)) for i, g in enumerate(groups) if index in g)
        blocks = [(own[index], 0)] + [(array, row) for array in slots[at]]
        blocks += [(sibling[index], 0)] + [(array, row) for array in across[at]]
        return assemble(blocks, spots, by_rows[index], size)

    env = SimpleNamespace()
    firsts = jnp.sum((segments == 0).astype(jnp.int32), axis=1)
    seconds = jnp.sum((segments <= 1).astype(jnp.int32), axis=1)
    starts = jnp.stack([firsts, seconds], axis=1).reshape(-1)
    whole = jnp.concatenate([jnp.stack([x_at, core, y_at]).astype(jnp.int32), starts])
    scalars = (whole, jnp.log(1.0 - forget_half))
    gains = gain_half.reshape(heads, 1, v_width)
    state_type = jax.ShapeDtypeStruct((seq_count, heads, qk_width, v_width), BF16)
    rows_type = jax.ShapeDtypeStruct((4, seq_count, share_len, v_half), BF16)
    kq_type = jax.ShapeDtypeStruct((4, seq_count, share_len, 2 * heads * qk_width), BF16)
    gain_type = jax.ShapeDtypeStruct((seq_count, heads, 1, v_width), F32)
    pair_flops = seq_count * heads * chip_len * qk_width * v_width * 2

    def shaped(rows_in):
        return rows_in.reshape(4, seq_count, share_len, -1)

    def flat(rows_in):
        return rows_in.reshape(4 * share_rows, -1)

    x_share = tokens.reshape(share_rows, width).astype(F32)
    cot_share = cotangent.reshape(share_rows, width)

    def work_norm():
        h1, ln1_normed, ln1_scale = norm_rows(x_share, ln1_gain)
        env.ln1 = (ln1_normed, ln1_scale)
        env.h = h1.astype(BF16)
        env.hy = over_y(env.h)
        return [env.h]

    def work_core():
        env.hc, env.hcy = over_core(env.h), over_core(env.hy)
        env.cy = over_y(cot_share)
        return []

    def work_rows():
        env.h_one = jnp.concatenate([env.h, env.hy, env.hc, env.hcy], axis=0)
        return [env.h_one]

    def work_kq():
        env.wkq = weight(KQ)
        env.kq = nn(env.h_one, env.wkq).astype(BF16)
        return [env.kq]

    def work_v():
        env.wv = weight(V)
        env.v = nn(env.h_one, env.wv).astype(BF16)
        return [env.v]

    def work_state():
        (update,) = per_head(
            update_kernel,
            scalars,
            [(shaped(env.kq), ROWS), (shaped(env.v), ROWS)],
            [(state_type, STATES)],
            pair_flops,
        )
        env.state = lax.ppermute(update, CONTEXT, UP_X)
        env.cc, env.ccy = over_core(cot_share), over_core(env.cy)
        return [update]

    def work_gate():
        env.wg = weight(G)
        env.gate = nn(env.h_one, env.wg).astype(BF16)
        return [env.gate]

    def work_retained():
        gated, env.retained = per_head(
            forward_kernel,
            scalars,
            [
                (shaped(env.kq), ROWS),
                (shaped(env.v), ROWS),
                (shaped(env.gate), ROWS),
                (env.state, STATES),
                (gains, GAINS),
            ],
            [(rows_type, ROWS), (rows_type, ROWS)],
            5 * pair_flops,
        )
        env.gated = flat(gated)
        return [env.gated]

    def work_out_far():
        env.wo = weight(O)
        far = nn(part(env.gated, 2, 4), env.wo).astype(BF16)
        env.far = over_core(far)
        return [far]

    def work_out_near():
        near = nn(part(env.gated, 1, 2), env.wo) + env.far[share_rows:].astype(F32)
        near = near.astype(BF16)
        env.near = over_y(near)
        return [near]

    def work_out_own():
        env.own = nn(part(env.gated, 0, 1), env.wo) + x_share
        env.own = env.own + env.far[:share_rows].astype(F32)
        return [env.own]

    def work_cot():
        env.cot = jnp.concatenate([cot_share, env.cy, env.cc, env.ccy], axis=0)
        return [env.cot]

    def work_d_hidden():
        env.w2 = weight(W2)
        env.d_hidden = nt(env.cot, env.w2)
        return [env.d_hidden]

    def work_middle():
        env.middle = env.own + env.near.astype(F32)
        h2, ln2_normed, ln2_scale = norm_rows(env.middle, ln2_gain)
        env.ln2 = (ln2_normed, ln2_scale)
        env.h2 = h2.astype(BF16)
        env.h2y, env.h2c = over_y(env.h2), over_core(env.h2)
        return [env.h2]

    def work_up():
        env.w1 = weight(W1)
        return [env.w1]

    def work_h2():
        env.h2cy = over_core(env.h2y)
        env.w3 = weight(W3)
        return [env.w3]

    plan = [
        [work_norm],
        [],
        [work_core],
        [work_rows],
        [work_kq, work_v],
        [work_state],
        [work_gate, work_cot],
        [work_retained, work_out_far, work_out_near, work_out_own],
        [],
        [work_middle],
        [work_d_hidden, work_up, work_h2],
    ]
    stacks = [jnp.concatenate([own[index] for index in group], axis=0) for group in groups]
    up = down = kept = to_send = None
    for tick, works in enumerate(plan):
        at, hop = divmod(tick, 3)
        moving = at < len(groups)
        if to_send is not None:
            which, value = to_send
            slots[which].append(value)
            across[which].append(over_x(value))
        sent, to_send = to_send, None
        if moving:
            if hop == 0:
                up, down = stacks[at], stacks[at]
            up = lax.ppermute(up, FSDP, UP_Z[hop])
            down = lax.ppermute(down, FSDP, DOWN_Z[hop])
        held = []
        for work in works:
            held += work()
        if not moving:
            continue
        held += [across[sent[0]][-1]] if sent is not None else []
        names = [n for n in ("h_one", "kq", "gate", "gated", "cot") if hasattr(env, n)]
        ahead = stacks[at + 1 : at + 2] if hop == 2 else []
        tied = list(tie(up, down, *[getattr(env, n) for n in names], *ahead, *held))
        up, down = tied[:2]
        for n, value in zip(names, tied[2:]):
            setattr(env, n, value)
        if ahead:
            stacks[at + 1] = tied[2 + len(names)]
        if hop == 0:
            kept = down
            to_send = (at, jnp.where(z_at > 0, up, down))
        elif hop == 1:
            to_send = (at, jnp.where(z_at >= 2, up, down))
        else:
            to_send = (at, jnp.where(z_at == z_last, up, jnp.where(z_at == 0, down, kept)))

    h_one, gated, gate_pre = env.h_one, env.gated, env.gate
    wkq, wv, wg, wo, w1, w2, w3 = env.wkq, env.wv, env.wg, env.wo, env.w1, env.w2, env.w3
    cot_full, d_hidden, middle = env.cot, env.d_hidden, env.middle

    token = [h_one]

    def step(run, *args):
        *args, _ = tie(*args, token[0])
        out = run(*args)
        token[0] = out[0] if isinstance(out, (tuple, list)) else out
        return out

    def columns(array, index):
        size = array.shape[1] // 2
        return lax.dynamic_slice_in_dim(array, index * size, size, 1)

    def theirs(rows, left, right):
        if rows:
            return tn(columns(left, 1 - x_at), right).astype(BF16)
        return tn(left, columns(right, 1 - x_at)).astype(BF16)

    def ours(rows, left, right, got):
        if rows:
            total = tn(columns(left, x_at), right)
        else:
            total = tn(left, columns(right, x_at))
        return (total + got.astype(F32)).astype(BF16)

    def blocks_at(parts, offset):
        at = jnp.clip(z_at + offset, 0, z_last) * size
        blocks = []
        for rows, total in parts:
            block = lax.dynamic_slice_in_dim(total, at, size, int(rows))
            blocks += [block] if rows else jnp.split(block, block.shape[1] // size, axis=1)
        return jnp.concatenate(blocks, axis=0).astype(F32)

    def hop_terms(kinds, reach, *arrays):
        parts = list(zip(kinds, arrays))
        up, down = blocks_at(parts, reach), blocks_at(parts, -reach)
        if len(arrays) > len(kinds):
            up, down = up + arrays[-2].astype(F32), down + arrays[-1].astype(F32)
        return up.astype(BF16), down.astype(BF16)

    def last_terms(kinds, *arrays):
        total = blocks_at(list(zip(kinds, arrays)), 0)
        return (total + arrays[-2].astype(F32) + arrays[-1].astype(F32)).astype(BF16)

    def join_x(firsts, mine, beside):
        blocks, row = [], 0
        for x_summed in firsts:
            count = 1 if x_summed else 2
            one, other = (a[row * size : (row + count) * size] for a in (mine, beside))
            if x_summed:
                blocks += [jnp.where(x_at == 0, one, other), jnp.where(x_at == 0, other, one)]
            else:
                blocks.append((one.astype(F32) + other.astype(F32)).astype(BF16))
            row += count
        return jnp.concatenate(blocks, axis=0)

    def deliver(kinds, firsts, totals):
        got = ()
        for hop in range(3):
            up, down = step(partial(hop_terms, kinds, 3 - hop), *totals, *got)
            up = lax.ppermute(up, FSDP, UP_SUM[hop])
            down = lax.ppermute(down, FSDP, DOWN_SUM[hop])
            got = (up, down)
            yield
        mine = step(partial(last_terms, kinds), *totals, *got)
        beside = over_x(mine)
        yield
        both = step(partial(join_x, firsts), mine, beside)
        yield both, over_core(both)

    def quarters(pair, at):
        both, other = pair
        mine, theirs = (a[2 * at * size : (2 * at + 2) * size] for a in (both, other))
        first, second = jnp.where(core == 0, mine, theirs), jnp.where(core == 0, theirs, mine)
        return [first[:size], first[size:], second[:size], second[size:]]

    def shard(pair, at, rows):
        return jnp.concatenate(quarters(pair, at), axis=1 - int(rows)).astype(F32)

    def activate(h_two, d_hidden, w1, w3):
        fc_a, fc_b = nn(h_two, w1), nn(h_two, w3)
        silu_a = jax.nn.silu(fc_a)
        hidden = (silu_a * fc_b).astype(BF16)
        d_fca = (d_hidden * fc_b * swish_slope(fc_a)).astype(BF16)
        d_fcb = (d_hidden * silu_a).astype(BF16)
        return hidden, d_fca, d_fcb

    h_two = jnp.concatenate([env.h2, env.h2y, env.h2c, env.h2cy], axis=0)
    hidden, d_fca, d_fcb = step(activate, h_two, d_hidden, w1, w3)

    def chip_total(rows, left, right):
        return step(lambda a, b: tn(a, b).astype(BF16), left, right)

    fc_lefts, fc_rights = (d_fca, d_fcb), (w1, w3)

    def products(lefts, rights, first, rows, kind, *extras):
        count = len(lefts)

        def run(*arrays):
            added = [(a, row) for a, (_, row) in zip(arrays[count:], extras)]
            return sum_of_products(arrays[:count], rights, first * share_rows, rows * share_rows, added, kind)

        return step(run, *lefts, *(a for a, _ in extras))

    far = over_core(products(fc_lefts, fc_rights, 2, 2, BF16))
    down_total = chip_total(True, hidden, cot_full)
    down = deliver([True], [False], [down_total])
    next(down)
    near = over_y(products(fc_lefts, fc_rights, 1, 1, BF16, (far, share_rows)))
    gate_got = over_x(step(partial(theirs, False), h_two, d_fca))
    own_part = products(fc_lefts, fc_rights, 0, 1, F32, (far, 0))
    up_got = over_x(step(partial(theirs, False), h_two, d_fcb))
    out_far = over_core(step(lambda a, b: nn(part(a, 2, 4), b).astype(BF16), hidden, w2))
    next(down)
    out_near = step(
        lambda a, b, c: (nn(part(a, 1, 2), b) + c[share_rows:].astype(F32)).astype(BF16),
        hidden,
        w2,
        out_far,
    )

    def middle_back(own_part, near):
        d_h2 = own_part + near.astype(F32)
        ln2_normed, ln2_scale = env.ln2
        d_middle = cot_share.astype(F32) + norm_back(d_h2, ln2_normed, ln2_scale, ln2_gain)
        return d_middle.astype(BF16), d_middle, jnp.sum(d_h2 * ln2_normed, axis=0)

    d_mid_low, d_middle, g_ln2 = step(middle_back, own_part, near)
    d_mid_y, d_mid_c = over_y(d_mid_low), over_core(d_mid_low)
    fc_gate_total = step(partial(ours, False), h_two, d_fca, gate_got)
    next(down)
    out_own = step(
        lambda a, b, c, d: nn(part(a, 0, 1), b) + c[:share_rows].astype(F32) + d,
        hidden,
        w2,
        out_far,
        middle,
    )
    d_mid_y, out_near = step(lambda a, b: (a, b), d_mid_y, out_near)
    d_mid_cy = over_core(d_mid_y)
    out_near = over_y(out_near)
    fc_up_total = step(partial(ours, False), h_two, d_fcb, up_got)
    fc = deliver([False, False], [True, True], [fc_gate_total, fc_up_total])
    next(fc)

    def gate_back(share, y, c, cy):
        d_branch = jnp.concatenate([share, y, c, cy], axis=0)
        return nt(d_branch, wo).astype(BF16), d_branch

    d_gated, d_branch = step(gate_back, d_mid_low, d_mid_y, d_mid_c, d_mid_cy)
    kq, values, state_in = shaped(env.kq), shaped(env.v), env.state

    def retained_back(d_gated, kq):
        return per_head(
            norm_back_kernel,
            scalars,
            [
                (shaped(d_gated), ROWS),
                (shaped(gate_pre), ROWS),
                (env.retained, ROWS),
                (kq, ROWS),
                (gains, GAINS),
            ],
            [(rows_type, ROWS), (rows_type, ROWS), (gain_type, STATES), (state_type, STATES)],
            pair_flops,
        )

    d_gate, d_retained, g_norm, leaving = step(retained_back, d_gated, kq)
    d_gate = flat(d_gate)
    g_norm = jnp.sum(g_norm, axis=0).reshape(v_half)
    state_grad = lax.ppermute(leaving, CONTEXT, DOWN_X)
    next(down)
    out_total = chip_total(True, gated, d_branch)
    next(fc)
    gate_total = chip_total(False, h_one, d_gate)
    out_gate = deliver([True, False], [False, False], [out_total, gate_total])
    next(out_gate)

    def pair_back(d_retained, state_grad):
        return per_head(
            backward_kernel,
            scalars,
            [
                (kq, ROWS),
                (values, ROWS),
                (d_retained, ROWS),
                (state_in, STATES),
                (state_grad, STATES),
            ],
            [(kq_type, ROWS), (rows_type, ROWS)],
            13 * pair_flops,
        )

    dkq_low, dv_low = step(pair_back, d_retained, state_grad)
    dkq_low, dv_low = flat(dkq_low), flat(dv_low)
    v_got = over_x(step(partial(theirs, False), h_one, dv_low))
    next(fc)
    kq_got = over_x(step(partial(theirs, False), h_one, dkq_low))
    h1_lefts, h1_rights = (dkq_low, dv_low, d_gate), (wkq, wv, wg)
    far = over_core(products(h1_lefts, h1_rights, 2, 2, BF16))
    next(out_gate)
    next(fc)
    g_down = next(down)
    near = over_y(products(h1_lefts, h1_rights, 1, 1, BF16, (far, share_rows)))
    own_part = products(h1_lefts, h1_rights, 0, 1, F32, (far, 0))
    v_total = step(partial(ours, False), h_one, dv_low, v_got)
    value = deliver([False], [True], [v_total])
    next(out_gate)
    next(value)
    g_fc = next(fc)
    output = step(lambda a, b: (a + b.astype(F32)).astype(BF16), out_own, out_near)
    next(value)
    kq_total = step(partial(ours, False), h_one, dkq_low, kq_got)
    key_query = deliver([False], [True], [kq_total])
    next(out_gate)
    next(key_query)
    next(value)
    next(key_query)

    def tokens_back(own_part, near):
        d_h1 = own_part + near.astype(F32)
        ln1_normed, ln1_scale = env.ln1
        grad = d_middle + norm_back(d_h1, ln1_normed, ln1_scale, ln1_gain)
        return grad, jnp.sum(d_h1 * ln1_normed, axis=0)

    grad_tokens, g_ln1 = step(tokens_back, own_part, near)
    next(value)
    next(key_query)
    g_out_gate = next(out_gate)
    next(key_query)
    g_value = next(value)
    sides = quarters(next(key_query), 0)
    g_key = jnp.concatenate([side[:, :qk_width] for side in sides], axis=1).astype(F32)
    g_query = jnp.concatenate([side[:, qk_width:] for side in sides], axis=1).astype(F32)

    norm_size = lax.axis_size(TENSOR) * norm_gain.shape[0]
    norm_all = lax.dynamic_update_slice_in_dim(
        jnp.zeros((norm_size,), F32), g_norm, (2 * y_at + core) * v_half, 0
    )
    gain_sums = jnp.concatenate([g_ln1, g_ln2, norm_all])
    for axis in (TENSOR, CONTEXT, FSDP):
        gain_sums = butterfly(gain_sums, axis)
    g_ln1, g_ln2 = gain_sums[:width], gain_sums[width : 2 * width]
    g_norm = lax.dynamic_slice_in_dim(
        gain_sums, 2 * width + y_at * norm_gain.shape[0], norm_gain.shape[0]
    )
    return (
        output.reshape(tokens.shape),
        grad_tokens.reshape(tokens.shape),
        g_ln1,
        g_query,
        g_key,
        shard(g_value, 0, False),
        shard(g_out_gate, 1, False),
        g_norm,
        shard(g_out_gate, 0, True),
        g_ln2,
        shard(g_fc, 0, False),
        shard(g_fc, 1, False),
        shard(g_down, 0, True),
    )


def body(tensor_size, *arrays):
    heads_here = arrays[2].shape[0]
    paired = tensor_size == 2 and heads_here % 2 == 0 and lax.axis_size(CONTEXT) == 4
    paired = paired and lax.axis_size(FSDP) == 4
    return (paired_body if paired else general_body)(*arrays)


def solution(mesh):
    in_specs = (
        P(FSDP, (CONTEXT, TENSOR), None),
        P(FSDP, None),
        P(TENSOR),
        P(),
        P(FSDP, TENSOR),
        P(FSDP, TENSOR),
        P(FSDP, TENSOR),
        P(FSDP, TENSOR),
        P(TENSOR),
        P(TENSOR, FSDP),
        P(),
        P(FSDP, TENSOR),
        P(FSDP, TENSOR),
        P(TENSOR, FSDP),
        P(FSDP, (CONTEXT, TENSOR), None),
    )
    out_specs = (
        P(FSDP, (CONTEXT, TENSOR), None),
        P(FSDP, (CONTEXT, TENSOR), None),
        P(),
        P(FSDP, TENSOR),
        P(FSDP, TENSOR),
        P(FSDP, TENSOR),
        P(FSDP, TENSOR),
        P(TENSOR),
        P(TENSOR, FSDP),
        P(),
        P(FSDP, TENSOR),
        P(FSDP, TENSOR),
        P(TENSOR, FSDP),
    )
    return jax.shard_map(partial(body, mesh.shape[TENSOR]), mesh=mesh, in_specs=in_specs, out_specs=out_specs, check_vma=False)
```

```python
from functools import partial
from types import SimpleNamespace

import jax
import jax.numpy as jnp
from jax import lax
from jax.experimental import pallas as pl
from jax.experimental.pallas import tpu as pltpu
from jax.sharding import PartitionSpec as P

FSDP, CONTEXT, TENSOR = "fsdp", "context", "tensor"

careful = partial(jnp.einsum, precision=lax.Precision.HIGH)


def entering(part, axis, combine, identity):
    place = lax.axis_index(axis)
    gathered = jax.tree.map(lambda a: lax.all_gather(a, axis), part)
    state = jax.tree.map(lambda a, e: jnp.zeros_like(a) + jnp.asarray(e, a.dtype), part, identity)

    def one(step, state):
        return combine(
            state, jax.tree.map(lambda a: lax.dynamic_index_in_dim(a, step, 0, False), gathered)
        )

    return lax.fori_loop(0, place, one, state)


def carried_in(value, axis, combine, identity):
    count, place = (lax.axis_size(axis), lax.axis_index(axis))
    everything = jax.tree.map(
        lambda part, kind: lax.all_gather(part.astype(kind), axis),
        value,
        jax.tree.map(lambda a: jnp.bfloat16 if a.dtype == jnp.float32 else a.dtype, value),
    )
    start = jax.tree.map(
        lambda part, zero: jnp.broadcast_to(jnp.asarray(zero, part.dtype), part.shape),
        value,
        identity,
    )

    def step(k, before):
        at = count - 1 - k
        reached = at > place
        new = combine(
            before, jax.tree.map(lambda part, own: part[at].astype(own.dtype), everything, value)
        )
        return jax.tree.map(lambda a, b: jnp.where(reached, a, b), new, before)

    return lax.fori_loop(0, count, step, start)


def norm_rows(values, gain_vec, epsilon=1e-05):
    centred = values - jnp.mean(values, axis=-1, keepdims=True)
    scale = lax.rsqrt(jnp.mean(centred * centred, axis=-1, keepdims=True) + epsilon)
    normed = centred * scale
    return (normed * gain_vec, normed, scale)


def norm_back(grad_in, normed, scale, gain_vec):
    d_normed = grad_in * gain_vec
    first_mean = jnp.mean(d_normed, axis=-1, keepdims=True)
    second_mean = jnp.mean(d_normed * normed, axis=-1, keepdims=True)
    return scale * (d_normed - first_mean - normed * second_mean)


def swish_slope(values):
    sigma = jax.nn.sigmoid(values)
    return sigma * (1.0 + values * (1.0 - sigma))


def compose(earlier, latter):
    return (earlier[0] * latter[0], latter[0][:, :, None, None] * earlier[1] + latter[1])


def share_gather(piece):
    return lax.all_gather(piece, TENSOR, axis=1, tiled=True)


def branch_sum(terms):
    return lax.psum_scatter(terms, TENSOR, scatter_dimension=1, tiled=True)


def input_sum(terms):
    return lax.psum_scatter(
        terms.astype(jnp.bfloat16), TENSOR, scatter_dimension=1, tiled=True
    ).astype(jnp.float32)


def mixer_fetch(w_query, w_key, w_value, w_gate, w_out):
    return (
        lax.all_gather(w_query, FSDP, axis=0, tiled=True),
        lax.all_gather(w_key, FSDP, axis=0, tiled=True),
        lax.all_gather(w_value, FSDP, axis=0, tiled=True),
        lax.all_gather(w_gate, FSDP, axis=0, tiled=True),
        lax.all_gather(w_out, FSDP, axis=1, tiled=True),
    )


def mlp_fetch(w_fc_gate, w_fc_up, w_fc_down):
    return (
        lax.all_gather(w_fc_gate, FSDP, axis=0, tiled=True),
        lax.all_gather(w_fc_up, FSDP, axis=0, tiled=True),
        lax.all_gather(w_fc_down, FSDP, axis=1, tiled=True),
    )


def product(form, left, right):
    return jnp.einsum(form, left, right, preferred_element_type=jnp.float32)


def general_body(
    tokens,
    segments,
    forget,
    ln1_gain,
    w_query,
    w_key,
    w_value,
    w_gate,
    norm_gain,
    w_out,
    ln2_gain,
    w_fc_gate,
    w_fc_up,
    w_fc_down,
    cotangent,
):
    heads_here = forget.shape[0]
    qk_width = w_query.shape[1] // heads_here
    v_width = w_value.shape[1] // heads_here
    v_local = heads_here * v_width
    gain_heads = norm_gain.reshape(heads_here, v_width)
    x_share = tokens.astype(jnp.float32)
    h1_share, ln1_normed, ln1_scale = norm_rows(x_share, ln1_gain)
    h_one = share_gather(h1_share.astype(jnp.bfloat16))
    wq_all, wk_all, wv_all, wg_all, wo_all = mixer_fetch(w_query, w_key, w_value, w_gate, w_out)
    seq_count, stretch_len = (h_one.shape[0], h_one.shape[1])
    query = product("btd,dq->btq", h_one, wq_all).astype(jnp.bfloat16)
    keys = product("btd,dq->btq", h_one, wk_all).astype(jnp.bfloat16)
    values = product("btd,dv->btv", h_one, wv_all).astype(jnp.bfloat16)
    gate_pre = product("btd,dv->btv", h_one, wg_all)
    query_heads = query.reshape(seq_count, stretch_len, heads_here, qk_width)
    keys_heads = keys.reshape(seq_count, stretch_len, heads_here, qk_width)
    query_full = query_heads.astype(jnp.float32) * 0.0625
    keys_full = keys_heads.astype(jnp.float32)
    values_full = values.astype(jnp.float32).reshape(seq_count, stretch_len, heads_here, v_width)
    log_keep = jnp.log(1.0 - forget)
    ctx_place = lax.axis_index(CONTEXT)
    seg_stretch = lax.dynamic_slice_in_dim(segments, ctx_place * stretch_len, stretch_len, 1)
    seg_prev = lax.dynamic_slice_in_dim(segments, jnp.maximum(ctx_place * stretch_len - 1, 0), 1, 1)
    live_mask = (seg_stretch == seg_prev).astype(jnp.float32)
    steps_idx = jnp.arange(stretch_len, dtype=jnp.float32)
    step_gap = jnp.maximum(steps_idx[:, None] - steps_idx[None, :], 0.0)
    causal = steps_idx[:, None] >= steps_idx[None, :]
    same_doc = (seg_stretch[:, :, None] == seg_stretch[:, None, :]) & causal[None]
    weights_mask = jnp.where(
        same_doc[:, None], jnp.exp(step_gap[None] * log_keep[:, None, None])[None], 0.0
    )
    inflow = live_mask[:, :, None] * jnp.exp((steps_idx[:, None] + 1.0) * log_keep[None, :])[None]
    outflow = (seg_stretch == seg_stretch[:, -1:]).astype(jnp.float32)[:, :, None] * jnp.exp(
        (stretch_len - 1.0 - steps_idx)[:, None] * log_keep[None, :]
    )[None]
    carry_decay = live_mask[:, -1:] * jnp.exp(stretch_len * log_keep)[None, :]
    update = careful("bshd,bsh,bshe->bhde", keys_full, outflow, values_full)
    identity = (jnp.ones_like(carry_decay), jnp.zeros_like(update))
    state_in = entering((carry_decay, update), CONTEXT, compose, identity)[1]
    scores = product("bthd,bshd->bhts", query_heads, keys_heads) * 0.0625 * weights_mask
    retained = careful("bhts,bshe->bthe", scores, values_full)
    retained = retained + inflow[..., None] * careful("bthd,bhde->bthe", query_full, state_in)
    normed_out, gn_normed, gn_scale = norm_rows(retained, gain_heads, 0.01)
    norm_flat = normed_out.reshape(seq_count, stretch_len, v_local)
    gate_act = jax.nn.silu(gate_pre)
    gated = (gate_act * norm_flat).astype(jnp.bfloat16)
    middle = x_share + branch_sum(product("btv,vd->btd", gated, wo_all))
    h2_share, ln2_normed, ln2_scale = norm_rows(middle, ln2_gain)
    h_two = share_gather(h2_share.astype(jnp.bfloat16))
    w1_all, w3_all, w2_all = mlp_fetch(w_fc_gate, w_fc_up, w_fc_down)
    fc_a = product("btd,df->btf", h_two, w1_all)
    fc_b = product("btd,df->btf", h_two, w3_all)
    silu_a = jax.nn.silu(fc_a)
    hidden = (silu_a * fc_b).astype(jnp.bfloat16)
    output = (middle + branch_sum(product("btf,fd->btd", hidden, w2_all))).astype(jnp.bfloat16)
    wq_all, wk_all, wv_all, wg_all, wo_all = mixer_fetch(w_query, w_key, w_value, w_gate, w_out)
    w1_all, w3_all, w2_all = mlp_fetch(w_fc_gate, w_fc_up, w_fc_down)
    cot_full = share_gather(cotangent)
    d_hidden = product("btd,fd->btf", cot_full, w2_all)
    g_down = product("btf,btd->fd", hidden, cot_full)
    d_fca = (d_hidden * fc_b * swish_slope(fc_a)).astype(jnp.bfloat16)
    d_fcb = (d_hidden * silu_a).astype(jnp.bfloat16)
    g_fc_gate = product("btd,btf->df", h_two, d_fca)
    g_fc_up = product("btd,btf->df", h_two, d_fcb)
    d_h2 = input_sum(product("btf,df->btd", d_fca, w1_all) + product("btf,df->btd", d_fcb, w3_all))
    d_middle = cotangent.astype(jnp.float32) + norm_back(d_h2, ln2_normed, ln2_scale, ln2_gain)
    g_ln2 = jnp.sum(d_h2 * ln2_normed, axis=(0, 1))
    d_branch = share_gather(d_middle.astype(jnp.bfloat16))
    d_gated = product("btd,vd->btv", d_branch, wo_all)
    g_out = product("btv,btd->vd", gated, d_branch)
    d_gate = (d_gated * norm_flat * swish_slope(gate_pre)).astype(jnp.bfloat16)
    d_normed = (d_gated * gate_act).reshape(seq_count, stretch_len, heads_here, v_width)
    g_norm = jnp.sum(d_normed * gn_normed, axis=(0, 1)).reshape(v_local)
    d_retained = norm_back(d_normed, gn_normed, gn_scale, gain_heads)
    d_scores = careful("bthe,bshe->bhts", d_retained, values_full) * weights_mask
    d_values = careful("bhts,bthe->bshe", scores, d_retained)
    d_query = careful("bhts,bshd->bthd", d_scores, keys_full)
    d_query = d_query + inflow[..., None] * careful("bthe,bhde->bthd", d_retained, state_in)
    d_keys = careful("bhts,bthd->bshd", d_scores, query_full)
    leaving = careful("bthd,bth,bthe->bhde", query_full, inflow, d_retained)
    state_grad = carried_in((carry_decay, leaving), CONTEXT, compose, identity)[1]
    d_keys = d_keys + outflow[..., None] * careful("bshe,bhde->bshd", values_full, state_grad)
    d_values = d_values + outflow[..., None] * careful("bshd,bhde->bshe", keys_full, state_grad)
    dq_low = (
        (d_query * 0.0625)
        .reshape(seq_count, stretch_len, heads_here * qk_width)
        .astype(jnp.bfloat16)
    )
    dk_low = d_keys.reshape(seq_count, stretch_len, heads_here * qk_width).astype(jnp.bfloat16)
    dv_low = d_values.reshape(seq_count, stretch_len, v_local).astype(jnp.bfloat16)
    g_query = product("btd,btq->dq", h_one, dq_low)
    g_key = product("btd,btq->dq", h_one, dk_low)
    g_value = product("btd,btv->dv", h_one, dv_low)
    g_gate = product("btd,btv->dv", h_one, d_gate)
    d_h1 = product("btq,dq->btd", dq_low, wq_all) + product("btq,dq->btd", dk_low, wk_all)
    d_h1 = d_h1 + product("btv,dv->btd", dv_low, wv_all) + product("btv,dv->btd", d_gate, wg_all)
    d_h1 = input_sum(d_h1)
    grad_tokens = d_middle + norm_back(d_h1, ln1_normed, ln1_scale, ln1_gain)
    g_ln1 = jnp.sum(d_h1 * ln1_normed, axis=(0, 1))
    tensor_place = lax.axis_index(TENSOR)
    norm_full = lax.dynamic_update_slice(
        jnp.zeros((v_local * lax.axis_size(TENSOR),), jnp.float32),
        g_norm,
        (tensor_place * v_local,),
    )
    g_ln1, g_ln2, norm_full = lax.psum((g_ln1, g_ln2, norm_full), (FSDP, CONTEXT, TENSOR))
    g_norm = lax.dynamic_slice_in_dim(norm_full, tensor_place * v_local, v_local)
    weight_grads = (g_query, g_key, g_value, g_gate, g_out, g_fc_gate, g_fc_up, g_down)
    summed = (
        lax.psum(weight_grads[0].astype(jnp.bfloat16), CONTEXT).astype(jnp.float32),
        lax.psum(weight_grads[1].astype(jnp.bfloat16), CONTEXT).astype(jnp.float32),
        lax.psum(weight_grads[2].astype(jnp.bfloat16), CONTEXT).astype(jnp.float32),
        lax.psum(weight_grads[3].astype(jnp.bfloat16), CONTEXT).astype(jnp.float32),
        lax.psum(weight_grads[4].astype(jnp.bfloat16), CONTEXT).astype(jnp.float32),
        lax.psum(weight_grads[5].astype(jnp.bfloat16), CONTEXT).astype(jnp.float32),
        lax.psum(weight_grads[6].astype(jnp.bfloat16), CONTEXT).astype(jnp.float32),
        lax.psum(weight_grads[7].astype(jnp.bfloat16), CONTEXT).astype(jnp.float32),
    )
    shards = (
        lax.psum_scatter(
            summed[0].astype(jnp.bfloat16), FSDP, scatter_dimension=0, tiled=True
        ).astype(jnp.float32),
        lax.psum_scatter(
            summed[1].astype(jnp.bfloat16), FSDP, scatter_dimension=0, tiled=True
        ).astype(jnp.float32),
        lax.psum_scatter(
            summed[2].astype(jnp.bfloat16), FSDP, scatter_dimension=0, tiled=True
        ).astype(jnp.float32),
        lax.psum_scatter(
            summed[3].astype(jnp.bfloat16), FSDP, scatter_dimension=0, tiled=True
        ).astype(jnp.float32),
        lax.psum_scatter(
            summed[4].astype(jnp.bfloat16), FSDP, scatter_dimension=1, tiled=True
        ).astype(jnp.float32),
        lax.psum_scatter(
            summed[5].astype(jnp.bfloat16), FSDP, scatter_dimension=0, tiled=True
        ).astype(jnp.float32),
        lax.psum_scatter(
            summed[6].astype(jnp.bfloat16), FSDP, scatter_dimension=0, tiled=True
        ).astype(jnp.float32),
        lax.psum_scatter(
            summed[7].astype(jnp.bfloat16), FSDP, scatter_dimension=1, tiled=True
        ).astype(jnp.float32),
    )
    return (
        output,
        grad_tokens,
        g_ln1,
        shards[0],
        shards[1],
        shards[2],
        shards[3],
        g_norm,
        shards[4],
        g_ln2,
        shards[5],
        shards[6],
        shards[7],
    )


F32 = jnp.float32
BF16 = jnp.bfloat16
BOTH_X = [(0, 2), (2, 0), (1, 3), (3, 1)]
UP_X = [(0, 2), (1, 3)]
DOWN_X = [(2, 0), (3, 1)]
CORES = [(0, 1), (1, 0), (2, 3), (3, 2)]
SCALE = 0.0625
ROWS, GAINS, STATES = range(3)
FREE = pl.CostEstimate(flops=0, transcendentals=0, bytes_accessed=0)
DOWN_Z = [[(3, 2), (2, 1), (1, 0)], [(2, 1), (1, 0)], [(1, 0)]]


def over_x(value):
    return lax.ppermute(value, CONTEXT, BOTH_X)


def over_core(value):
    return lax.ppermute(value, CONTEXT, CORES)


def over_y(value):
    return lax.ppermute(value, TENSOR, [(0, 1), (1, 0)])


def tie(*values):
    return lax.optimization_barrier(values)


def butterfly(value, axis):
    size = lax.axis_size(axis)
    step = 1
    while step < size:
        value = value + lax.ppermute(value, axis, [(i, i ^ step) for i in range(size)])
        step *= 2
    return value


def quarter_of(weight, dim, index):
    size = weight.shape[dim] // 4
    return lax.dynamic_slice_in_dim(weight, index * size, size, dim)


def assemble_kernel(spot_ref, *refs):
    at = pl.program_id(0)
    for index, block in enumerate(refs[:8]):

        @pl.when(at == index)
        def _(block=block):
            refs[8][...] = block[...]


def assemble(blocks, spots, by_rows, size):
    shape = (2 * size, 4 * size) if by_rows else (4 * size, 2 * size)

    def spot(at, spots_ref):
        z_from, x_from = spots_ref[at], spots_ref[8 + at]
        return (x_from, z_from) if by_rows else (z_from, x_from)

    return pl.pallas_call(
        assemble_kernel,
        out_shape=jax.ShapeDtypeStruct(shape, BF16),
        grid_spec=pltpu.PrefetchScalarGridSpec(
            num_scalar_prefetch=1,
            grid=(8,),
            in_specs=[
                pl.BlockSpec((size, size), lambda at, spots_ref, row=row: (row, 0))
                for _, row in blocks
            ],
            out_specs=pl.BlockSpec((size, size), spot),
        ),
        compiler_params=pltpu.CompilerParams(vmem_limit_bytes=32 << 20),
        cost_estimate=FREE,
    )(spots, *(array for array, _ in blocks))


def sum_kernel(product, count, *refs):
    lefts, rights, extras, out_ref = refs[:count], refs[count : 2 * count], refs[2 * count : -1], refs[-1]
    total = product(lefts[0][...], rights[0][...])
    for left, right in zip(lefts[1:], rights[1:]):
        total = total + product(left[...], right[...])
    for extra in extras:
        total = total + extra[...].astype(F32)
    out_ref[...] = total.astype(out_ref.dtype)


def sum_of_products(product, lefts, rights, first, rows, kind, extras=()):
    by_columns = product is nn
    width = rights[0].shape[1 if by_columns else 0]
    block, tile = min(1024, rows), min(512, width)

    def right_spec(right):
        if by_columns:
            return pl.BlockSpec((right.shape[0], tile), lambda n, m: (0, n))
        return pl.BlockSpec((tile, right.shape[1]), lambda n, m: (n, 0))

    def tile_spec(from_row):
        return pl.BlockSpec((block, tile), lambda n, m: (from_row // block + m, n))

    return pl.pallas_call(
        partial(sum_kernel, product, len(lefts)),
        grid=(width // tile, rows // block),
        out_shape=jax.ShapeDtypeStruct((rows, width), kind),
        in_specs=[
            pl.BlockSpec((block, left.shape[1]), lambda n, m: (first // block + m, 0))
            for left in lefts
        ]
        + [right_spec(right) for right in rights]
        + [tile_spec(from_row) for _, from_row in extras],
        out_specs=tile_spec(0),
        compiler_params=pltpu.CompilerParams(vmem_limit_bytes=60 << 20),
        cost_estimate=FREE,
    )(*lefts, *rights, *(array for array, _ in extras))


def quarter_kernel(spots_ref, left, right, *rest):
    total = tn(left[...], right[...])
    for extra in rest[:-1]:
        total = total + extra[...].astype(F32)
    rest[-1][...] = total.astype(BF16)


def quarter_product(left, right, index, extras=()):
    tokens, width = left.shape
    size, block = right.shape[1] // 2, min(1024, width)
    return pl.pallas_call(
        quarter_kernel,
        out_shape=jax.ShapeDtypeStruct((width, size), BF16),
        grid_spec=pltpu.PrefetchScalarGridSpec(
            num_scalar_prefetch=1,
            grid=(width // block,),
            in_specs=[
                pl.BlockSpec((tokens, block), lambda m, at: (0, m)),
                pl.BlockSpec((tokens, size), lambda m, at: (0, at[0])),
            ]
            + [pl.BlockSpec((block, size), lambda m, at: (m, 0)) for _ in extras],
            out_specs=pl.BlockSpec((block, size), lambda m, at: (m, 0)),
        ),
        compiler_params=pltpu.CompilerParams(vmem_limit_bytes=60 << 20),
        cost_estimate=FREE,
    )(index.reshape(1).astype(jnp.int32), left, right, *extras)


def split_kernel(left, right, out):
    out[0] = tn(left[...], right[...]).astype(BF16)


def split_product(left, right, count):
    tokens, rows = left.shape
    size = right.shape[1] // count
    return pl.pallas_call(
        split_kernel,
        grid=(count,),
        out_shape=jax.ShapeDtypeStruct((count, rows, size), BF16),
        in_specs=[
            pl.BlockSpec((tokens, rows), lambda n: (0, 0)),
            pl.BlockSpec((tokens, size), lambda n: (0, n)),
        ],
        out_specs=pl.BlockSpec((1, rows, size), lambda n: (n, 0, 0)),
        compiler_params=pltpu.CompilerParams(vmem_limit_bytes=60 << 20),
        cost_estimate=FREE,
    )(left, right)


def unit_kernel(h_ref, w1_ref, w3_ref, d_hidden_ref, hidden_ref, d_a_ref, d_b_ref):
    fc_a, fc_b = nn(h_ref[...], w1_ref[...]), nn(h_ref[...], w3_ref[...])
    d_hidden = d_hidden_ref[...].astype(F32)
    sigma = jax.nn.sigmoid(fc_a)
    silu_a = fc_a * sigma
    hidden_ref[...] = (silu_a * fc_b).astype(BF16)
    d_a_ref[...] = (d_hidden * fc_b * (sigma * (1.0 + fc_a * (1.0 - sigma)))).astype(BF16)
    d_b_ref[...] = (d_hidden * silu_a).astype(BF16)


def hidden_units(h_two, w1, w3, d_hidden):
    rows, width = h_two.shape
    count = w1.shape[1]
    block, tile = min(512, rows), min(512, count)
    weight = pl.BlockSpec((width, tile), lambda n, m: (0, n))
    spot = pl.BlockSpec((block, tile), lambda n, m: (m, n))
    return pl.pallas_call(
        unit_kernel,
        grid=(count // tile, rows // block),
        out_shape=[jax.ShapeDtypeStruct((rows, count), BF16)] * 3,
        in_specs=[pl.BlockSpec((block, width), lambda n, m: (m, 0)), weight, weight, spot],
        out_specs=[spot] * 3,
        compiler_params=pltpu.CompilerParams(vmem_limit_bytes=60 << 20),
        cost_estimate=FREE,
    )(h_two, w1, w3, d_hidden)


def nn(left, right):
    return lax.dot_general(left, right, (((1,), (0,)), ((), ())), preferred_element_type=F32)


def nt(left, right):
    return lax.dot_general(left, right, (((1,), (1,)), ((), ())), preferred_element_type=F32)


def tn(left, right):
    return lax.dot_general(left, right, (((0,), (0,)), ((), ())), preferred_element_type=F32)


def where_is(whole, chunk, piece_len):
    share_len = piece_len // 2
    spots = []
    for shape, dim in (((piece_len, 1), 0), ((1, piece_len), 1)):
        at = lax.broadcasted_iota(jnp.int32, shape, dim) + whole[2] * share_len
        spots.append(jnp.where(at >= piece_len, at - piece_len, at))
    start = whole[0] * (2 * piece_len) + chunk * piece_len
    return spots[0], spots[1], start


def document(whole, spot):
    seq = pl.program_id(0)
    first, second = whole[3 + 2 * seq], whole[4 + 2 * seq]
    return jnp.where(spot >= second, 2, jnp.where(spot >= first, 1, 0))


def fade(gap, log_keep):
    return jnp.exp(jnp.maximum(gap, 0).astype(F32) * log_keep)


def piece_terms(whole, log_keep, chunk, piece_len):
    rows, cols, start = where_is(whole, chunk, piece_len)
    doc_rows, doc_cols = document(whole, start + rows), document(whole, start + cols)
    before, last = document(whole, start - 1), document(whole, start + piece_len - 1)
    within = jnp.where(
        (rows >= cols) & (doc_rows == doc_cols), fade(rows - cols, log_keep) * SCALE, 0.0
    )
    inflow = jnp.where(doc_rows == before, fade(rows + 1, log_keep) * SCALE, 0.0)
    outflow = jnp.where(doc_rows == last, fade(piece_len - 1 - rows, log_keep), 0.0)
    whole_gap = jnp.full((1, 1), piece_len, jnp.int32)
    over = jnp.where(before == last, fade(whole_gap, log_keep), 0.0)
    return within, inflow, outflow, over


def piece_of(ref, whole, chunk):
    group = lax.rem(chunk + whole[1], 2) * 2
    value = ref[pl.ds(group, 2), 0]
    return value.reshape(value.shape[0] * value.shape[1], value.shape[2])


def put_piece(ref, whole, chunk, value):
    group = lax.rem(chunk + whole[1], 2) * 2
    ref[pl.ds(group, 2), 0] = value.astype(ref.dtype).reshape(2, value.shape[0] // 2, value.shape[1])


def split_kq(ref, whole, chunk):
    both = piece_of(ref, whole, chunk)
    width = both.shape[1] // 2
    return both[:, :width], both[:, width:]


def update_kernel(whole, keeps, kq_ref, v_ref, out_ref):
    log_keep = keeps[pl.program_id(1)]
    piece_len = 2 * kq_ref.shape[2]
    total = jnp.zeros(out_ref.shape[2:], F32)
    for chunk in range(2):
        rows, _, start = where_is(whole, chunk, piece_len)
        last = document(whole, whole[0] * (2 * piece_len) + 2 * piece_len - 1)
        gap = (2 - chunk) * piece_len - 1 - rows
        weight = jnp.where(document(whole, start + rows) == last, fade(gap, log_keep), 0.0)
        keys, _ = split_kq(kq_ref, whole, chunk)
        values = piece_of(v_ref, whole, chunk)
        total = total + tn((keys.astype(F32) * weight).astype(BF16), values)
    out_ref[0, 0] = total.astype(BF16)


def next_state(state, keys, values, outflow, over):
    return over * state + tn((keys.astype(F32) * outflow).astype(BF16), values)


def forward_kernel(
    whole, keeps, kq_ref, v_ref, gate_ref, state_ref, gain_ref, gated_ref, retained_ref
):
    log_keep = keeps[pl.program_id(1)]
    piece_len = 2 * kq_ref.shape[2]
    state = state_ref[0, 0].astype(F32)
    for chunk in range(2):
        within, inflow, outflow, over = piece_terms(whole, log_keep, chunk, piece_len)
        keys, query = split_kq(kq_ref, whole, chunk)
        values = piece_of(v_ref, whole, chunk)
        scores = (nt(query, keys) * within).astype(BF16)
        retained = nn(scores, values) + inflow * nn(query, state.astype(BF16))
        if chunk == 0:
            state = next_state(state, keys, values, outflow, over)
        put_piece(retained_ref, whole, chunk, retained)
        normed, _, _ = norm_rows(retained, gain_ref[0], 0.01)
        gate = piece_of(gate_ref, whole, chunk).astype(F32)
        put_piece(gated_ref, whole, chunk, gate * jax.nn.sigmoid(gate) * normed)


def norm_back_kernel(
    whole,
    keeps,
    d_gated_ref,
    gate_ref,
    retained_ref,
    kq_ref,
    gain_ref,
    d_gate_ref,
    d_retained_ref,
    d_gain_ref,
    leaving_ref,
):
    log_keep = keeps[pl.program_id(1)]
    piece_len = 2 * kq_ref.shape[2]
    total = jnp.zeros(leaving_ref.shape[2:], F32)
    gain = gain_ref[0]
    d_gain = jnp.zeros(gain.shape, F32)
    for chunk in range(2):
        rows, _, start = where_is(whole, chunk, piece_len)
        before = document(whole, whole[0] * (2 * piece_len) - 1)
        gap = chunk * piece_len + rows + 1
        weight = jnp.where(
            document(whole, start + rows) == before, fade(gap, log_keep) * SCALE, 0.0
        )
        _, query = split_kq(kq_ref, whole, chunk)
        retained = piece_of(retained_ref, whole, chunk).astype(F32)
        normed, unit, scale = norm_rows(retained, gain, 0.01)
        gate = piece_of(gate_ref, whole, chunk).astype(F32)
        d_gated = piece_of(d_gated_ref, whole, chunk).astype(F32)
        sigma = jax.nn.sigmoid(gate)
        put_piece(
            d_gate_ref, whole, chunk, d_gated * normed * sigma * (1.0 + gate * (1.0 - sigma))
        )
        d_normed = d_gated * gate * sigma
        d_gain = d_gain + jnp.sum(d_normed * unit, axis=0, keepdims=True)
        d_retained = norm_back(d_normed, unit, scale, gain)
        put_piece(d_retained_ref, whole, chunk, d_retained)
        total = total + tn(query, (d_retained * weight).astype(BF16))
    d_gain_ref[0, 0] = d_gain
    leaving_ref[0, 0] = total.astype(BF16)


def backward_kernel(
    whole, keeps, kq_ref, v_ref, d_retained_ref, state_ref, d_state_ref, d_kq_ref, d_v_ref
):
    log_keep = keeps[pl.program_id(1)]
    piece_len = 2 * kq_ref.shape[2]
    terms = [piece_terms(whole, log_keep, chunk, piece_len) for chunk in range(2)]
    state = state_ref[0, 0].astype(F32)
    keys, _ = split_kq(kq_ref, whole, 0)
    _, _, outflow, over = terms[0]
    states = [state, next_state(state, keys, piece_of(v_ref, whole, 0), outflow, over)]
    d_state = d_state_ref[0, 0].astype(F32)
    for chunk in (1, 0):
        within, inflow, outflow, over = terms[chunk]
        keys, query = split_kq(kq_ref, whole, chunk)
        values = piece_of(v_ref, whole, chunk)
        d_ret = piece_of(d_retained_ref, whole, chunk)
        state_low, d_state_low = states[chunk].astype(BF16), d_state.astype(BF16)
        scores = (nt(query, keys) * within).astype(BF16)
        d_scores = (nt(d_ret, values) * within).astype(BF16)
        d_values = tn(scores, d_ret) + outflow * nn(keys, d_state_low)
        put_piece(d_v_ref, whole, chunk, d_values)
        d_query = nn(d_scores, keys) + inflow * nt(d_ret, state_low)
        d_keys = tn(d_scores, query) + outflow * nt(values, d_state_low)
        put_piece(d_kq_ref, whole, chunk, jnp.concatenate([d_keys, d_query], axis=1))
        if chunk == 1:
            entering = tn(query, (d_ret.astype(F32) * inflow).astype(BF16))
            d_state = over * d_state + entering


def per_head(kernel, scalars, blocks, outs):
    def spec(array, kind):
        if kind == ROWS:
            width = array.shape[3] // heads
            return pl.BlockSpec((4, 1, array.shape[2], width), lambda b, h, *_: (0, b, 0, h))
        if kind == GAINS:
            return pl.BlockSpec((1, *array.shape[1:]), lambda b, h, *_: (h, 0, 0))
        return pl.BlockSpec((1, 1, *array.shape[2:]), lambda b, h, *_: (b, h, 0, 0))

    heads = scalars[1].shape[0]
    seq_count = (scalars[0].shape[0] - 3) // 2
    return pl.pallas_call(
        kernel,
        out_shape=[a for a, _ in outs],
        grid_spec=pltpu.PrefetchScalarGridSpec(
            num_scalar_prefetch=2,
            grid=(seq_count, heads),
            in_specs=[spec(*block) for block in blocks],
            out_specs=[spec(*out) for out in outs],
        ),
        compiler_params=pltpu.CompilerParams(vmem_limit_bytes=56 << 20),
        cost_estimate=FREE,
    )(*scalars, *(a for a, _ in blocks))


def both_quarters(mine, across, first, dim):
    return jnp.concatenate(
        [jnp.where(first, mine, across), jnp.where(first, across, mine)], axis=dim
    )


def paired_body(
    tokens,
    segments,
    forget,
    ln1_gain,
    w_query,
    w_key,
    w_value,
    w_gate,
    norm_gain,
    w_out,
    ln2_gain,
    w_fc_gate,
    w_fc_up,
    w_fc_down,
    cotangent,
):
    place = lax.axis_index(CONTEXT)
    x_at, core, y_at = place // 2, place % 2, lax.axis_index(TENSOR)
    z_at = lax.axis_index(FSDP)
    heads = forget.shape[0] // 2
    qk_width = w_query.shape[1] // forget.shape[0]
    v_width = w_value.shape[1] // forget.shape[0]
    width = tokens.shape[2]
    seq_count, share_len = tokens.shape[0], tokens.shape[1]
    share_rows = seq_count * share_len
    piece_len = 2 * share_len
    chip_len = 2 * piece_len
    v_half = heads * v_width
    forget_half = lax.dynamic_slice_in_dim(forget, core * heads, heads)
    gain_half = lax.dynamic_slice_in_dim(norm_gain, core * v_half, v_half)

    def part(array, first, last):
        return array[first * share_rows : last * share_rows]

    def unit(x_index):
        q = core * 2 + x_index
        key_query = [quarter_of(w_key, 1, q), quarter_of(w_query, 1, q)]
        return [
            jnp.concatenate(key_query, axis=1),
            quarter_of(w_value, 1, q),
            quarter_of(w_gate, 1, q),
            quarter_of(w_out, 0, q),
            quarter_of(w_fc_down, 0, q),
            quarter_of(w_fc_gate, 1, q),
            quarter_of(w_fc_up, 1, q),
        ]

    KQ, V, G, O, W2, W1, W3 = range(7)
    by_rows = [False, False, False, True, True, False, False]
    own, sibling = unit(x_at), unit(1 - x_at)
    size = own[0].shape[0]
    z_last = lax.axis_size(FSDP) - 1
    z_count = z_last + 1
    z_away = [(z_at + hop) % z_count for hop in range(1, z_count)]
    spots = jnp.stack([*range(z_count), *z_away, z_at] + [x_at] * 4 + [1 - x_at] * 4)
    spots = spots.astype(jnp.int32)
    fetched, across = [None] * 7, [None] * 7

    def weight(index):
        blocks = [(fetched[index], row) for row in range(4)]
        blocks += [(across[index], row) for row in range(3)] + [(sibling[index], 0)]
        return assemble(blocks, spots, by_rows[index], size)

    env = SimpleNamespace()
    firsts = jnp.sum((segments == 0).astype(jnp.int32), axis=1)
    seconds = jnp.sum((segments <= 1).astype(jnp.int32), axis=1)
    starts = jnp.stack([firsts, seconds], axis=1).reshape(-1)
    whole = jnp.concatenate([jnp.stack([x_at, core, y_at]).astype(jnp.int32), starts])
    scalars = (whole, jnp.log(1.0 - forget_half))
    gains = gain_half.reshape(heads, 1, v_width)
    state_type = jax.ShapeDtypeStruct((seq_count, heads, qk_width, v_width), BF16)
    rows_type = jax.ShapeDtypeStruct((4, seq_count, share_len, v_half), BF16)
    kq_type = jax.ShapeDtypeStruct((4, seq_count, share_len, 2 * heads * qk_width), BF16)
    gain_type = jax.ShapeDtypeStruct((seq_count, heads, 1, v_width), F32)

    def shaped(rows_in):
        return rows_in.reshape(4, seq_count, share_len, -1)

    def flat(rows_in):
        return rows_in.reshape(4 * share_rows, -1)

    x_share = tokens.reshape(share_rows, width).astype(F32)
    cot_share = cotangent.reshape(share_rows, width)

    def work_norm():
        h1, ln1_normed, ln1_scale = norm_rows(x_share, ln1_gain)
        env.ln1 = (ln1_normed, ln1_scale)
        env.h = h1.astype(BF16)
        env.hy = over_y(env.h)
        return [env.h]

    def work_core():
        env.hc, env.hcy = over_core(env.h), over_core(env.hy)
        env.cy = over_y(cot_share)
        return []

    def work_rows():
        env.h_one = jnp.concatenate([env.h, env.hy, env.hc, env.hcy], axis=0)
        return [env.h_one]

    def work_kq():
        env.wkq = weight(KQ)
        env.kq = sum_of_products(nn, [env.h_one], [env.wkq], 0, 4 * share_rows, BF16)
        return [env.kq]

    def work_v():
        env.wv = weight(V)
        env.v = sum_of_products(nn, [env.h_one], [env.wv], 0, 4 * share_rows, BF16)
        return [env.v]

    def work_state():
        (update,) = per_head(
            update_kernel,
            scalars,
            [(shaped(env.kq), ROWS), (shaped(env.v), ROWS)],
            [(state_type, STATES)],
        )
        env.state = lax.ppermute(update, CONTEXT, UP_X)
        env.cc, env.ccy = over_core(cot_share), over_core(env.cy)
        return [update]

    def work_gate():
        env.wg = weight(G)
        env.gate = sum_of_products(nn, [env.h_one], [env.wg], 0, 4 * share_rows, BF16)
        return [env.gate]

    def work_retained():
        gated, env.retained = per_head(
            forward_kernel,
            scalars,
            [
                (shaped(env.kq), ROWS),
                (shaped(env.v), ROWS),
                (shaped(env.gate), ROWS),
                (env.state, STATES),
                (gains, GAINS),
            ],
            [(rows_type, ROWS), (rows_type, ROWS)],
        )
        env.gated = flat(gated)
        return [env.gated]

    def work_out_far():
        env.wo = weight(O)
        far = sum_of_products(nn, [env.gated], [env.wo], 2 * share_rows, 2 * share_rows, BF16)
        env.far = over_core(far)
        return [far]

    def work_out_near():
        near = sum_of_products(
            nn, [env.gated], [env.wo], share_rows, share_rows, BF16, [(env.far, share_rows)]
        )
        env.near = over_y(near)
        return [near]

    def work_out_own():
        extras = [(env.far, 0), (tokens.reshape(share_rows, width), 0)]
        env.own = sum_of_products(nn, [env.gated], [env.wo], 0, share_rows, F32, extras)
        return [env.own]

    def work_cot():
        env.cot = jnp.concatenate([cot_share, env.cy, env.cc, env.ccy], axis=0)
        return [env.cot]

    def work_d_hidden():
        env.w2 = weight(W2)
        env.d_hidden = sum_of_products(nt, [env.cot], [env.w2], 0, 4 * share_rows, BF16)
        return [env.d_hidden]

    def work_middle():
        env.middle = env.own + env.near.astype(F32)
        h2, ln2_normed, ln2_scale = norm_rows(env.middle, ln2_gain)
        env.ln2 = (ln2_normed, ln2_scale)
        env.h2 = h2.astype(BF16)
        env.h2y, env.h2c = over_y(env.h2), over_core(env.h2)
        return [env.h2]

    def work_up():
        env.w1 = weight(W1)
        return [env.w1]

    def work_h2():
        env.h2cy = over_core(env.h2y)
        env.w3 = weight(W3)
        return [env.w3]

    plan = [
        [work_norm],
        [work_core],
        [work_rows, work_kq, work_v],
        [work_state],
        [work_gate, work_retained, work_out_far],
        [work_out_near, work_out_own, work_cot],
        [work_d_hidden, work_middle],
        [work_up, work_h2],
    ]
    for tick, works in enumerate(plan):
        moving = tick < len(own)
        if moving:
            fetched[tick] = lax.all_gather(own[tick], FSDP, axis=0, tiled=True)
        if tick:
            got = fetched[tick - 1]
            away = [lax.dynamic_slice_in_dim(got, z * size, size, 0) for z in z_away]
            across[tick - 1] = over_x(jnp.concatenate(away, axis=0))
        held = []
        for work in works:
            held += work()
        if not moving:
            continue
        names = [n for n in ("h_one", "kq", "gate", "gated", "cot") if hasattr(env, n)]
        held = held + ([across[tick - 1]] if tick else [])
        tied = list(tie(fetched[tick], *own[tick + 1 :], *[getattr(env, n) for n in names], *held))
        fetched[tick] = tied.pop(0)
        for index in range(tick + 1, len(own)):
            own[index] = tied.pop(0)
        for n in names:
            setattr(env, n, tied.pop(0))

    h_one, gated, gate_pre = env.h_one, env.gated, env.gate
    wkq, wv, wg, wo, w1, w2, w3 = env.wkq, env.wv, env.wg, env.wo, env.w1, env.w2, env.w3
    cot_full, d_hidden, middle = env.cot, env.d_hidden, env.middle

    token = [h_one]

    def step(run, *args):
        *args, _ = tie(*args, token[0])
        out = run(*args)
        token[0] = out[0] if isinstance(out, (tuple, list)) else out
        return out

    def whole_product(product, lefts, rights, first, rows, kind, *extras):
        count = len(lefts)

        def run(*arrays):
            added = [(a, row) for a, (_, row) in zip(arrays[count:], extras)]
            return sum_of_products(
                product, arrays[:count], rights, first * share_rows, rows * share_rows, kind, added
            )

        return step(run, *lefts, *(a for a, _ in extras))

    def theirs(left, right):
        return over_x(step(lambda a, b: quarter_product(a, b, 1 - x_at), left, right))

    def ours(left, right, got):
        total = step(lambda a, b, c: quarter_product(a, b, x_at, [c]), left, right, got)
        return lax.psum_scatter(total, FSDP, scatter_dimension=0, tiled=True)

    def chip_rows(left, right):
        total = step(lambda a, b: split_product(a, b, z_count), left, right)
        return lax.psum_scatter(total, FSDP, scatter_dimension=0, tiled=False)

    def begin_finish(*mine):
        mine = step(lambda *a: jnp.concatenate(a, axis=0), *mine)
        return mine, over_x(mine)

    def end_finish(firsts, mine, beside):
        def join(mine, beside):
            blocks, row = [], 0
            for x_summed in firsts:
                count = 1 if x_summed else 2
                one, other = (a[row * size : (row + count) * size] for a in (mine, beside))
                if x_summed:
                    blocks += [jnp.where(x_at == 0, one, other), jnp.where(x_at == 0, other, one)]
                else:
                    blocks.append((one.astype(F32) + other.astype(F32)).astype(BF16))
                row += count
            return jnp.concatenate(blocks, axis=0)

        both = step(join, mine, beside)
        return both, over_core(both)

    def quarters(pair, at):
        both, other = pair
        mine, theirs = (a[2 * at * size : (2 * at + 2) * size] for a in (both, other))
        first, second = jnp.where(core == 0, mine, theirs), jnp.where(core == 0, theirs, mine)
        return [first[:size], first[size:], second[:size], second[size:]]

    def shard(pair, at, rows):
        return jnp.concatenate(quarters(pair, at), axis=1 - int(rows)).astype(F32)

    h_two = jnp.concatenate([env.h2, env.h2y, env.h2c, env.h2cy], axis=0)
    hidden, d_fca, d_fcb = step(hidden_units, h_two, w1, w3, d_hidden)

    fc_lefts, fc_rights = (d_fca, d_fcb), (w1, w3)
    far = over_core(whole_product(nt, fc_lefts, fc_rights, 2, 2, BF16))
    down_mine = chip_rows(hidden, cot_full)
    near = over_y(whole_product(nt, fc_lefts, fc_rights, 1, 1, BF16, (far, share_rows)))
    gate_got = theirs(h_two, d_fca)
    own_part = whole_product(nt, fc_lefts, fc_rights, 0, 1, F32, (far, 0))
    up_got = theirs(h_two, d_fcb)
    out_far = over_core(whole_product(nn, [hidden], [w2], 2, 2, BF16))

    def middle_back(own_part, near):
        d_h2 = own_part + near.astype(F32)
        ln2_normed, ln2_scale = env.ln2
        d_middle = cot_share.astype(F32) + norm_back(d_h2, ln2_normed, ln2_scale, ln2_gain)
        return d_middle.astype(BF16), d_middle, jnp.sum(d_h2 * ln2_normed, axis=0)

    d_mid_low, d_middle, g_ln2 = step(middle_back, own_part, near)
    d_mid_y, d_mid_c = over_y(d_mid_low), over_core(d_mid_low)
    fc_gate_mine = ours(h_two, d_fca, gate_got)
    out_near = whole_product(nn, [hidden], [w2], 1, 1, BF16, (out_far, share_rows))
    out_own = whole_product(nn, [hidden], [w2], 0, 1, F32, (out_far, 0), (middle, 0))
    d_mid_y, out_near = step(lambda a, b: (a, b), d_mid_y, out_near)
    d_mid_cy = over_core(d_mid_y)
    out_near = over_y(out_near)
    fc_up_mine = ours(h_two, d_fcb, up_got)

    def gate_back(share, y, c, cy):
        d_branch = jnp.concatenate([share, y, c, cy], axis=0)
        return sum_of_products(nt, [d_branch], [wo], 0, 4 * share_rows, BF16), d_branch

    d_gated, d_branch = step(gate_back, d_mid_low, d_mid_y, d_mid_c, d_mid_cy)
    kq, values, state_in = shaped(env.kq), shaped(env.v), env.state

    def retained_back(d_gated, kq):
        return per_head(
            norm_back_kernel,
            scalars,
            [
                (shaped(d_gated), ROWS),
                (shaped(gate_pre), ROWS),
                (env.retained, ROWS),
                (kq, ROWS),
                (gains, GAINS),
            ],
            [(rows_type, ROWS), (rows_type, ROWS), (gain_type, STATES), (state_type, STATES)],
        )

    d_gate, d_retained, g_norm, leaving = step(retained_back, d_gated, kq)
    d_gate = flat(d_gate)
    g_norm = jnp.sum(g_norm, axis=0).reshape(v_half)
    state_grad = lax.ppermute(leaving, CONTEXT, DOWN_X)
    out_mine = chip_rows(gated, d_branch)
    gg_got = theirs(h_one, d_gate)
    down_begun = begin_finish(down_mine)

    def pair_back(d_retained, state_grad):
        return per_head(
            backward_kernel,
            scalars,
            [
                (kq, ROWS),
                (values, ROWS),
                (d_retained, ROWS),
                (state_in, STATES),
                (state_grad, STATES),
            ],
            [(kq_type, ROWS), (rows_type, ROWS)],
        )

    dkq_low, dv_low = step(pair_back, d_retained, state_grad)
    dkq_low, dv_low = flat(dkq_low), flat(dv_low)
    v_got = theirs(h_one, dv_low)
    kq_got = theirs(h_one, dkq_low)
    h1_lefts, h1_rights = (dkq_low, dv_low, d_gate), (wkq, wv, wg)
    far = over_core(whole_product(nt, h1_lefts, h1_rights, 2, 2, BF16))
    gg_mine = ours(h_one, d_gate, gg_got)
    near = over_y(whole_product(nt, h1_lefts, h1_rights, 1, 1, BF16, (far, share_rows)))
    own_part = whole_product(nt, h1_lefts, h1_rights, 0, 1, F32, (far, 0))
    g_down = end_finish([False], *down_begun)
    fc_begun = begin_finish(fc_gate_mine, fc_up_mine)
    v_mine = ours(h_one, dv_low, v_got)
    output = step(lambda a, b: (a + b.astype(F32)).astype(BF16), out_own, out_near)
    g_fc = end_finish([True, True], *fc_begun)
    kq_mine = ours(h_one, dkq_low, kq_got)

    def tokens_back(own_part, near):
        d_h1 = own_part + near.astype(F32)
        ln1_normed, ln1_scale = env.ln1
        grad = d_middle + norm_back(d_h1, ln1_normed, ln1_scale, ln1_gain)
        return grad, jnp.sum(d_h1 * ln1_normed, axis=0)

    grad_tokens, g_ln1 = step(tokens_back, own_part, near)
    out_begun = begin_finish(out_mine, gg_mine)
    v_begun = begin_finish(v_mine)
    g_out_gate = end_finish([False, True], *out_begun)
    kq_begun = begin_finish(kq_mine)
    g_value = end_finish([True], *v_begun)
    g_kq = end_finish([True], *kq_begun)
    sides = quarters(g_kq, 0)
    g_key = jnp.concatenate([side[:, :qk_width] for side in sides], axis=1).astype(F32)
    g_query = jnp.concatenate([side[:, qk_width:] for side in sides], axis=1).astype(F32)

    norm_size = lax.axis_size(TENSOR) * norm_gain.shape[0]
    norm_all = lax.dynamic_update_slice_in_dim(
        jnp.zeros((norm_size,), F32), g_norm, (2 * y_at + core) * v_half, 0
    )
    gain_sums = jnp.concatenate([g_ln1, g_ln2, norm_all])
    for axis in (TENSOR, CONTEXT, FSDP):
        gain_sums = butterfly(gain_sums, axis)
    g_ln1, g_ln2 = gain_sums[:width], gain_sums[width : 2 * width]
    g_norm = lax.dynamic_slice_in_dim(
        gain_sums, 2 * width + y_at * norm_gain.shape[0], norm_gain.shape[0]
    )
    return (
        output.reshape(tokens.shape),
        grad_tokens.reshape(tokens.shape),
        g_ln1,
        g_query,
        g_key,
        shard(g_value, 0, False),
        shard(g_out_gate, 1, False),
        g_norm,
        shard(g_out_gate, 0, True),
        g_ln2,
        shard(g_fc, 0, False),
        shard(g_fc, 1, False),
        shard(g_down, 0, True),
    )


def body(tensor_size, *arrays):
    heads_here = arrays[2].shape[0]
    paired = tensor_size == 2 and heads_here % 2 == 0 and lax.axis_size(CONTEXT) == 4
    paired = paired and lax.axis_size(FSDP) == 4
    return (paired_body if paired else general_body)(*arrays)


def solution(mesh):
    in_specs = (
        P(FSDP, (CONTEXT, TENSOR), None),
        P(FSDP, None),
        P(TENSOR),
        P(),
        P(FSDP, TENSOR),
        P(FSDP, TENSOR),
        P(FSDP, TENSOR),
        P(FSDP, TENSOR),
        P(TENSOR),
        P(TENSOR, FSDP),
        P(),
        P(FSDP, TENSOR),
        P(FSDP, TENSOR),
        P(TENSOR, FSDP),
        P(FSDP, (CONTEXT, TENSOR), None),
    )
    out_specs = (
        P(FSDP, (CONTEXT, TENSOR), None),
        P(FSDP, (CONTEXT, TENSOR), None),
        P(),
        P(FSDP, TENSOR),
        P(FSDP, TENSOR),
        P(FSDP, TENSOR),
        P(FSDP, TENSOR),
        P(TENSOR),
        P(TENSOR, FSDP),
        P(),
        P(FSDP, TENSOR),
        P(FSDP, TENSOR),
        P(TENSOR, FSDP),
    )
    return jax.shard_map(partial(body, mesh.shape[TENSOR]), mesh=mesh, in_specs=in_specs, out_specs=out_specs, check_vma=False)
```

```python
from functools import partial
from types import SimpleNamespace

import jax
import jax.numpy as jnp
from jax import lax
from jax.experimental import pallas as pl
from jax.experimental.pallas import tpu as pltpu
from jax.sharding import PartitionSpec as P

FSDP, CONTEXT, TENSOR = "fsdp", "context", "tensor"

careful = partial(jnp.einsum, precision=lax.Precision.HIGH)


def entering(part, axis, combine, identity):
    place = lax.axis_index(axis)
    gathered = jax.tree.map(lambda a: lax.all_gather(a, axis), part)
    state = jax.tree.map(lambda a, e: jnp.zeros_like(a) + jnp.asarray(e, a.dtype), part, identity)

    def one(step, state):
        return combine(
            state, jax.tree.map(lambda a: lax.dynamic_index_in_dim(a, step, 0, False), gathered)
        )

    return lax.fori_loop(0, place, one, state)


def carried_in(value, axis, combine, identity):
    count, place = (lax.axis_size(axis), lax.axis_index(axis))
    everything = jax.tree.map(
        lambda part, kind: lax.all_gather(part.astype(kind), axis),
        value,
        jax.tree.map(lambda a: jnp.bfloat16 if a.dtype == jnp.float32 else a.dtype, value),
    )
    start = jax.tree.map(
        lambda part, zero: jnp.broadcast_to(jnp.asarray(zero, part.dtype), part.shape),
        value,
        identity,
    )

    def step(k, before):
        at = count - 1 - k
        reached = at > place
        new = combine(
            before, jax.tree.map(lambda part, own: part[at].astype(own.dtype), everything, value)
        )
        return jax.tree.map(lambda a, b: jnp.where(reached, a, b), new, before)

    return lax.fori_loop(0, count, step, start)


def norm_rows(values, gain_vec, epsilon=1e-05):
    centred = values - jnp.mean(values, axis=-1, keepdims=True)
    scale = lax.rsqrt(jnp.mean(centred * centred, axis=-1, keepdims=True) + epsilon)
    normed = centred * scale
    return (normed * gain_vec, normed, scale)


def norm_back(grad_in, normed, scale, gain_vec):
    d_normed = grad_in * gain_vec
    first_mean = jnp.mean(d_normed, axis=-1, keepdims=True)
    second_mean = jnp.mean(d_normed * normed, axis=-1, keepdims=True)
    return scale * (d_normed - first_mean - normed * second_mean)


def swish_slope(values):
    sigma = jax.nn.sigmoid(values)
    return sigma * (1.0 + values * (1.0 - sigma))


def compose(earlier, latter):
    return (earlier[0] * latter[0], latter[0][:, :, None, None] * earlier[1] + latter[1])


def share_gather(piece):
    return lax.all_gather(piece, TENSOR, axis=1, tiled=True)


def branch_sum(terms):
    return lax.psum_scatter(terms, TENSOR, scatter_dimension=1, tiled=True)


def input_sum(terms):
    return lax.psum_scatter(
        terms.astype(jnp.bfloat16), TENSOR, scatter_dimension=1, tiled=True
    ).astype(jnp.float32)


def mixer_fetch(w_query, w_key, w_value, w_gate, w_out):
    return (
        lax.all_gather(w_query, FSDP, axis=0, tiled=True),
        lax.all_gather(w_key, FSDP, axis=0, tiled=True),
        lax.all_gather(w_value, FSDP, axis=0, tiled=True),
        lax.all_gather(w_gate, FSDP, axis=0, tiled=True),
        lax.all_gather(w_out, FSDP, axis=1, tiled=True),
    )


def mlp_fetch(w_fc_gate, w_fc_up, w_fc_down):
    return (
        lax.all_gather(w_fc_gate, FSDP, axis=0, tiled=True),
        lax.all_gather(w_fc_up, FSDP, axis=0, tiled=True),
        lax.all_gather(w_fc_down, FSDP, axis=1, tiled=True),
    )


def product(form, left, right):
    return jnp.einsum(form, left, right, preferred_element_type=jnp.float32)


def general_body(
    tokens,
    segments,
    forget,
    ln1_gain,
    w_query,
    w_key,
    w_value,
    w_gate,
    norm_gain,
    w_out,
    ln2_gain,
    w_fc_gate,
    w_fc_up,
    w_fc_down,
    cotangent,
):
    heads_here = forget.shape[0]
    qk_width = w_query.shape[1] // heads_here
    v_width = w_value.shape[1] // heads_here
    v_local = heads_here * v_width
    gain_heads = norm_gain.reshape(heads_here, v_width)
    x_share = tokens.astype(jnp.float32)
    h1_share, ln1_normed, ln1_scale = norm_rows(x_share, ln1_gain)
    h_one = share_gather(h1_share.astype(jnp.bfloat16))
    wq_all, wk_all, wv_all, wg_all, wo_all = mixer_fetch(w_query, w_key, w_value, w_gate, w_out)
    seq_count, stretch_len = (h_one.shape[0], h_one.shape[1])
    query = product("btd,dq->btq", h_one, wq_all).astype(jnp.bfloat16)
    keys = product("btd,dq->btq", h_one, wk_all).astype(jnp.bfloat16)
    values = product("btd,dv->btv", h_one, wv_all).astype(jnp.bfloat16)
    gate_pre = product("btd,dv->btv", h_one, wg_all)
    query_heads = query.reshape(seq_count, stretch_len, heads_here, qk_width)
    keys_heads = keys.reshape(seq_count, stretch_len, heads_here, qk_width)
    query_full = query_heads.astype(jnp.float32) * 0.0625
    keys_full = keys_heads.astype(jnp.float32)
    values_full = values.astype(jnp.float32).reshape(seq_count, stretch_len, heads_here, v_width)
    log_keep = jnp.log(1.0 - forget)
    ctx_place = lax.axis_index(CONTEXT)
    seg_stretch = lax.dynamic_slice_in_dim(segments, ctx_place * stretch_len, stretch_len, 1)
    seg_prev = lax.dynamic_slice_in_dim(segments, jnp.maximum(ctx_place * stretch_len - 1, 0), 1, 1)
    live_mask = (seg_stretch == seg_prev).astype(jnp.float32)
    steps_idx = jnp.arange(stretch_len, dtype=jnp.float32)
    step_gap = jnp.maximum(steps_idx[:, None] - steps_idx[None, :], 0.0)
    causal = steps_idx[:, None] >= steps_idx[None, :]
    same_doc = (seg_stretch[:, :, None] == seg_stretch[:, None, :]) & causal[None]
    weights_mask = jnp.where(
        same_doc[:, None], jnp.exp(step_gap[None] * log_keep[:, None, None])[None], 0.0
    )
    inflow = live_mask[:, :, None] * jnp.exp((steps_idx[:, None] + 1.0) * log_keep[None, :])[None]
    outflow = (seg_stretch == seg_stretch[:, -1:]).astype(jnp.float32)[:, :, None] * jnp.exp(
        (stretch_len - 1.0 - steps_idx)[:, None] * log_keep[None, :]
    )[None]
    carry_decay = live_mask[:, -1:] * jnp.exp(stretch_len * log_keep)[None, :]
    update = careful("bshd,bsh,bshe->bhde", keys_full, outflow, values_full)
    identity = (jnp.ones_like(carry_decay), jnp.zeros_like(update))
    state_in = entering((carry_decay, update), CONTEXT, compose, identity)[1]
    scores = product("bthd,bshd->bhts", query_heads, keys_heads) * 0.0625 * weights_mask
    retained = careful("bhts,bshe->bthe", scores, values_full)
    retained = retained + inflow[..., None] * careful("bthd,bhde->bthe", query_full, state_in)
    normed_out, gn_normed, gn_scale = norm_rows(retained, gain_heads, 0.01)
    norm_flat = normed_out.reshape(seq_count, stretch_len, v_local)
    gate_act = jax.nn.silu(gate_pre)
    gated = (gate_act * norm_flat).astype(jnp.bfloat16)
    middle = x_share + branch_sum(product("btv,vd->btd", gated, wo_all))
    h2_share, ln2_normed, ln2_scale = norm_rows(middle, ln2_gain)
    h_two = share_gather(h2_share.astype(jnp.bfloat16))
    w1_all, w3_all, w2_all = mlp_fetch(w_fc_gate, w_fc_up, w_fc_down)
    fc_a = product("btd,df->btf", h_two, w1_all)
    fc_b = product("btd,df->btf", h_two, w3_all)
    silu_a = jax.nn.silu(fc_a)
    hidden = (silu_a * fc_b).astype(jnp.bfloat16)
    output = (middle + branch_sum(product("btf,fd->btd", hidden, w2_all))).astype(jnp.bfloat16)
    wq_all, wk_all, wv_all, wg_all, wo_all = mixer_fetch(w_query, w_key, w_value, w_gate, w_out)
    w1_all, w3_all, w2_all = mlp_fetch(w_fc_gate, w_fc_up, w_fc_down)
    cot_full = share_gather(cotangent)
    d_hidden = product("btd,fd->btf", cot_full, w2_all)
    g_down = product("btf,btd->fd", hidden, cot_full)
    d_fca = (d_hidden * fc_b * swish_slope(fc_a)).astype(jnp.bfloat16)
    d_fcb = (d_hidden * silu_a).astype(jnp.bfloat16)
    g_fc_gate = product("btd,btf->df", h_two, d_fca)
    g_fc_up = product("btd,btf->df", h_two, d_fcb)
    d_h2 = input_sum(product("btf,df->btd", d_fca, w1_all) + product("btf,df->btd", d_fcb, w3_all))
    d_middle = cotangent.astype(jnp.float32) + norm_back(d_h2, ln2_normed, ln2_scale, ln2_gain)
    g_ln2 = jnp.sum(d_h2 * ln2_normed, axis=(0, 1))
    d_branch = share_gather(d_middle.astype(jnp.bfloat16))
    d_gated = product("btd,vd->btv", d_branch, wo_all)
    g_out = product("btv,btd->vd", gated, d_branch)
    d_gate = (d_gated * norm_flat * swish_slope(gate_pre)).astype(jnp.bfloat16)
    d_normed = (d_gated * gate_act).reshape(seq_count, stretch_len, heads_here, v_width)
    g_norm = jnp.sum(d_normed * gn_normed, axis=(0, 1)).reshape(v_local)
    d_retained = norm_back(d_normed, gn_normed, gn_scale, gain_heads)
    d_scores = careful("bthe,bshe->bhts", d_retained, values_full) * weights_mask
    d_values = careful("bhts,bthe->bshe", scores, d_retained)
    d_query = careful("bhts,bshd->bthd", d_scores, keys_full)
    d_query = d_query + inflow[..., None] * careful("bthe,bhde->bthd", d_retained, state_in)
    d_keys = careful("bhts,bthd->bshd", d_scores, query_full)
    leaving = careful("bthd,bth,bthe->bhde", query_full, inflow, d_retained)
    state_grad = carried_in((carry_decay, leaving), CONTEXT, compose, identity)[1]
    d_keys = d_keys + outflow[..., None] * careful("bshe,bhde->bshd", values_full, state_grad)
    d_values = d_values + outflow[..., None] * careful("bshd,bhde->bshe", keys_full, state_grad)
    dq_low = (
        (d_query * 0.0625)
        .reshape(seq_count, stretch_len, heads_here * qk_width)
        .astype(jnp.bfloat16)
    )
    dk_low = d_keys.reshape(seq_count, stretch_len, heads_here * qk_width).astype(jnp.bfloat16)
    dv_low = d_values.reshape(seq_count, stretch_len, v_local).astype(jnp.bfloat16)
    g_query = product("btd,btq->dq", h_one, dq_low)
    g_key = product("btd,btq->dq", h_one, dk_low)
    g_value = product("btd,btv->dv", h_one, dv_low)
    g_gate = product("btd,btv->dv", h_one, d_gate)
    d_h1 = product("btq,dq->btd", dq_low, wq_all) + product("btq,dq->btd", dk_low, wk_all)
    d_h1 = d_h1 + product("btv,dv->btd", dv_low, wv_all) + product("btv,dv->btd", d_gate, wg_all)
    d_h1 = input_sum(d_h1)
    grad_tokens = d_middle + norm_back(d_h1, ln1_normed, ln1_scale, ln1_gain)
    g_ln1 = jnp.sum(d_h1 * ln1_normed, axis=(0, 1))
    tensor_place = lax.axis_index(TENSOR)
    norm_full = lax.dynamic_update_slice(
        jnp.zeros((v_local * lax.axis_size(TENSOR),), jnp.float32),
        g_norm,
        (tensor_place * v_local,),
    )
    g_ln1, g_ln2, norm_full = lax.psum((g_ln1, g_ln2, norm_full), (FSDP, CONTEXT, TENSOR))
    g_norm = lax.dynamic_slice_in_dim(norm_full, tensor_place * v_local, v_local)
    weight_grads = (g_query, g_key, g_value, g_gate, g_out, g_fc_gate, g_fc_up, g_down)
    summed = (
        lax.psum(weight_grads[0].astype(jnp.bfloat16), CONTEXT).astype(jnp.float32),
        lax.psum(weight_grads[1].astype(jnp.bfloat16), CONTEXT).astype(jnp.float32),
        lax.psum(weight_grads[2].astype(jnp.bfloat16), CONTEXT).astype(jnp.float32),
        lax.psum(weight_grads[3].astype(jnp.bfloat16), CONTEXT).astype(jnp.float32),
        lax.psum(weight_grads[4].astype(jnp.bfloat16), CONTEXT).astype(jnp.float32),
        lax.psum(weight_grads[5].astype(jnp.bfloat16), CONTEXT).astype(jnp.float32),
        lax.psum(weight_grads[6].astype(jnp.bfloat16), CONTEXT).astype(jnp.float32),
        lax.psum(weight_grads[7].astype(jnp.bfloat16), CONTEXT).astype(jnp.float32),
    )
    shards = (
        lax.psum_scatter(
            summed[0].astype(jnp.bfloat16), FSDP, scatter_dimension=0, tiled=True
        ).astype(jnp.float32),
        lax.psum_scatter(
            summed[1].astype(jnp.bfloat16), FSDP, scatter_dimension=0, tiled=True
        ).astype(jnp.float32),
        lax.psum_scatter(
            summed[2].astype(jnp.bfloat16), FSDP, scatter_dimension=0, tiled=True
        ).astype(jnp.float32),
        lax.psum_scatter(
            summed[3].astype(jnp.bfloat16), FSDP, scatter_dimension=0, tiled=True
        ).astype(jnp.float32),
        lax.psum_scatter(
            summed[4].astype(jnp.bfloat16), FSDP, scatter_dimension=1, tiled=True
        ).astype(jnp.float32),
        lax.psum_scatter(
            summed[5].astype(jnp.bfloat16), FSDP, scatter_dimension=0, tiled=True
        ).astype(jnp.float32),
        lax.psum_scatter(
            summed[6].astype(jnp.bfloat16), FSDP, scatter_dimension=0, tiled=True
        ).astype(jnp.float32),
        lax.psum_scatter(
            summed[7].astype(jnp.bfloat16), FSDP, scatter_dimension=1, tiled=True
        ).astype(jnp.float32),
    )
    return (
        output,
        grad_tokens,
        g_ln1,
        shards[0],
        shards[1],
        shards[2],
        shards[3],
        g_norm,
        shards[4],
        g_ln2,
        shards[5],
        shards[6],
        shards[7],
    )


F32 = jnp.float32
BF16 = jnp.bfloat16
BOTH_X = [(0, 2), (2, 0), (1, 3), (3, 1)]
UP_X = [(0, 2), (1, 3)]
DOWN_X = [(2, 0), (3, 1)]
CORES = [(0, 1), (1, 0), (2, 3), (3, 2)]
UP_Z = [[(0, 1), (1, 2), (2, 3)], [(1, 2), (2, 3)]]
DOWN_Z = [[(3, 2), (2, 1), (1, 0)], [(2, 1), (1, 0)]]
LAST_Z = [(2, 3), (1, 0)]
SCALE = 0.0625
ROWS, GAINS, STATES = range(3)
FREE = pl.CostEstimate(flops=0, transcendentals=0, bytes_accessed=0)
DOWN_Z = [[(3, 2), (2, 1), (1, 0)], [(2, 1), (1, 0)], [(1, 0)]]


def over_x(value):
    return lax.ppermute(value, CONTEXT, BOTH_X)


def over_core(value):
    return lax.ppermute(value, CONTEXT, CORES)


def over_y(value):
    return lax.ppermute(value, TENSOR, [(0, 1), (1, 0)])


def tie(*values):
    return lax.optimization_barrier(values)


def butterfly(value, axis):
    size = lax.axis_size(axis)
    step = 1
    while step < size:
        value = value + lax.ppermute(value, axis, [(i, i ^ step) for i in range(size)])
        step *= 2
    return value


def quarter_of(weight, dim, index):
    size = weight.shape[dim] // 4
    return lax.dynamic_slice_in_dim(weight, index * size, size, dim)


def assemble_kernel(spot_ref, *refs):
    at = pl.program_id(0)
    for index, block in enumerate(refs[:8]):

        @pl.when(at == index)
        def _(block=block):
            refs[8][...] = block[...]


def assemble(blocks, spots, by_rows, size):
    shape = (2 * size, 4 * size) if by_rows else (4 * size, 2 * size)

    def spot(at, spots_ref):
        z_from, x_from = spots_ref[at], spots_ref[8 + at]
        return (x_from, z_from) if by_rows else (z_from, x_from)

    return pl.pallas_call(
        assemble_kernel,
        out_shape=jax.ShapeDtypeStruct(shape, BF16),
        grid_spec=pltpu.PrefetchScalarGridSpec(
            num_scalar_prefetch=1,
            grid=(8,),
            in_specs=[
                pl.BlockSpec((size, size), lambda at, spots_ref, row=row: (row, 0))
                for _, row in blocks
            ],
            out_specs=pl.BlockSpec((size, size), spot),
        ),
        compiler_params=pltpu.CompilerParams(vmem_limit_bytes=32 << 20),
        cost_estimate=FREE,
    )(spots, *(array for array, _ in blocks))


def sum_kernel(product, count, *refs):
    lefts, rights, extras, out_ref = refs[:count], refs[count : 2 * count], refs[2 * count : -1], refs[-1]
    total = product(lefts[0][...], rights[0][...])
    for left, right in zip(lefts[1:], rights[1:]):
        total = total + product(left[...], right[...])
    for extra in extras:
        total = total + extra[...].astype(F32)
    out_ref[...] = total.astype(out_ref.dtype)


def sum_of_products(product, lefts, rights, first, rows, kind, extras=()):
    by_columns = product is nn
    width = rights[0].shape[1 if by_columns else 0]
    block, tile = min(1024, rows), min(512, width)

    def right_spec(right):
        if by_columns:
            return pl.BlockSpec((right.shape[0], tile), lambda n, m: (0, n))
        return pl.BlockSpec((tile, right.shape[1]), lambda n, m: (n, 0))

    def tile_spec(from_row):
        return pl.BlockSpec((block, tile), lambda n, m: (from_row // block + m, n))

    return pl.pallas_call(
        partial(sum_kernel, product, len(lefts)),
        grid=(width // tile, rows // block),
        out_shape=jax.ShapeDtypeStruct((rows, width), kind),
        in_specs=[
            pl.BlockSpec((block, left.shape[1]), lambda n, m: (first // block + m, 0))
            for left in lefts
        ]
        + [right_spec(right) for right in rights]
        + [tile_spec(from_row) for _, from_row in extras],
        out_specs=tile_spec(0),
        compiler_params=pltpu.CompilerParams(vmem_limit_bytes=60 << 20),
        cost_estimate=FREE,
    )(*lefts, *rights, *(array for array, _ in extras))


def quarter_kernel(spots_ref, left, right, *rest):
    total = tn(left[...], right[...])
    for extra in rest[:-1]:
        total = total + extra[...].astype(F32)
    rest[-1][...] = total.astype(BF16)


def quarter_product(left, right, index, extras=()):
    tokens, width = left.shape
    size, block = right.shape[1] // 2, min(1024, width)
    return pl.pallas_call(
        quarter_kernel,
        out_shape=jax.ShapeDtypeStruct((width, size), BF16),
        grid_spec=pltpu.PrefetchScalarGridSpec(
            num_scalar_prefetch=1,
            grid=(width // block,),
            in_specs=[
                pl.BlockSpec((tokens, block), lambda m, at: (0, m)),
                pl.BlockSpec((tokens, size), lambda m, at: (0, at[0])),
            ]
            + [pl.BlockSpec((block, size), lambda m, at: (m, 0)) for _ in extras],
            out_specs=pl.BlockSpec((block, size), lambda m, at: (m, 0)),
        ),
        compiler_params=pltpu.CompilerParams(vmem_limit_bytes=60 << 20),
        cost_estimate=FREE,
    )(index.reshape(1).astype(jnp.int32), left, right, *extras)


def split_kernel(left, right, out):
    out[0] = tn(left[...], right[...]).astype(BF16)


def split_product(left, right, count):
    tokens, rows = left.shape
    size = right.shape[1] // count
    return pl.pallas_call(
        split_kernel,
        grid=(count,),
        out_shape=jax.ShapeDtypeStruct((count, rows, size), BF16),
        in_specs=[
            pl.BlockSpec((tokens, rows), lambda n: (0, 0)),
            pl.BlockSpec((tokens, size), lambda n: (0, n)),
        ],
        out_specs=pl.BlockSpec((1, rows, size), lambda n: (n, 0, 0)),
        compiler_params=pltpu.CompilerParams(vmem_limit_bytes=60 << 20),
        cost_estimate=FREE,
    )(left, right)


def unit_kernel(h_ref, w1_ref, w3_ref, d_hidden_ref, hidden_ref, d_a_ref, d_b_ref):
    fc_a, fc_b = nn(h_ref[...], w1_ref[...]), nn(h_ref[...], w3_ref[...])
    d_hidden = d_hidden_ref[...].astype(F32)
    sigma = jax.nn.sigmoid(fc_a)
    silu_a = fc_a * sigma
    hidden_ref[...] = (silu_a * fc_b).astype(BF16)
    d_a_ref[...] = (d_hidden * fc_b * (sigma * (1.0 + fc_a * (1.0 - sigma)))).astype(BF16)
    d_b_ref[...] = (d_hidden * silu_a).astype(BF16)


def hidden_units(h_two, w1, w3, d_hidden):
    rows, width = h_two.shape
    count = w1.shape[1]
    block, tile = min(512, rows), min(512, count)
    weight = pl.BlockSpec((width, tile), lambda n, m: (0, n))
    spot = pl.BlockSpec((block, tile), lambda n, m: (m, n))
    return pl.pallas_call(
        unit_kernel,
        grid=(count // tile, rows // block),
        out_shape=[jax.ShapeDtypeStruct((rows, count), BF16)] * 3,
        in_specs=[pl.BlockSpec((block, width), lambda n, m: (m, 0)), weight, weight, spot],
        out_specs=[spot] * 3,
        compiler_params=pltpu.CompilerParams(vmem_limit_bytes=60 << 20),
        cost_estimate=FREE,
    )(h_two, w1, w3, d_hidden)


def nn(left, right):
    return lax.dot_general(left, right, (((1,), (0,)), ((), ())), preferred_element_type=F32)


def nt(left, right):
    return lax.dot_general(left, right, (((1,), (1,)), ((), ())), preferred_element_type=F32)


def tn(left, right):
    return lax.dot_general(left, right, (((0,), (0,)), ((), ())), preferred_element_type=F32)


def where_is(whole, chunk, piece_len):
    share_len = piece_len // 2
    spots = []
    for shape, dim in (((piece_len, 1), 0), ((1, piece_len), 1)):
        at = lax.broadcasted_iota(jnp.int32, shape, dim) + whole[2] * share_len
        spots.append(jnp.where(at >= piece_len, at - piece_len, at))
    start = whole[0] * (2 * piece_len) + chunk * piece_len
    return spots[0], spots[1], start


def document(whole, spot):
    seq = pl.program_id(0)
    first, second = whole[3 + 2 * seq], whole[4 + 2 * seq]
    return jnp.where(spot >= second, 2, jnp.where(spot >= first, 1, 0))


def fade(gap, log_keep):
    return jnp.exp(jnp.maximum(gap, 0).astype(F32) * log_keep)


def piece_terms(whole, log_keep, chunk, piece_len):
    rows, cols, start = where_is(whole, chunk, piece_len)
    doc_rows, doc_cols = document(whole, start + rows), document(whole, start + cols)
    before, last = document(whole, start - 1), document(whole, start + piece_len - 1)
    within = jnp.where(
        (rows >= cols) & (doc_rows == doc_cols), fade(rows - cols, log_keep) * SCALE, 0.0
    )
    inflow = jnp.where(doc_rows == before, fade(rows + 1, log_keep) * SCALE, 0.0)
    outflow = jnp.where(doc_rows == last, fade(piece_len - 1 - rows, log_keep), 0.0)
    whole_gap = jnp.full((1, 1), piece_len, jnp.int32)
    over = jnp.where(before == last, fade(whole_gap, log_keep), 0.0)
    return within, inflow, outflow, over


def piece_of(ref, whole, chunk):
    group = lax.rem(chunk + whole[1], 2) * 2
    value = ref[pl.ds(group, 2), 0]
    return value.reshape(value.shape[0] * value.shape[1], value.shape[2])


def put_piece(ref, whole, chunk, value):
    group = lax.rem(chunk + whole[1], 2) * 2
    ref[pl.ds(group, 2), 0] = value.astype(ref.dtype).reshape(2, value.shape[0] // 2, value.shape[1])


def split_kq(ref, whole, chunk):
    both = piece_of(ref, whole, chunk)
    width = both.shape[1] // 2
    return both[:, :width], both[:, width:]


def update_kernel(whole, keeps, kq_ref, v_ref, out_ref):
    log_keep = keeps[pl.program_id(1)]
    piece_len = 2 * kq_ref.shape[2]
    total = jnp.zeros(out_ref.shape[2:], F32)
    for chunk in range(2):
        rows, _, start = where_is(whole, chunk, piece_len)
        last = document(whole, whole[0] * (2 * piece_len) + 2 * piece_len - 1)
        gap = (2 - chunk) * piece_len - 1 - rows
        weight = jnp.where(document(whole, start + rows) == last, fade(gap, log_keep), 0.0)
        keys, _ = split_kq(kq_ref, whole, chunk)
        values = piece_of(v_ref, whole, chunk)
        total = total + tn((keys.astype(F32) * weight).astype(BF16), values)
    out_ref[0, 0] = total.astype(BF16)


def next_state(state, keys, values, outflow, over):
    return over * state + tn((keys.astype(F32) * outflow).astype(BF16), values)


def forward_kernel(
    whole, keeps, kq_ref, v_ref, gate_ref, state_ref, gain_ref, gated_ref, retained_ref
):
    log_keep = keeps[pl.program_id(1)]
    piece_len = 2 * kq_ref.shape[2]
    state = state_ref[0, 0].astype(F32)
    for chunk in range(2):
        within, inflow, outflow, over = piece_terms(whole, log_keep, chunk, piece_len)
        keys, query = split_kq(kq_ref, whole, chunk)
        values = piece_of(v_ref, whole, chunk)
        scores = (nt(query, keys) * within).astype(BF16)
        retained = nn(scores, values) + inflow * nn(query, state.astype(BF16))
        if chunk == 0:
            state = next_state(state, keys, values, outflow, over)
        put_piece(retained_ref, whole, chunk, retained)
        normed, _, _ = norm_rows(retained, gain_ref[0], 0.01)
        gate = piece_of(gate_ref, whole, chunk).astype(F32)
        put_piece(gated_ref, whole, chunk, gate * jax.nn.sigmoid(gate) * normed)


def norm_back_kernel(
    whole,
    keeps,
    d_gated_ref,
    gate_ref,
    retained_ref,
    kq_ref,
    gain_ref,
    d_gate_ref,
    d_retained_ref,
    d_gain_ref,
    leaving_ref,
):
    log_keep = keeps[pl.program_id(1)]
    piece_len = 2 * kq_ref.shape[2]
    total = jnp.zeros(leaving_ref.shape[2:], F32)
    gain = gain_ref[0]
    d_gain = jnp.zeros(gain.shape, F32)
    for chunk in range(2):
        rows, _, start = where_is(whole, chunk, piece_len)
        before = document(whole, whole[0] * (2 * piece_len) - 1)
        gap = chunk * piece_len + rows + 1
        weight = jnp.where(
            document(whole, start + rows) == before, fade(gap, log_keep) * SCALE, 0.0
        )
        _, query = split_kq(kq_ref, whole, chunk)
        retained = piece_of(retained_ref, whole, chunk).astype(F32)
        normed, unit, scale = norm_rows(retained, gain, 0.01)
        gate = piece_of(gate_ref, whole, chunk).astype(F32)
        d_gated = piece_of(d_gated_ref, whole, chunk).astype(F32)
        sigma = jax.nn.sigmoid(gate)
        put_piece(
            d_gate_ref, whole, chunk, d_gated * normed * sigma * (1.0 + gate * (1.0 - sigma))
        )
        d_normed = d_gated * gate * sigma
        d_gain = d_gain + jnp.sum(d_normed * unit, axis=0, keepdims=True)
        d_retained = norm_back(d_normed, unit, scale, gain)
        put_piece(d_retained_ref, whole, chunk, d_retained)
        total = total + tn(query, (d_retained * weight).astype(BF16))
    d_gain_ref[0, 0] = d_gain
    leaving_ref[0, 0] = total.astype(BF16)


def backward_kernel(
    whole, keeps, kq_ref, v_ref, d_retained_ref, state_ref, d_state_ref, d_kq_ref, d_v_ref
):
    log_keep = keeps[pl.program_id(1)]
    piece_len = 2 * kq_ref.shape[2]
    terms = [piece_terms(whole, log_keep, chunk, piece_len) for chunk in range(2)]
    state = state_ref[0, 0].astype(F32)
    keys, _ = split_kq(kq_ref, whole, 0)
    _, _, outflow, over = terms[0]
    states = [state, next_state(state, keys, piece_of(v_ref, whole, 0), outflow, over)]
    d_state = d_state_ref[0, 0].astype(F32)
    for chunk in (1, 0):
        within, inflow, outflow, over = terms[chunk]
        keys, query = split_kq(kq_ref, whole, chunk)
        values = piece_of(v_ref, whole, chunk)
        d_ret = piece_of(d_retained_ref, whole, chunk)
        state_low, d_state_low = states[chunk].astype(BF16), d_state.astype(BF16)
        scores = (nt(query, keys) * within).astype(BF16)
        d_scores = (nt(d_ret, values) * within).astype(BF16)
        d_values = tn(scores, d_ret) + outflow * nn(keys, d_state_low)
        put_piece(d_v_ref, whole, chunk, d_values)
        d_query = nn(d_scores, keys) + inflow * nt(d_ret, state_low)
        d_keys = tn(d_scores, query) + outflow * nt(values, d_state_low)
        put_piece(d_kq_ref, whole, chunk, jnp.concatenate([d_keys, d_query], axis=1))
        if chunk == 1:
            entering = tn(query, (d_ret.astype(F32) * inflow).astype(BF16))
            d_state = over * d_state + entering


def per_head(kernel, scalars, blocks, outs):
    def spec(array, kind):
        if kind == ROWS:
            width = array.shape[3] // heads
            return pl.BlockSpec((4, 1, array.shape[2], width), lambda b, h, *_: (0, b, 0, h))
        if kind == GAINS:
            return pl.BlockSpec((1, *array.shape[1:]), lambda b, h, *_: (h, 0, 0))
        return pl.BlockSpec((1, 1, *array.shape[2:]), lambda b, h, *_: (b, h, 0, 0))

    heads = scalars[1].shape[0]
    seq_count = (scalars[0].shape[0] - 3) // 2
    return pl.pallas_call(
        kernel,
        out_shape=[a for a, _ in outs],
        grid_spec=pltpu.PrefetchScalarGridSpec(
            num_scalar_prefetch=2,
            grid=(seq_count, heads),
            in_specs=[spec(*block) for block in blocks],
            out_specs=[spec(*out) for out in outs],
        ),
        compiler_params=pltpu.CompilerParams(vmem_limit_bytes=56 << 20),
        cost_estimate=FREE,
    )(*scalars, *(a for a, _ in blocks))


def both_quarters(mine, across, first, dim):
    return jnp.concatenate(
        [jnp.where(first, mine, across), jnp.where(first, across, mine)], axis=dim
    )


def paired_body(
    tokens,
    segments,
    forget,
    ln1_gain,
    w_query,
    w_key,
    w_value,
    w_gate,
    norm_gain,
    w_out,
    ln2_gain,
    w_fc_gate,
    w_fc_up,
    w_fc_down,
    cotangent,
):
    place = lax.axis_index(CONTEXT)
    x_at, core, y_at = place // 2, place % 2, lax.axis_index(TENSOR)
    z_at = lax.axis_index(FSDP)
    heads = forget.shape[0] // 2
    qk_width = w_query.shape[1] // forget.shape[0]
    v_width = w_value.shape[1] // forget.shape[0]
    width = tokens.shape[2]
    seq_count, share_len = tokens.shape[0], tokens.shape[1]
    share_rows = seq_count * share_len
    piece_len = 2 * share_len
    chip_len = 2 * piece_len
    v_half = heads * v_width
    forget_half = lax.dynamic_slice_in_dim(forget, core * heads, heads)
    gain_half = lax.dynamic_slice_in_dim(norm_gain, core * v_half, v_half)

    def part(array, first, last):
        return array[first * share_rows : last * share_rows]

    def unit(x_index):
        q = core * 2 + x_index
        key_query = [quarter_of(w_key, 1, q), quarter_of(w_query, 1, q)]
        return [
            jnp.concatenate(key_query, axis=1),
            quarter_of(w_value, 1, q),
            quarter_of(w_gate, 1, q),
            quarter_of(w_out, 0, q),
            quarter_of(w_fc_down, 0, q),
            quarter_of(w_fc_gate, 1, q),
            quarter_of(w_fc_up, 1, q),
        ]

    KQ, V, G, O, W2, W1, W3 = range(7)
    by_rows = [False, False, False, True, True, False, False]
    own, sibling = unit(x_at), unit(1 - x_at)
    size = own[0].shape[0]
    z_last = lax.axis_size(FSDP) - 1
    z_count = z_last + 1
    s_one = jnp.where(z_at == 0, 1, z_at - 1)
    s_three = jnp.where(z_at == z_last, 0, jnp.where(z_at == 1, 2, z_last))
    z_spots = [z_at, s_one, z_at ^ 2, s_three]
    spots = jnp.stack(z_spots + z_spots + [x_at] * 4 + [1 - x_at] * 4).astype(jnp.int32)
    groups = [[KQ, V], [G], [O], [W2, W1, W3]]
    slots, across = [[], [], [], []], [[], [], [], []]

    def weight(index):
        at, row = next((i, g.index(index)) for i, g in enumerate(groups) if index in g)
        blocks = [(own[index], 0)] + [(array, row) for array in slots[at]]
        blocks += [(sibling[index], 0)] + [(array, row) for array in across[at]]
        return assemble(blocks, spots, by_rows[index], size)

    env = SimpleNamespace()
    firsts = jnp.sum((segments == 0).astype(jnp.int32), axis=1)
    seconds = jnp.sum((segments <= 1).astype(jnp.int32), axis=1)
    starts = jnp.stack([firsts, seconds], axis=1).reshape(-1)
    whole = jnp.concatenate([jnp.stack([x_at, core, y_at]).astype(jnp.int32), starts])
    scalars = (whole, jnp.log(1.0 - forget_half))
    gains = gain_half.reshape(heads, 1, v_width)
    state_type = jax.ShapeDtypeStruct((seq_count, heads, qk_width, v_width), BF16)
    rows_type = jax.ShapeDtypeStruct((4, seq_count, share_len, v_half), BF16)
    kq_type = jax.ShapeDtypeStruct((4, seq_count, share_len, 2 * heads * qk_width), BF16)
    gain_type = jax.ShapeDtypeStruct((seq_count, heads, 1, v_width), F32)

    def shaped(rows_in):
        return rows_in.reshape(4, seq_count, share_len, -1)

    def flat(rows_in):
        return rows_in.reshape(4 * share_rows, -1)

    x_share = tokens.reshape(share_rows, width).astype(F32)
    cot_share = cotangent.reshape(share_rows, width)

    def work_norm():
        h1, ln1_normed, ln1_scale = norm_rows(x_share, ln1_gain)
        env.ln1 = (ln1_normed, ln1_scale)
        env.h = h1.astype(BF16)
        env.hy = over_y(env.h)
        return [env.h]

    def work_core():
        env.hc, env.hcy = over_core(env.h), over_core(env.hy)
        env.cy = over_y(cot_share)
        return []

    def work_rows():
        env.h_one = jnp.concatenate([env.h, env.hy, env.hc, env.hcy], axis=0)
        return [env.h_one]

    def work_kq():
        env.wkq = weight(KQ)
        env.kq = sum_of_products(nn, [env.h_one], [env.wkq], 0, 4 * share_rows, BF16)
        return [env.kq]

    def work_v():
        env.wv = weight(V)
        env.v = sum_of_products(nn, [env.h_one], [env.wv], 0, 4 * share_rows, BF16)
        return [env.v]

    def work_state():
        (update,) = per_head(
            update_kernel,
            scalars,
            [(shaped(env.kq), ROWS), (shaped(env.v), ROWS)],
            [(state_type, STATES)],
        )
        env.state = lax.ppermute(update, CONTEXT, UP_X)
        env.cc, env.ccy = over_core(cot_share), over_core(env.cy)
        return [update]

    def work_gate():
        env.wg = weight(G)
        env.gate = sum_of_products(nn, [env.h_one], [env.wg], 0, 4 * share_rows, BF16)
        return [env.gate]

    def work_retained():
        gated, env.retained = per_head(
            forward_kernel,
            scalars,
            [
                (shaped(env.kq), ROWS),
                (shaped(env.v), ROWS),
                (shaped(env.gate), ROWS),
                (env.state, STATES),
                (gains, GAINS),
            ],
            [(rows_type, ROWS), (rows_type, ROWS)],
        )
        env.gated = flat(gated)
        return [env.gated]

    def work_out_far():
        env.wo = weight(O)
        far = sum_of_products(nn, [env.gated], [env.wo], 2 * share_rows, 2 * share_rows, BF16)
        env.far = over_core(far)
        return [far]

    def work_out_near():
        env.far = tie(env.far, *env.moved)[0]
        near = sum_of_products(
            nn, [env.gated], [env.wo], share_rows, share_rows, BF16, [(env.far, share_rows)]
        )
        env.near = over_y(near)
        return [near]

    def work_out_own():
        extras = [(env.far, 0), (tokens.reshape(share_rows, width), 0)]
        env.own = sum_of_products(nn, [env.gated], [env.wo], 0, share_rows, F32, extras)
        return [env.own]

    def work_cot():
        env.cot = jnp.concatenate([cot_share, env.cy, env.cc, env.ccy], axis=0)
        return [env.cot]

    def work_d_hidden():
        env.w2 = weight(W2)
        env.d_hidden = sum_of_products(nt, [env.cot], [env.w2], 0, 4 * share_rows, BF16)
        return [env.d_hidden]

    def work_middle():
        env.near = tie(env.near, *env.moved)[0]
        env.middle = env.own + env.near.astype(F32)
        h2, ln2_normed, ln2_scale = norm_rows(env.middle, ln2_gain)
        env.ln2 = (ln2_normed, ln2_scale)
        env.h2 = h2.astype(BF16)
        env.h2y, env.h2c = over_y(env.h2), over_core(env.h2)
        return [env.h2]

    def work_up():
        env.w1 = weight(W1)
        return [env.w1]

    def work_h2():
        env.h2cy = over_core(env.h2y)
        env.w3 = weight(W3)
        return [env.w3]

    plan = [
        [work_norm],
        [],
        [work_core],
        [work_rows],
        [work_kq],
        [work_v],
        [work_state],
        [work_gate, work_cot],
        [work_retained],
        [work_out_far, work_out_near, work_out_own],
        [],
        [work_middle],
        [work_up, work_h2, work_d_hidden],
    ]
    stacks = [jnp.concatenate([own[index] for index in group], axis=0) for group in groups]
    up = down = kept = to_send = None
    for tick, works in enumerate(plan):
        at, hop = divmod(tick, 3)
        moving = at < len(groups)
        sent, to_send = to_send, None
        if sent is not None:
            slots[sent[0]].append(sent[1])
            across[sent[0]].append(over_x(sent[1]))
        if moving and hop < 2:
            up = stacks[at] if hop == 0 else up
            down = stacks[at] if hop == 0 else down
            got = [lax.ppermute(up, FSDP, UP_Z[hop]), lax.ppermute(down, FSDP, DOWN_Z[hop])]
        elif moving:
            got = [lax.ppermute(slots[at][1], FSDP, LAST_Z)]
        env.moved = got if moving else []
        held = []
        for work in works:
            held += work()
        if not moving:
            continue
        names = [n for n in ("h_one", "kq", "gate", "gated", "cot") if hasattr(env, n)]
        if at == len(groups) - 1:
            names, held = [], []
        held = held + ([across[sent[0]][-1]] if sent is not None else [])
        ahead = stacks[at + 1 : at + 2] if hop == 2 else []
        tied = list(tie(*got, *[getattr(env, n) for n in names], *ahead, *held))
        got = [tied.pop(0) for _ in got]
        for n in names:
            setattr(env, n, tied.pop(0))
        if ahead:
            stacks[at + 1] = tied.pop(0)
        if hop == 0:
            up, down = kept = got
            to_send = (at, jnp.where(z_at > 0, up, down))
        elif hop == 1:
            up, down = got
            to_send = (at, jnp.where(z_at >= 2, up, down))
        else:
            ends = (z_at == 0) | (z_at == z_last)
            to_send = (at, jnp.where(ends, got[0], kept[1]))

    h_one, gated, gate_pre = env.h_one, env.gated, env.gate
    wkq, wv, wg, wo, w1, w2, w3 = env.wkq, env.wv, env.wg, env.wo, env.w1, env.w2, env.w3
    cot_full, d_hidden, middle = env.cot, env.d_hidden, env.middle

    token = [h_one]

    def step(run, *args):
        *args, _ = tie(*args, token[0])
        out = run(*args)
        token[0] = out[0] if isinstance(out, (tuple, list)) else out
        return out

    def whole_product(product, lefts, rights, first, rows, kind, *extras):
        count = len(lefts)

        def run(*arrays):
            added = [(a, row) for a, (_, row) in zip(arrays[count:], extras)]
            return sum_of_products(
                product, arrays[:count], rights, first * share_rows, rows * share_rows, kind, added
            )

        return step(run, *lefts, *(a for a, _ in extras))

    def theirs(left, right):
        return over_x(step(lambda a, b: quarter_product(a, b, 1 - x_at), left, right))

    def ours(left, right, got):
        total = step(lambda a, b, c: quarter_product(a, b, x_at, [c]), left, right, got)
        return lax.psum_scatter(total, FSDP, scatter_dimension=0, tiled=True)

    def chip_rows(left, right):
        total = step(lambda a, b: split_product(a, b, z_count), left, right)
        return lax.psum_scatter(total, FSDP, scatter_dimension=0, tiled=False)

    def begin_finish(*mine):
        mine = step(lambda *a: jnp.concatenate(a, axis=0), *mine)
        return mine, over_x(mine)

    def end_finish(firsts, mine, beside):
        def join(mine, beside):
            blocks, row = [], 0
            for x_summed in firsts:
                count = 1 if x_summed else 2
                one, other = (a[row * size : (row + count) * size] for a in (mine, beside))
                if x_summed:
                    blocks += [jnp.where(x_at == 0, one, other), jnp.where(x_at == 0, other, one)]
                else:
                    blocks.append((one.astype(F32) + other.astype(F32)).astype(BF16))
                row += count
            return jnp.concatenate(blocks, axis=0)

        both = step(join, mine, beside)
        return both, over_core(both)

    def quarters(pair, at):
        both, other = pair
        mine, theirs = (a[2 * at * size : (2 * at + 2) * size] for a in (both, other))
        first, second = jnp.where(core == 0, mine, theirs), jnp.where(core == 0, theirs, mine)
        return [first[:size], first[size:], second[:size], second[size:]]

    def shard(pair, at, rows):
        return jnp.concatenate(quarters(pair, at), axis=1 - int(rows)).astype(F32)

    h_two = jnp.concatenate([env.h2, env.h2y, env.h2c, env.h2cy], axis=0)
    hidden, d_fca, d_fcb = step(hidden_units, h_two, w1, w3, d_hidden)

    fc_lefts, fc_rights = (d_fca, d_fcb), (w1, w3)
    far = over_core(whole_product(nt, fc_lefts, fc_rights, 2, 2, BF16))
    down_mine = chip_rows(hidden, cot_full)
    near = over_y(whole_product(nt, fc_lefts, fc_rights, 1, 1, BF16, (far, share_rows)))
    gate_got = theirs(h_two, d_fca)
    own_part = whole_product(nt, fc_lefts, fc_rights, 0, 1, F32, (far, 0))
    up_got = theirs(h_two, d_fcb)
    out_far = over_core(whole_product(nn, [hidden], [w2], 2, 2, BF16))

    def middle_back(own_part, near):
        d_h2 = own_part + near.astype(F32)
        ln2_normed, ln2_scale = env.ln2
        d_middle = cot_share.astype(F32) + norm_back(d_h2, ln2_normed, ln2_scale, ln2_gain)
        return d_middle.astype(BF16), d_middle, jnp.sum(d_h2 * ln2_normed, axis=0)

    near, gate_got = tie(near, gate_got)
    d_mid_low, d_middle, g_ln2 = step(middle_back, own_part, near)
    d_mid_y, d_mid_c = over_y(d_mid_low), over_core(d_mid_low)
    fc_gate_mine = ours(h_two, d_fca, gate_got)
    out_near = whole_product(nn, [hidden], [w2], 1, 1, BF16, (out_far, share_rows))
    out_own = whole_product(nn, [hidden], [w2], 0, 1, F32, (out_far, 0), (middle, 0))
    down_begun = begin_finish(down_mine)
    d_mid_y, out_near, up_got = step(lambda *a: a, d_mid_y, out_near, up_got)
    d_mid_cy = over_core(d_mid_y)
    out_near = over_y(out_near)
    fc_up_mine = ours(h_two, d_fcb, up_got)

    def gate_back(share, y, c, cy):
        d_branch = jnp.concatenate([share, y, c, cy], axis=0)
        return sum_of_products(nt, [d_branch], [wo], 0, 4 * share_rows, BF16), d_branch

    fc_gate_mine, d_mid_cy = tie(fc_gate_mine, d_mid_cy)
    d_gated, d_branch = step(gate_back, d_mid_low, d_mid_y, d_mid_c, d_mid_cy)
    kq, values, state_in = shaped(env.kq), shaped(env.v), env.state

    def retained_back(d_gated, kq):
        return per_head(
            norm_back_kernel,
            scalars,
            [
                (shaped(d_gated), ROWS),
                (shaped(gate_pre), ROWS),
                (env.retained, ROWS),
                (kq, ROWS),
                (gains, GAINS),
            ],
            [(rows_type, ROWS), (rows_type, ROWS), (gain_type, STATES), (state_type, STATES)],
        )

    d_gate, d_retained, g_norm, leaving = step(retained_back, d_gated, kq)
    d_gate = flat(d_gate)
    g_norm = jnp.sum(g_norm, axis=0).reshape(v_half)
    state_grad = lax.ppermute(leaving, CONTEXT, DOWN_X)
    g_down = end_finish([False], *down_begun)
    out_mine = chip_rows(gated, d_branch)
    gg_theirs = step(lambda a, b: quarter_product(a, b, 1 - x_at), h_one, d_gate)
    state_grad, gg_theirs = tie(state_grad, gg_theirs)
    gg_got = over_x(gg_theirs)

    def pair_back(d_retained, state_grad):
        return per_head(
            backward_kernel,
            scalars,
            [
                (kq, ROWS),
                (values, ROWS),
                (d_retained, ROWS),
                (state_in, STATES),
                (state_grad, STATES),
            ],
            [(kq_type, ROWS), (rows_type, ROWS)],
        )

    fc_up_mine, state_grad = tie(fc_up_mine, state_grad)
    dkq_low, dv_low = step(pair_back, d_retained, state_grad)
    dkq_low, dv_low = flat(dkq_low), flat(dv_low)
    v_got = theirs(h_one, dv_low)
    kq_got = theirs(h_one, dkq_low)
    h1_lefts, h1_rights = (dkq_low, dv_low, d_gate), (wkq, wv, wg)
    output = step(lambda a, b: (a + b.astype(F32)).astype(BF16), out_own, out_near)
    gg_mine = ours(h_one, d_gate, gg_got)
    far = over_core(whole_product(nt, h1_lefts, h1_rights, 2, 2, BF16))
    out_mine, v_got = tie(out_mine, v_got)
    v_mine = ours(h_one, dv_low, v_got)
    near = over_y(whole_product(nt, h1_lefts, h1_rights, 1, 1, BF16, (far, share_rows)))
    own_part = whole_product(nt, h1_lefts, h1_rights, 0, 1, F32, (far, 0))
    kq_mine = ours(h_one, dkq_low, kq_got)
    fc_begun = begin_finish(fc_gate_mine, fc_up_mine)

    def tokens_back(own_part, near):
        d_h1 = own_part + near.astype(F32)
        ln1_normed, ln1_scale = env.ln1
        grad = d_middle + norm_back(d_h1, ln1_normed, ln1_scale, ln1_gain)
        return grad, jnp.sum(d_h1 * ln1_normed, axis=0)

    grad_tokens, g_ln1 = step(tokens_back, own_part, near)
    out_begun = begin_finish(out_mine, gg_mine)
    g_fc = end_finish([True, True], *fc_begun)
    v_begun = begin_finish(v_mine)
    g_out_gate = end_finish([False, True], *out_begun)
    g_value = end_finish([True], *v_begun)
    kq_begun = begin_finish(kq_mine)
    g_kq = end_finish([True], *kq_begun)
    sides = quarters(g_kq, 0)
    g_key = jnp.concatenate([side[:, :qk_width] for side in sides], axis=1).astype(F32)
    g_query = jnp.concatenate([side[:, qk_width:] for side in sides], axis=1).astype(F32)

    norm_size = lax.axis_size(TENSOR) * norm_gain.shape[0]
    norm_all = lax.dynamic_update_slice_in_dim(
        jnp.zeros((norm_size,), F32), g_norm, (2 * y_at + core) * v_half, 0
    )
    gain_sums = jnp.concatenate([g_ln1, g_ln2, norm_all])
    for axis in (TENSOR, CONTEXT, FSDP):
        gain_sums = butterfly(gain_sums, axis)
    g_ln1, g_ln2 = gain_sums[:width], gain_sums[width : 2 * width]
    g_norm = lax.dynamic_slice_in_dim(
        gain_sums, 2 * width + y_at * norm_gain.shape[0], norm_gain.shape[0]
    )
    return (
        output.reshape(tokens.shape),
        grad_tokens.reshape(tokens.shape),
        g_ln1,
        g_query,
        g_key,
        shard(g_value, 0, False),
        shard(g_out_gate, 1, False),
        g_norm,
        shard(g_out_gate, 0, True),
        g_ln2,
        shard(g_fc, 0, False),
        shard(g_fc, 1, False),
        shard(g_down, 0, True),
    )


def body(tensor_size, *arrays):
    heads_here = arrays[2].shape[0]
    paired = tensor_size == 2 and heads_here % 2 == 0 and lax.axis_size(CONTEXT) == 4
    paired = paired and lax.axis_size(FSDP) == 4
    return (paired_body if paired else general_body)(*arrays)


def solution(mesh):
    in_specs = (
        P(FSDP, (CONTEXT, TENSOR), None),
        P(FSDP, None),
        P(TENSOR),
        P(),
        P(FSDP, TENSOR),
        P(FSDP, TENSOR),
        P(FSDP, TENSOR),
        P(FSDP, TENSOR),
        P(TENSOR),
        P(TENSOR, FSDP),
        P(),
        P(FSDP, TENSOR),
        P(FSDP, TENSOR),
        P(TENSOR, FSDP),
        P(FSDP, (CONTEXT, TENSOR), None),
    )
    out_specs = (
        P(FSDP, (CONTEXT, TENSOR), None),
        P(FSDP, (CONTEXT, TENSOR), None),
        P(),
        P(FSDP, TENSOR),
        P(FSDP, TENSOR),
        P(FSDP, TENSOR),
        P(FSDP, TENSOR),
        P(TENSOR),
        P(TENSOR, FSDP),
        P(),
        P(FSDP, TENSOR),
        P(FSDP, TENSOR),
        P(TENSOR, FSDP),
    )
    return jax.shard_map(partial(body, mesh.shape[TENSOR]), mesh=mesh, in_specs=in_specs, out_specs=out_specs, check_vma=False)
```

```python
from functools import partial
from types import SimpleNamespace

import jax
import jax.numpy as jnp
from jax import lax
from jax.experimental import pallas as pl
from jax.experimental.pallas import tpu as pltpu
from jax.sharding import PartitionSpec as P

FSDP, CONTEXT, TENSOR = "fsdp", "context", "tensor"

careful = partial(jnp.einsum, precision=lax.Precision.HIGH)


def entering(part, axis, combine, identity):
    place = lax.axis_index(axis)
    gathered = jax.tree.map(lambda a: lax.all_gather(a, axis), part)
    state = jax.tree.map(lambda a, e: jnp.zeros_like(a) + jnp.asarray(e, a.dtype), part, identity)

    def one(step, state):
        return combine(
            state, jax.tree.map(lambda a: lax.dynamic_index_in_dim(a, step, 0, False), gathered)
        )

    return lax.fori_loop(0, place, one, state)


def carried_in(value, axis, combine, identity):
    count, place = (lax.axis_size(axis), lax.axis_index(axis))
    everything = jax.tree.map(
        lambda part, kind: lax.all_gather(part.astype(kind), axis),
        value,
        jax.tree.map(lambda a: jnp.bfloat16 if a.dtype == jnp.float32 else a.dtype, value),
    )
    start = jax.tree.map(
        lambda part, zero: jnp.broadcast_to(jnp.asarray(zero, part.dtype), part.shape),
        value,
        identity,
    )

    def step(k, before):
        at = count - 1 - k
        reached = at > place
        new = combine(
            before, jax.tree.map(lambda part, own: part[at].astype(own.dtype), everything, value)
        )
        return jax.tree.map(lambda a, b: jnp.where(reached, a, b), new, before)

    return lax.fori_loop(0, count, step, start)


def norm_rows(values, gain_vec, epsilon=1e-05):
    centred = values - jnp.mean(values, axis=-1, keepdims=True)
    scale = lax.rsqrt(jnp.mean(centred * centred, axis=-1, keepdims=True) + epsilon)
    normed = centred * scale
    return (normed * gain_vec, normed, scale)


def norm_back(grad_in, normed, scale, gain_vec):
    d_normed = grad_in * gain_vec
    first_mean = jnp.mean(d_normed, axis=-1, keepdims=True)
    second_mean = jnp.mean(d_normed * normed, axis=-1, keepdims=True)
    return scale * (d_normed - first_mean - normed * second_mean)


def swish_slope(values):
    sigma = jax.nn.sigmoid(values)
    return sigma * (1.0 + values * (1.0 - sigma))


def compose(earlier, latter):
    return (earlier[0] * latter[0], latter[0][:, :, None, None] * earlier[1] + latter[1])


def share_gather(piece):
    return lax.all_gather(piece, TENSOR, axis=1, tiled=True)


def branch_sum(terms):
    return lax.psum_scatter(terms, TENSOR, scatter_dimension=1, tiled=True)


def input_sum(terms):
    return lax.psum_scatter(
        terms.astype(jnp.bfloat16), TENSOR, scatter_dimension=1, tiled=True
    ).astype(jnp.float32)


def mixer_fetch(w_query, w_key, w_value, w_gate, w_out):
    return (
        lax.all_gather(w_query, FSDP, axis=0, tiled=True),
        lax.all_gather(w_key, FSDP, axis=0, tiled=True),
        lax.all_gather(w_value, FSDP, axis=0, tiled=True),
        lax.all_gather(w_gate, FSDP, axis=0, tiled=True),
        lax.all_gather(w_out, FSDP, axis=1, tiled=True),
    )


def mlp_fetch(w_fc_gate, w_fc_up, w_fc_down):
    return (
        lax.all_gather(w_fc_gate, FSDP, axis=0, tiled=True),
        lax.all_gather(w_fc_up, FSDP, axis=0, tiled=True),
        lax.all_gather(w_fc_down, FSDP, axis=1, tiled=True),
    )


def product(form, left, right):
    return jnp.einsum(form, left, right, preferred_element_type=jnp.float32)


def general_body(
    tokens,
    segments,
    forget,
    ln1_gain,
    w_query,
    w_key,
    w_value,
    w_gate,
    norm_gain,
    w_out,
    ln2_gain,
    w_fc_gate,
    w_fc_up,
    w_fc_down,
    cotangent,
):
    heads_here = forget.shape[0]
    qk_width = w_query.shape[1] // heads_here
    v_width = w_value.shape[1] // heads_here
    v_local = heads_here * v_width
    gain_heads = norm_gain.reshape(heads_here, v_width)
    x_share = tokens.astype(jnp.float32)
    h1_share, ln1_normed, ln1_scale = norm_rows(x_share, ln1_gain)
    h_one = share_gather(h1_share.astype(jnp.bfloat16))
    wq_all, wk_all, wv_all, wg_all, wo_all = mixer_fetch(w_query, w_key, w_value, w_gate, w_out)
    seq_count, stretch_len = (h_one.shape[0], h_one.shape[1])
    query = product("btd,dq->btq", h_one, wq_all).astype(jnp.bfloat16)
    keys = product("btd,dq->btq", h_one, wk_all).astype(jnp.bfloat16)
    values = product("btd,dv->btv", h_one, wv_all).astype(jnp.bfloat16)
    gate_pre = product("btd,dv->btv", h_one, wg_all)
    query_heads = query.reshape(seq_count, stretch_len, heads_here, qk_width)
    keys_heads = keys.reshape(seq_count, stretch_len, heads_here, qk_width)
    query_full = query_heads.astype(jnp.float32) * 0.0625
    keys_full = keys_heads.astype(jnp.float32)
    values_full = values.astype(jnp.float32).reshape(seq_count, stretch_len, heads_here, v_width)
    log_keep = jnp.log(1.0 - forget)
    ctx_place = lax.axis_index(CONTEXT)
    seg_stretch = lax.dynamic_slice_in_dim(segments, ctx_place * stretch_len, stretch_len, 1)
    seg_prev = lax.dynamic_slice_in_dim(segments, jnp.maximum(ctx_place * stretch_len - 1, 0), 1, 1)
    live_mask = (seg_stretch == seg_prev).astype(jnp.float32)
    steps_idx = jnp.arange(stretch_len, dtype=jnp.float32)
    step_gap = jnp.maximum(steps_idx[:, None] - steps_idx[None, :], 0.0)
    causal = steps_idx[:, None] >= steps_idx[None, :]
    same_doc = (seg_stretch[:, :, None] == seg_stretch[:, None, :]) & causal[None]
    weights_mask = jnp.where(
        same_doc[:, None], jnp.exp(step_gap[None] * log_keep[:, None, None])[None], 0.0
    )
    inflow = live_mask[:, :, None] * jnp.exp((steps_idx[:, None] + 1.0) * log_keep[None, :])[None]
    outflow = (seg_stretch == seg_stretch[:, -1:]).astype(jnp.float32)[:, :, None] * jnp.exp(
        (stretch_len - 1.0 - steps_idx)[:, None] * log_keep[None, :]
    )[None]
    carry_decay = live_mask[:, -1:] * jnp.exp(stretch_len * log_keep)[None, :]
    update = careful("bshd,bsh,bshe->bhde", keys_full, outflow, values_full)
    identity = (jnp.ones_like(carry_decay), jnp.zeros_like(update))
    state_in = entering((carry_decay, update), CONTEXT, compose, identity)[1]
    scores = product("bthd,bshd->bhts", query_heads, keys_heads) * 0.0625 * weights_mask
    retained = careful("bhts,bshe->bthe", scores, values_full)
    retained = retained + inflow[..., None] * careful("bthd,bhde->bthe", query_full, state_in)
    normed_out, gn_normed, gn_scale = norm_rows(retained, gain_heads, 0.01)
    norm_flat = normed_out.reshape(seq_count, stretch_len, v_local)
    gate_act = jax.nn.silu(gate_pre)
    gated = (gate_act * norm_flat).astype(jnp.bfloat16)
    middle = x_share + branch_sum(product("btv,vd->btd", gated, wo_all))
    h2_share, ln2_normed, ln2_scale = norm_rows(middle, ln2_gain)
    h_two = share_gather(h2_share.astype(jnp.bfloat16))
    w1_all, w3_all, w2_all = mlp_fetch(w_fc_gate, w_fc_up, w_fc_down)
    fc_a = product("btd,df->btf", h_two, w1_all)
    fc_b = product("btd,df->btf", h_two, w3_all)
    silu_a = jax.nn.silu(fc_a)
    hidden = (silu_a * fc_b).astype(jnp.bfloat16)
    output = (middle + branch_sum(product("btf,fd->btd", hidden, w2_all))).astype(jnp.bfloat16)
    wq_all, wk_all, wv_all, wg_all, wo_all = mixer_fetch(w_query, w_key, w_value, w_gate, w_out)
    w1_all, w3_all, w2_all = mlp_fetch(w_fc_gate, w_fc_up, w_fc_down)
    cot_full = share_gather(cotangent)
    d_hidden = product("btd,fd->btf", cot_full, w2_all)
    g_down = product("btf,btd->fd", hidden, cot_full)
    d_fca = (d_hidden * fc_b * swish_slope(fc_a)).astype(jnp.bfloat16)
    d_fcb = (d_hidden * silu_a).astype(jnp.bfloat16)
    g_fc_gate = product("btd,btf->df", h_two, d_fca)
    g_fc_up = product("btd,btf->df", h_two, d_fcb)
    d_h2 = input_sum(product("btf,df->btd", d_fca, w1_all) + product("btf,df->btd", d_fcb, w3_all))
    d_middle = cotangent.astype(jnp.float32) + norm_back(d_h2, ln2_normed, ln2_scale, ln2_gain)
    g_ln2 = jnp.sum(d_h2 * ln2_normed, axis=(0, 1))
    d_branch = share_gather(d_middle.astype(jnp.bfloat16))
    d_gated = product("btd,vd->btv", d_branch, wo_all)
    g_out = product("btv,btd->vd", gated, d_branch)
    d_gate = (d_gated * norm_flat * swish_slope(gate_pre)).astype(jnp.bfloat16)
    d_normed = (d_gated * gate_act).reshape(seq_count, stretch_len, heads_here, v_width)
    g_norm = jnp.sum(d_normed * gn_normed, axis=(0, 1)).reshape(v_local)
    d_retained = norm_back(d_normed, gn_normed, gn_scale, gain_heads)
    d_scores = careful("bthe,bshe->bhts", d_retained, values_full) * weights_mask
    d_values = careful("bhts,bthe->bshe", scores, d_retained)
    d_query = careful("bhts,bshd->bthd", d_scores, keys_full)
    d_query = d_query + inflow[..., None] * careful("bthe,bhde->bthd", d_retained, state_in)
    d_keys = careful("bhts,bthd->bshd", d_scores, query_full)
    leaving = careful("bthd,bth,bthe->bhde", query_full, inflow, d_retained)
    state_grad = carried_in((carry_decay, leaving), CONTEXT, compose, identity)[1]
    d_keys = d_keys + outflow[..., None] * careful("bshe,bhde->bshd", values_full, state_grad)
    d_values = d_values + outflow[..., None] * careful("bshd,bhde->bshe", keys_full, state_grad)
    dq_low = (
        (d_query * 0.0625)
        .reshape(seq_count, stretch_len, heads_here * qk_width)
        .astype(jnp.bfloat16)
    )
    dk_low = d_keys.reshape(seq_count, stretch_len, heads_here * qk_width).astype(jnp.bfloat16)
    dv_low = d_values.reshape(seq_count, stretch_len, v_local).astype(jnp.bfloat16)
    g_query = product("btd,btq->dq", h_one, dq_low)
    g_key = product("btd,btq->dq", h_one, dk_low)
    g_value = product("btd,btv->dv", h_one, dv_low)
    g_gate = product("btd,btv->dv", h_one, d_gate)
    d_h1 = product("btq,dq->btd", dq_low, wq_all) + product("btq,dq->btd", dk_low, wk_all)
    d_h1 = d_h1 + product("btv,dv->btd", dv_low, wv_all) + product("btv,dv->btd", d_gate, wg_all)
    d_h1 = input_sum(d_h1)
    grad_tokens = d_middle + norm_back(d_h1, ln1_normed, ln1_scale, ln1_gain)
    g_ln1 = jnp.sum(d_h1 * ln1_normed, axis=(0, 1))
    tensor_place = lax.axis_index(TENSOR)
    norm_full = lax.dynamic_update_slice(
        jnp.zeros((v_local * lax.axis_size(TENSOR),), jnp.float32),
        g_norm,
        (tensor_place * v_local,),
    )
    g_ln1, g_ln2, norm_full = lax.psum((g_ln1, g_ln2, norm_full), (FSDP, CONTEXT, TENSOR))
    g_norm = lax.dynamic_slice_in_dim(norm_full, tensor_place * v_local, v_local)
    weight_grads = (g_query, g_key, g_value, g_gate, g_out, g_fc_gate, g_fc_up, g_down)
    summed = (
        lax.psum(weight_grads[0].astype(jnp.bfloat16), CONTEXT).astype(jnp.float32),
        lax.psum(weight_grads[1].astype(jnp.bfloat16), CONTEXT).astype(jnp.float32),
        lax.psum(weight_grads[2].astype(jnp.bfloat16), CONTEXT).astype(jnp.float32),
        lax.psum(weight_grads[3].astype(jnp.bfloat16), CONTEXT).astype(jnp.float32),
        lax.psum(weight_grads[4].astype(jnp.bfloat16), CONTEXT).astype(jnp.float32),
        lax.psum(weight_grads[5].astype(jnp.bfloat16), CONTEXT).astype(jnp.float32),
        lax.psum(weight_grads[6].astype(jnp.bfloat16), CONTEXT).astype(jnp.float32),
        lax.psum(weight_grads[7].astype(jnp.bfloat16), CONTEXT).astype(jnp.float32),
    )
    shards = (
        lax.psum_scatter(
            summed[0].astype(jnp.bfloat16), FSDP, scatter_dimension=0, tiled=True
        ).astype(jnp.float32),
        lax.psum_scatter(
            summed[1].astype(jnp.bfloat16), FSDP, scatter_dimension=0, tiled=True
        ).astype(jnp.float32),
        lax.psum_scatter(
            summed[2].astype(jnp.bfloat16), FSDP, scatter_dimension=0, tiled=True
        ).astype(jnp.float32),
        lax.psum_scatter(
            summed[3].astype(jnp.bfloat16), FSDP, scatter_dimension=0, tiled=True
        ).astype(jnp.float32),
        lax.psum_scatter(
            summed[4].astype(jnp.bfloat16), FSDP, scatter_dimension=1, tiled=True
        ).astype(jnp.float32),
        lax.psum_scatter(
            summed[5].astype(jnp.bfloat16), FSDP, scatter_dimension=0, tiled=True
        ).astype(jnp.float32),
        lax.psum_scatter(
            summed[6].astype(jnp.bfloat16), FSDP, scatter_dimension=0, tiled=True
        ).astype(jnp.float32),
        lax.psum_scatter(
            summed[7].astype(jnp.bfloat16), FSDP, scatter_dimension=1, tiled=True
        ).astype(jnp.float32),
    )
    return (
        output,
        grad_tokens,
        g_ln1,
        shards[0],
        shards[1],
        shards[2],
        shards[3],
        g_norm,
        shards[4],
        g_ln2,
        shards[5],
        shards[6],
        shards[7],
    )


F32 = jnp.float32
BF16 = jnp.bfloat16
BOTH_X = [(0, 2), (2, 0), (1, 3), (3, 1)]
UP_X = [(0, 2), (1, 3)]
DOWN_X = [(2, 0), (3, 1)]
CORES = [(0, 1), (1, 0), (2, 3), (3, 2)]
UP_Z = [[(0, 1), (1, 2), (2, 3)], [(1, 2), (2, 3)]]
DOWN_Z = [[(3, 2), (2, 1), (1, 0)], [(2, 1), (1, 0)]]
LAST_Z = [(2, 3), (1, 0)]
SCALE = 0.0625
ROWS, GAINS, STATES = range(3)


def cost(flops):
    return pl.CostEstimate(flops=flops, transcendentals=0, bytes_accessed=0)


COPYING = 2 << 30
DOWN_Z = [[(3, 2), (2, 1), (1, 0)], [(2, 1), (1, 0)], [(1, 0)]]


def over_x(value):
    return lax.ppermute(value, CONTEXT, BOTH_X)


def over_core(value):
    return lax.ppermute(value, CONTEXT, CORES)


def over_y(value):
    return lax.ppermute(value, TENSOR, [(0, 1), (1, 0)])


def tie(*values):
    return lax.optimization_barrier(values)


def butterfly(value, axis):
    size = lax.axis_size(axis)
    step = 1
    while step < size:
        value = value + lax.ppermute(value, axis, [(i, i ^ step) for i in range(size)])
        step *= 2
    return value


def quarter_of(weight, dim, index):
    size = weight.shape[dim] // 4
    return lax.dynamic_slice_in_dim(weight, index * size, size, dim)


def assemble_kernel(spot_ref, *refs):
    at = pl.program_id(0)
    for index, block in enumerate(refs[:8]):

        @pl.when(at == index)
        def _(block=block):
            refs[8][...] = block[...]


def assemble(blocks, spots, by_rows, size):
    shape = (2 * size, 4 * size) if by_rows else (4 * size, 2 * size)

    def spot(at, spots_ref):
        z_from, x_from = spots_ref[at], spots_ref[8 + at]
        return (x_from, z_from) if by_rows else (z_from, x_from)

    return pl.pallas_call(
        assemble_kernel,
        out_shape=jax.ShapeDtypeStruct(shape, BF16),
        grid_spec=pltpu.PrefetchScalarGridSpec(
            num_scalar_prefetch=1,
            grid=(8,),
            in_specs=[
                pl.BlockSpec((size, size), lambda at, spots_ref, row=row: (row, 0))
                for _, row in blocks
            ],
            out_specs=pl.BlockSpec((size, size), spot),
        ),
        compiler_params=pltpu.CompilerParams(vmem_limit_bytes=32 << 20),
        cost_estimate=cost(COPYING),
    )(spots, *(array for array, _ in blocks))


def sum_kernel(product, count, outs, *refs):
    lefts, rights, extras = refs[:count], refs[count : 2 * count], refs[2 * count : -outs]
    total = product(lefts[0][...], rights[0][...])
    for left, right in zip(lefts[1:], rights[1:]):
        total = total + product(left[...], right[...])
    for extra in extras:
        total = total + extra[...].astype(F32)
    size = total.shape[0] // outs
    for index, out_ref in enumerate(refs[-outs:]):
        out_ref[...] = total[index * size : (index + 1) * size].astype(out_ref.dtype)


def sum_of_products(product, lefts, rights, first, rows, kind, extras=(), outs=1):
    by_columns = product is nn
    width = rights[0].shape[1 if by_columns else 0]
    block, tile = min(1024, rows), min(512, width)
    if outs > 1:
        block = rows

    def right_spec(right):
        if by_columns:
            return pl.BlockSpec((right.shape[0], tile), lambda n, m: (0, n))
        return pl.BlockSpec((tile, right.shape[1]), lambda n, m: (n, 0))

    def tile_spec(from_row, size):
        return pl.BlockSpec((size, tile), lambda n, m: (from_row // size + m, n))

    out_shape = [jax.ShapeDtypeStruct((rows // outs, width), kind)] * outs
    result = pl.pallas_call(
        partial(sum_kernel, product, len(lefts), outs),
        grid=(width // tile, rows // block),
        out_shape=out_shape,
        in_specs=[
            pl.BlockSpec((block, left.shape[1]), lambda n, m: (first // block + m, 0))
            for left in lefts
        ]
        + [right_spec(right) for right in rights]
        + [tile_spec(from_row, block) for _, from_row in extras],
        out_specs=[tile_spec(0, block // outs)] * outs,
        compiler_params=pltpu.CompilerParams(vmem_limit_bytes=60 << 20),
        cost_estimate=cost(2 * rows * width * sum(left.shape[1] for left in lefts)),
    )(*lefts, *rights, *(array for array, _ in extras))
    return result[0] if outs == 1 else result


def quarter_kernel(spots_ref, left, right, *rest):
    total = tn(left[...], right[...])
    for extra in rest[:-1]:
        total = total + extra[...].astype(F32)
    rest[-1][...] = total.astype(BF16)


def quarter_product(left, right, index, extras=()):
    tokens, width = left.shape
    size, block = right.shape[1] // 2, min(1024, width)
    return pl.pallas_call(
        quarter_kernel,
        out_shape=jax.ShapeDtypeStruct((width, size), BF16),
        grid_spec=pltpu.PrefetchScalarGridSpec(
            num_scalar_prefetch=1,
            grid=(width // block,),
            in_specs=[
                pl.BlockSpec((tokens, block), lambda m, at: (0, m)),
                pl.BlockSpec((tokens, size), lambda m, at: (0, at[0])),
            ]
            + [pl.BlockSpec((block, size), lambda m, at: (m, 0)) for _ in extras],
            out_specs=pl.BlockSpec((block, size), lambda m, at: (m, 0)),
        ),
        compiler_params=pltpu.CompilerParams(vmem_limit_bytes=60 << 20),
        cost_estimate=cost(2 * tokens * width * size),
    )(index.reshape(1).astype(jnp.int32), left, right, *extras)


def split_kernel(left, right, out):
    out[0] = tn(left[...], right[...]).astype(BF16)


def split_product(left, right, count):
    tokens, rows = left.shape
    size = right.shape[1] // count
    return pl.pallas_call(
        split_kernel,
        grid=(count,),
        out_shape=jax.ShapeDtypeStruct((count, rows, size), BF16),
        in_specs=[
            pl.BlockSpec((tokens, rows), lambda n: (0, 0)),
            pl.BlockSpec((tokens, size), lambda n: (0, n)),
        ],
        out_specs=pl.BlockSpec((1, rows, size), lambda n: (n, 0, 0)),
        compiler_params=pltpu.CompilerParams(vmem_limit_bytes=60 << 20),
        cost_estimate=cost(2 * tokens * rows * size * count),
    )(left, right)


def unit_kernel(h_ref, w1_ref, w3_ref, d_hidden_ref, hidden_ref, d_a_ref, d_b_ref):
    fc_a, fc_b = nn(h_ref[...], w1_ref[...]), nn(h_ref[...], w3_ref[...])
    d_hidden = d_hidden_ref[...].astype(F32)
    sigma = jax.nn.sigmoid(fc_a)
    silu_a = fc_a * sigma
    hidden_ref[...] = (silu_a * fc_b).astype(BF16)
    d_a_ref[...] = (d_hidden * fc_b * (sigma * (1.0 + fc_a * (1.0 - sigma)))).astype(BF16)
    d_b_ref[...] = (d_hidden * silu_a).astype(BF16)


def hidden_units(h_two, w1, w3, d_hidden):
    rows, width = h_two.shape
    count = w1.shape[1]
    block, tile = min(512, rows), min(512, count)
    weight = pl.BlockSpec((width, tile), lambda n, m: (0, n))
    spot = pl.BlockSpec((block, tile), lambda n, m: (m, n))
    return pl.pallas_call(
        unit_kernel,
        grid=(count // tile, rows // block),
        out_shape=[jax.ShapeDtypeStruct((rows, count), BF16)] * 3,
        in_specs=[pl.BlockSpec((block, width), lambda n, m: (m, 0)), weight, weight, spot],
        out_specs=[spot] * 3,
        compiler_params=pltpu.CompilerParams(vmem_limit_bytes=60 << 20),
        cost_estimate=cost(4 * rows * width * count),
    )(h_two, w1, w3, d_hidden)


def stack_kernel(count, *refs):
    at = pl.program_id(0)
    for index, share in enumerate(refs[:-1]):

        @pl.when(at // count == index)
        def _(share=share):
            refs[-1][...] = share[...]


def stack_rows(*shares):
    rows, width = shares[0].shape
    count = 2 if rows % 32 == 0 else 1
    block = rows // count

    def spec(index):
        return pl.BlockSpec((block, width), lambda at: (jnp.clip(at - index * count, 0, count - 1), 0))

    return pl.pallas_call(
        partial(stack_kernel, count),
        grid=(len(shares) * count,),
        out_shape=jax.ShapeDtypeStruct((len(shares) * rows, width), shares[0].dtype),
        in_specs=[spec(index) for index in range(len(shares))],
        out_specs=pl.BlockSpec((block, width), lambda at: (at, 0)),
        compiler_params=pltpu.CompilerParams(vmem_limit_bytes=48 << 20),
        cost_estimate=cost(2 * COPYING),
    )(*shares)


def nn(left, right):
    return lax.dot_general(left, right, (((1,), (0,)), ((), ())), preferred_element_type=F32)


def nt(left, right):
    return lax.dot_general(left, right, (((1,), (1,)), ((), ())), preferred_element_type=F32)


def tn(left, right):
    return lax.dot_general(left, right, (((0,), (0,)), ((), ())), preferred_element_type=F32)


def where_is(whole, chunk, piece_len):
    share_len = piece_len // 2
    spots = []
    for shape, dim in (((piece_len, 1), 0), ((1, piece_len), 1)):
        at = lax.broadcasted_iota(jnp.int32, shape, dim) + whole[2] * share_len
        spots.append(jnp.where(at >= piece_len, at - piece_len, at))
    start = whole[0] * (2 * piece_len) + chunk * piece_len
    return spots[0], spots[1], start


def document(whole, spot):
    seq = pl.program_id(0)
    first, second = whole[3 + 2 * seq], whole[4 + 2 * seq]
    return jnp.where(spot >= second, 2, jnp.where(spot >= first, 1, 0))


def fade(gap, log_keep):
    return jnp.exp(jnp.maximum(gap, 0).astype(F32) * log_keep)


def piece_terms(whole, log_keep, chunk, piece_len):
    rows, cols, start = where_is(whole, chunk, piece_len)
    doc_rows, doc_cols = document(whole, start + rows), document(whole, start + cols)
    before, last = document(whole, start - 1), document(whole, start + piece_len - 1)
    within = jnp.where(
        (rows >= cols) & (doc_rows == doc_cols), fade(rows - cols, log_keep) * SCALE, 0.0
    )
    inflow = jnp.where(doc_rows == before, fade(rows + 1, log_keep) * SCALE, 0.0)
    outflow = jnp.where(doc_rows == last, fade(piece_len - 1 - rows, log_keep), 0.0)
    whole_gap = jnp.full((1, 1), piece_len, jnp.int32)
    over = jnp.where(before == last, fade(whole_gap, log_keep), 0.0)
    return within, inflow, outflow, over


def piece_of(ref, whole, chunk):
    group = lax.rem(chunk + whole[1], 2) * 2
    value = ref[pl.ds(group, 2), 0]
    return value.reshape(value.shape[0] * value.shape[1], value.shape[2])


def put_piece(ref, whole, chunk, value):
    group = lax.rem(chunk + whole[1], 2) * 2
    ref[pl.ds(group, 2), 0] = value.astype(ref.dtype).reshape(2, value.shape[0] // 2, value.shape[1])


def split_kq(ref, whole, chunk):
    both = piece_of(ref, whole, chunk)
    width = both.shape[1] // 2
    return both[:, :width], both[:, width:]


def update_kernel(whole, keeps, kq_ref, v_ref, out_ref):
    log_keep = keeps[pl.program_id(1)]
    piece_len = 2 * kq_ref.shape[2]
    total = jnp.zeros(out_ref.shape[2:], F32)
    for chunk in range(2):
        rows, _, start = where_is(whole, chunk, piece_len)
        last = document(whole, whole[0] * (2 * piece_len) + 2 * piece_len - 1)
        gap = (2 - chunk) * piece_len - 1 - rows
        weight = jnp.where(document(whole, start + rows) == last, fade(gap, log_keep), 0.0)
        keys, _ = split_kq(kq_ref, whole, chunk)
        values = piece_of(v_ref, whole, chunk)
        total = total + tn((keys.astype(F32) * weight).astype(BF16), values)
    out_ref[0, 0] = total.astype(BF16)


def next_state(state, keys, values, outflow, over):
    return over * state + tn((keys.astype(F32) * outflow).astype(BF16), values)


def forward_kernel(
    whole, keeps, kq_ref, v_ref, gate_ref, state_ref, gain_ref, gated_ref, retained_ref
):
    log_keep = keeps[pl.program_id(1)]
    piece_len = 2 * kq_ref.shape[2]
    state = state_ref[0, 0].astype(F32)
    for chunk in range(2):
        within, inflow, outflow, over = piece_terms(whole, log_keep, chunk, piece_len)
        keys, query = split_kq(kq_ref, whole, chunk)
        values = piece_of(v_ref, whole, chunk)
        scores = (nt(query, keys) * within).astype(BF16)
        retained = nn(scores, values) + inflow * nn(query, state.astype(BF16))
        if chunk == 0:
            state = next_state(state, keys, values, outflow, over)
        put_piece(retained_ref, whole, chunk, retained)
        normed, _, _ = norm_rows(retained, gain_ref[0], 0.01)
        gate = piece_of(gate_ref, whole, chunk).astype(F32)
        put_piece(gated_ref, whole, chunk, gate * jax.nn.sigmoid(gate) * normed)


def norm_back_kernel(
    whole,
    keeps,
    d_gated_ref,
    gate_ref,
    retained_ref,
    kq_ref,
    gain_ref,
    d_gate_ref,
    d_retained_ref,
    d_gain_ref,
    leaving_ref,
):
    log_keep = keeps[pl.program_id(1)]
    piece_len = 2 * kq_ref.shape[2]
    total = jnp.zeros(leaving_ref.shape[2:], F32)
    gain = gain_ref[0]
    d_gain = jnp.zeros(gain.shape, F32)
    for chunk in range(2):
        rows, _, start = where_is(whole, chunk, piece_len)
        before = document(whole, whole[0] * (2 * piece_len) - 1)
        gap = chunk * piece_len + rows + 1
        weight = jnp.where(
            document(whole, start + rows) == before, fade(gap, log_keep) * SCALE, 0.0
        )
        _, query = split_kq(kq_ref, whole, chunk)
        retained = piece_of(retained_ref, whole, chunk).astype(F32)
        normed, unit, scale = norm_rows(retained, gain, 0.01)
        gate = piece_of(gate_ref, whole, chunk).astype(F32)
        d_gated = piece_of(d_gated_ref, whole, chunk).astype(F32)
        sigma = jax.nn.sigmoid(gate)
        put_piece(
            d_gate_ref, whole, chunk, d_gated * normed * sigma * (1.0 + gate * (1.0 - sigma))
        )
        d_normed = d_gated * gate * sigma
        d_gain = d_gain + jnp.sum(d_normed * unit, axis=0, keepdims=True)
        d_retained = norm_back(d_normed, unit, scale, gain)
        put_piece(d_retained_ref, whole, chunk, d_retained)
        total = total + tn(query, (d_retained * weight).astype(BF16))
    d_gain_ref[0, 0] = d_gain
    leaving_ref[0, 0] = total.astype(BF16)


def backward_kernel(
    whole, keeps, kq_ref, v_ref, d_retained_ref, state_ref, d_state_ref, d_kq_ref, d_v_ref
):
    log_keep = keeps[pl.program_id(1)]
    piece_len = 2 * kq_ref.shape[2]
    terms = [piece_terms(whole, log_keep, chunk, piece_len) for chunk in range(2)]
    state = state_ref[0, 0].astype(F32)
    keys, _ = split_kq(kq_ref, whole, 0)
    _, _, outflow, over = terms[0]
    states = [state, next_state(state, keys, piece_of(v_ref, whole, 0), outflow, over)]
    d_state = d_state_ref[0, 0].astype(F32)
    for chunk in (1, 0):
        within, inflow, outflow, over = terms[chunk]
        keys, query = split_kq(kq_ref, whole, chunk)
        values = piece_of(v_ref, whole, chunk)
        d_ret = piece_of(d_retained_ref, whole, chunk)
        state_low, d_state_low = states[chunk].astype(BF16), d_state.astype(BF16)
        scores = (nt(query, keys) * within).astype(BF16)
        d_scores = (nt(d_ret, values) * within).astype(BF16)
        d_values = tn(scores, d_ret) + outflow * nn(keys, d_state_low)
        put_piece(d_v_ref, whole, chunk, d_values)
        d_query = nn(d_scores, keys) + inflow * nt(d_ret, state_low)
        d_keys = tn(d_scores, query) + outflow * nt(values, d_state_low)
        put_piece(d_kq_ref, whole, chunk, jnp.concatenate([d_keys, d_query], axis=1))
        if chunk == 1:
            entering = tn(query, (d_ret.astype(F32) * inflow).astype(BF16))
            d_state = over * d_state + entering


def per_head(kernel, scalars, blocks, outs, flops=12 << 30):
    def spec(array, kind):
        if kind == ROWS:
            width = array.shape[3] // heads
            return pl.BlockSpec((4, 1, array.shape[2], width), lambda b, h, *_: (0, b, 0, h))
        if kind == GAINS:
            return pl.BlockSpec((1, *array.shape[1:]), lambda b, h, *_: (h, 0, 0))
        return pl.BlockSpec((1, 1, *array.shape[2:]), lambda b, h, *_: (b, h, 0, 0))

    heads = scalars[1].shape[0]
    seq_count = (scalars[0].shape[0] - 3) // 2
    return pl.pallas_call(
        kernel,
        out_shape=[a for a, _ in outs],
        grid_spec=pltpu.PrefetchScalarGridSpec(
            num_scalar_prefetch=2,
            grid=(seq_count, heads),
            in_specs=[spec(*block) for block in blocks],
            out_specs=[spec(*out) for out in outs],
        ),
        compiler_params=pltpu.CompilerParams(vmem_limit_bytes=56 << 20),
        cost_estimate=cost(flops),
    )(*scalars, *(a for a, _ in blocks))


def both_quarters(mine, across, first, dim):
    return jnp.concatenate(
        [jnp.where(first, mine, across), jnp.where(first, across, mine)], axis=dim
    )


def paired_body(
    tokens,
    segments,
    forget,
    ln1_gain,
    w_query,
    w_key,
    w_value,
    w_gate,
    norm_gain,
    w_out,
    ln2_gain,
    w_fc_gate,
    w_fc_up,
    w_fc_down,
    cotangent,
):
    place = lax.axis_index(CONTEXT)
    x_at, core, y_at = place // 2, place % 2, lax.axis_index(TENSOR)
    z_at = lax.axis_index(FSDP)
    heads = forget.shape[0] // 2
    qk_width = w_query.shape[1] // forget.shape[0]
    v_width = w_value.shape[1] // forget.shape[0]
    width = tokens.shape[2]
    seq_count, share_len = tokens.shape[0], tokens.shape[1]
    share_rows = seq_count * share_len
    piece_len = 2 * share_len
    chip_len = 2 * piece_len
    v_half = heads * v_width
    forget_half = lax.dynamic_slice_in_dim(forget, core * heads, heads)
    gain_half = lax.dynamic_slice_in_dim(norm_gain, core * v_half, v_half)

    def part(array, first, last):
        return array[first * share_rows : last * share_rows]

    def unit(x_index):
        q = core * 2 + x_index
        key_query = [quarter_of(w_key, 1, q), quarter_of(w_query, 1, q)]
        return [
            jnp.concatenate(key_query, axis=1),
            quarter_of(w_value, 1, q),
            quarter_of(w_gate, 1, q),
            quarter_of(w_out, 0, q),
            quarter_of(w_fc_down, 0, q),
            quarter_of(w_fc_gate, 1, q),
            quarter_of(w_fc_up, 1, q),
        ]

    KQ, V, G, O, W2, W1, W3 = range(7)
    by_rows = [False, False, False, True, True, False, False]
    own, sibling = unit(x_at), unit(1 - x_at)
    size = own[0].shape[0]
    z_last = lax.axis_size(FSDP) - 1
    z_count = z_last + 1
    s_one = jnp.where(z_at == 0, 1, z_at - 1)
    s_three = jnp.where(z_at == z_last, 0, jnp.where(z_at == 1, 2, z_last))
    z_spots = [z_at, s_one, z_at ^ 2, s_three]
    spots = jnp.stack(z_spots + z_spots + [x_at] * 4 + [1 - x_at] * 4).astype(jnp.int32)
    groups = [[KQ, V], [G, O], [W2, W1, W3]]
    slots, across = [[], [], []], [[], [], []]

    def weight(index):
        at, row = next((i, g.index(index)) for i, g in enumerate(groups) if index in g)
        blocks = [(own[index], 0)] + [(array, row) for array in slots[at]]
        blocks += [(sibling[index], 0)] + [(array, row) for array in across[at]]
        return assemble(blocks, spots, by_rows[index], size)

    env = SimpleNamespace()
    firsts = jnp.sum((segments == 0).astype(jnp.int32), axis=1)
    seconds = jnp.sum((segments <= 1).astype(jnp.int32), axis=1)
    starts = jnp.stack([firsts, seconds], axis=1).reshape(-1)
    whole = jnp.concatenate([jnp.stack([x_at, core, y_at]).astype(jnp.int32), starts])
    scalars = (whole, jnp.log(1.0 - forget_half))
    gains = gain_half.reshape(heads, 1, v_width)
    state_type = jax.ShapeDtypeStruct((seq_count, heads, qk_width, v_width), BF16)
    rows_type = jax.ShapeDtypeStruct((4, seq_count, share_len, v_half), BF16)
    kq_type = jax.ShapeDtypeStruct((4, seq_count, share_len, 2 * heads * qk_width), BF16)
    gain_type = jax.ShapeDtypeStruct((seq_count, heads, 1, v_width), F32)

    def shaped(rows_in):
        return rows_in.reshape(4, seq_count, share_len, -1)

    def flat(rows_in):
        return rows_in.reshape(4 * share_rows, -1)

    x_share = tokens.reshape(share_rows, width).astype(F32)
    cot_share = cotangent.reshape(share_rows, width)

    def work_norm():
        h1, ln1_normed, ln1_scale = norm_rows(x_share, ln1_gain)
        env.ln1 = (ln1_normed, ln1_scale)
        env.h = h1.astype(BF16)
        env.hy = over_y(env.h)
        return [env.h]

    def work_core():
        env.hc, env.hcy = over_core(env.h), over_core(env.hy)
        env.cy = over_y(cot_share)
        return []

    def work_rows():
        env.h_one = stack_rows(env.h, env.hy, env.hc, env.hcy)
        return [env.h_one]

    def work_kq():
        env.wkq = weight(KQ)
        env.kq = sum_of_products(nn, [env.h_one], [env.wkq], 0, 4 * share_rows, BF16)
        return [env.kq]

    def work_v():
        env.wv = weight(V)
        env.v = sum_of_products(nn, [env.h_one], [env.wv], 0, 4 * share_rows, BF16)
        return [env.v]

    def work_state():
        (update,) = per_head(
            update_kernel,
            scalars,
            [(shaped(env.kq), ROWS), (shaped(env.v), ROWS)],
            [(state_type, STATES)],
            4 << 30,
        )
        env.state = lax.ppermute(update, CONTEXT, UP_X)
        env.cc, env.ccy = over_core(cot_share), over_core(env.cy)
        return [update]

    def work_gate():
        env.wg = weight(G)
        env.gate = sum_of_products(nn, [env.h_one], [env.wg], 0, 4 * share_rows, BF16)
        return [env.gate]

    def work_retained():
        gated, env.retained = per_head(
            forward_kernel,
            scalars,
            [
                (shaped(env.kq), ROWS),
                (shaped(env.v), ROWS),
                (shaped(env.gate), ROWS),
                (env.state, STATES),
                (gains, GAINS),
            ],
            [(rows_type, ROWS), (rows_type, ROWS)],
        )
        env.gated = flat(gated)
        return [env.gated]

    def work_out_far():
        env.wo = weight(O)
        own, other = sum_of_products(
            nn, [env.gated], [env.wo], 2 * share_rows, 2 * share_rows, BF16, (), 2
        )
        env.far_other, env.far_own = over_core(other), over_core(own)
        return [other]

    def work_out_near():
        near = sum_of_products(
            nn, [env.gated], [env.wo], share_rows, share_rows, BF16, [(env.far_other, 0)]
        )
        env.near = over_y(near)
        return [near]

    def work_out_own():
        extras = [(env.far_own, 0), (tokens.reshape(share_rows, width), 0)]
        env.own = sum_of_products(nn, [env.gated], [env.wo], 0, share_rows, F32, extras)
        return [env.own]

    def work_cot():
        env.cot = stack_rows(cot_share, env.cy, env.cc, env.ccy)
        return [env.cot]

    def work_d_hidden():
        env.w2 = weight(W2)
        env.d_hidden = sum_of_products(nt, [env.cot], [env.w2], 0, 4 * share_rows, BF16)
        return [env.d_hidden]

    def work_middle():
        env.middle = env.own + env.near.astype(F32)
        h2, ln2_normed, ln2_scale = norm_rows(env.middle, ln2_gain)
        env.ln2 = (ln2_normed, ln2_scale)
        env.h2 = h2.astype(BF16)
        env.h2y, env.h2c = over_y(env.h2), over_core(env.h2)
        return [env.h2]

    def work_up():
        env.w1 = weight(W1)
        return [env.w1]

    def work_h2():
        env.h2cy = over_core(env.h2y)
        env.w3 = weight(W3)
        return [env.w3]

    plan = [
        [work_norm],
        [],
        [work_core],
        [work_rows],
        [work_kq],
        [work_v, work_state],
        [work_cot, work_gate],
        [work_retained, work_out_far],
        [work_out_near, work_out_own],
        [work_middle],
        [work_d_hidden, work_up, work_h2],
    ]
    stacks = [jnp.concatenate([own[index] for index in group], axis=0) for group in groups]
    up = down = kept = to_send = None
    for tick, works in enumerate(plan):
        at, hop = divmod(tick, 3)
        moving = at < len(groups)
        sent, to_send = to_send, None
        if sent is not None:
            slots[sent[0]].append(sent[1])
            across[sent[0]].append(over_x(sent[1]))
        if moving and hop < 2:
            up = stacks[at] if hop == 0 else up
            down = stacks[at] if hop == 0 else down
            got = [lax.ppermute(up, FSDP, UP_Z[hop]), lax.ppermute(down, FSDP, DOWN_Z[hop])]
        elif moving:
            got = [lax.ppermute(slots[at][1], FSDP, LAST_Z)]
        held = []
        for work in works:
            held += work()
        if not moving:
            continue
        names = [n for n in ("h_one", "kq", "gate", "gated", "cot") if hasattr(env, n)]
        held = held + ([across[sent[0]][-1]] if sent is not None else [])
        ahead = stacks[at + 1 : at + 2] if hop == 2 else []
        tied = list(tie(*got, *[getattr(env, n) for n in names], *ahead, *held))
        got = [tied.pop(0) for _ in got]
        for n in names:
            setattr(env, n, tied.pop(0))
        if ahead:
            stacks[at + 1] = tied.pop(0)
        if hop == 0:
            up, down = kept = got
            to_send = (at, jnp.where(z_at > 0, up, down))
        elif hop == 1:
            up, down = got
            to_send = (at, jnp.where(z_at >= 2, up, down))
        else:
            ends = (z_at == 0) | (z_at == z_last)
            to_send = (at, jnp.where(ends, got[0], kept[1]))

    h_one, gated, gate_pre = env.h_one, env.gated, env.gate
    wkq, wv, wg, wo, w1, w2, w3 = env.wkq, env.wv, env.wg, env.wo, env.w1, env.w2, env.w3
    cot_full, d_hidden, middle = env.cot, env.d_hidden, env.middle

    token = [h_one]

    def step(run, *args):
        *args, _ = tie(*args, token[0])
        out = run(*args)
        token[0] = out[0] if isinstance(out, (tuple, list)) else out
        return out

    def far_product(product, lefts, rights):
        def run(*arrays):
            return sum_of_products(
                product, arrays, rights, 2 * share_rows, 2 * share_rows, BF16, (), 2
            )

        own, other = step(run, *lefts)
        return over_core(other), over_core(own)

    def whole_product(product, lefts, rights, first, rows, kind, *extras):
        count = len(lefts)

        def run(*arrays):
            added = [(a, row) for a, (_, row) in zip(arrays[count:], extras)]
            return sum_of_products(
                product, arrays[:count], rights, first * share_rows, rows * share_rows, kind, added
            )

        return step(run, *lefts, *(a for a, _ in extras))

    def theirs(left, right):
        return over_x(step(lambda a, b: quarter_product(a, b, 1 - x_at), left, right))

    def ours(left, right, got):
        total = step(lambda a, b, c: quarter_product(a, b, x_at, [c]), left, right, got)
        return lax.psum_scatter(total, FSDP, scatter_dimension=0, tiled=True)

    def chip_rows(left, right):
        total = step(lambda a, b: split_product(a, b, z_count), left, right)
        return lax.psum_scatter(total, FSDP, scatter_dimension=0, tiled=False)

    def begin_finish(*mine):
        mine = step(lambda *a: jnp.concatenate(a, axis=0), *mine)
        return mine, over_x(mine)

    def end_finish(firsts, mine, beside):
        def join(mine, beside):
            blocks, row = [], 0
            for x_summed in firsts:
                count = 1 if x_summed else 2
                one, other = (a[row * size : (row + count) * size] for a in (mine, beside))
                if x_summed:
                    blocks += [jnp.where(x_at == 0, one, other), jnp.where(x_at == 0, other, one)]
                else:
                    blocks.append((one.astype(F32) + other.astype(F32)).astype(BF16))
                row += count
            return jnp.concatenate(blocks, axis=0)

        both = step(join, mine, beside)
        return both, over_core(both)

    def quarters(pair, at):
        both, other = pair
        mine, theirs = (a[2 * at * size : (2 * at + 2) * size] for a in (both, other))
        first, second = jnp.where(core == 0, mine, theirs), jnp.where(core == 0, theirs, mine)
        return [first[:size], first[size:], second[:size], second[size:]]

    def shard(pair, at, rows):
        return jnp.concatenate(quarters(pair, at), axis=1 - int(rows)).astype(F32)

    h_two = stack_rows(env.h2, env.h2y, env.h2c, env.h2cy)
    hidden, d_fca, d_fcb = step(hidden_units, h_two, w1, w3, d_hidden)

    fc_lefts, fc_rights = (d_fca, d_fcb), (w1, w3)
    far_other, far_own = far_product(nt, fc_lefts, fc_rights)
    down_mine = chip_rows(hidden, cot_full)
    near = over_y(whole_product(nt, fc_lefts, fc_rights, 1, 1, BF16, (far_other, 0)))
    gate_got = theirs(h_two, d_fca)
    own_part = whole_product(nt, fc_lefts, fc_rights, 0, 1, F32, (far_own, 0))
    up_got = theirs(h_two, d_fcb)
    out_far_other, out_far_own = far_product(nn, [hidden], [w2])

    def middle_back(own_part, near):
        d_h2 = own_part + near.astype(F32)
        ln2_normed, ln2_scale = env.ln2
        d_middle = cot_share.astype(F32) + norm_back(d_h2, ln2_normed, ln2_scale, ln2_gain)
        return d_middle.astype(BF16), d_middle, jnp.sum(d_h2 * ln2_normed, axis=0)

    d_mid_low, d_middle, g_ln2 = step(middle_back, own_part, near)
    d_mid_y, d_mid_c = over_y(d_mid_low), over_core(d_mid_low)
    fc_gate_mine = ours(h_two, d_fca, gate_got)
    out_near = whole_product(nn, [hidden], [w2], 1, 1, BF16, (out_far_other, 0))
    out_own = whole_product(nn, [hidden], [w2], 0, 1, F32, (out_far_own, 0), (middle, 0))
    down_begun = begin_finish(down_mine)
    d_mid_y, out_near, up_got = step(lambda *a: a, d_mid_y, out_near, up_got)
    d_mid_cy = over_core(d_mid_y)
    out_near = over_y(out_near)
    fc_up_mine = ours(h_two, d_fcb, up_got)

    def gate_back(share, y, c, cy):
        d_branch = stack_rows(share, y, c, cy)
        return sum_of_products(nt, [d_branch], [wo], 0, 4 * share_rows, BF16), d_branch

    d_gated, d_branch = step(gate_back, d_mid_low, d_mid_y, d_mid_c, d_mid_cy)
    kq, values, state_in = shaped(env.kq), shaped(env.v), env.state

    def retained_back(d_gated, kq):
        return per_head(
            norm_back_kernel,
            scalars,
            [
                (shaped(d_gated), ROWS),
                (shaped(gate_pre), ROWS),
                (env.retained, ROWS),
                (kq, ROWS),
                (gains, GAINS),
            ],
            [(rows_type, ROWS), (rows_type, ROWS), (gain_type, STATES), (state_type, STATES)],
        )

    d_gate, d_retained, g_norm, leaving = step(retained_back, d_gated, kq)
    d_gate = flat(d_gate)
    g_norm = jnp.sum(g_norm, axis=0).reshape(v_half)
    state_grad = lax.ppermute(leaving, CONTEXT, DOWN_X)
    g_down = end_finish([False], *down_begun)
    out_mine = chip_rows(gated, d_branch)
    gg_theirs = step(lambda a, b: quarter_product(a, b, 1 - x_at), h_one, d_gate)
    state_grad, gg_theirs = tie(state_grad, gg_theirs)
    gg_got = over_x(gg_theirs)

    def pair_back(d_retained, state_grad):
        return per_head(
            backward_kernel,
            scalars,
            [
                (kq, ROWS),
                (values, ROWS),
                (d_retained, ROWS),
                (state_in, STATES),
                (state_grad, STATES),
            ],
            [(kq_type, ROWS), (rows_type, ROWS)],
        )

    fc_gate_mine, state_grad = tie(fc_gate_mine, state_grad)
    dkq_low, dv_low = step(pair_back, d_retained, state_grad)
    dkq_low, dv_low = flat(dkq_low), flat(dv_low)
    v_got = theirs(h_one, dv_low)
    kq_got = theirs(h_one, dkq_low)
    h1_lefts, h1_rights = (dkq_low, dv_low, d_gate), (wkq, wv, wg)
    output = step(lambda a, b: (a + b.astype(F32)).astype(BF16), out_own, out_near)
    fc_up_mine, gg_got = tie(fc_up_mine, gg_got)
    gg_mine = ours(h_one, d_gate, gg_got)
    far_other, far_own = far_product(nt, h1_lefts, h1_rights)
    v_mine = ours(h_one, dv_low, v_got)
    near = over_y(whole_product(nt, h1_lefts, h1_rights, 1, 1, BF16, (far_other, 0)))
    own_part = whole_product(nt, h1_lefts, h1_rights, 0, 1, F32, (far_own, 0))
    fc_begun = begin_finish(fc_gate_mine, fc_up_mine)
    kq_mine = ours(h_one, dkq_low, kq_got)

    def tokens_back(own_part, near):
        d_h1 = own_part + near.astype(F32)
        ln1_normed, ln1_scale = env.ln1
        grad = d_middle + norm_back(d_h1, ln1_normed, ln1_scale, ln1_gain)
        return grad, jnp.sum(d_h1 * ln1_normed, axis=0)

    grad_tokens, g_ln1 = step(tokens_back, own_part, near)
    g_fc = end_finish([True, True], *fc_begun)
    out_begun = begin_finish(out_mine, gg_mine)
    v_begun = begin_finish(v_mine)
    g_out_gate = end_finish([False, True], *out_begun)
    g_value = end_finish([True], *v_begun)
    kq_begun = begin_finish(kq_mine)
    g_kq = end_finish([True], *kq_begun)
    sides = quarters(g_kq, 0)
    g_key = jnp.concatenate([side[:, :qk_width] for side in sides], axis=1).astype(F32)
    g_query = jnp.concatenate([side[:, qk_width:] for side in sides], axis=1).astype(F32)

    norm_size = lax.axis_size(TENSOR) * norm_gain.shape[0]
    norm_all = lax.dynamic_update_slice_in_dim(
        jnp.zeros((norm_size,), F32), g_norm, (2 * y_at + core) * v_half, 0
    )
    gain_sums = jnp.concatenate([g_ln1, g_ln2, norm_all])
    for axis in (TENSOR, CONTEXT, FSDP):
        gain_sums = butterfly(gain_sums, axis)
    g_ln1, g_ln2 = gain_sums[:width], gain_sums[width : 2 * width]
    g_norm = lax.dynamic_slice_in_dim(
        gain_sums, 2 * width + y_at * norm_gain.shape[0], norm_gain.shape[0]
    )
    return (
        output.reshape(tokens.shape),
        grad_tokens.reshape(tokens.shape),
        g_ln1,
        g_query,
        g_key,
        shard(g_value, 0, False),
        shard(g_out_gate, 1, False),
        g_norm,
        shard(g_out_gate, 0, True),
        g_ln2,
        shard(g_fc, 0, False),
        shard(g_fc, 1, False),
        shard(g_down, 0, True),
    )


def body(tensor_size, *arrays):
    heads_here = arrays[2].shape[0]
    paired = tensor_size == 2 and heads_here % 2 == 0 and lax.axis_size(CONTEXT) == 4
    paired = paired and lax.axis_size(FSDP) == 4
    return (paired_body if paired else general_body)(*arrays)


def solution(mesh):
    in_specs = (
        P(FSDP, (CONTEXT, TENSOR), None),
        P(FSDP, None),
        P(TENSOR),
        P(),
        P(FSDP, TENSOR),
        P(FSDP, TENSOR),
        P(FSDP, TENSOR),
        P(FSDP, TENSOR),
        P(TENSOR),
        P(TENSOR, FSDP),
        P(),
        P(FSDP, TENSOR),
        P(FSDP, TENSOR),
        P(TENSOR, FSDP),
        P(FSDP, (CONTEXT, TENSOR), None),
    )
    out_specs = (
        P(FSDP, (CONTEXT, TENSOR), None),
        P(FSDP, (CONTEXT, TENSOR), None),
        P(),
        P(FSDP, TENSOR),
        P(FSDP, TENSOR),
        P(FSDP, TENSOR),
        P(FSDP, TENSOR),
        P(TENSOR),
        P(TENSOR, FSDP),
        P(),
        P(FSDP, TENSOR),
        P(FSDP, TENSOR),
        P(TENSOR, FSDP),
    )
    return jax.shard_map(partial(body, mesh.shape[TENSOR]), mesh=mesh, in_specs=in_specs, out_specs=out_specs, check_vma=False)
```

```python
from functools import partial
from types import SimpleNamespace

import jax
import jax.numpy as jnp
from jax import lax
from jax.experimental import pallas as pl
from jax.experimental.pallas import tpu as pltpu
from jax.sharding import PartitionSpec as P

FSDP, CONTEXT, TENSOR = "fsdp", "context", "tensor"

careful = partial(jnp.einsum, precision=lax.Precision.HIGH)


def entering(part, axis, combine, identity):
    place = lax.axis_index(axis)
    gathered = jax.tree.map(lambda a: lax.all_gather(a, axis), part)
    state = jax.tree.map(lambda a, e: jnp.zeros_like(a) + jnp.asarray(e, a.dtype), part, identity)

    def one(step, state):
        return combine(
            state, jax.tree.map(lambda a: lax.dynamic_index_in_dim(a, step, 0, False), gathered)
        )

    return lax.fori_loop(0, place, one, state)


def carried_in(value, axis, combine, identity):
    count, place = (lax.axis_size(axis), lax.axis_index(axis))
    everything = jax.tree.map(
        lambda part, kind: lax.all_gather(part.astype(kind), axis),
        value,
        jax.tree.map(lambda a: jnp.bfloat16 if a.dtype == jnp.float32 else a.dtype, value),
    )
    start = jax.tree.map(
        lambda part, zero: jnp.broadcast_to(jnp.asarray(zero, part.dtype), part.shape),
        value,
        identity,
    )

    def step(k, before):
        at = count - 1 - k
        reached = at > place
        new = combine(
            before, jax.tree.map(lambda part, own: part[at].astype(own.dtype), everything, value)
        )
        return jax.tree.map(lambda a, b: jnp.where(reached, a, b), new, before)

    return lax.fori_loop(0, count, step, start)


def norm_rows(values, gain_vec, epsilon=1e-05):
    centred = values - jnp.mean(values, axis=-1, keepdims=True)
    scale = lax.rsqrt(jnp.mean(centred * centred, axis=-1, keepdims=True) + epsilon)
    normed = centred * scale
    return (normed * gain_vec, normed, scale)


def norm_back(grad_in, normed, scale, gain_vec):
    d_normed = grad_in * gain_vec
    first_mean = jnp.mean(d_normed, axis=-1, keepdims=True)
    second_mean = jnp.mean(d_normed * normed, axis=-1, keepdims=True)
    return scale * (d_normed - first_mean - normed * second_mean)


def swish_slope(values):
    sigma = jax.nn.sigmoid(values)
    return sigma * (1.0 + values * (1.0 - sigma))


def compose(earlier, latter):
    return (earlier[0] * latter[0], latter[0][:, :, None, None] * earlier[1] + latter[1])


def share_gather(piece):
    return lax.all_gather(piece, TENSOR, axis=1, tiled=True)


def branch_sum(terms):
    return lax.psum_scatter(terms, TENSOR, scatter_dimension=1, tiled=True)


def input_sum(terms):
    return lax.psum_scatter(
        terms.astype(jnp.bfloat16), TENSOR, scatter_dimension=1, tiled=True
    ).astype(jnp.float32)


def mixer_fetch(w_query, w_key, w_value, w_gate, w_out):
    return (
        lax.all_gather(w_query, FSDP, axis=0, tiled=True),
        lax.all_gather(w_key, FSDP, axis=0, tiled=True),
        lax.all_gather(w_value, FSDP, axis=0, tiled=True),
        lax.all_gather(w_gate, FSDP, axis=0, tiled=True),
        lax.all_gather(w_out, FSDP, axis=1, tiled=True),
    )


def mlp_fetch(w_fc_gate, w_fc_up, w_fc_down):
    return (
        lax.all_gather(w_fc_gate, FSDP, axis=0, tiled=True),
        lax.all_gather(w_fc_up, FSDP, axis=0, tiled=True),
        lax.all_gather(w_fc_down, FSDP, axis=1, tiled=True),
    )


def product(form, left, right):
    return jnp.einsum(form, left, right, preferred_element_type=jnp.float32)


def general_body(
    tokens,
    segments,
    forget,
    ln1_gain,
    w_query,
    w_key,
    w_value,
    w_gate,
    norm_gain,
    w_out,
    ln2_gain,
    w_fc_gate,
    w_fc_up,
    w_fc_down,
    cotangent,
):
    heads_here = forget.shape[0]
    qk_width = w_query.shape[1] // heads_here
    v_width = w_value.shape[1] // heads_here
    v_local = heads_here * v_width
    gain_heads = norm_gain.reshape(heads_here, v_width)
    x_share = tokens.astype(jnp.float32)
    h1_share, ln1_normed, ln1_scale = norm_rows(x_share, ln1_gain)
    h_one = share_gather(h1_share.astype(jnp.bfloat16))
    wq_all, wk_all, wv_all, wg_all, wo_all = mixer_fetch(w_query, w_key, w_value, w_gate, w_out)
    seq_count, stretch_len = (h_one.shape[0], h_one.shape[1])
    query = product("btd,dq->btq", h_one, wq_all).astype(jnp.bfloat16)
    keys = product("btd,dq->btq", h_one, wk_all).astype(jnp.bfloat16)
    values = product("btd,dv->btv", h_one, wv_all).astype(jnp.bfloat16)
    gate_pre = product("btd,dv->btv", h_one, wg_all)
    query_heads = query.reshape(seq_count, stretch_len, heads_here, qk_width)
    keys_heads = keys.reshape(seq_count, stretch_len, heads_here, qk_width)
    query_full = query_heads.astype(jnp.float32) * 0.0625
    keys_full = keys_heads.astype(jnp.float32)
    values_full = values.astype(jnp.float32).reshape(seq_count, stretch_len, heads_here, v_width)
    log_keep = jnp.log(1.0 - forget)
    ctx_place = lax.axis_index(CONTEXT)
    seg_stretch = lax.dynamic_slice_in_dim(segments, ctx_place * stretch_len, stretch_len, 1)
    seg_prev = lax.dynamic_slice_in_dim(segments, jnp.maximum(ctx_place * stretch_len - 1, 0), 1, 1)
    live_mask = (seg_stretch == seg_prev).astype(jnp.float32)
    steps_idx = jnp.arange(stretch_len, dtype=jnp.float32)
    step_gap = jnp.maximum(steps_idx[:, None] - steps_idx[None, :], 0.0)
    causal = steps_idx[:, None] >= steps_idx[None, :]
    same_doc = (seg_stretch[:, :, None] == seg_stretch[:, None, :]) & causal[None]
    weights_mask = jnp.where(
        same_doc[:, None], jnp.exp(step_gap[None] * log_keep[:, None, None])[None], 0.0
    )
    inflow = live_mask[:, :, None] * jnp.exp((steps_idx[:, None] + 1.0) * log_keep[None, :])[None]
    outflow = (seg_stretch == seg_stretch[:, -1:]).astype(jnp.float32)[:, :, None] * jnp.exp(
        (stretch_len - 1.0 - steps_idx)[:, None] * log_keep[None, :]
    )[None]
    carry_decay = live_mask[:, -1:] * jnp.exp(stretch_len * log_keep)[None, :]
    update = careful("bshd,bsh,bshe->bhde", keys_full, outflow, values_full)
    identity = (jnp.ones_like(carry_decay), jnp.zeros_like(update))
    state_in = entering((carry_decay, update), CONTEXT, compose, identity)[1]
    scores = product("bthd,bshd->bhts", query_heads, keys_heads) * 0.0625 * weights_mask
    retained = careful("bhts,bshe->bthe", scores, values_full)
    retained = retained + inflow[..., None] * careful("bthd,bhde->bthe", query_full, state_in)
    normed_out, gn_normed, gn_scale = norm_rows(retained, gain_heads, 0.01)
    norm_flat = normed_out.reshape(seq_count, stretch_len, v_local)
    gate_act = jax.nn.silu(gate_pre)
    gated = (gate_act * norm_flat).astype(jnp.bfloat16)
    middle = x_share + branch_sum(product("btv,vd->btd", gated, wo_all))
    h2_share, ln2_normed, ln2_scale = norm_rows(middle, ln2_gain)
    h_two = share_gather(h2_share.astype(jnp.bfloat16))
    w1_all, w3_all, w2_all = mlp_fetch(w_fc_gate, w_fc_up, w_fc_down)
    fc_a = product("btd,df->btf", h_two, w1_all)
    fc_b = product("btd,df->btf", h_two, w3_all)
    silu_a = jax.nn.silu(fc_a)
    hidden = (silu_a * fc_b).astype(jnp.bfloat16)
    output = (middle + branch_sum(product("btf,fd->btd", hidden, w2_all))).astype(jnp.bfloat16)
    wq_all, wk_all, wv_all, wg_all, wo_all = mixer_fetch(w_query, w_key, w_value, w_gate, w_out)
    w1_all, w3_all, w2_all = mlp_fetch(w_fc_gate, w_fc_up, w_fc_down)
    cot_full = share_gather(cotangent)
    d_hidden = product("btd,fd->btf", cot_full, w2_all)
    g_down = product("btf,btd->fd", hidden, cot_full)
    d_fca = (d_hidden * fc_b * swish_slope(fc_a)).astype(jnp.bfloat16)
    d_fcb = (d_hidden * silu_a).astype(jnp.bfloat16)
    g_fc_gate = product("btd,btf->df", h_two, d_fca)
    g_fc_up = product("btd,btf->df", h_two, d_fcb)
    d_h2 = input_sum(product("btf,df->btd", d_fca, w1_all) + product("btf,df->btd", d_fcb, w3_all))
    d_middle = cotangent.astype(jnp.float32) + norm_back(d_h2, ln2_normed, ln2_scale, ln2_gain)
    g_ln2 = jnp.sum(d_h2 * ln2_normed, axis=(0, 1))
    d_branch = share_gather(d_middle.astype(jnp.bfloat16))
    d_gated = product("btd,vd->btv", d_branch, wo_all)
    g_out = product("btv,btd->vd", gated, d_branch)
    d_gate = (d_gated * norm_flat * swish_slope(gate_pre)).astype(jnp.bfloat16)
    d_normed = (d_gated * gate_act).reshape(seq_count, stretch_len, heads_here, v_width)
    g_norm = jnp.sum(d_normed * gn_normed, axis=(0, 1)).reshape(v_local)
    d_retained = norm_back(d_normed, gn_normed, gn_scale, gain_heads)
    d_scores = careful("bthe,bshe->bhts", d_retained, values_full) * weights_mask
    d_values = careful("bhts,bthe->bshe", scores, d_retained)
    d_query = careful("bhts,bshd->bthd", d_scores, keys_full)
    d_query = d_query + inflow[..., None] * careful("bthe,bhde->bthd", d_retained, state_in)
    d_keys = careful("bhts,bthd->bshd", d_scores, query_full)
    leaving = careful("bthd,bth,bthe->bhde", query_full, inflow, d_retained)
    state_grad = carried_in((carry_decay, leaving), CONTEXT, compose, identity)[1]
    d_keys = d_keys + outflow[..., None] * careful("bshe,bhde->bshd", values_full, state_grad)
    d_values = d_values + outflow[..., None] * careful("bshd,bhde->bshe", keys_full, state_grad)
    dq_low = (
        (d_query * 0.0625)
        .reshape(seq_count, stretch_len, heads_here * qk_width)
        .astype(jnp.bfloat16)
    )
    dk_low = d_keys.reshape(seq_count, stretch_len, heads_here * qk_width).astype(jnp.bfloat16)
    dv_low = d_values.reshape(seq_count, stretch_len, v_local).astype(jnp.bfloat16)
    g_query = product("btd,btq->dq", h_one, dq_low)
    g_key = product("btd,btq->dq", h_one, dk_low)
    g_value = product("btd,btv->dv", h_one, dv_low)
    g_gate = product("btd,btv->dv", h_one, d_gate)
    d_h1 = product("btq,dq->btd", dq_low, wq_all) + product("btq,dq->btd", dk_low, wk_all)
    d_h1 = d_h1 + product("btv,dv->btd", dv_low, wv_all) + product("btv,dv->btd", d_gate, wg_all)
    d_h1 = input_sum(d_h1)
    grad_tokens = d_middle + norm_back(d_h1, ln1_normed, ln1_scale, ln1_gain)
    g_ln1 = jnp.sum(d_h1 * ln1_normed, axis=(0, 1))
    tensor_place = lax.axis_index(TENSOR)
    norm_full = lax.dynamic_update_slice(
        jnp.zeros((v_local * lax.axis_size(TENSOR),), jnp.float32),
        g_norm,
        (tensor_place * v_local,),
    )
    g_ln1, g_ln2, norm_full = lax.psum((g_ln1, g_ln2, norm_full), (FSDP, CONTEXT, TENSOR))
    g_norm = lax.dynamic_slice_in_dim(norm_full, tensor_place * v_local, v_local)
    weight_grads = (g_query, g_key, g_value, g_gate, g_out, g_fc_gate, g_fc_up, g_down)
    summed = (
        lax.psum(weight_grads[0].astype(jnp.bfloat16), CONTEXT).astype(jnp.float32),
        lax.psum(weight_grads[1].astype(jnp.bfloat16), CONTEXT).astype(jnp.float32),
        lax.psum(weight_grads[2].astype(jnp.bfloat16), CONTEXT).astype(jnp.float32),
        lax.psum(weight_grads[3].astype(jnp.bfloat16), CONTEXT).astype(jnp.float32),
        lax.psum(weight_grads[4].astype(jnp.bfloat16), CONTEXT).astype(jnp.float32),
        lax.psum(weight_grads[5].astype(jnp.bfloat16), CONTEXT).astype(jnp.float32),
        lax.psum(weight_grads[6].astype(jnp.bfloat16), CONTEXT).astype(jnp.float32),
        lax.psum(weight_grads[7].astype(jnp.bfloat16), CONTEXT).astype(jnp.float32),
    )
    shards = (
        lax.psum_scatter(
            summed[0].astype(jnp.bfloat16), FSDP, scatter_dimension=0, tiled=True
        ).astype(jnp.float32),
        lax.psum_scatter(
            summed[1].astype(jnp.bfloat16), FSDP, scatter_dimension=0, tiled=True
        ).astype(jnp.float32),
        lax.psum_scatter(
            summed[2].astype(jnp.bfloat16), FSDP, scatter_dimension=0, tiled=True
        ).astype(jnp.float32),
        lax.psum_scatter(
            summed[3].astype(jnp.bfloat16), FSDP, scatter_dimension=0, tiled=True
        ).astype(jnp.float32),
        lax.psum_scatter(
            summed[4].astype(jnp.bfloat16), FSDP, scatter_dimension=1, tiled=True
        ).astype(jnp.float32),
        lax.psum_scatter(
            summed[5].astype(jnp.bfloat16), FSDP, scatter_dimension=0, tiled=True
        ).astype(jnp.float32),
        lax.psum_scatter(
            summed[6].astype(jnp.bfloat16), FSDP, scatter_dimension=0, tiled=True
        ).astype(jnp.float32),
        lax.psum_scatter(
            summed[7].astype(jnp.bfloat16), FSDP, scatter_dimension=1, tiled=True
        ).astype(jnp.float32),
    )
    return (
        output,
        grad_tokens,
        g_ln1,
        shards[0],
        shards[1],
        shards[2],
        shards[3],
        g_norm,
        shards[4],
        g_ln2,
        shards[5],
        shards[6],
        shards[7],
    )


F32 = jnp.float32
BF16 = jnp.bfloat16
BOTH_X = [(0, 2), (2, 0), (1, 3), (3, 1)]
UP_X = [(0, 2), (1, 3)]
DOWN_X = [(2, 0), (3, 1)]
CORES = [(0, 1), (1, 0), (2, 3), (3, 2)]
UP_Z = [[(0, 1), (1, 2), (2, 3)], [(1, 2), (2, 3)]]
DOWN_Z = [[(3, 2), (2, 1), (1, 0)], [(2, 1), (1, 0)]]
LAST_Z = [(2, 3), (1, 0)]
SCALE = 0.0625
ROWS, GAINS, STATES = range(3)


def cost(flops):
    return pl.CostEstimate(flops=flops, transcendentals=0, bytes_accessed=0)


COPYING = 2 << 30
DOWN_Z = [[(3, 2), (2, 1), (1, 0)], [(2, 1), (1, 0)], [(1, 0)]]


def over_x(value):
    return lax.ppermute(value, CONTEXT, BOTH_X)


def over_core(value):
    return lax.ppermute(value, CONTEXT, CORES)


def over_y(value):
    return lax.ppermute(value, TENSOR, [(0, 1), (1, 0)])


def tie(*values):
    return lax.optimization_barrier(values)


def butterfly(value, axis):
    size = lax.axis_size(axis)
    step = 1
    while step < size:
        value = value + lax.ppermute(value, axis, [(i, i ^ step) for i in range(size)])
        step *= 2
    return value


def quarter_of(weight, dim, index):
    size = weight.shape[dim] // 4
    return lax.dynamic_slice_in_dim(weight, index * size, size, dim)


def assemble_kernel(spot_ref, *refs):
    at = pl.program_id(0)
    for index, block in enumerate(refs[:8]):

        @pl.when(at == index)
        def _(block=block):
            refs[8][...] = block[...]


def assemble(blocks, spots, by_rows, size):
    shape = (2 * size, 4 * size) if by_rows else (4 * size, 2 * size)

    def spot(at, spots_ref):
        z_from, x_from = spots_ref[at], spots_ref[8 + at]
        return (x_from, z_from) if by_rows else (z_from, x_from)

    return pl.pallas_call(
        assemble_kernel,
        out_shape=jax.ShapeDtypeStruct(shape, BF16),
        grid_spec=pltpu.PrefetchScalarGridSpec(
            num_scalar_prefetch=1,
            grid=(8,),
            in_specs=[
                pl.BlockSpec((size, size), lambda at, spots_ref, row=row: (row, 0))
                for _, row in blocks
            ],
            out_specs=pl.BlockSpec((size, size), spot),
        ),
        compiler_params=pltpu.CompilerParams(vmem_limit_bytes=32 << 20),
        cost_estimate=cost(COPYING),
    )(spots, *(array for array, _ in blocks))


def sum_kernel(product, count, outs, *refs):
    lefts, rights, extras = refs[:count], refs[count : 2 * count], refs[2 * count : -outs]
    total = product(lefts[0][...], rights[0][...])
    for left, right in zip(lefts[1:], rights[1:]):
        total = total + product(left[...], right[...])
    for extra in extras:
        total = total + extra[...].astype(F32)
    size = total.shape[0] // outs
    for index, out_ref in enumerate(refs[-outs:]):
        out_ref[...] = total[index * size : (index + 1) * size].astype(out_ref.dtype)


def sum_of_products(product, lefts, rights, first, rows, kind, extras=(), outs=1):
    by_columns = product is nn
    width = rights[0].shape[1 if by_columns else 0]
    block, tile = min(1024, rows), min(512, width)
    if outs > 1:
        block = rows

    def right_spec(right):
        if by_columns:
            return pl.BlockSpec((right.shape[0], tile), lambda n, m: (0, n))
        return pl.BlockSpec((tile, right.shape[1]), lambda n, m: (n, 0))

    def tile_spec(from_row, size):
        return pl.BlockSpec((size, tile), lambda n, m: (from_row // size + m, n))

    out_shape = [jax.ShapeDtypeStruct((rows // outs, width), kind)] * outs
    result = pl.pallas_call(
        partial(sum_kernel, product, len(lefts), outs),
        grid=(width // tile, rows // block),
        out_shape=out_shape,
        in_specs=[
            pl.BlockSpec((block, left.shape[1]), lambda n, m: (first // block + m, 0))
            for left in lefts
        ]
        + [right_spec(right) for right in rights]
        + [tile_spec(from_row, block) for _, from_row in extras],
        out_specs=[tile_spec(0, block // outs)] * outs,
        compiler_params=pltpu.CompilerParams(vmem_limit_bytes=60 << 20),
        cost_estimate=cost(2 * rows * width * sum(left.shape[1] for left in lefts)),
    )(*lefts, *rights, *(array for array, _ in extras))
    return result[0] if outs == 1 else result


def quarter_kernel(spots_ref, left, right, *rest):
    total = tn(left[...], right[...])
    for extra in rest[:-1]:
        total = total + extra[...].astype(F32)
    rest[-1][...] = total.astype(BF16)


def quarter_product(left, right, index, extras=()):
    tokens, width = left.shape
    size, block = right.shape[1] // 2, min(1024, width)
    return pl.pallas_call(
        quarter_kernel,
        out_shape=jax.ShapeDtypeStruct((width, size), BF16),
        grid_spec=pltpu.PrefetchScalarGridSpec(
            num_scalar_prefetch=1,
            grid=(width // block,),
            in_specs=[
                pl.BlockSpec((tokens, block), lambda m, at: (0, m)),
                pl.BlockSpec((tokens, size), lambda m, at: (0, at[0])),
            ]
            + [pl.BlockSpec((block, size), lambda m, at: (m, 0)) for _ in extras],
            out_specs=pl.BlockSpec((block, size), lambda m, at: (m, 0)),
        ),
        compiler_params=pltpu.CompilerParams(vmem_limit_bytes=60 << 20),
        cost_estimate=cost(2 * tokens * width * size),
    )(index.reshape(1).astype(jnp.int32), left, right, *extras)


def split_kernel(left, right, out):
    out[0] = tn(left[...], right[...]).astype(BF16)


def split_product(left, right, count):
    tokens, rows = left.shape
    size = right.shape[1] // count
    return pl.pallas_call(
        split_kernel,
        grid=(count,),
        out_shape=jax.ShapeDtypeStruct((count, rows, size), BF16),
        in_specs=[
            pl.BlockSpec((tokens, rows), lambda n: (0, 0)),
            pl.BlockSpec((tokens, size), lambda n: (0, n)),
        ],
        out_specs=pl.BlockSpec((1, rows, size), lambda n: (n, 0, 0)),
        compiler_params=pltpu.CompilerParams(vmem_limit_bytes=60 << 20),
        cost_estimate=cost(2 * tokens * rows * size * count),
    )(left, right)


def unit_kernel(h_ref, w1_ref, w3_ref, d_hidden_ref, hidden_ref, d_a_ref, d_b_ref):
    fc_a, fc_b = nn(h_ref[...], w1_ref[...]), nn(h_ref[...], w3_ref[...])
    d_hidden = d_hidden_ref[...].astype(F32)
    sigma = jax.nn.sigmoid(fc_a)
    silu_a = fc_a * sigma
    hidden_ref[...] = (silu_a * fc_b).astype(BF16)
    d_a_ref[...] = (d_hidden * fc_b * (sigma * (1.0 + fc_a * (1.0 - sigma)))).astype(BF16)
    d_b_ref[...] = (d_hidden * silu_a).astype(BF16)


def hidden_units(h_two, w1, w3, d_hidden):
    rows, width = h_two.shape
    count = w1.shape[1]
    block, tile = min(512, rows), min(512, count)
    weight = pl.BlockSpec((width, tile), lambda n, m: (0, n))
    spot = pl.BlockSpec((block, tile), lambda n, m: (m, n))
    return pl.pallas_call(
        unit_kernel,
        grid=(count // tile, rows // block),
        out_shape=[jax.ShapeDtypeStruct((rows, count), BF16)] * 3,
        in_specs=[pl.BlockSpec((block, width), lambda n, m: (m, 0)), weight, weight, spot],
        out_specs=[spot] * 3,
        compiler_params=pltpu.CompilerParams(vmem_limit_bytes=60 << 20),
        cost_estimate=cost(4 * rows * width * count),
    )(h_two, w1, w3, d_hidden)


def stack_kernel(*refs):
    count = len(refs) - 4
    shares, out_ref, held, sems_in, sems_out = refs[:count], *refs[count:]
    rows = shares[0].shape[0]
    ins, outs = [], []
    for index, share in enumerate(shares):
        ins.append(pltpu.make_async_copy(share, held.at[index], sems_in.at[index]))
        spot = out_ref.at[pl.ds(index * rows, rows)]
        outs.append(pltpu.make_async_copy(held.at[index], spot, sems_out.at[index]))
    for copy in ins:
        copy.start()
    for copy, onward in zip(ins, outs):
        copy.wait()
        onward.start()
    for onward in outs:
        onward.wait()


def stack_rows(*shares):
    rows, width = shares[0].shape
    count = len(shares)
    return pl.pallas_call(
        stack_kernel,
        out_shape=jax.ShapeDtypeStruct((count * rows, width), shares[0].dtype),
        in_specs=[pl.BlockSpec(memory_space=pl.ANY)] * count,
        out_specs=pl.BlockSpec(memory_space=pl.ANY),
        scratch_shapes=[
            pltpu.VMEM((count, rows, width), shares[0].dtype),
            pltpu.SemaphoreType.DMA((count,)),
            pltpu.SemaphoreType.DMA((count,)),
        ],
        compiler_params=pltpu.CompilerParams(vmem_limit_bytes=48 << 20),
        cost_estimate=cost(2 * COPYING),
    )(*shares)


def nn(left, right):
    return lax.dot_general(left, right, (((1,), (0,)), ((), ())), preferred_element_type=F32)


def nt(left, right):
    return lax.dot_general(left, right, (((1,), (1,)), ((), ())), preferred_element_type=F32)


def tn(left, right):
    return lax.dot_general(left, right, (((0,), (0,)), ((), ())), preferred_element_type=F32)


def where_is(whole, chunk, piece_len):
    share_len = piece_len // 2
    spots = []
    for shape, dim in (((piece_len, 1), 0), ((1, piece_len), 1)):
        at = lax.broadcasted_iota(jnp.int32, shape, dim) + whole[2] * share_len
        spots.append(jnp.where(at >= piece_len, at - piece_len, at))
    start = whole[0] * (2 * piece_len) + chunk * piece_len
    return spots[0], spots[1], start


def document(whole, spot):
    seq = pl.program_id(0)
    first, second = whole[3 + 2 * seq], whole[4 + 2 * seq]
    return jnp.where(spot >= second, 2, jnp.where(spot >= first, 1, 0))


def fade(gap, log_keep):
    return jnp.exp(jnp.maximum(gap, 0).astype(F32) * log_keep)


def piece_terms(whole, log_keep, chunk, piece_len):
    rows, cols, start = where_is(whole, chunk, piece_len)
    doc_rows, doc_cols = document(whole, start + rows), document(whole, start + cols)
    before, last = document(whole, start - 1), document(whole, start + piece_len - 1)
    within = jnp.where(
        (rows >= cols) & (doc_rows == doc_cols), fade(rows - cols, log_keep) * SCALE, 0.0
    )
    inflow = jnp.where(doc_rows == before, fade(rows + 1, log_keep) * SCALE, 0.0)
    outflow = jnp.where(doc_rows == last, fade(piece_len - 1 - rows, log_keep), 0.0)
    whole_gap = jnp.full((1, 1), piece_len, jnp.int32)
    over = jnp.where(before == last, fade(whole_gap, log_keep), 0.0)
    return within, inflow, outflow, over


def piece_of(ref, whole, chunk):
    group = lax.rem(chunk + whole[1], 2) * 2
    value = ref[pl.ds(group, 2), 0]
    return value.reshape(value.shape[0] * value.shape[1], value.shape[2])


def put_piece(ref, whole, chunk, value):
    group = lax.rem(chunk + whole[1], 2) * 2
    ref[pl.ds(group, 2), 0] = value.astype(ref.dtype).reshape(2, value.shape[0] // 2, value.shape[1])


def split_kq(ref, whole, chunk):
    both = piece_of(ref, whole, chunk)
    width = both.shape[1] // 2
    return both[:, :width], both[:, width:]


def update_kernel(whole, keeps, kq_ref, v_ref, out_ref):
    log_keep = keeps[pl.program_id(1)]
    piece_len = 2 * kq_ref.shape[2]
    total = jnp.zeros(out_ref.shape[2:], F32)
    for chunk in range(2):
        rows, _, start = where_is(whole, chunk, piece_len)
        last = document(whole, whole[0] * (2 * piece_len) + 2 * piece_len - 1)
        gap = (2 - chunk) * piece_len - 1 - rows
        weight = jnp.where(document(whole, start + rows) == last, fade(gap, log_keep), 0.0)
        keys, _ = split_kq(kq_ref, whole, chunk)
        values = piece_of(v_ref, whole, chunk)
        total = total + tn((keys.astype(F32) * weight).astype(BF16), values)
    out_ref[0, 0] = total.astype(BF16)


def next_state(state, keys, values, outflow, over):
    return over * state + tn((keys.astype(F32) * outflow).astype(BF16), values)


def forward_kernel(
    whole, keeps, kq_ref, v_ref, gate_ref, state_ref, gain_ref, gated_ref, retained_ref
):
    log_keep = keeps[pl.program_id(1)]
    piece_len = 2 * kq_ref.shape[2]
    state = state_ref[0, 0].astype(F32)
    for chunk in range(2):
        within, inflow, outflow, over = piece_terms(whole, log_keep, chunk, piece_len)
        keys, query = split_kq(kq_ref, whole, chunk)
        values = piece_of(v_ref, whole, chunk)
        scores = (nt(query, keys) * within).astype(BF16)
        retained = nn(scores, values) + inflow * nn(query, state.astype(BF16))
        if chunk == 0:
            state = next_state(state, keys, values, outflow, over)
        put_piece(retained_ref, whole, chunk, retained)
        normed, _, _ = norm_rows(retained, gain_ref[0], 0.01)
        gate = piece_of(gate_ref, whole, chunk).astype(F32)
        put_piece(gated_ref, whole, chunk, gate * jax.nn.sigmoid(gate) * normed)


def norm_back_kernel(
    whole,
    keeps,
    d_gated_ref,
    gate_ref,
    retained_ref,
    kq_ref,
    gain_ref,
    d_gate_ref,
    d_retained_ref,
    d_gain_ref,
    leaving_ref,
):
    log_keep = keeps[pl.program_id(1)]
    piece_len = 2 * kq_ref.shape[2]
    total = jnp.zeros(leaving_ref.shape[2:], F32)
    gain = gain_ref[0]
    d_gain = jnp.zeros(gain.shape, F32)
    for chunk in range(2):
        rows, _, start = where_is(whole, chunk, piece_len)
        before = document(whole, whole[0] * (2 * piece_len) - 1)
        gap = chunk * piece_len + rows + 1
        weight = jnp.where(
            document(whole, start + rows) == before, fade(gap, log_keep) * SCALE, 0.0
        )
        _, query = split_kq(kq_ref, whole, chunk)
        retained = piece_of(retained_ref, whole, chunk).astype(F32)
        normed, unit, scale = norm_rows(retained, gain, 0.01)
        gate = piece_of(gate_ref, whole, chunk).astype(F32)
        d_gated = piece_of(d_gated_ref, whole, chunk).astype(F32)
        sigma = jax.nn.sigmoid(gate)
        put_piece(
            d_gate_ref, whole, chunk, d_gated * normed * sigma * (1.0 + gate * (1.0 - sigma))
        )
        d_normed = d_gated * gate * sigma
        d_gain = d_gain + jnp.sum(d_normed * unit, axis=0, keepdims=True)
        d_retained = norm_back(d_normed, unit, scale, gain)
        put_piece(d_retained_ref, whole, chunk, d_retained)
        total = total + tn(query, (d_retained * weight).astype(BF16))
    d_gain_ref[0, 0] = d_gain
    leaving_ref[0, 0] = total.astype(BF16)


def backward_kernel(
    whole, keeps, kq_ref, v_ref, d_retained_ref, state_ref, d_state_ref, d_kq_ref, d_v_ref
):
    log_keep = keeps[pl.program_id(1)]
    piece_len = 2 * kq_ref.shape[2]
    terms = [piece_terms(whole, log_keep, chunk, piece_len) for chunk in range(2)]
    state = state_ref[0, 0].astype(F32)
    keys, _ = split_kq(kq_ref, whole, 0)
    _, _, outflow, over = terms[0]
    states = [state, next_state(state, keys, piece_of(v_ref, whole, 0), outflow, over)]
    d_state = d_state_ref[0, 0].astype(F32)
    for chunk in (1, 0):
        within, inflow, outflow, over = terms[chunk]
        keys, query = split_kq(kq_ref, whole, chunk)
        values = piece_of(v_ref, whole, chunk)
        d_ret = piece_of(d_retained_ref, whole, chunk)
        state_low, d_state_low = states[chunk].astype(BF16), d_state.astype(BF16)
        scores = (nt(query, keys) * within).astype(BF16)
        d_scores = (nt(d_ret, values) * within).astype(BF16)
        d_values = tn(scores, d_ret) + outflow * nn(keys, d_state_low)
        put_piece(d_v_ref, whole, chunk, d_values)
        d_query = nn(d_scores, keys) + inflow * nt(d_ret, state_low)
        d_keys = tn(d_scores, query) + outflow * nt(values, d_state_low)
        put_piece(d_kq_ref, whole, chunk, jnp.concatenate([d_keys, d_query], axis=1))
        if chunk == 1:
            entering = tn(query, (d_ret.astype(F32) * inflow).astype(BF16))
            d_state = over * d_state + entering


def per_head(kernel, scalars, blocks, outs, flops=12 << 30):
    def spec(array, kind):
        if kind == ROWS:
            width = array.shape[3] // heads
            return pl.BlockSpec((4, 1, array.shape[2], width), lambda b, h, *_: (0, b, 0, h))
        if kind == GAINS:
            return pl.BlockSpec((1, *array.shape[1:]), lambda b, h, *_: (h, 0, 0))
        return pl.BlockSpec((1, 1, *array.shape[2:]), lambda b, h, *_: (b, h, 0, 0))

    heads = scalars[1].shape[0]
    seq_count = (scalars[0].shape[0] - 3) // 2
    return pl.pallas_call(
        kernel,
        out_shape=[a for a, _ in outs],
        grid_spec=pltpu.PrefetchScalarGridSpec(
            num_scalar_prefetch=2,
            grid=(seq_count, heads),
            in_specs=[spec(*block) for block in blocks],
            out_specs=[spec(*out) for out in outs],
        ),
        compiler_params=pltpu.CompilerParams(vmem_limit_bytes=56 << 20),
        cost_estimate=cost(flops),
    )(*scalars, *(a for a, _ in blocks))


def both_quarters(mine, across, first, dim):
    return jnp.concatenate(
        [jnp.where(first, mine, across), jnp.where(first, across, mine)], axis=dim
    )


def paired_body(
    tokens,
    segments,
    forget,
    ln1_gain,
    w_query,
    w_key,
    w_value,
    w_gate,
    norm_gain,
    w_out,
    ln2_gain,
    w_fc_gate,
    w_fc_up,
    w_fc_down,
    cotangent,
):
    place = lax.axis_index(CONTEXT)
    x_at, core, y_at = place // 2, place % 2, lax.axis_index(TENSOR)
    z_at = lax.axis_index(FSDP)
    heads = forget.shape[0] // 2
    qk_width = w_query.shape[1] // forget.shape[0]
    v_width = w_value.shape[1] // forget.shape[0]
    width = tokens.shape[2]
    seq_count, share_len = tokens.shape[0], tokens.shape[1]
    share_rows = seq_count * share_len
    piece_len = 2 * share_len
    chip_len = 2 * piece_len
    v_half = heads * v_width
    forget_half = lax.dynamic_slice_in_dim(forget, core * heads, heads)
    gain_half = lax.dynamic_slice_in_dim(norm_gain, core * v_half, v_half)

    def part(array, first, last):
        return array[first * share_rows : last * share_rows]

    def unit(x_index):
        q = core * 2 + x_index
        key_query = [quarter_of(w_key, 1, q), quarter_of(w_query, 1, q)]
        return [
            jnp.concatenate(key_query, axis=1),
            quarter_of(w_value, 1, q),
            quarter_of(w_gate, 1, q),
            quarter_of(w_out, 0, q),
            quarter_of(w_fc_down, 0, q),
            quarter_of(w_fc_gate, 1, q),
            quarter_of(w_fc_up, 1, q),
        ]

    KQ, V, G, O, W2, W1, W3 = range(7)
    by_rows = [False, False, False, True, True, False, False]
    own, sibling = unit(x_at), unit(1 - x_at)
    size = own[0].shape[0]
    z_last = lax.axis_size(FSDP) - 1
    z_count = z_last + 1
    s_one = jnp.where(z_at == 0, 1, z_at - 1)
    s_three = jnp.where(z_at == z_last, 0, jnp.where(z_at == 1, 2, z_last))
    z_spots = [z_at, s_one, z_at ^ 2, s_three]
    spots = jnp.stack(z_spots + z_spots + [x_at] * 4 + [1 - x_at] * 4).astype(jnp.int32)
    groups = [[KQ, V], [G, O], [W2, W1, W3]]
    slots, across = [[], [], []], [[], [], []]

    def weight(index):
        at, row = next((i, g.index(index)) for i, g in enumerate(groups) if index in g)
        blocks = [(own[index], 0)] + [(array, row) for array in slots[at]]
        blocks += [(sibling[index], 0)] + [(array, row) for array in across[at]]
        return assemble(blocks, spots, by_rows[index], size)

    env = SimpleNamespace()
    firsts = jnp.sum((segments == 0).astype(jnp.int32), axis=1)
    seconds = jnp.sum((segments <= 1).astype(jnp.int32), axis=1)
    starts = jnp.stack([firsts, seconds], axis=1).reshape(-1)
    whole = jnp.concatenate([jnp.stack([x_at, core, y_at]).astype(jnp.int32), starts])
    scalars = (whole, jnp.log(1.0 - forget_half))
    gains = gain_half.reshape(heads, 1, v_width)
    state_type = jax.ShapeDtypeStruct((seq_count, heads, qk_width, v_width), BF16)
    rows_type = jax.ShapeDtypeStruct((4, seq_count, share_len, v_half), BF16)
    kq_type = jax.ShapeDtypeStruct((4, seq_count, share_len, 2 * heads * qk_width), BF16)
    gain_type = jax.ShapeDtypeStruct((seq_count, heads, 1, v_width), F32)

    def shaped(rows_in):
        return rows_in.reshape(4, seq_count, share_len, -1)

    def flat(rows_in):
        return rows_in.reshape(4 * share_rows, -1)

    x_share = tokens.reshape(share_rows, width).astype(F32)
    cot_share = cotangent.reshape(share_rows, width)

    def work_norm():
        h1, ln1_normed, ln1_scale = norm_rows(x_share, ln1_gain)
        env.ln1 = (ln1_normed, ln1_scale)
        env.h = h1.astype(BF16)
        env.hy = over_y(env.h)
        return [env.h]

    def work_core():
        env.hc, env.hcy = over_core(env.h), over_core(env.hy)
        env.cy = over_y(cot_share)
        return []

    def work_rows():
        env.h_one = stack_rows(env.h, env.hy, env.hc, env.hcy)
        return [env.h_one]

    def work_kq():
        env.wkq = weight(KQ)
        env.kq = sum_of_products(nn, [env.h_one], [env.wkq], 0, 4 * share_rows, BF16)
        return [env.kq]

    def work_v():
        env.wv = weight(V)
        env.v = sum_of_products(nn, [env.h_one], [env.wv], 0, 4 * share_rows, BF16)
        return [env.v]

    def work_state():
        (update,) = per_head(
            update_kernel,
            scalars,
            [(shaped(env.kq), ROWS), (shaped(env.v), ROWS)],
            [(state_type, STATES)],
            4 << 30,
        )
        env.state = lax.ppermute(update, CONTEXT, UP_X)
        env.cc, env.ccy = over_core(cot_share), over_core(env.cy)
        return [update]

    def work_gate():
        env.wg = weight(G)
        env.gate = sum_of_products(nn, [env.h_one], [env.wg], 0, 4 * share_rows, BF16)
        return [env.gate]

    def work_retained():
        gated, env.retained = per_head(
            forward_kernel,
            scalars,
            [
                (shaped(env.kq), ROWS),
                (shaped(env.v), ROWS),
                (shaped(env.gate), ROWS),
                (env.state, STATES),
                (gains, GAINS),
            ],
            [(rows_type, ROWS), (rows_type, ROWS)],
        )
        env.gated = flat(gated)
        return [env.gated]

    def work_out_far():
        env.wo = weight(O)
        own, other = sum_of_products(
            nn, [env.gated], [env.wo], 2 * share_rows, 2 * share_rows, BF16, (), 2
        )
        env.far_other, env.far_own = over_core(other), over_core(own)
        return [other]

    def work_out_near():
        near = sum_of_products(
            nn, [env.gated], [env.wo], share_rows, share_rows, BF16, [(env.far_other, 0)]
        )
        env.near = over_y(near)
        return [near]

    def work_out_own():
        extras = [(env.far_own, 0), (tokens.reshape(share_rows, width), 0)]
        env.own = sum_of_products(nn, [env.gated], [env.wo], 0, share_rows, F32, extras)
        return [env.own]

    def work_cot():
        env.cot = stack_rows(cot_share, env.cy, env.cc, env.ccy)
        return [env.cot]

    def work_d_hidden():
        env.w2 = weight(W2)
        env.d_hidden = sum_of_products(nt, [env.cot], [env.w2], 0, 4 * share_rows, BF16)
        return [env.d_hidden]

    def work_middle():
        env.middle = env.own + env.near.astype(F32)
        h2, ln2_normed, ln2_scale = norm_rows(env.middle, ln2_gain)
        env.ln2 = (ln2_normed, ln2_scale)
        env.h2 = h2.astype(BF16)
        env.h2y, env.h2c = over_y(env.h2), over_core(env.h2)
        return [env.h2]

    def work_up():
        env.w1 = weight(W1)
        return [env.w1]

    def work_h2():
        env.w3 = weight(W3)
        env.h2y, env.d_hidden, env.w1, env.w3 = tie(env.h2y, env.d_hidden, env.w1, env.w3)
        env.h2cy = over_core(env.h2y)
        return [env.w3]

    plan = [
        [work_norm],
        [],
        [work_core],
        [work_rows],
        [work_kq],
        [work_v, work_state],
        [work_cot, work_gate],
        [work_retained, work_out_far],
        [work_out_near, work_out_own],
        [work_middle],
        [work_d_hidden, work_up, work_h2],
    ]
    stacks = [jnp.concatenate([own[index] for index in group], axis=0) for group in groups]
    up = down = kept = to_send = None
    for tick, works in enumerate(plan):
        at, hop = divmod(tick, 3)
        moving = at < len(groups)
        sent, to_send = to_send, None
        if sent is not None:
            slots[sent[0]].append(sent[1])
            across[sent[0]].append(over_x(sent[1]))
        if moving and hop < 2:
            up = stacks[at] if hop == 0 else up
            down = stacks[at] if hop == 0 else down
            got = [lax.ppermute(up, FSDP, UP_Z[hop]), lax.ppermute(down, FSDP, DOWN_Z[hop])]
        elif moving:
            got = [lax.ppermute(slots[at][1], FSDP, LAST_Z)]
        held = []
        for work in works:
            held += work()
        if not moving:
            continue
        names = [n for n in ("h_one", "kq", "gate", "gated", "cot") if hasattr(env, n)]
        held = held + ([across[sent[0]][-1]] if sent is not None else [])
        ahead = stacks[at + 1 : at + 2] if hop == 2 else []
        tied = list(tie(*got, *[getattr(env, n) for n in names], *ahead, *held))
        got = [tied.pop(0) for _ in got]
        for n in names:
            setattr(env, n, tied.pop(0))
        if hasattr(env, "far_other"):
            env.far_other = tie(env.far_other, *got)[0]
        if ahead:
            stacks[at + 1] = tied.pop(0)
        if hop == 0:
            up, down = kept = got
            to_send = (at, jnp.where(z_at > 0, up, down))
        elif hop == 1:
            up, down = got
            to_send = (at, jnp.where(z_at >= 2, up, down))
        else:
            ends = (z_at == 0) | (z_at == z_last)
            to_send = (at, jnp.where(ends, got[0], kept[1]))

    h_one, gated, gate_pre = env.h_one, env.gated, env.gate
    wkq, wv, wg, wo, w1, w2, w3 = env.wkq, env.wv, env.wg, env.wo, env.w1, env.w2, env.w3
    cot_full, d_hidden, middle = env.cot, env.d_hidden, env.middle

    token = [h_one]

    def step(run, *args):
        *args, _ = tie(*args, token[0])
        out = run(*args)
        token[0] = out[0] if isinstance(out, (tuple, list)) else out
        return out

    def far_product(product, lefts, rights):
        def run(*arrays):
            return sum_of_products(
                product, arrays, rights, 2 * share_rows, 2 * share_rows, BF16, (), 2
            )

        own, other = step(run, *lefts)
        return over_core(other), over_core(own)

    def whole_product(product, lefts, rights, first, rows, kind, *extras):
        count = len(lefts)

        def run(*arrays):
            added = [(a, row) for a, (_, row) in zip(arrays[count:], extras)]
            return sum_of_products(
                product, arrays[:count], rights, first * share_rows, rows * share_rows, kind, added
            )

        return step(run, *lefts, *(a for a, _ in extras))

    def theirs(left, right):
        return over_x(step(lambda a, b: quarter_product(a, b, 1 - x_at), left, right))

    def ours(left, right, got):
        total = step(lambda a, b, c: quarter_product(a, b, x_at, [c]), left, right, got)
        return lax.psum_scatter(total, FSDP, scatter_dimension=0, tiled=True)

    def chip_rows(left, right):
        total = step(lambda a, b: split_product(a, b, z_count), left, right)
        return lax.psum_scatter(total, FSDP, scatter_dimension=0, tiled=False)

    def begin_finish(*mine):
        mine = step(lambda *a: jnp.concatenate(a, axis=0), *mine)
        return mine, over_x(mine)

    def end_finish(firsts, mine, beside):
        def join(mine, beside):
            blocks, row = [], 0
            for x_summed in firsts:
                count = 1 if x_summed else 2
                one, other = (a[row * size : (row + count) * size] for a in (mine, beside))
                if x_summed:
                    blocks += [jnp.where(x_at == 0, one, other), jnp.where(x_at == 0, other, one)]
                else:
                    blocks.append((one.astype(F32) + other.astype(F32)).astype(BF16))
                row += count
            return jnp.concatenate(blocks, axis=0)

        both = step(join, mine, beside)
        return both, over_core(both)

    def quarters(pair, at):
        both, other = pair
        mine, theirs = (a[2 * at * size : (2 * at + 2) * size] for a in (both, other))
        first, second = jnp.where(core == 0, mine, theirs), jnp.where(core == 0, theirs, mine)
        return [first[:size], first[size:], second[:size], second[size:]]

    def shard(pair, at, rows):
        return jnp.concatenate(quarters(pair, at), axis=1 - int(rows)).astype(F32)

    h_two = stack_rows(env.h2, env.h2y, env.h2c, env.h2cy)
    hidden, d_fca, d_fcb = step(hidden_units, h_two, w1, w3, d_hidden)

    fc_lefts, fc_rights = (d_fca, d_fcb), (w1, w3)
    far_other, far_own = far_product(nt, fc_lefts, fc_rights)
    down_mine = chip_rows(hidden, cot_full)
    near = over_y(whole_product(nt, fc_lefts, fc_rights, 1, 1, BF16, (far_other, 0)))
    gate_got = theirs(h_two, d_fca)
    own_part = whole_product(nt, fc_lefts, fc_rights, 0, 1, F32, (far_own, 0))
    up_got = theirs(h_two, d_fcb)
    out_far_other, out_far_own = far_product(nn, [hidden], [w2])

    def middle_back(own_part, near):
        d_h2 = own_part + near.astype(F32)
        ln2_normed, ln2_scale = env.ln2
        d_middle = cot_share.astype(F32) + norm_back(d_h2, ln2_normed, ln2_scale, ln2_gain)
        return d_middle.astype(BF16), d_middle, jnp.sum(d_h2 * ln2_normed, axis=0)

    d_mid_low, d_middle, g_ln2 = step(middle_back, own_part, near)
    d_mid_y, d_mid_c = over_y(d_mid_low), over_core(d_mid_low)
    fc_gate_mine = ours(h_two, d_fca, gate_got)
    out_near = whole_product(nn, [hidden], [w2], 1, 1, BF16, (out_far_other, 0))
    out_own = whole_product(nn, [hidden], [w2], 0, 1, F32, (out_far_own, 0), (middle, 0))
    d_mid_y, out_near, up_got = step(lambda *a: a, d_mid_y, out_near, up_got)
    d_mid_cy = over_core(d_mid_y)
    out_near = over_y(out_near)
    fc_up_mine = ours(h_two, d_fcb, up_got)

    def gate_back(share, y, c, cy):
        d_branch = stack_rows(share, y, c, cy)
        return sum_of_products(nt, [d_branch], [wo], 0, 4 * share_rows, BF16), d_branch

    d_gated, d_branch = step(gate_back, d_mid_low, d_mid_y, d_mid_c, d_mid_cy)
    kq, values, state_in = shaped(env.kq), shaped(env.v), env.state

    def retained_back(d_gated, kq):
        return per_head(
            norm_back_kernel,
            scalars,
            [
                (shaped(d_gated), ROWS),
                (shaped(gate_pre), ROWS),
                (env.retained, ROWS),
                (kq, ROWS),
                (gains, GAINS),
            ],
            [(rows_type, ROWS), (rows_type, ROWS), (gain_type, STATES), (state_type, STATES)],
        )

    d_gate, d_retained, g_norm, leaving = step(retained_back, d_gated, kq)
    d_gate = flat(d_gate)
    g_norm = jnp.sum(g_norm, axis=0).reshape(v_half)
    state_grad = lax.ppermute(leaving, CONTEXT, DOWN_X)
    out_mine = chip_rows(gated, d_branch)
    gg_theirs = step(lambda a, b: quarter_product(a, b, 1 - x_at), h_one, d_gate)
    state_grad, gg_theirs = tie(state_grad, gg_theirs)
    gg_got = over_x(gg_theirs)

    def pair_back(d_retained, state_grad):
        return per_head(
            backward_kernel,
            scalars,
            [
                (kq, ROWS),
                (values, ROWS),
                (d_retained, ROWS),
                (state_in, STATES),
                (state_grad, STATES),
            ],
            [(kq_type, ROWS), (rows_type, ROWS)],
        )

    fc_gate_mine, down_mine, state_grad = tie(fc_gate_mine, down_mine, state_grad)
    dkq_low, dv_low = step(pair_back, d_retained, state_grad)
    dkq_low, dv_low = flat(dkq_low), flat(dv_low)
    v_got = theirs(h_one, dv_low)
    kq_got = theirs(h_one, dkq_low)
    h1_lefts, h1_rights = (dkq_low, dv_low, d_gate), (wkq, wv, wg)
    output = step(lambda a, b: (a + b.astype(F32)).astype(BF16), out_own, out_near)
    fc_up_mine, gg_got = tie(fc_up_mine, gg_got)
    gg_mine = ours(h_one, d_gate, gg_got)
    far_other, far_own = far_product(nt, h1_lefts, h1_rights)
    v_mine = ours(h_one, dv_low, v_got)
    near = over_y(whole_product(nt, h1_lefts, h1_rights, 1, 1, BF16, (far_other, 0)))
    own_part = whole_product(nt, h1_lefts, h1_rights, 0, 1, F32, (far_own, 0))
    fc_begun = begin_finish(fc_gate_mine, fc_up_mine)
    out_mine, kq_got = tie(out_mine, kq_got)
    kq_mine = ours(h_one, dkq_low, kq_got)
    down_begun = begin_finish(down_mine)

    def tokens_back(own_part, near):
        d_h1 = own_part + near.astype(F32)
        ln1_normed, ln1_scale = env.ln1
        grad = d_middle + norm_back(d_h1, ln1_normed, ln1_scale, ln1_gain)
        return grad, jnp.sum(d_h1 * ln1_normed, axis=0)

    grad_tokens, g_ln1 = step(tokens_back, own_part, near)
    g_fc = end_finish([True, True], *fc_begun)
    g_down = end_finish([False], *down_begun)
    out_begun = begin_finish(out_mine, gg_mine)
    v_begun = begin_finish(v_mine)
    kq_begun = begin_finish(kq_mine)
    g_out_gate = end_finish([False, True], *out_begun)
    g_value = end_finish([True], *v_begun)
    g_kq = end_finish([True], *kq_begun)
    sides = quarters(g_kq, 0)
    g_key = jnp.concatenate([side[:, :qk_width] for side in sides], axis=1).astype(F32)
    g_query = jnp.concatenate([side[:, qk_width:] for side in sides], axis=1).astype(F32)

    norm_size = lax.axis_size(TENSOR) * norm_gain.shape[0]
    norm_all = lax.dynamic_update_slice_in_dim(
        jnp.zeros((norm_size,), F32), g_norm, (2 * y_at + core) * v_half, 0
    )
    gain_sums = jnp.concatenate([g_ln1, g_ln2, norm_all])
    for axis in (TENSOR, CONTEXT, FSDP):
        gain_sums = butterfly(gain_sums, axis)
    g_ln1, g_ln2 = gain_sums[:width], gain_sums[width : 2 * width]
    g_norm = lax.dynamic_slice_in_dim(
        gain_sums, 2 * width + y_at * norm_gain.shape[0], norm_gain.shape[0]
    )
    return (
        output.reshape(tokens.shape),
        grad_tokens.reshape(tokens.shape),
        g_ln1,
        g_query,
        g_key,
        shard(g_value, 0, False),
        shard(g_out_gate, 1, False),
        g_norm,
        shard(g_out_gate, 0, True),
        g_ln2,
        shard(g_fc, 0, False),
        shard(g_fc, 1, False),
        shard(g_down, 0, True),
    )


def body(tensor_size, *arrays):
    heads_here = arrays[2].shape[0]
    paired = tensor_size == 2 and heads_here % 2 == 0 and lax.axis_size(CONTEXT) == 4
    paired = paired and lax.axis_size(FSDP) == 4
    return (paired_body if paired else general_body)(*arrays)


def solution(mesh):
    in_specs = (
        P(FSDP, (CONTEXT, TENSOR), None),
        P(FSDP, None),
        P(TENSOR),
        P(),
        P(FSDP, TENSOR),
        P(FSDP, TENSOR),
        P(FSDP, TENSOR),
        P(FSDP, TENSOR),
        P(TENSOR),
        P(TENSOR, FSDP),
        P(),
        P(FSDP, TENSOR),
        P(FSDP, TENSOR),
        P(TENSOR, FSDP),
        P(FSDP, (CONTEXT, TENSOR), None),
    )
    out_specs = (
        P(FSDP, (CONTEXT, TENSOR), None),
        P(FSDP, (CONTEXT, TENSOR), None),
        P(),
        P(FSDP, TENSOR),
        P(FSDP, TENSOR),
        P(FSDP, TENSOR),
        P(FSDP, TENSOR),
        P(TENSOR),
        P(TENSOR, FSDP),
        P(),
        P(FSDP, TENSOR),
        P(FSDP, TENSOR),
        P(TENSOR, FSDP),
    )
    return jax.shard_map(partial(body, mesh.shape[TENSOR]), mesh=mesh, in_specs=in_specs, out_specs=out_specs, check_vma=False)
```

```python
from functools import partial
from types import SimpleNamespace

import jax
import jax.numpy as jnp
from jax import lax
from jax.experimental import pallas as pl
from jax.experimental.pallas import tpu as pltpu
from jax.sharding import PartitionSpec as P

FSDP, CONTEXT, TENSOR = "fsdp", "context", "tensor"

careful = partial(jnp.einsum, precision=lax.Precision.HIGH)


def entering(part, axis, combine, identity):
    place = lax.axis_index(axis)
    gathered = jax.tree.map(lambda a: lax.all_gather(a, axis), part)
    state = jax.tree.map(lambda a, e: jnp.zeros_like(a) + jnp.asarray(e, a.dtype), part, identity)

    def one(step, state):
        return combine(
            state, jax.tree.map(lambda a: lax.dynamic_index_in_dim(a, step, 0, False), gathered)
        )

    return lax.fori_loop(0, place, one, state)


def carried_in(value, axis, combine, identity):
    count, place = (lax.axis_size(axis), lax.axis_index(axis))
    everything = jax.tree.map(
        lambda part, kind: lax.all_gather(part.astype(kind), axis),
        value,
        jax.tree.map(lambda a: jnp.bfloat16 if a.dtype == jnp.float32 else a.dtype, value),
    )
    start = jax.tree.map(
        lambda part, zero: jnp.broadcast_to(jnp.asarray(zero, part.dtype), part.shape),
        value,
        identity,
    )

    def step(k, before):
        at = count - 1 - k
        reached = at > place
        new = combine(
            before, jax.tree.map(lambda part, own: part[at].astype(own.dtype), everything, value)
        )
        return jax.tree.map(lambda a, b: jnp.where(reached, a, b), new, before)

    return lax.fori_loop(0, count, step, start)


def norm_rows(values, gain_vec, epsilon=1e-05):
    centred = values - jnp.mean(values, axis=-1, keepdims=True)
    scale = lax.rsqrt(jnp.mean(centred * centred, axis=-1, keepdims=True) + epsilon)
    normed = centred * scale
    return (normed * gain_vec, normed, scale)


def norm_back(grad_in, normed, scale, gain_vec):
    d_normed = grad_in * gain_vec
    first_mean = jnp.mean(d_normed, axis=-1, keepdims=True)
    second_mean = jnp.mean(d_normed * normed, axis=-1, keepdims=True)
    return scale * (d_normed - first_mean - normed * second_mean)


def swish_slope(values):
    sigma = jax.nn.sigmoid(values)
    return sigma * (1.0 + values * (1.0 - sigma))


def compose(earlier, latter):
    return (earlier[0] * latter[0], latter[0][:, :, None, None] * earlier[1] + latter[1])


def share_gather(piece):
    return lax.all_gather(piece, TENSOR, axis=1, tiled=True)


def branch_sum(terms):
    return lax.psum_scatter(terms, TENSOR, scatter_dimension=1, tiled=True)


def input_sum(terms):
    return lax.psum_scatter(
        terms.astype(jnp.bfloat16), TENSOR, scatter_dimension=1, tiled=True
    ).astype(jnp.float32)


def mixer_fetch(w_query, w_key, w_value, w_gate, w_out):
    return (
        lax.all_gather(w_query, FSDP, axis=0, tiled=True),
        lax.all_gather(w_key, FSDP, axis=0, tiled=True),
        lax.all_gather(w_value, FSDP, axis=0, tiled=True),
        lax.all_gather(w_gate, FSDP, axis=0, tiled=True),
        lax.all_gather(w_out, FSDP, axis=1, tiled=True),
    )


def mlp_fetch(w_fc_gate, w_fc_up, w_fc_down):
    return (
        lax.all_gather(w_fc_gate, FSDP, axis=0, tiled=True),
        lax.all_gather(w_fc_up, FSDP, axis=0, tiled=True),
        lax.all_gather(w_fc_down, FSDP, axis=1, tiled=True),
    )


def product(form, left, right):
    return jnp.einsum(form, left, right, preferred_element_type=jnp.float32)


def general_body(
    tokens,
    segments,
    forget,
    ln1_gain,
    w_query,
    w_key,
    w_value,
    w_gate,
    norm_gain,
    w_out,
    ln2_gain,
    w_fc_gate,
    w_fc_up,
    w_fc_down,
    cotangent,
):
    heads_here = forget.shape[0]
    qk_width = w_query.shape[1] // heads_here
    v_width = w_value.shape[1] // heads_here
    v_local = heads_here * v_width
    gain_heads = norm_gain.reshape(heads_here, v_width)
    x_share = tokens.astype(jnp.float32)
    h1_share, ln1_normed, ln1_scale = norm_rows(x_share, ln1_gain)
    h_one = share_gather(h1_share.astype(jnp.bfloat16))
    wq_all, wk_all, wv_all, wg_all, wo_all = mixer_fetch(w_query, w_key, w_value, w_gate, w_out)
    seq_count, stretch_len = (h_one.shape[0], h_one.shape[1])
    query = product("btd,dq->btq", h_one, wq_all).astype(jnp.bfloat16)
    keys = product("btd,dq->btq", h_one, wk_all).astype(jnp.bfloat16)
    values = product("btd,dv->btv", h_one, wv_all).astype(jnp.bfloat16)
    gate_pre = product("btd,dv->btv", h_one, wg_all)
    query_heads = query.reshape(seq_count, stretch_len, heads_here, qk_width)
    keys_heads = keys.reshape(seq_count, stretch_len, heads_here, qk_width)
    query_full = query_heads.astype(jnp.float32) * 0.0625
    keys_full = keys_heads.astype(jnp.float32)
    values_full = values.astype(jnp.float32).reshape(seq_count, stretch_len, heads_here, v_width)
    log_keep = jnp.log(1.0 - forget)
    ctx_place = lax.axis_index(CONTEXT)
    seg_stretch = lax.dynamic_slice_in_dim(segments, ctx_place * stretch_len, stretch_len, 1)
    seg_prev = lax.dynamic_slice_in_dim(segments, jnp.maximum(ctx_place * stretch_len - 1, 0), 1, 1)
    live_mask = (seg_stretch == seg_prev).astype(jnp.float32)
    steps_idx = jnp.arange(stretch_len, dtype=jnp.float32)
    step_gap = jnp.maximum(steps_idx[:, None] - steps_idx[None, :], 0.0)
    causal = steps_idx[:, None] >= steps_idx[None, :]
    same_doc = (seg_stretch[:, :, None] == seg_stretch[:, None, :]) & causal[None]
    weights_mask = jnp.where(
        same_doc[:, None], jnp.exp(step_gap[None] * log_keep[:, None, None])[None], 0.0
    )
    inflow = live_mask[:, :, None] * jnp.exp((steps_idx[:, None] + 1.0) * log_keep[None, :])[None]
    outflow = (seg_stretch == seg_stretch[:, -1:]).astype(jnp.float32)[:, :, None] * jnp.exp(
        (stretch_len - 1.0 - steps_idx)[:, None] * log_keep[None, :]
    )[None]
    carry_decay = live_mask[:, -1:] * jnp.exp(stretch_len * log_keep)[None, :]
    update = careful("bshd,bsh,bshe->bhde", keys_full, outflow, values_full)
    identity = (jnp.ones_like(carry_decay), jnp.zeros_like(update))
    state_in = entering((carry_decay, update), CONTEXT, compose, identity)[1]
    scores = product("bthd,bshd->bhts", query_heads, keys_heads) * 0.0625 * weights_mask
    retained = careful("bhts,bshe->bthe", scores, values_full)
    retained = retained + inflow[..., None] * careful("bthd,bhde->bthe", query_full, state_in)
    normed_out, gn_normed, gn_scale = norm_rows(retained, gain_heads, 0.01)
    norm_flat = normed_out.reshape(seq_count, stretch_len, v_local)
    gate_act = jax.nn.silu(gate_pre)
    gated = (gate_act * norm_flat).astype(jnp.bfloat16)
    middle = x_share + branch_sum(product("btv,vd->btd", gated, wo_all))
    h2_share, ln2_normed, ln2_scale = norm_rows(middle, ln2_gain)
    h_two = share_gather(h2_share.astype(jnp.bfloat16))
    w1_all, w3_all, w2_all = mlp_fetch(w_fc_gate, w_fc_up, w_fc_down)
    fc_a = product("btd,df->btf", h_two, w1_all)
    fc_b = product("btd,df->btf", h_two, w3_all)
    silu_a = jax.nn.silu(fc_a)
    hidden = (silu_a * fc_b).astype(jnp.bfloat16)
    output = (middle + branch_sum(product("btf,fd->btd", hidden, w2_all))).astype(jnp.bfloat16)
    wq_all, wk_all, wv_all, wg_all, wo_all = mixer_fetch(w_query, w_key, w_value, w_gate, w_out)
    w1_all, w3_all, w2_all = mlp_fetch(w_fc_gate, w_fc_up, w_fc_down)
    cot_full = share_gather(cotangent)
    d_hidden = product("btd,fd->btf", cot_full, w2_all)
    g_down = product("btf,btd->fd", hidden, cot_full)
    d_fca = (d_hidden * fc_b * swish_slope(fc_a)).astype(jnp.bfloat16)
    d_fcb = (d_hidden * silu_a).astype(jnp.bfloat16)
    g_fc_gate = product("btd,btf->df", h_two, d_fca)
    g_fc_up = product("btd,btf->df", h_two, d_fcb)
    d_h2 = input_sum(product("btf,df->btd", d_fca, w1_all) + product("btf,df->btd", d_fcb, w3_all))
    d_middle = cotangent.astype(jnp.float32) + norm_back(d_h2, ln2_normed, ln2_scale, ln2_gain)
    g_ln2 = jnp.sum(d_h2 * ln2_normed, axis=(0, 1))
    d_branch = share_gather(d_middle.astype(jnp.bfloat16))
    d_gated = product("btd,vd->btv", d_branch, wo_all)
    g_out = product("btv,btd->vd", gated, d_branch)
    d_gate = (d_gated * norm_flat * swish_slope(gate_pre)).astype(jnp.bfloat16)
    d_normed = (d_gated * gate_act).reshape(seq_count, stretch_len, heads_here, v_width)
    g_norm = jnp.sum(d_normed * gn_normed, axis=(0, 1)).reshape(v_local)
    d_retained = norm_back(d_normed, gn_normed, gn_scale, gain_heads)
    d_scores = careful("bthe,bshe->bhts", d_retained, values_full) * weights_mask
    d_values = careful("bhts,bthe->bshe", scores, d_retained)
    d_query = careful("bhts,bshd->bthd", d_scores, keys_full)
    d_query = d_query + inflow[..., None] * careful("bthe,bhde->bthd", d_retained, state_in)
    d_keys = careful("bhts,bthd->bshd", d_scores, query_full)
    leaving = careful("bthd,bth,bthe->bhde", query_full, inflow, d_retained)
    state_grad = carried_in((carry_decay, leaving), CONTEXT, compose, identity)[1]
    d_keys = d_keys + outflow[..., None] * careful("bshe,bhde->bshd", values_full, state_grad)
    d_values = d_values + outflow[..., None] * careful("bshd,bhde->bshe", keys_full, state_grad)
    dq_low = (
        (d_query * 0.0625)
        .reshape(seq_count, stretch_len, heads_here * qk_width)
        .astype(jnp.bfloat16)
    )
    dk_low = d_keys.reshape(seq_count, stretch_len, heads_here * qk_width).astype(jnp.bfloat16)
    dv_low = d_values.reshape(seq_count, stretch_len, v_local).astype(jnp.bfloat16)
    g_query = product("btd,btq->dq", h_one, dq_low)
    g_key = product("btd,btq->dq", h_one, dk_low)
    g_value = product("btd,btv->dv", h_one, dv_low)
    g_gate = product("btd,btv->dv", h_one, d_gate)
    d_h1 = product("btq,dq->btd", dq_low, wq_all) + product("btq,dq->btd", dk_low, wk_all)
    d_h1 = d_h1 + product("btv,dv->btd", dv_low, wv_all) + product("btv,dv->btd", d_gate, wg_all)
    d_h1 = input_sum(d_h1)
    grad_tokens = d_middle + norm_back(d_h1, ln1_normed, ln1_scale, ln1_gain)
    g_ln1 = jnp.sum(d_h1 * ln1_normed, axis=(0, 1))
    tensor_place = lax.axis_index(TENSOR)
    norm_full = lax.dynamic_update_slice(
        jnp.zeros((v_local * lax.axis_size(TENSOR),), jnp.float32),
        g_norm,
        (tensor_place * v_local,),
    )
    g_ln1, g_ln2, norm_full = lax.psum((g_ln1, g_ln2, norm_full), (FSDP, CONTEXT, TENSOR))
    g_norm = lax.dynamic_slice_in_dim(norm_full, tensor_place * v_local, v_local)
    weight_grads = (g_query, g_key, g_value, g_gate, g_out, g_fc_gate, g_fc_up, g_down)
    summed = (
        lax.psum(weight_grads[0].astype(jnp.bfloat16), CONTEXT).astype(jnp.float32),
        lax.psum(weight_grads[1].astype(jnp.bfloat16), CONTEXT).astype(jnp.float32),
        lax.psum(weight_grads[2].astype(jnp.bfloat16), CONTEXT).astype(jnp.float32),
        lax.psum(weight_grads[3].astype(jnp.bfloat16), CONTEXT).astype(jnp.float32),
        lax.psum(weight_grads[4].astype(jnp.bfloat16), CONTEXT).astype(jnp.float32),
        lax.psum(weight_grads[5].astype(jnp.bfloat16), CONTEXT).astype(jnp.float32),
        lax.psum(weight_grads[6].astype(jnp.bfloat16), CONTEXT).astype(jnp.float32),
        lax.psum(weight_grads[7].astype(jnp.bfloat16), CONTEXT).astype(jnp.float32),
    )
    shards = (
        lax.psum_scatter(
            summed[0].astype(jnp.bfloat16), FSDP, scatter_dimension=0, tiled=True
        ).astype(jnp.float32),
        lax.psum_scatter(
            summed[1].astype(jnp.bfloat16), FSDP, scatter_dimension=0, tiled=True
        ).astype(jnp.float32),
        lax.psum_scatter(
            summed[2].astype(jnp.bfloat16), FSDP, scatter_dimension=0, tiled=True
        ).astype(jnp.float32),
        lax.psum_scatter(
            summed[3].astype(jnp.bfloat16), FSDP, scatter_dimension=0, tiled=True
        ).astype(jnp.float32),
        lax.psum_scatter(
            summed[4].astype(jnp.bfloat16), FSDP, scatter_dimension=1, tiled=True
        ).astype(jnp.float32),
        lax.psum_scatter(
            summed[5].astype(jnp.bfloat16), FSDP, scatter_dimension=0, tiled=True
        ).astype(jnp.float32),
        lax.psum_scatter(
            summed[6].astype(jnp.bfloat16), FSDP, scatter_dimension=0, tiled=True
        ).astype(jnp.float32),
        lax.psum_scatter(
            summed[7].astype(jnp.bfloat16), FSDP, scatter_dimension=1, tiled=True
        ).astype(jnp.float32),
    )
    return (
        output,
        grad_tokens,
        g_ln1,
        shards[0],
        shards[1],
        shards[2],
        shards[3],
        g_norm,
        shards[4],
        g_ln2,
        shards[5],
        shards[6],
        shards[7],
    )


F32 = jnp.float32
BF16 = jnp.bfloat16
BOTH_X = [(0, 2), (2, 0), (1, 3), (3, 1)]
UP_X = [(0, 2), (1, 3)]
DOWN_X = [(2, 0), (3, 1)]
CORES = [(0, 1), (1, 0), (2, 3), (3, 2)]
UP_Z = [[(0, 1), (1, 2), (2, 3)], [(1, 2), (2, 3)]]
DOWN_Z = [[(3, 2), (2, 1), (1, 0)], [(2, 1), (1, 0)]]
LAST_Z = [(2, 3), (1, 0)]
SCALE = 0.0625
ROWS, GAINS, STATES = range(3)


def cost(flops):
    return pl.CostEstimate(flops=3 * flops // 5, transcendentals=0, bytes_accessed=0)


COPYING = 2 << 30
DOWN_Z = [[(3, 2), (2, 1), (1, 0)], [(2, 1), (1, 0)], [(1, 0)]]


def over_x(value):
    return lax.ppermute(value, CONTEXT, BOTH_X)


def over_core(value):
    return lax.ppermute(value, CONTEXT, CORES)


def over_y(value):
    return lax.ppermute(value, TENSOR, [(0, 1), (1, 0)])


def tie(*values):
    return lax.optimization_barrier(values)


def butterfly(value, axis):
    size = lax.axis_size(axis)
    step = 1
    while step < size:
        value = value + lax.ppermute(value, axis, [(i, i ^ step) for i in range(size)])
        step *= 2
    return value


def quarter_of(weight, dim, index):
    size = weight.shape[dim] // 4
    return lax.dynamic_slice_in_dim(weight, index * size, size, dim)


def assemble_kernel(spot_ref, *refs):
    at = pl.program_id(0)
    for index, block in enumerate(refs[:8]):

        @pl.when(at == index)
        def _(block=block):
            refs[8][...] = block[...]


def assemble(blocks, spots, by_rows, size):
    shape = (2 * size, 4 * size) if by_rows else (4 * size, 2 * size)

    def spot(at, spots_ref):
        z_from, x_from = spots_ref[at], spots_ref[8 + at]
        return (x_from, z_from) if by_rows else (z_from, x_from)

    return pl.pallas_call(
        assemble_kernel,
        out_shape=jax.ShapeDtypeStruct(shape, BF16),
        grid_spec=pltpu.PrefetchScalarGridSpec(
            num_scalar_prefetch=1,
            grid=(8,),
            in_specs=[
                pl.BlockSpec((size, size), lambda at, spots_ref, row=row: (row, 0))
                for _, row in blocks
            ],
            out_specs=pl.BlockSpec((size, size), spot),
        ),
        compiler_params=pltpu.CompilerParams(vmem_limit_bytes=32 << 20),
        cost_estimate=cost(COPYING),
    )(spots, *(array for array, _ in blocks))


def sum_kernel(product, count, outs, *refs):
    lefts, rights, extras = refs[:count], refs[count : 2 * count], refs[2 * count : -outs]
    total = product(lefts[0][...], rights[0][...])
    for left, right in zip(lefts[1:], rights[1:]):
        total = total + product(left[...], right[...])
    for extra in extras:
        total = total + extra[...].astype(F32)
    size = total.shape[0] // outs
    for index, out_ref in enumerate(refs[-outs:]):
        out_ref[...] = total[index * size : (index + 1) * size].astype(out_ref.dtype)


def sum_of_products(product, lefts, rights, first, rows, kind, extras=(), outs=1):
    by_columns = product is nn
    width = rights[0].shape[1 if by_columns else 0]
    block, tile = min(1024, rows), min(512, width)
    if outs > 1:
        block = rows

    def right_spec(right):
        if by_columns:
            return pl.BlockSpec((right.shape[0], tile), lambda n, m: (0, n))
        return pl.BlockSpec((tile, right.shape[1]), lambda n, m: (n, 0))

    def tile_spec(from_row, size):
        return pl.BlockSpec((size, tile), lambda n, m: (from_row // size + m, n))

    out_shape = [jax.ShapeDtypeStruct((rows // outs, width), kind)] * outs
    result = pl.pallas_call(
        partial(sum_kernel, product, len(lefts), outs),
        grid=(width // tile, rows // block),
        out_shape=out_shape,
        in_specs=[
            pl.BlockSpec((block, left.shape[1]), lambda n, m: (first // block + m, 0))
            for left in lefts
        ]
        + [right_spec(right) for right in rights]
        + [tile_spec(from_row, block) for _, from_row in extras],
        out_specs=[tile_spec(0, block // outs)] * outs,
        compiler_params=pltpu.CompilerParams(vmem_limit_bytes=60 << 20),
        cost_estimate=cost(2 * rows * width * sum(left.shape[1] for left in lefts)),
    )(*lefts, *rights, *(array for array, _ in extras))
    return result[0] if outs == 1 else result


def quarter_kernel(spots_ref, left, right, *rest):
    total = tn(left[...], right[...])
    for extra in rest[:-1]:
        total = total + extra[...].astype(F32)
    rest[-1][...] = total.astype(BF16)


def quarter_product(left, right, index, extras=()):
    tokens, width = left.shape
    size, block = right.shape[1] // 2, min(1024, width)
    return pl.pallas_call(
        quarter_kernel,
        out_shape=jax.ShapeDtypeStruct((width, size), BF16),
        grid_spec=pltpu.PrefetchScalarGridSpec(
            num_scalar_prefetch=1,
            grid=(width // block,),
            in_specs=[
                pl.BlockSpec((tokens, block), lambda m, at: (0, m)),
                pl.BlockSpec((tokens, size), lambda m, at: (0, at[0])),
            ]
            + [pl.BlockSpec((block, size), lambda m, at: (m, 0)) for _ in extras],
            out_specs=pl.BlockSpec((block, size), lambda m, at: (m, 0)),
        ),
        compiler_params=pltpu.CompilerParams(vmem_limit_bytes=60 << 20),
        cost_estimate=cost(2 * tokens * width * size),
    )(index.reshape(1).astype(jnp.int32), left, right, *extras)


def split_kernel(left, right, out):
    out[0] = tn(left[...], right[...]).astype(BF16)


def split_product(left, right, count):
    tokens, rows = left.shape
    size = right.shape[1] // count
    return pl.pallas_call(
        split_kernel,
        grid=(count,),
        out_shape=jax.ShapeDtypeStruct((count, rows, size), BF16),
        in_specs=[
            pl.BlockSpec((tokens, rows), lambda n: (0, 0)),
            pl.BlockSpec((tokens, size), lambda n: (0, n)),
        ],
        out_specs=pl.BlockSpec((1, rows, size), lambda n: (n, 0, 0)),
        compiler_params=pltpu.CompilerParams(vmem_limit_bytes=60 << 20),
        cost_estimate=cost(2 * tokens * rows * size * count),
    )(left, right)


def unit_kernel(h_ref, w1_ref, w3_ref, d_hidden_ref, hidden_ref, d_a_ref, d_b_ref):
    fc_a, fc_b = nn(h_ref[...], w1_ref[...]), nn(h_ref[...], w3_ref[...])
    d_hidden = d_hidden_ref[...].astype(F32)
    sigma = jax.nn.sigmoid(fc_a)
    silu_a = fc_a * sigma
    hidden_ref[...] = (silu_a * fc_b).astype(BF16)
    d_a_ref[...] = (d_hidden * fc_b * (sigma * (1.0 + fc_a * (1.0 - sigma)))).astype(BF16)
    d_b_ref[...] = (d_hidden * silu_a).astype(BF16)


def hidden_units(h_two, w1, w3, d_hidden):
    rows, width = h_two.shape
    count = w1.shape[1]
    block, tile = min(512, rows), min(512, count)
    weight = pl.BlockSpec((width, tile), lambda n, m: (0, n))
    spot = pl.BlockSpec((block, tile), lambda n, m: (m, n))
    return pl.pallas_call(
        unit_kernel,
        grid=(count // tile, rows // block),
        out_shape=[jax.ShapeDtypeStruct((rows, count), BF16)] * 3,
        in_specs=[pl.BlockSpec((block, width), lambda n, m: (m, 0)), weight, weight, spot],
        out_specs=[spot] * 3,
        compiler_params=pltpu.CompilerParams(vmem_limit_bytes=60 << 20),
        cost_estimate=cost(4 * rows * width * count),
    )(h_two, w1, w3, d_hidden)


def stack_kernel(*refs):
    count = len(refs) - 4
    shares, out_ref, held, sems_in, sems_out = refs[:count], *refs[count:]
    rows = shares[0].shape[0]
    ins, outs = [], []
    for index, share in enumerate(shares):
        ins.append(pltpu.make_async_copy(share, held.at[index], sems_in.at[index]))
        spot = out_ref.at[pl.ds(index * rows, rows)]
        outs.append(pltpu.make_async_copy(held.at[index], spot, sems_out.at[index]))
    for copy in ins:
        copy.start()
    for copy, onward in zip(ins, outs):
        copy.wait()
        onward.start()
    for onward in outs:
        onward.wait()


def stack_rows(*shares):
    rows, width = shares[0].shape
    count = len(shares)
    return pl.pallas_call(
        stack_kernel,
        out_shape=jax.ShapeDtypeStruct((count * rows, width), shares[0].dtype),
        in_specs=[pl.BlockSpec(memory_space=pl.ANY)] * count,
        out_specs=pl.BlockSpec(memory_space=pl.ANY),
        scratch_shapes=[
            pltpu.VMEM((count, rows, width), shares[0].dtype),
            pltpu.SemaphoreType.DMA((count,)),
            pltpu.SemaphoreType.DMA((count,)),
        ],
        compiler_params=pltpu.CompilerParams(vmem_limit_bytes=48 << 20),
        cost_estimate=cost(2 * COPYING),
    )(*shares)


def nn(left, right):
    return lax.dot_general(left, right, (((1,), (0,)), ((), ())), preferred_element_type=F32)


def nt(left, right):
    return lax.dot_general(left, right, (((1,), (1,)), ((), ())), preferred_element_type=F32)


def tn(left, right):
    return lax.dot_general(left, right, (((0,), (0,)), ((), ())), preferred_element_type=F32)


def where_is(whole, chunk, piece_len):
    share_len = piece_len // 2
    spots = []
    for shape, dim in (((piece_len, 1), 0), ((1, piece_len), 1)):
        at = lax.broadcasted_iota(jnp.int32, shape, dim) + whole[2] * share_len
        spots.append(jnp.where(at >= piece_len, at - piece_len, at))
    start = whole[0] * (2 * piece_len) + chunk * piece_len
    return spots[0], spots[1], start


def document(whole, spot):
    seq = pl.program_id(0)
    first, second = whole[3 + 2 * seq], whole[4 + 2 * seq]
    return jnp.where(spot >= second, 2, jnp.where(spot >= first, 1, 0))


def fade(gap, log_keep):
    return jnp.exp(jnp.maximum(gap, 0).astype(F32) * log_keep)


def piece_terms(whole, log_keep, chunk, piece_len):
    rows, cols, start = where_is(whole, chunk, piece_len)
    doc_rows, doc_cols = document(whole, start + rows), document(whole, start + cols)
    before, last = document(whole, start - 1), document(whole, start + piece_len - 1)
    within = jnp.where(
        (rows >= cols) & (doc_rows == doc_cols), fade(rows - cols, log_keep) * SCALE, 0.0
    )
    inflow = jnp.where(doc_rows == before, fade(rows + 1, log_keep) * SCALE, 0.0)
    outflow = jnp.where(doc_rows == last, fade(piece_len - 1 - rows, log_keep), 0.0)
    whole_gap = jnp.full((1, 1), piece_len, jnp.int32)
    over = jnp.where(before == last, fade(whole_gap, log_keep), 0.0)
    return within, inflow, outflow, over


def piece_of(ref, whole, chunk):
    group = lax.rem(chunk + whole[1], 2) * 2
    value = ref[pl.ds(group, 2), 0]
    return value.reshape(value.shape[0] * value.shape[1], value.shape[2])


def put_piece(ref, whole, chunk, value):
    group = lax.rem(chunk + whole[1], 2) * 2
    ref[pl.ds(group, 2), 0] = value.astype(ref.dtype).reshape(2, value.shape[0] // 2, value.shape[1])


def split_kq(ref, whole, chunk):
    both = piece_of(ref, whole, chunk)
    width = both.shape[1] // 2
    return both[:, :width], both[:, width:]


def update_kernel(whole, keeps, kq_ref, v_ref, out_ref):
    log_keep = keeps[pl.program_id(1)]
    piece_len = 2 * kq_ref.shape[2]
    total = jnp.zeros(out_ref.shape[2:], F32)
    for chunk in range(2):
        rows, _, start = where_is(whole, chunk, piece_len)
        last = document(whole, whole[0] * (2 * piece_len) + 2 * piece_len - 1)
        gap = (2 - chunk) * piece_len - 1 - rows
        weight = jnp.where(document(whole, start + rows) == last, fade(gap, log_keep), 0.0)
        keys, _ = split_kq(kq_ref, whole, chunk)
        values = piece_of(v_ref, whole, chunk)
        total = total + tn((keys.astype(F32) * weight).astype(BF16), values)
    out_ref[0, 0] = total.astype(BF16)


def next_state(state, keys, values, outflow, over):
    return over * state + tn((keys.astype(F32) * outflow).astype(BF16), values)


def forward_kernel(
    whole, keeps, kq_ref, v_ref, gate_ref, state_ref, gain_ref, gated_ref, retained_ref
):
    log_keep = keeps[pl.program_id(1)]
    piece_len = 2 * kq_ref.shape[2]
    state = state_ref[0, 0].astype(F32)
    for chunk in range(2):
        within, inflow, outflow, over = piece_terms(whole, log_keep, chunk, piece_len)
        keys, query = split_kq(kq_ref, whole, chunk)
        values = piece_of(v_ref, whole, chunk)
        scores = (nt(query, keys) * within).astype(BF16)
        retained = nn(scores, values) + inflow * nn(query, state.astype(BF16))
        if chunk == 0:
            state = next_state(state, keys, values, outflow, over)
        put_piece(retained_ref, whole, chunk, retained)
        normed, _, _ = norm_rows(retained, gain_ref[0], 0.01)
        gate = piece_of(gate_ref, whole, chunk).astype(F32)
        put_piece(gated_ref, whole, chunk, gate * jax.nn.sigmoid(gate) * normed)


def norm_back_kernel(
    whole,
    keeps,
    d_gated_ref,
    gate_ref,
    retained_ref,
    kq_ref,
    gain_ref,
    d_gate_ref,
    d_retained_ref,
    d_gain_ref,
    leaving_ref,
):
    log_keep = keeps[pl.program_id(1)]
    piece_len = 2 * kq_ref.shape[2]
    total = jnp.zeros(leaving_ref.shape[2:], F32)
    gain = gain_ref[0]
    d_gain = jnp.zeros(gain.shape, F32)
    for chunk in range(2):
        rows, _, start = where_is(whole, chunk, piece_len)
        before = document(whole, whole[0] * (2 * piece_len) - 1)
        gap = chunk * piece_len + rows + 1
        weight = jnp.where(
            document(whole, start + rows) == before, fade(gap, log_keep) * SCALE, 0.0
        )
        _, query = split_kq(kq_ref, whole, chunk)
        retained = piece_of(retained_ref, whole, chunk).astype(F32)
        normed, unit, scale = norm_rows(retained, gain, 0.01)
        gate = piece_of(gate_ref, whole, chunk).astype(F32)
        d_gated = piece_of(d_gated_ref, whole, chunk).astype(F32)
        sigma = jax.nn.sigmoid(gate)
        put_piece(
            d_gate_ref, whole, chunk, d_gated * normed * sigma * (1.0 + gate * (1.0 - sigma))
        )
        d_normed = d_gated * gate * sigma
        d_gain = d_gain + jnp.sum(d_normed * unit, axis=0, keepdims=True)
        d_retained = norm_back(d_normed, unit, scale, gain)
        put_piece(d_retained_ref, whole, chunk, d_retained)
        total = total + tn(query, (d_retained * weight).astype(BF16))
    d_gain_ref[0, 0] = d_gain
    leaving_ref[0, 0] = total.astype(BF16)


def backward_kernel(
    whole, keeps, kq_ref, v_ref, d_retained_ref, state_ref, d_state_ref, d_kq_ref, d_v_ref
):
    log_keep = keeps[pl.program_id(1)]
    piece_len = 2 * kq_ref.shape[2]
    terms = [piece_terms(whole, log_keep, chunk, piece_len) for chunk in range(2)]
    state = state_ref[0, 0].astype(F32)
    keys, _ = split_kq(kq_ref, whole, 0)
    _, _, outflow, over = terms[0]
    states = [state, next_state(state, keys, piece_of(v_ref, whole, 0), outflow, over)]
    d_state = d_state_ref[0, 0].astype(F32)
    for chunk in (1, 0):
        within, inflow, outflow, over = terms[chunk]
        keys, query = split_kq(kq_ref, whole, chunk)
        values = piece_of(v_ref, whole, chunk)
        d_ret = piece_of(d_retained_ref, whole, chunk)
        state_low, d_state_low = states[chunk].astype(BF16), d_state.astype(BF16)
        scores = (nt(query, keys) * within).astype(BF16)
        d_scores = (nt(d_ret, values) * within).astype(BF16)
        d_values = tn(scores, d_ret) + outflow * nn(keys, d_state_low)
        put_piece(d_v_ref, whole, chunk, d_values)
        d_query = nn(d_scores, keys) + inflow * nt(d_ret, state_low)
        d_keys = tn(d_scores, query) + outflow * nt(values, d_state_low)
        put_piece(d_kq_ref, whole, chunk, jnp.concatenate([d_keys, d_query], axis=1))
        if chunk == 1:
            entering = tn(query, (d_ret.astype(F32) * inflow).astype(BF16))
            d_state = over * d_state + entering


def per_head(kernel, scalars, blocks, outs, flops=12 << 30):
    def spec(array, kind):
        if kind == ROWS:
            width = array.shape[3] // heads
            return pl.BlockSpec((4, 1, array.shape[2], width), lambda b, h, *_: (0, b, 0, h))
        if kind == GAINS:
            return pl.BlockSpec((1, *array.shape[1:]), lambda b, h, *_: (h, 0, 0))
        return pl.BlockSpec((1, 1, *array.shape[2:]), lambda b, h, *_: (b, h, 0, 0))

    heads = scalars[1].shape[0]
    seq_count = (scalars[0].shape[0] - 3) // 2
    return pl.pallas_call(
        kernel,
        out_shape=[a for a, _ in outs],
        grid_spec=pltpu.PrefetchScalarGridSpec(
            num_scalar_prefetch=2,
            grid=(seq_count, heads),
            in_specs=[spec(*block) for block in blocks],
            out_specs=[spec(*out) for out in outs],
        ),
        compiler_params=pltpu.CompilerParams(vmem_limit_bytes=56 << 20),
        cost_estimate=cost(flops),
    )(*scalars, *(a for a, _ in blocks))


def both_quarters(mine, across, first, dim):
    return jnp.concatenate(
        [jnp.where(first, mine, across), jnp.where(first, across, mine)], axis=dim
    )


def paired_body(
    tokens,
    segments,
    forget,
    ln1_gain,
    w_query,
    w_key,
    w_value,
    w_gate,
    norm_gain,
    w_out,
    ln2_gain,
    w_fc_gate,
    w_fc_up,
    w_fc_down,
    cotangent,
):
    place = lax.axis_index(CONTEXT)
    x_at, core, y_at = place // 2, place % 2, lax.axis_index(TENSOR)
    z_at = lax.axis_index(FSDP)
    heads = forget.shape[0] // 2
    qk_width = w_query.shape[1] // forget.shape[0]
    v_width = w_value.shape[1] // forget.shape[0]
    width = tokens.shape[2]
    seq_count, share_len = tokens.shape[0], tokens.shape[1]
    share_rows = seq_count * share_len
    piece_len = 2 * share_len
    chip_len = 2 * piece_len
    v_half = heads * v_width
    forget_half = lax.dynamic_slice_in_dim(forget, core * heads, heads)
    gain_half = lax.dynamic_slice_in_dim(norm_gain, core * v_half, v_half)

    def part(array, first, last):
        return array[first * share_rows : last * share_rows]

    def unit(x_index):
        q = core * 2 + x_index
        key_query = [quarter_of(w_key, 1, q), quarter_of(w_query, 1, q)]
        return [
            jnp.concatenate(key_query, axis=1),
            quarter_of(w_value, 1, q),
            quarter_of(w_gate, 1, q),
            quarter_of(w_out, 0, q),
            quarter_of(w_fc_down, 0, q),
            quarter_of(w_fc_gate, 1, q),
            quarter_of(w_fc_up, 1, q),
        ]

    KQ, V, G, O, W2, W1, W3 = range(7)
    by_rows = [False, False, False, True, True, False, False]
    own, sibling = unit(x_at), unit(1 - x_at)
    size = own[0].shape[0]
    z_last = lax.axis_size(FSDP) - 1
    z_count = z_last + 1
    s_one = jnp.where(z_at == 0, 1, z_at - 1)
    s_three = jnp.where(z_at == z_last, 0, jnp.where(z_at == 1, 2, z_last))
    z_spots = [z_at, s_one, z_at ^ 2, s_three]
    spots = jnp.stack(z_spots + z_spots + [x_at] * 4 + [1 - x_at] * 4).astype(jnp.int32)
    groups = [[KQ, V], [G, O], [W2, W1, W3]]
    slots, across = [[], [], []], [[], [], []]

    def weight(index):
        at, row = next((i, g.index(index)) for i, g in enumerate(groups) if index in g)
        blocks = [(own[index], 0)] + [(array, row) for array in slots[at]]
        blocks += [(sibling[index], 0)] + [pieces[row] for pieces in across[at]]
        return assemble(blocks, spots, by_rows[index], size)

    env = SimpleNamespace()
    firsts = jnp.sum((segments == 0).astype(jnp.int32), axis=1)
    seconds = jnp.sum((segments <= 1).astype(jnp.int32), axis=1)
    starts = jnp.stack([firsts, seconds], axis=1).reshape(-1)
    whole = jnp.concatenate([jnp.stack([x_at, core, y_at]).astype(jnp.int32), starts])
    scalars = (whole, jnp.log(1.0 - forget_half))
    gains = gain_half.reshape(heads, 1, v_width)
    state_type = jax.ShapeDtypeStruct((seq_count, heads, qk_width, v_width), BF16)
    rows_type = jax.ShapeDtypeStruct((4, seq_count, share_len, v_half), BF16)
    kq_type = jax.ShapeDtypeStruct((4, seq_count, share_len, 2 * heads * qk_width), BF16)
    gain_type = jax.ShapeDtypeStruct((seq_count, heads, 1, v_width), F32)

    def shaped(rows_in):
        return rows_in.reshape(4, seq_count, share_len, -1)

    def flat(rows_in):
        return rows_in.reshape(4 * share_rows, -1)

    x_share = tokens.reshape(share_rows, width).astype(F32)
    cot_share = cotangent.reshape(share_rows, width)

    def work_norm():
        h1, ln1_normed, ln1_scale = norm_rows(x_share, ln1_gain)
        env.ln1 = (ln1_normed, ln1_scale)
        env.h = h1.astype(BF16)
        env.hy = over_y(env.h)
        return [env.h]

    def work_core():
        env.hc, env.hcy = over_core(env.h), over_core(env.hy)
        env.cy = over_y(cot_share)
        return []

    def work_rows():
        env.h_one = stack_rows(env.h, env.hy, env.hc, env.hcy)
        return [env.h_one]

    def work_kq():
        env.wkq = weight(KQ)
        env.kq = sum_of_products(nn, [env.h_one], [env.wkq], 0, 4 * share_rows, BF16)
        return [env.kq]

    def work_v():
        env.wv = weight(V)
        env.v = sum_of_products(nn, [env.h_one], [env.wv], 0, 4 * share_rows, BF16)
        return [env.v]

    def work_state():
        (update,) = per_head(
            update_kernel,
            scalars,
            [(shaped(env.kq), ROWS), (shaped(env.v), ROWS)],
            [(state_type, STATES)],
            4 << 30,
        )
        env.state = lax.ppermute(update, CONTEXT, UP_X)
        env.cc, env.ccy = over_core(cot_share), over_core(env.cy)
        return [update]

    def work_gate():
        env.wg = weight(G)
        env.gate = sum_of_products(nn, [env.h_one], [env.wg], 0, 4 * share_rows, BF16)
        return [env.gate]

    def work_retained():
        gated, env.retained = per_head(
            forward_kernel,
            scalars,
            [
                (shaped(env.kq), ROWS),
                (shaped(env.v), ROWS),
                (shaped(env.gate), ROWS),
                (env.state, STATES),
                (gains, GAINS),
            ],
            [(rows_type, ROWS), (rows_type, ROWS)],
        )
        env.gated = flat(gated)
        return [env.gated]

    def work_out_far():
        env.wo = weight(O)
        own, other = sum_of_products(
            nn, [env.gated], [env.wo], 2 * share_rows, 2 * share_rows, BF16, (), 2
        )
        env.far_other, env.far_own = over_core(other), over_core(own)
        return [other]

    def work_out_near():
        near = sum_of_products(
            nn, [env.gated], [env.wo], share_rows, share_rows, BF16, [(env.far_other, 0)]
        )
        env.near = over_y(near)
        return [near]

    def work_out_own():
        extras = [(env.far_own, 0), (tokens.reshape(share_rows, width), 0)]
        env.own = sum_of_products(nn, [env.gated], [env.wo], 0, share_rows, F32, extras)
        return [env.own]

    def work_cot():
        env.cot = stack_rows(cot_share, env.cy, env.cc, env.ccy)
        return [env.cot]

    def work_d_hidden():
        env.w2 = weight(W2)
        env.d_hidden = sum_of_products(nt, [env.cot], [env.w2], 0, 4 * share_rows, BF16)
        return [env.d_hidden]

    def work_middle():
        env.middle = env.own + env.near.astype(F32)
        h2, ln2_normed, ln2_scale = norm_rows(env.middle, ln2_gain)
        env.ln2 = (ln2_normed, ln2_scale)
        env.h2 = h2.astype(BF16)
        env.h2y, env.h2c = over_y(env.h2), over_core(env.h2)
        return [env.h2]

    def work_up():
        env.w1 = weight(W1)
        return [env.w1]

    def work_h2():
        env.w3 = weight(W3)
        env.h2y, env.d_hidden, env.w1, env.w3 = tie(env.h2y, env.d_hidden, env.w1, env.w3)
        env.h2cy = over_core(env.h2y)
        return [env.w3]

    plan = [
        [work_norm],
        [],
        [work_core],
        [work_rows],
        [work_kq],
        [work_v, work_state],
        [work_gate, work_retained],
        [work_out_far, work_out_near, work_out_own],
        [work_cot, work_middle],
        [work_d_hidden, work_up, work_h2],
    ]
    stacks = [jnp.concatenate([own[index] for index in group], axis=0) for group in groups]
    up = down = kept = to_send = None
    for tick, works in enumerate(plan):
        at, hop = divmod(tick, 3)
        moving = at < len(groups)
        sent, to_send = to_send, None
        came = []
        if sent is not None:
            which, value = sent
            slots[which].append(value)
            cuts = [0, size, value.shape[0]] if len(slots[which]) == 3 and which else [0, value.shape[0]]
            pieces = []
            for first, last in zip(cuts, cuts[1:]):
                piece = value[first:last]
                if first and which == 1:
                    piece, env.state = tie(piece, env.state)
                came.append(over_x(piece))
                pieces += [(came[-1], row) for row in range((last - first) // size)]
            across[which].append(pieces)
        if moving and hop < 2:
            up = stacks[at] if hop == 0 else up
            down = stacks[at] if hop == 0 else down
            got = [lax.ppermute(up, FSDP, UP_Z[hop]), lax.ppermute(down, FSDP, DOWN_Z[hop])]
        elif moving:
            got = [lax.ppermute(slots[at][1], FSDP, LAST_Z)]
        held = []
        for work in works:
            held += work()
        if not moving:
            continue
        names = [n for n in ("h_one", "kq", "gate", "gated", "cot") if hasattr(env, n)]
        held = held + came
        ahead = stacks[at + 1 : at + 2] if hop == 2 else []
        tied = list(tie(*got, *[getattr(env, n) for n in names], *ahead, *held))
        got = [tied.pop(0) for _ in got]
        for n in names:
            setattr(env, n, tied.pop(0))
        if ahead:
            stacks[at + 1] = tied.pop(0)
        if hop == 0:
            up, down = kept = got
            to_send = (at, jnp.where(z_at > 0, up, down))
        elif hop == 1:
            up, down = got
            to_send = (at, jnp.where(z_at >= 2, up, down))
        else:
            ends = (z_at == 0) | (z_at == z_last)
            to_send = (at, jnp.where(ends, got[0], kept[1]))

    h_one, gated, gate_pre = env.h_one, env.gated, env.gate
    wkq, wv, wg, wo, w1, w2, w3 = env.wkq, env.wv, env.wg, env.wo, env.w1, env.w2, env.w3
    cot_full, d_hidden, middle = env.cot, env.d_hidden, env.middle

    token = [h_one]

    def step(run, *args):
        *args, _ = tie(*args, token[0])
        out = run(*args)
        token[0] = out[0] if isinstance(out, (tuple, list)) else out
        return out

    def far_product(product, lefts, rights):
        def run(*arrays):
            return sum_of_products(
                product, arrays, rights, 2 * share_rows, 2 * share_rows, BF16, (), 2
            )

        own, other = step(run, *lefts)
        return over_core(other), over_core(own)

    def whole_product(product, lefts, rights, first, rows, kind, *extras):
        count = len(lefts)

        def run(*arrays):
            added = [(a, row) for a, (_, row) in zip(arrays[count:], extras)]
            return sum_of_products(
                product, arrays[:count], rights, first * share_rows, rows * share_rows, kind, added
            )

        return step(run, *lefts, *(a for a, _ in extras))

    def theirs(left, right):
        return over_x(step(lambda a, b: quarter_product(a, b, 1 - x_at), left, right))

    def ours(left, right, got):
        total = step(lambda a, b, c: quarter_product(a, b, x_at, [c]), left, right, got)
        return lax.psum_scatter(total, FSDP, scatter_dimension=0, tiled=True)

    def chip_rows(left, right):
        total = step(lambda a, b: split_product(a, b, z_count), left, right)
        return lax.psum_scatter(total, FSDP, scatter_dimension=0, tiled=False)

    def begin_finish(*mine):
        mine = step(lambda *a: jnp.concatenate(a, axis=0), *mine)
        return mine, over_x(mine)

    def end_finish(firsts, mine, beside):
        def join(mine, beside):
            blocks, row = [], 0
            for x_summed in firsts:
                count = 1 if x_summed else 2
                one, other = (a[row * size : (row + count) * size] for a in (mine, beside))
                if x_summed:
                    blocks += [jnp.where(x_at == 0, one, other), jnp.where(x_at == 0, other, one)]
                else:
                    blocks.append((one.astype(F32) + other.astype(F32)).astype(BF16))
                row += count
            return jnp.concatenate(blocks, axis=0)

        both = step(join, mine, beside)
        return both, over_core(both)

    def quarters(pair, at):
        both, other = pair
        mine, theirs = (a[2 * at * size : (2 * at + 2) * size] for a in (both, other))
        first, second = jnp.where(core == 0, mine, theirs), jnp.where(core == 0, theirs, mine)
        return [first[:size], first[size:], second[:size], second[size:]]

    def shard(pair, at, rows):
        return jnp.concatenate(quarters(pair, at), axis=1 - int(rows)).astype(F32)

    h_two = stack_rows(env.h2, env.h2y, env.h2c, env.h2cy)
    hidden, d_fca, d_fcb = step(hidden_units, h_two, w1, w3, d_hidden)

    fc_lefts, fc_rights = (d_fca, d_fcb), (w1, w3)
    far_other, far_own = far_product(nt, fc_lefts, fc_rights)
    down_mine = chip_rows(hidden, cot_full)
    near = over_y(whole_product(nt, fc_lefts, fc_rights, 1, 1, BF16, (far_other, 0)))
    gate_got = theirs(h_two, d_fca)
    own_part = whole_product(nt, fc_lefts, fc_rights, 0, 1, F32, (far_own, 0))
    up_got = theirs(h_two, d_fcb)
    out_far_other, out_far_own = far_product(nn, [hidden], [w2])

    def middle_back(own_part, near):
        d_h2 = own_part + near.astype(F32)
        ln2_normed, ln2_scale = env.ln2
        d_middle = cot_share.astype(F32) + norm_back(d_h2, ln2_normed, ln2_scale, ln2_gain)
        return d_middle.astype(BF16), d_middle, jnp.sum(d_h2 * ln2_normed, axis=0)

    d_mid_low, d_middle, g_ln2 = step(middle_back, own_part, near)
    d_mid_y, d_mid_c = over_y(d_mid_low), over_core(d_mid_low)
    fc_gate_mine = ours(h_two, d_fca, gate_got)
    out_near = whole_product(nn, [hidden], [w2], 1, 1, BF16, (out_far_other, 0))
    out_own = whole_product(nn, [hidden], [w2], 0, 1, F32, (out_far_own, 0), (middle, 0))
    d_mid_y, out_near, up_got = step(lambda *a: a, d_mid_y, out_near, up_got)
    d_mid_cy = over_core(d_mid_y)
    out_near = over_y(out_near)
    down_begun = begin_finish(down_mine)

    def gate_back(share, y, c, cy):
        d_branch = stack_rows(share, y, c, cy)
        return sum_of_products(nt, [d_branch], [wo], 0, 4 * share_rows, BF16), d_branch

    d_gated, d_branch = step(gate_back, d_mid_low, d_mid_y, d_mid_c, d_mid_cy)
    down_beside, d_gated = tie(down_begun[1], d_gated)
    kq, values, state_in = shaped(env.kq), shaped(env.v), env.state

    def retained_back(d_gated, kq):
        return per_head(
            norm_back_kernel,
            scalars,
            [
                (shaped(d_gated), ROWS),
                (shaped(gate_pre), ROWS),
                (env.retained, ROWS),
                (kq, ROWS),
                (gains, GAINS),
            ],
            [(rows_type, ROWS), (rows_type, ROWS), (gain_type, STATES), (state_type, STATES)],
        )

    d_gate, d_retained, g_norm, leaving = step(retained_back, d_gated, kq)
    d_gate = flat(d_gate)
    g_norm = jnp.sum(g_norm, axis=0).reshape(v_half)
    state_grad = lax.ppermute(leaving, CONTEXT, DOWN_X)
    out_mine = chip_rows(gated, d_branch)
    gg_theirs = step(lambda a, b: quarter_product(a, b, 1 - x_at), h_one, d_gate)
    state_grad, gg_theirs = tie(state_grad, gg_theirs)
    gg_got = over_x(gg_theirs)

    def pair_back(d_retained, state_grad):
        return per_head(
            backward_kernel,
            scalars,
            [
                (kq, ROWS),
                (values, ROWS),
                (d_retained, ROWS),
                (state_in, STATES),
                (state_grad, STATES),
            ],
            [(kq_type, ROWS), (rows_type, ROWS)],
        )

    fc_up_mine = ours(h_two, d_fcb, up_got)
    g_down = end_finish([False], down_begun[0], down_beside)
    dkq_low, dv_low = step(pair_back, d_retained, state_grad)
    dkq_low, dv_low = flat(dkq_low), flat(dv_low)
    v_got = theirs(h_one, dv_low)
    kq_got = theirs(h_one, dkq_low)
    h1_lefts, h1_rights = (dkq_low, dv_low, d_gate), (wkq, wv, wg)
    output = step(lambda a, b: (a + b.astype(F32)).astype(BF16), out_own, out_near)
    fc_gate_mine, gg_got = tie(fc_gate_mine, gg_got)
    gg_mine = ours(h_one, d_gate, gg_got)
    far_other, far_own = far_product(nt, h1_lefts, h1_rights)
    v_mine = ours(h_one, dv_low, v_got)
    near = over_y(whole_product(nt, h1_lefts, h1_rights, 1, 1, BF16, (far_other, 0)))
    own_part = whole_product(nt, h1_lefts, h1_rights, 0, 1, F32, (far_own, 0))
    out_begun = begin_finish(out_mine, fc_gate_mine)
    kq_mine = ours(h_one, dkq_low, kq_got)

    def tokens_back(own_part, near):
        d_h1 = own_part + near.astype(F32)
        ln1_normed, ln1_scale = env.ln1
        grad = d_middle + norm_back(d_h1, ln1_normed, ln1_scale, ln1_gain)
        return grad, jnp.sum(d_h1 * ln1_normed, axis=0)

    grad_tokens, g_ln1 = step(tokens_back, own_part, near)
    rest_begun = begin_finish(fc_up_mine, gg_mine, v_mine)
    g_out = end_finish([False, True], *out_begun)
    kq_begun = begin_finish(kq_mine)
    g_rest = end_finish([True, True, True], *rest_begun)
    g_kq = end_finish([True], *kq_begun)
    sides = quarters(g_kq, 0)
    g_key = jnp.concatenate([side[:, :qk_width] for side in sides], axis=1).astype(F32)
    g_query = jnp.concatenate([side[:, qk_width:] for side in sides], axis=1).astype(F32)

    norm_size = lax.axis_size(TENSOR) * norm_gain.shape[0]
    norm_all = lax.dynamic_update_slice_in_dim(
        jnp.zeros((norm_size,), F32), g_norm, (2 * y_at + core) * v_half, 0
    )
    gain_sums = jnp.concatenate([g_ln1, g_ln2, norm_all])
    for axis in (TENSOR, FSDP, CONTEXT):
        gain_sums = butterfly(gain_sums, axis)
    g_ln1, g_ln2 = gain_sums[:width], gain_sums[width : 2 * width]
    g_norm = lax.dynamic_slice_in_dim(
        gain_sums, 2 * width + y_at * norm_gain.shape[0], norm_gain.shape[0]
    )
    return (
        output.reshape(tokens.shape),
        grad_tokens.reshape(tokens.shape),
        g_ln1,
        g_query,
        g_key,
        shard(g_rest, 2, False),
        shard(g_rest, 1, False),
        g_norm,
        shard(g_out, 0, True),
        g_ln2,
        shard(g_out, 1, False),
        shard(g_rest, 0, False),
        shard(g_down, 0, True),
    )


def body(tensor_size, *arrays):
    heads_here = arrays[2].shape[0]
    paired = tensor_size == 2 and heads_here % 2 == 0 and lax.axis_size(CONTEXT) == 4
    paired = paired and lax.axis_size(FSDP) == 4
    return (paired_body if paired else general_body)(*arrays)


def solution(mesh):
    in_specs = (
        P(FSDP, (CONTEXT, TENSOR), None),
        P(FSDP, None),
        P(TENSOR),
        P(),
        P(FSDP, TENSOR),
        P(FSDP, TENSOR),
        P(FSDP, TENSOR),
        P(FSDP, TENSOR),
        P(TENSOR),
        P(TENSOR, FSDP),
        P(),
        P(FSDP, TENSOR),
        P(FSDP, TENSOR),
        P(TENSOR, FSDP),
        P(FSDP, (CONTEXT, TENSOR), None),
    )
    out_specs = (
        P(FSDP, (CONTEXT, TENSOR), None),
        P(FSDP, (CONTEXT, TENSOR), None),
        P(),
        P(FSDP, TENSOR),
        P(FSDP, TENSOR),
        P(FSDP, TENSOR),
        P(FSDP, TENSOR),
        P(TENSOR),
        P(TENSOR, FSDP),
        P(),
        P(FSDP, TENSOR),
        P(FSDP, TENSOR),
        P(TENSOR, FSDP),
    )
    return jax.shard_map(partial(body, mesh.shape[TENSOR]), mesh=mesh, in_specs=in_specs, out_specs=out_specs, check_vma=False)
```

```python
from functools import partial
from types import SimpleNamespace

import jax
import jax.numpy as jnp
from jax import lax
from jax.experimental import pallas as pl
from jax.experimental.pallas import tpu as pltpu
from jax.sharding import PartitionSpec as P

FSDP, CONTEXT, TENSOR = "fsdp", "context", "tensor"

careful = partial(jnp.einsum, precision=lax.Precision.HIGH)


def entering(part, axis, combine, identity):
    place = lax.axis_index(axis)
    gathered = jax.tree.map(lambda a: lax.all_gather(a, axis), part)
    state = jax.tree.map(lambda a, e: jnp.zeros_like(a) + jnp.asarray(e, a.dtype), part, identity)

    def one(step, state):
        return combine(
            state, jax.tree.map(lambda a: lax.dynamic_index_in_dim(a, step, 0, False), gathered)
        )

    return lax.fori_loop(0, place, one, state)


def carried_in(value, axis, combine, identity):
    count, place = (lax.axis_size(axis), lax.axis_index(axis))
    everything = jax.tree.map(
        lambda part, kind: lax.all_gather(part.astype(kind), axis),
        value,
        jax.tree.map(lambda a: jnp.bfloat16 if a.dtype == jnp.float32 else a.dtype, value),
    )
    start = jax.tree.map(
        lambda part, zero: jnp.broadcast_to(jnp.asarray(zero, part.dtype), part.shape),
        value,
        identity,
    )

    def step(k, before):
        at = count - 1 - k
        reached = at > place
        new = combine(
            before, jax.tree.map(lambda part, own: part[at].astype(own.dtype), everything, value)
        )
        return jax.tree.map(lambda a, b: jnp.where(reached, a, b), new, before)

    return lax.fori_loop(0, count, step, start)


def norm_rows(values, gain_vec, epsilon=1e-05):
    centred = values - jnp.mean(values, axis=-1, keepdims=True)
    scale = lax.rsqrt(jnp.mean(centred * centred, axis=-1, keepdims=True) + epsilon)
    normed = centred * scale
    return (normed * gain_vec, normed, scale)


def norm_back(grad_in, normed, scale, gain_vec):
    d_normed = grad_in * gain_vec
    first_mean = jnp.mean(d_normed, axis=-1, keepdims=True)
    second_mean = jnp.mean(d_normed * normed, axis=-1, keepdims=True)
    return scale * (d_normed - first_mean - normed * second_mean)


def swish_slope(values):
    sigma = jax.nn.sigmoid(values)
    return sigma * (1.0 + values * (1.0 - sigma))


def compose(earlier, latter):
    return (earlier[0] * latter[0], latter[0][:, :, None, None] * earlier[1] + latter[1])


def share_gather(piece):
    return lax.all_gather(piece, TENSOR, axis=1, tiled=True)


def branch_sum(terms):
    return lax.psum_scatter(terms, TENSOR, scatter_dimension=1, tiled=True)


def input_sum(terms):
    return lax.psum_scatter(
        terms.astype(jnp.bfloat16), TENSOR, scatter_dimension=1, tiled=True
    ).astype(jnp.float32)


def mixer_fetch(w_query, w_key, w_value, w_gate, w_out):
    return (
        lax.all_gather(w_query, FSDP, axis=0, tiled=True),
        lax.all_gather(w_key, FSDP, axis=0, tiled=True),
        lax.all_gather(w_value, FSDP, axis=0, tiled=True),
        lax.all_gather(w_gate, FSDP, axis=0, tiled=True),
        lax.all_gather(w_out, FSDP, axis=1, tiled=True),
    )


def mlp_fetch(w_fc_gate, w_fc_up, w_fc_down):
    return (
        lax.all_gather(w_fc_gate, FSDP, axis=0, tiled=True),
        lax.all_gather(w_fc_up, FSDP, axis=0, tiled=True),
        lax.all_gather(w_fc_down, FSDP, axis=1, tiled=True),
    )


def product(form, left, right):
    return jnp.einsum(form, left, right, preferred_element_type=jnp.float32)


def general_body(
    tokens,
    segments,
    forget,
    ln1_gain,
    w_query,
    w_key,
    w_value,
    w_gate,
    norm_gain,
    w_out,
    ln2_gain,
    w_fc_gate,
    w_fc_up,
    w_fc_down,
    cotangent,
):
    heads_here = forget.shape[0]
    qk_width = w_query.shape[1] // heads_here
    v_width = w_value.shape[1] // heads_here
    v_local = heads_here * v_width
    gain_heads = norm_gain.reshape(heads_here, v_width)
    x_share = tokens.astype(jnp.float32)
    h1_share, ln1_normed, ln1_scale = norm_rows(x_share, ln1_gain)
    h_one = share_gather(h1_share.astype(jnp.bfloat16))
    wq_all, wk_all, wv_all, wg_all, wo_all = mixer_fetch(w_query, w_key, w_value, w_gate, w_out)
    seq_count, stretch_len = (h_one.shape[0], h_one.shape[1])
    query = product("btd,dq->btq", h_one, wq_all).astype(jnp.bfloat16)
    keys = product("btd,dq->btq", h_one, wk_all).astype(jnp.bfloat16)
    values = product("btd,dv->btv", h_one, wv_all).astype(jnp.bfloat16)
    gate_pre = product("btd,dv->btv", h_one, wg_all)
    query_heads = query.reshape(seq_count, stretch_len, heads_here, qk_width)
    keys_heads = keys.reshape(seq_count, stretch_len, heads_here, qk_width)
    query_full = query_heads.astype(jnp.float32) * 0.0625
    keys_full = keys_heads.astype(jnp.float32)
    values_full = values.astype(jnp.float32).reshape(seq_count, stretch_len, heads_here, v_width)
    log_keep = jnp.log(1.0 - forget)
    ctx_place = lax.axis_index(CONTEXT)
    seg_stretch = lax.dynamic_slice_in_dim(segments, ctx_place * stretch_len, stretch_len, 1)
    seg_prev = lax.dynamic_slice_in_dim(segments, jnp.maximum(ctx_place * stretch_len - 1, 0), 1, 1)
    live_mask = (seg_stretch == seg_prev).astype(jnp.float32)
    steps_idx = jnp.arange(stretch_len, dtype=jnp.float32)
    step_gap = jnp.maximum(steps_idx[:, None] - steps_idx[None, :], 0.0)
    causal = steps_idx[:, None] >= steps_idx[None, :]
    same_doc = (seg_stretch[:, :, None] == seg_stretch[:, None, :]) & causal[None]
    weights_mask = jnp.where(
        same_doc[:, None], jnp.exp(step_gap[None] * log_keep[:, None, None])[None], 0.0
    )
    inflow = live_mask[:, :, None] * jnp.exp((steps_idx[:, None] + 1.0) * log_keep[None, :])[None]
    outflow = (seg_stretch == seg_stretch[:, -1:]).astype(jnp.float32)[:, :, None] * jnp.exp(
        (stretch_len - 1.0 - steps_idx)[:, None] * log_keep[None, :]
    )[None]
    carry_decay = live_mask[:, -1:] * jnp.exp(stretch_len * log_keep)[None, :]
    update = careful("bshd,bsh,bshe->bhde", keys_full, outflow, values_full)
    identity = (jnp.ones_like(carry_decay), jnp.zeros_like(update))
    state_in = entering((carry_decay, update), CONTEXT, compose, identity)[1]
    scores = product("bthd,bshd->bhts", query_heads, keys_heads) * 0.0625 * weights_mask
    retained = careful("bhts,bshe->bthe", scores, values_full)
    retained = retained + inflow[..., None] * careful("bthd,bhde->bthe", query_full, state_in)
    normed_out, gn_normed, gn_scale = norm_rows(retained, gain_heads, 0.01)
    norm_flat = normed_out.reshape(seq_count, stretch_len, v_local)
    gate_act = jax.nn.silu(gate_pre)
    gated = (gate_act * norm_flat).astype(jnp.bfloat16)
    middle = x_share + branch_sum(product("btv,vd->btd", gated, wo_all))
    h2_share, ln2_normed, ln2_scale = norm_rows(middle, ln2_gain)
    h_two = share_gather(h2_share.astype(jnp.bfloat16))
    w1_all, w3_all, w2_all = mlp_fetch(w_fc_gate, w_fc_up, w_fc_down)
    fc_a = product("btd,df->btf", h_two, w1_all)
    fc_b = product("btd,df->btf", h_two, w3_all)
    silu_a = jax.nn.silu(fc_a)
    hidden = (silu_a * fc_b).astype(jnp.bfloat16)
    output = (middle + branch_sum(product("btf,fd->btd", hidden, w2_all))).astype(jnp.bfloat16)
    wq_all, wk_all, wv_all, wg_all, wo_all = mixer_fetch(w_query, w_key, w_value, w_gate, w_out)
    w1_all, w3_all, w2_all = mlp_fetch(w_fc_gate, w_fc_up, w_fc_down)
    cot_full = share_gather(cotangent)
    d_hidden = product("btd,fd->btf", cot_full, w2_all)
    g_down = product("btf,btd->fd", hidden, cot_full)
    d_fca = (d_hidden * fc_b * swish_slope(fc_a)).astype(jnp.bfloat16)
    d_fcb = (d_hidden * silu_a).astype(jnp.bfloat16)
    g_fc_gate = product("btd,btf->df", h_two, d_fca)
    g_fc_up = product("btd,btf->df", h_two, d_fcb)
    d_h2 = input_sum(product("btf,df->btd", d_fca, w1_all) + product("btf,df->btd", d_fcb, w3_all))
    d_middle = cotangent.astype(jnp.float32) + norm_back(d_h2, ln2_normed, ln2_scale, ln2_gain)
    g_ln2 = jnp.sum(d_h2 * ln2_normed, axis=(0, 1))
    d_branch = share_gather(d_middle.astype(jnp.bfloat16))
    d_gated = product("btd,vd->btv", d_branch, wo_all)
    g_out = product("btv,btd->vd", gated, d_branch)
    d_gate = (d_gated * norm_flat * swish_slope(gate_pre)).astype(jnp.bfloat16)
    d_normed = (d_gated * gate_act).reshape(seq_count, stretch_len, heads_here, v_width)
    g_norm = jnp.sum(d_normed * gn_normed, axis=(0, 1)).reshape(v_local)
    d_retained = norm_back(d_normed, gn_normed, gn_scale, gain_heads)
    d_scores = careful("bthe,bshe->bhts", d_retained, values_full) * weights_mask
    d_values = careful("bhts,bthe->bshe", scores, d_retained)
    d_query = careful("bhts,bshd->bthd", d_scores, keys_full)
    d_query = d_query + inflow[..., None] * careful("bthe,bhde->bthd", d_retained, state_in)
    d_keys = careful("bhts,bthd->bshd", d_scores, query_full)
    leaving = careful("bthd,bth,bthe->bhde", query_full, inflow, d_retained)
    state_grad = carried_in((carry_decay, leaving), CONTEXT, compose, identity)[1]
    d_keys = d_keys + outflow[..., None] * careful("bshe,bhde->bshd", values_full, state_grad)
    d_values = d_values + outflow[..., None] * careful("bshd,bhde->bshe", keys_full, state_grad)
    dq_low = (
        (d_query * 0.0625)
        .reshape(seq_count, stretch_len, heads_here * qk_width)
        .astype(jnp.bfloat16)
    )
    dk_low = d_keys.reshape(seq_count, stretch_len, heads_here * qk_width).astype(jnp.bfloat16)
    dv_low = d_values.reshape(seq_count, stretch_len, v_local).astype(jnp.bfloat16)
    g_query = product("btd,btq->dq", h_one, dq_low)
    g_key = product("btd,btq->dq", h_one, dk_low)
    g_value = product("btd,btv->dv", h_one, dv_low)
    g_gate = product("btd,btv->dv", h_one, d_gate)
    d_h1 = product("btq,dq->btd", dq_low, wq_all) + product("btq,dq->btd", dk_low, wk_all)
    d_h1 = d_h1 + product("btv,dv->btd", dv_low, wv_all) + product("btv,dv->btd", d_gate, wg_all)
    d_h1 = input_sum(d_h1)
    grad_tokens = d_middle + norm_back(d_h1, ln1_normed, ln1_scale, ln1_gain)
    g_ln1 = jnp.sum(d_h1 * ln1_normed, axis=(0, 1))
    tensor_place = lax.axis_index(TENSOR)
    norm_full = lax.dynamic_update_slice(
        jnp.zeros((v_local * lax.axis_size(TENSOR),), jnp.float32),
        g_norm,
        (tensor_place * v_local,),
    )
    g_ln1, g_ln2, norm_full = lax.psum((g_ln1, g_ln2, norm_full), (FSDP, CONTEXT, TENSOR))
    g_norm = lax.dynamic_slice_in_dim(norm_full, tensor_place * v_local, v_local)
    weight_grads = (g_query, g_key, g_value, g_gate, g_out, g_fc_gate, g_fc_up, g_down)
    summed = (
        lax.psum(weight_grads[0].astype(jnp.bfloat16), CONTEXT).astype(jnp.float32),
        lax.psum(weight_grads[1].astype(jnp.bfloat16), CONTEXT).astype(jnp.float32),
        lax.psum(weight_grads[2].astype(jnp.bfloat16), CONTEXT).astype(jnp.float32),
        lax.psum(weight_grads[3].astype(jnp.bfloat16), CONTEXT).astype(jnp.float32),
        lax.psum(weight_grads[4].astype(jnp.bfloat16), CONTEXT).astype(jnp.float32),
        lax.psum(weight_grads[5].astype(jnp.bfloat16), CONTEXT).astype(jnp.float32),
        lax.psum(weight_grads[6].astype(jnp.bfloat16), CONTEXT).astype(jnp.float32),
        lax.psum(weight_grads[7].astype(jnp.bfloat16), CONTEXT).astype(jnp.float32),
    )
    shards = (
        lax.psum_scatter(
            summed[0].astype(jnp.bfloat16), FSDP, scatter_dimension=0, tiled=True
        ).astype(jnp.float32),
        lax.psum_scatter(
            summed[1].astype(jnp.bfloat16), FSDP, scatter_dimension=0, tiled=True
        ).astype(jnp.float32),
        lax.psum_scatter(
            summed[2].astype(jnp.bfloat16), FSDP, scatter_dimension=0, tiled=True
        ).astype(jnp.float32),
        lax.psum_scatter(
            summed[3].astype(jnp.bfloat16), FSDP, scatter_dimension=0, tiled=True
        ).astype(jnp.float32),
        lax.psum_scatter(
            summed[4].astype(jnp.bfloat16), FSDP, scatter_dimension=1, tiled=True
        ).astype(jnp.float32),
        lax.psum_scatter(
            summed[5].astype(jnp.bfloat16), FSDP, scatter_dimension=0, tiled=True
        ).astype(jnp.float32),
        lax.psum_scatter(
            summed[6].astype(jnp.bfloat16), FSDP, scatter_dimension=0, tiled=True
        ).astype(jnp.float32),
        lax.psum_scatter(
            summed[7].astype(jnp.bfloat16), FSDP, scatter_dimension=1, tiled=True
        ).astype(jnp.float32),
    )
    return (
        output,
        grad_tokens,
        g_ln1,
        shards[0],
        shards[1],
        shards[2],
        shards[3],
        g_norm,
        shards[4],
        g_ln2,
        shards[5],
        shards[6],
        shards[7],
    )


F32 = jnp.float32
BF16 = jnp.bfloat16
BOTH_X = [(0, 2), (2, 0), (1, 3), (3, 1)]
UP_X = [(0, 2), (1, 3)]
DOWN_X = [(2, 0), (3, 1)]
CORES = [(0, 1), (1, 0), (2, 3), (3, 2)]
UP_Z = [[(0, 1), (1, 2), (2, 3)], [(1, 2), (2, 3)]]
DOWN_Z = [[(3, 2), (2, 1), (1, 0)], [(2, 1), (1, 0)]]
LAST_Z = [(2, 3), (1, 0)]
SCALE = 0.0625
ROWS, GAINS, STATES = range(3)


def cost(flops):
    return pl.CostEstimate(flops=3 * flops // 5, transcendentals=0, bytes_accessed=0)


COPYING = 2 << 30
DOWN_Z = [[(3, 2), (2, 1), (1, 0)], [(2, 1), (1, 0)], [(1, 0)]]


def over_x(value):
    return lax.ppermute(value, CONTEXT, BOTH_X)


def over_core(value):
    return lax.ppermute(value, CONTEXT, CORES)


def over_y(value):
    return lax.ppermute(value, TENSOR, [(0, 1), (1, 0)])


def tie(*values):
    return lax.optimization_barrier(values)


def butterfly(value, axis):
    size = lax.axis_size(axis)
    step = 1
    while step < size:
        value = value + lax.ppermute(value, axis, [(i, i ^ step) for i in range(size)])
        step *= 2
    return value


def quarter_of(weight, dim, index):
    size = weight.shape[dim] // 4
    return lax.dynamic_slice_in_dim(weight, index * size, size, dim)


def assemble_kernel(spot_ref, *refs):
    at = pl.program_id(0)
    for index, block in enumerate(refs[:8]):

        @pl.when(at == index)
        def _(block=block):
            refs[8][...] = block[...]


def assemble(blocks, spots, by_rows, size):
    shape = (2 * size, 4 * size) if by_rows else (4 * size, 2 * size)

    def spot(at, spots_ref):
        z_from, x_from = spots_ref[at], spots_ref[8 + at]
        return (x_from, z_from) if by_rows else (z_from, x_from)

    return pl.pallas_call(
        assemble_kernel,
        out_shape=jax.ShapeDtypeStruct(shape, BF16),
        grid_spec=pltpu.PrefetchScalarGridSpec(
            num_scalar_prefetch=1,
            grid=(8,),
            in_specs=[
                pl.BlockSpec((size, size), lambda at, spots_ref, row=row: (row, 0))
                for _, row in blocks
            ],
            out_specs=pl.BlockSpec((size, size), spot),
        ),
        compiler_params=pltpu.CompilerParams(vmem_limit_bytes=32 << 20),
        cost_estimate=cost(COPYING),
    )(spots, *(array for array, _ in blocks))


def sum_kernel(product, count, outs, *refs):
    lefts, rights, extras = refs[:count], refs[count : 2 * count], refs[2 * count : -outs]
    total = product(lefts[0][...], rights[0][...])
    for left, right in zip(lefts[1:], rights[1:]):
        total = total + product(left[...], right[...])
    for extra in extras:
        total = total + extra[...].astype(F32)
    size = total.shape[0] // outs
    for index, out_ref in enumerate(refs[-outs:]):
        out_ref[...] = total[index * size : (index + 1) * size].astype(out_ref.dtype)


def sum_of_products(product, lefts, rights, first, rows, kind, extras=(), outs=1):
    by_columns = product is nn
    width = rights[0].shape[1 if by_columns else 0]
    block, tile = min(1024, rows), min(512, width)
    if outs > 1:
        block = rows

    def right_spec(right):
        if by_columns:
            return pl.BlockSpec((right.shape[0], tile), lambda n, m: (0, n))
        return pl.BlockSpec((tile, right.shape[1]), lambda n, m: (n, 0))

    def tile_spec(from_row, size):
        return pl.BlockSpec((size, tile), lambda n, m: (from_row // size + m, n))

    out_shape = [jax.ShapeDtypeStruct((rows // outs, width), kind)] * outs
    result = pl.pallas_call(
        partial(sum_kernel, product, len(lefts), outs),
        grid=(width // tile, rows // block),
        out_shape=out_shape,
        in_specs=[
            pl.BlockSpec((block, left.shape[1]), lambda n, m: (first // block + m, 0))
            for left in lefts
        ]
        + [right_spec(right) for right in rights]
        + [tile_spec(from_row, block) for _, from_row in extras],
        out_specs=[tile_spec(0, block // outs)] * outs,
        compiler_params=pltpu.CompilerParams(vmem_limit_bytes=60 << 20),
        cost_estimate=cost(2 * rows * width * sum(left.shape[1] for left in lefts)),
    )(*lefts, *rights, *(array for array, _ in extras))
    return result[0] if outs == 1 else result


def quarter_kernel(spots_ref, left, right, *rest):
    total = tn(left[...], right[...])
    for extra in rest[:-1]:
        total = total + extra[...].astype(F32)
    rest[-1][...] = total.astype(BF16)


def quarter_product(left, right, index, extras=()):
    tokens, width = left.shape
    size, block = right.shape[1] // 2, min(1024, width)
    return pl.pallas_call(
        quarter_kernel,
        out_shape=jax.ShapeDtypeStruct((width, size), BF16),
        grid_spec=pltpu.PrefetchScalarGridSpec(
            num_scalar_prefetch=1,
            grid=(width // block,),
            in_specs=[
                pl.BlockSpec((tokens, block), lambda m, at: (0, m)),
                pl.BlockSpec((tokens, size), lambda m, at: (0, at[0])),
            ]
            + [pl.BlockSpec((block, size), lambda m, at: (m, 0)) for _ in extras],
            out_specs=pl.BlockSpec((block, size), lambda m, at: (m, 0)),
        ),
        compiler_params=pltpu.CompilerParams(vmem_limit_bytes=60 << 20),
        cost_estimate=cost(2 * tokens * width * size),
    )(index.reshape(1).astype(jnp.int32), left, right, *extras)


def split_kernel(left, right, out):
    out[0] = tn(left[...], right[...]).astype(BF16)


def split_product(left, right, count):
    tokens, rows = left.shape
    size = right.shape[1] // count
    return pl.pallas_call(
        split_kernel,
        grid=(count,),
        out_shape=jax.ShapeDtypeStruct((count, rows, size), BF16),
        in_specs=[
            pl.BlockSpec((tokens, rows), lambda n: (0, 0)),
            pl.BlockSpec((tokens, size), lambda n: (0, n)),
        ],
        out_specs=pl.BlockSpec((1, rows, size), lambda n: (n, 0, 0)),
        compiler_params=pltpu.CompilerParams(vmem_limit_bytes=60 << 20),
        cost_estimate=cost(2 * tokens * rows * size * count),
    )(left, right)


def unit_kernel(h_ref, w1_ref, w3_ref, d_hidden_ref, hidden_ref, d_a_ref, d_b_ref):
    fc_a, fc_b = nn(h_ref[...], w1_ref[...]), nn(h_ref[...], w3_ref[...])
    d_hidden = d_hidden_ref[...].astype(F32)
    sigma = jax.nn.sigmoid(fc_a)
    silu_a = fc_a * sigma
    hidden_ref[...] = (silu_a * fc_b).astype(BF16)
    d_a_ref[...] = (d_hidden * fc_b * (sigma * (1.0 + fc_a * (1.0 - sigma)))).astype(BF16)
    d_b_ref[...] = (d_hidden * silu_a).astype(BF16)


def hidden_units(h_two, w1, w3, d_hidden):
    rows, width = h_two.shape
    count = w1.shape[1]
    block, tile = min(512, rows), min(512, count)
    weight = pl.BlockSpec((width, tile), lambda n, m: (0, n))
    spot = pl.BlockSpec((block, tile), lambda n, m: (m, n))
    return pl.pallas_call(
        unit_kernel,
        grid=(count // tile, rows // block),
        out_shape=[jax.ShapeDtypeStruct((rows, count), BF16)] * 3,
        in_specs=[pl.BlockSpec((block, width), lambda n, m: (m, 0)), weight, weight, spot],
        out_specs=[spot] * 3,
        compiler_params=pltpu.CompilerParams(vmem_limit_bytes=60 << 20),
        cost_estimate=cost(4 * rows * width * count),
    )(h_two, w1, w3, d_hidden)


def stack_kernel(*refs):
    count = len(refs) - 4
    shares, out_ref, held, sems_in, sems_out = refs[:count], *refs[count:]
    rows = shares[0].shape[0]
    ins, outs = [], []
    for index, share in enumerate(shares):
        ins.append(pltpu.make_async_copy(share, held.at[index], sems_in.at[index]))
        spot = out_ref.at[pl.ds(index * rows, rows)]
        outs.append(pltpu.make_async_copy(held.at[index], spot, sems_out.at[index]))
    for copy in ins:
        copy.start()
    for copy, onward in zip(ins, outs):
        copy.wait()
        onward.start()
    for onward in outs:
        onward.wait()


def stack_rows(*shares):
    rows, width = shares[0].shape
    count = len(shares)
    return pl.pallas_call(
        stack_kernel,
        out_shape=jax.ShapeDtypeStruct((count * rows, width), shares[0].dtype),
        in_specs=[pl.BlockSpec(memory_space=pl.ANY)] * count,
        out_specs=pl.BlockSpec(memory_space=pl.ANY),
        scratch_shapes=[
            pltpu.VMEM((count, rows, width), shares[0].dtype),
            pltpu.SemaphoreType.DMA((count,)),
            pltpu.SemaphoreType.DMA((count,)),
        ],
        compiler_params=pltpu.CompilerParams(vmem_limit_bytes=48 << 20),
        cost_estimate=cost(2 * COPYING),
    )(*shares)


def nn(left, right):
    return lax.dot_general(left, right, (((1,), (0,)), ((), ())), preferred_element_type=F32)


def nt(left, right):
    return lax.dot_general(left, right, (((1,), (1,)), ((), ())), preferred_element_type=F32)


def tn(left, right):
    return lax.dot_general(left, right, (((0,), (0,)), ((), ())), preferred_element_type=F32)


def where_is(whole, chunk, piece_len):
    share_len = piece_len // 2
    spots = []
    for shape, dim in (((piece_len, 1), 0), ((1, piece_len), 1)):
        at = lax.broadcasted_iota(jnp.int32, shape, dim) + whole[2] * share_len
        spots.append(jnp.where(at >= piece_len, at - piece_len, at))
    start = whole[0] * (2 * piece_len) + chunk * piece_len
    return spots[0], spots[1], start


def document(whole, spot):
    seq = pl.program_id(0)
    first, second = whole[3 + 2 * seq], whole[4 + 2 * seq]
    return jnp.where(spot >= second, 2, jnp.where(spot >= first, 1, 0))


def fade(gap, log_keep):
    return jnp.exp(jnp.maximum(gap, 0).astype(F32) * log_keep)


def piece_terms(whole, log_keep, chunk, piece_len):
    rows, cols, start = where_is(whole, chunk, piece_len)
    doc_rows, doc_cols = document(whole, start + rows), document(whole, start + cols)
    before, last = document(whole, start - 1), document(whole, start + piece_len - 1)
    within = jnp.where(
        (rows >= cols) & (doc_rows == doc_cols), fade(rows - cols, log_keep) * SCALE, 0.0
    )
    inflow = jnp.where(doc_rows == before, fade(rows + 1, log_keep) * SCALE, 0.0)
    outflow = jnp.where(doc_rows == last, fade(piece_len - 1 - rows, log_keep), 0.0)
    whole_gap = jnp.full((1, 1), piece_len, jnp.int32)
    over = jnp.where(before == last, fade(whole_gap, log_keep), 0.0)
    return within, inflow, outflow, over


def piece_of(ref, whole, chunk):
    group = lax.rem(chunk + whole[1], 2) * 2
    value = ref[pl.ds(group, 2), 0]
    return value.reshape(value.shape[0] * value.shape[1], value.shape[2])


def put_piece(ref, whole, chunk, value):
    group = lax.rem(chunk + whole[1], 2) * 2
    ref[pl.ds(group, 2), 0] = value.astype(ref.dtype).reshape(2, value.shape[0] // 2, value.shape[1])


def split_kq(ref, whole, chunk):
    both = piece_of(ref, whole, chunk)
    width = both.shape[1] // 2
    return both[:, :width], both[:, width:]


def update_kernel(whole, keeps, kq_ref, v_ref, out_ref):
    log_keep = keeps[pl.program_id(1)]
    piece_len = 2 * kq_ref.shape[2]
    total = jnp.zeros(out_ref.shape[2:], F32)
    for chunk in range(2):
        rows, _, start = where_is(whole, chunk, piece_len)
        last = document(whole, whole[0] * (2 * piece_len) + 2 * piece_len - 1)
        gap = (2 - chunk) * piece_len - 1 - rows
        weight = jnp.where(document(whole, start + rows) == last, fade(gap, log_keep), 0.0)
        keys, _ = split_kq(kq_ref, whole, chunk)
        values = piece_of(v_ref, whole, chunk)
        total = total + tn((keys.astype(F32) * weight).astype(BF16), values)
    out_ref[0, 0] = total.astype(BF16)


def next_state(state, keys, values, outflow, over):
    return over * state + tn((keys.astype(F32) * outflow).astype(BF16), values)


def forward_kernel(
    whole, keeps, kq_ref, v_ref, gate_ref, state_ref, gain_ref, gated_ref, retained_ref
):
    log_keep = keeps[pl.program_id(1)]
    piece_len = 2 * kq_ref.shape[2]
    state = state_ref[0, 0].astype(F32)
    for chunk in range(2):
        within, inflow, outflow, over = piece_terms(whole, log_keep, chunk, piece_len)
        keys, query = split_kq(kq_ref, whole, chunk)
        values = piece_of(v_ref, whole, chunk)
        scores = (nt(query, keys) * within).astype(BF16)
        retained = nn(scores, values) + inflow * nn(query, state.astype(BF16))
        if chunk == 0:
            state = next_state(state, keys, values, outflow, over)
        put_piece(retained_ref, whole, chunk, retained)
        normed, _, _ = norm_rows(retained, gain_ref[0], 0.01)
        gate = piece_of(gate_ref, whole, chunk).astype(F32)
        put_piece(gated_ref, whole, chunk, gate * jax.nn.sigmoid(gate) * normed)


def norm_back_kernel(
    whole,
    keeps,
    d_gated_ref,
    gate_ref,
    retained_ref,
    kq_ref,
    gain_ref,
    d_gate_ref,
    d_retained_ref,
    d_gain_ref,
    leaving_ref,
):
    log_keep = keeps[pl.program_id(1)]
    piece_len = 2 * kq_ref.shape[2]
    total = jnp.zeros(leaving_ref.shape[2:], F32)
    gain = gain_ref[0]
    d_gain = jnp.zeros(gain.shape, F32)
    for chunk in range(2):
        rows, _, start = where_is(whole, chunk, piece_len)
        before = document(whole, whole[0] * (2 * piece_len) - 1)
        gap = chunk * piece_len + rows + 1
        weight = jnp.where(
            document(whole, start + rows) == before, fade(gap, log_keep) * SCALE, 0.0
        )
        _, query = split_kq(kq_ref, whole, chunk)
        retained = piece_of(retained_ref, whole, chunk).astype(F32)
        normed, unit, scale = norm_rows(retained, gain, 0.01)
        gate = piece_of(gate_ref, whole, chunk).astype(F32)
        d_gated = piece_of(d_gated_ref, whole, chunk).astype(F32)
        sigma = jax.nn.sigmoid(gate)
        put_piece(
            d_gate_ref, whole, chunk, d_gated * normed * sigma * (1.0 + gate * (1.0 - sigma))
        )
        d_normed = d_gated * gate * sigma
        d_gain = d_gain + jnp.sum(d_normed * unit, axis=0, keepdims=True)
        d_retained = norm_back(d_normed, unit, scale, gain)
        put_piece(d_retained_ref, whole, chunk, d_retained)
        total = total + tn(query, (d_retained * weight).astype(BF16))
    d_gain_ref[0, 0] = d_gain
    leaving_ref[0, 0] = total.astype(BF16)


def backward_kernel(
    whole, keeps, kq_ref, v_ref, d_retained_ref, state_ref, d_state_ref, d_kq_ref, d_v_ref
):
    log_keep = keeps[pl.program_id(1)]
    piece_len = 2 * kq_ref.shape[2]
    terms = [piece_terms(whole, log_keep, chunk, piece_len) for chunk in range(2)]
    state = state_ref[0, 0].astype(F32)
    keys, _ = split_kq(kq_ref, whole, 0)
    _, _, outflow, over = terms[0]
    states = [state, next_state(state, keys, piece_of(v_ref, whole, 0), outflow, over)]
    d_state = d_state_ref[0, 0].astype(F32)
    for chunk in (1, 0):
        within, inflow, outflow, over = terms[chunk]
        keys, query = split_kq(kq_ref, whole, chunk)
        values = piece_of(v_ref, whole, chunk)
        d_ret = piece_of(d_retained_ref, whole, chunk)
        state_low, d_state_low = states[chunk].astype(BF16), d_state.astype(BF16)
        scores = (nt(query, keys) * within).astype(BF16)
        d_scores = (nt(d_ret, values) * within).astype(BF16)
        d_values = tn(scores, d_ret) + outflow * nn(keys, d_state_low)
        put_piece(d_v_ref, whole, chunk, d_values)
        d_query = nn(d_scores, keys) + inflow * nt(d_ret, state_low)
        d_keys = tn(d_scores, query) + outflow * nt(values, d_state_low)
        put_piece(d_kq_ref, whole, chunk, jnp.concatenate([d_keys, d_query], axis=1))
        if chunk == 1:
            entering = tn(query, (d_ret.astype(F32) * inflow).astype(BF16))
            d_state = over * d_state + entering


def per_head(kernel, scalars, blocks, outs, flops=12 << 30):
    def spec(array, kind):
        if kind == ROWS:
            width = array.shape[3] // heads
            return pl.BlockSpec((4, 1, array.shape[2], width), lambda b, h, *_: (0, b, 0, h))
        if kind == GAINS:
            return pl.BlockSpec((1, *array.shape[1:]), lambda b, h, *_: (h, 0, 0))
        return pl.BlockSpec((1, 1, *array.shape[2:]), lambda b, h, *_: (b, h, 0, 0))

    heads = scalars[1].shape[0]
    seq_count = (scalars[0].shape[0] - 3) // 2
    return pl.pallas_call(
        kernel,
        out_shape=[a for a, _ in outs],
        grid_spec=pltpu.PrefetchScalarGridSpec(
            num_scalar_prefetch=2,
            grid=(seq_count, heads),
            in_specs=[spec(*block) for block in blocks],
            out_specs=[spec(*out) for out in outs],
        ),
        compiler_params=pltpu.CompilerParams(vmem_limit_bytes=56 << 20),
        cost_estimate=cost(flops),
    )(*scalars, *(a for a, _ in blocks))


def both_quarters(mine, across, first, dim):
    return jnp.concatenate(
        [jnp.where(first, mine, across), jnp.where(first, across, mine)], axis=dim
    )


def paired_body(
    tokens,
    segments,
    forget,
    ln1_gain,
    w_query,
    w_key,
    w_value,
    w_gate,
    norm_gain,
    w_out,
    ln2_gain,
    w_fc_gate,
    w_fc_up,
    w_fc_down,
    cotangent,
):
    place = lax.axis_index(CONTEXT)
    x_at, core, y_at = place // 2, place % 2, lax.axis_index(TENSOR)
    z_at = lax.axis_index(FSDP)
    heads = forget.shape[0] // 2
    qk_width = w_query.shape[1] // forget.shape[0]
    v_width = w_value.shape[1] // forget.shape[0]
    width = tokens.shape[2]
    seq_count, share_len = tokens.shape[0], tokens.shape[1]
    share_rows = seq_count * share_len
    piece_len = 2 * share_len
    chip_len = 2 * piece_len
    v_half = heads * v_width
    forget_half = lax.dynamic_slice_in_dim(forget, core * heads, heads)
    gain_half = lax.dynamic_slice_in_dim(norm_gain, core * v_half, v_half)

    def part(array, first, last):
        return array[first * share_rows : last * share_rows]

    def unit(x_index):
        q = core * 2 + x_index
        key_query = [quarter_of(w_key, 1, q), quarter_of(w_query, 1, q)]
        return [
            jnp.concatenate(key_query, axis=1),
            quarter_of(w_value, 1, q),
            quarter_of(w_gate, 1, q),
            quarter_of(w_out, 0, q),
            quarter_of(w_fc_down, 0, q),
            quarter_of(w_fc_gate, 1, q),
            quarter_of(w_fc_up, 1, q),
        ]

    KQ, V, G, O, W2, W1, W3 = range(7)
    by_rows = [False, False, False, True, True, False, False]
    own, sibling = unit(x_at), unit(1 - x_at)
    size = own[0].shape[0]
    z_last = lax.axis_size(FSDP) - 1
    z_count = z_last + 1
    s_one = jnp.where(z_at == 0, 1, z_at - 1)
    s_three = jnp.where(z_at == z_last, 0, jnp.where(z_at == 1, 2, z_last))
    z_spots = [z_at, s_one, z_at ^ 2, s_three]
    spots = jnp.stack(z_spots + z_spots + [x_at] * 4 + [1 - x_at] * 4).astype(jnp.int32)
    groups = [[KQ, V], [G, O], [W2, W1, W3]]
    slots, across = [[], [], []], [[], [], []]

    def weight(index):
        at, row = next((i, g.index(index)) for i, g in enumerate(groups) if index in g)
        blocks = [(own[index], 0)] + [(array, row) for array in slots[at]]
        blocks += [(sibling[index], 0)] + [(array, row) for array in across[at]]
        return assemble(blocks, spots, by_rows[index], size)

    env = SimpleNamespace()
    firsts = jnp.sum((segments == 0).astype(jnp.int32), axis=1)
    seconds = jnp.sum((segments <= 1).astype(jnp.int32), axis=1)
    starts = jnp.stack([firsts, seconds], axis=1).reshape(-1)
    whole = jnp.concatenate([jnp.stack([x_at, core, y_at]).astype(jnp.int32), starts])
    scalars = (whole, jnp.log(1.0 - forget_half))
    gains = gain_half.reshape(heads, 1, v_width)
    state_type = jax.ShapeDtypeStruct((seq_count, heads, qk_width, v_width), BF16)
    rows_type = jax.ShapeDtypeStruct((4, seq_count, share_len, v_half), BF16)
    kq_type = jax.ShapeDtypeStruct((4, seq_count, share_len, 2 * heads * qk_width), BF16)
    gain_type = jax.ShapeDtypeStruct((seq_count, heads, 1, v_width), F32)

    def shaped(rows_in):
        return rows_in.reshape(4, seq_count, share_len, -1)

    def flat(rows_in):
        return rows_in.reshape(4 * share_rows, -1)

    x_share = tokens.reshape(share_rows, width).astype(F32)
    cot_share = cotangent.reshape(share_rows, width)

    def work_norm():
        h1, ln1_normed, ln1_scale = norm_rows(x_share, ln1_gain)
        env.ln1 = (ln1_normed, ln1_scale)
        env.h = h1.astype(BF16)
        env.hy = over_y(env.h)
        return [env.h]

    def work_core():
        env.hc, env.hcy = over_core(env.h), over_core(env.hy)
        env.cy = over_y(cot_share)
        return []

    def work_rows():
        env.h_one = stack_rows(env.h, env.hy, env.hc, env.hcy)
        return [env.h_one]

    def work_kq():
        env.wkq = weight(KQ)
        env.kq = sum_of_products(nn, [env.h_one], [env.wkq], 0, 4 * share_rows, BF16)
        return [env.kq]

    def work_v():
        env.wv = weight(V)
        env.v = sum_of_products(nn, [env.h_one], [env.wv], 0, 4 * share_rows, BF16)
        return [env.v]

    def work_state():
        (update,) = per_head(
            update_kernel,
            scalars,
            [(shaped(env.kq), ROWS), (shaped(env.v), ROWS)],
            [(state_type, STATES)],
            4 << 30,
        )
        env.state = lax.ppermute(update, CONTEXT, UP_X)
        env.cc, env.ccy = over_core(cot_share), over_core(env.cy)
        return [update]

    def work_gate():
        env.wg = weight(G)
        env.gate = sum_of_products(nn, [env.h_one], [env.wg], 0, 4 * share_rows, BF16)
        return [env.gate]

    def work_retained():
        gated, env.retained = per_head(
            forward_kernel,
            scalars,
            [
                (shaped(env.kq), ROWS),
                (shaped(env.v), ROWS),
                (shaped(env.gate), ROWS),
                (env.state, STATES),
                (gains, GAINS),
            ],
            [(rows_type, ROWS), (rows_type, ROWS)],
        )
        env.gated = flat(gated)
        return [env.gated]

    def work_out_far():
        env.wo = weight(O)
        own, other = sum_of_products(
            nn, [env.gated], [env.wo], 2 * share_rows, 2 * share_rows, BF16, (), 2
        )
        env.far_other, env.far_own = over_core(other), over_core(own)
        return [other]

    def work_out_near():
        near = sum_of_products(
            nn, [env.gated], [env.wo], share_rows, share_rows, BF16, [(env.far_other, 0)]
        )
        env.near = over_y(near)
        return [near]

    def work_out_own():
        extras = [(env.far_own, 0), (tokens.reshape(share_rows, width), 0)]
        env.own = sum_of_products(nn, [env.gated], [env.wo], 0, share_rows, F32, extras)
        return [env.own]

    def work_cot():
        env.cot = stack_rows(cot_share, env.cy, env.cc, env.ccy)
        return [env.cot]

    def work_d_hidden():
        env.w2 = weight(W2)
        env.d_hidden = sum_of_products(nt, [env.cot], [env.w2], 0, 4 * share_rows, BF16)
        return [env.d_hidden]

    def work_middle():
        env.middle = env.own + env.near.astype(F32)
        h2, ln2_normed, ln2_scale = norm_rows(env.middle, ln2_gain)
        env.ln2 = (ln2_normed, ln2_scale)
        env.h2 = h2.astype(BF16)
        env.h2y, env.h2c = over_y(env.h2), over_core(env.h2)
        return [env.h2]

    def work_up():
        env.w1 = weight(W1)
        return [env.w1]

    def work_h2():
        env.w3 = weight(W3)
        env.h2y, env.d_hidden, env.w1, env.w3 = tie(env.h2y, env.d_hidden, env.w1, env.w3)
        env.h2cy = over_core(env.h2y)
        return [env.w3]

    plan = [
        [work_norm],
        [],
        [work_core],
        [work_rows],
        [work_kq],
        [work_v, work_state],
        [work_cot, work_gate],
        [work_retained, work_out_far],
        [work_out_near, work_out_own],
        [work_middle],
        [work_d_hidden, work_up, work_h2],
    ]
    stacks = [jnp.concatenate([own[index] for index in group], axis=0) for group in groups]
    up = down = kept = to_send = None
    for tick, works in enumerate(plan):
        at, hop = divmod(tick, 3)
        moving = at < len(groups)
        sent, to_send = to_send, None
        if sent is not None:
            slots[sent[0]].append(sent[1])
            across[sent[0]].append(over_x(sent[1]))
        if moving and hop < 2:
            up = stacks[at] if hop == 0 else up
            down = stacks[at] if hop == 0 else down
            got = [lax.ppermute(up, FSDP, UP_Z[hop]), lax.ppermute(down, FSDP, DOWN_Z[hop])]
        elif moving:
            got = [lax.ppermute(slots[at][1], FSDP, LAST_Z)]
        held = []
        for work in works:
            held += work()
        if not moving:
            continue
        names = [n for n in ("h_one", "kq", "gate", "gated", "cot") if hasattr(env, n)]
        held = held + ([across[sent[0]][-1]] if sent is not None else [])
        ahead = stacks[at + 1 : at + 2] if hop == 2 else []
        tied = list(tie(*got, *[getattr(env, n) for n in names], *ahead, *held))
        got = [tied.pop(0) for _ in got]
        for n in names:
            setattr(env, n, tied.pop(0))
        if hasattr(env, "far_other"):
            env.far_other = tie(env.far_other, *got)[0]
        if ahead:
            stacks[at + 1] = tied.pop(0)
        if hop == 0:
            up, down = kept = got
            to_send = (at, jnp.where(z_at > 0, up, down))
        elif hop == 1:
            up, down = got
            to_send = (at, jnp.where(z_at >= 2, up, down))
        else:
            ends = (z_at == 0) | (z_at == z_last)
            to_send = (at, jnp.where(ends, got[0], kept[1]))

    h_one, gated, gate_pre = env.h_one, env.gated, env.gate
    wkq, wv, wg, wo, w1, w2, w3 = env.wkq, env.wv, env.wg, env.wo, env.w1, env.w2, env.w3
    cot_full, d_hidden, middle = env.cot, env.d_hidden, env.middle

    token = [h_one]

    def step(run, *args):
        *args, _ = tie(*args, token[0])
        out = run(*args)
        token[0] = out[0] if isinstance(out, (tuple, list)) else out
        return out

    def far_product(product, lefts, rights):
        def run(*arrays):
            return sum_of_products(
                product, arrays, rights, 2 * share_rows, 2 * share_rows, BF16, (), 2
            )

        own, other = step(run, *lefts)
        return over_core(other), over_core(own)

    def whole_product(product, lefts, rights, first, rows, kind, *extras):
        count = len(lefts)

        def run(*arrays):
            added = [(a, row) for a, (_, row) in zip(arrays[count:], extras)]
            return sum_of_products(
                product, arrays[:count], rights, first * share_rows, rows * share_rows, kind, added
            )

        return step(run, *lefts, *(a for a, _ in extras))

    def theirs(left, right):
        return over_x(step(lambda a, b: quarter_product(a, b, 1 - x_at), left, right))

    def ours(left, right, got):
        total = step(lambda a, b, c: quarter_product(a, b, x_at, [c]), left, right, got)
        return lax.psum_scatter(total, FSDP, scatter_dimension=0, tiled=True)

    def chip_rows(left, right):
        total = step(lambda a, b: split_product(a, b, z_count), left, right)
        return lax.psum_scatter(total, FSDP, scatter_dimension=0, tiled=False)

    def begin_finish(*mine):
        mine = step(lambda *a: jnp.concatenate(a, axis=0), *mine)
        return mine, over_x(mine)

    def end_finish(firsts, mine, beside):
        def join(mine, beside):
            blocks, row = [], 0
            for x_summed in firsts:
                count = 1 if x_summed else 2
                one, other = (a[row * size : (row + count) * size] for a in (mine, beside))
                if x_summed:
                    blocks += [jnp.where(x_at == 0, one, other), jnp.where(x_at == 0, other, one)]
                else:
                    blocks.append((one.astype(F32) + other.astype(F32)).astype(BF16))
                row += count
            return jnp.concatenate(blocks, axis=0)

        both = step(join, mine, beside)
        return both, over_core(both)

    def quarters(pair, at):
        both, other = pair
        mine, theirs = (a[2 * at * size : (2 * at + 2) * size] for a in (both, other))
        first, second = jnp.where(core == 0, mine, theirs), jnp.where(core == 0, theirs, mine)
        return [first[:size], first[size:], second[:size], second[size:]]

    def shard(pair, at, rows):
        return jnp.concatenate(quarters(pair, at), axis=1 - int(rows)).astype(F32)

    h_two = stack_rows(env.h2, env.h2y, env.h2c, env.h2cy)
    hidden, d_fca, d_fcb = step(hidden_units, h_two, w1, w3, d_hidden)

    fc_lefts, fc_rights = (d_fca, d_fcb), (w1, w3)
    far_other, far_own = far_product(nt, fc_lefts, fc_rights)
    down_mine = chip_rows(hidden, cot_full)
    near = over_y(whole_product(nt, fc_lefts, fc_rights, 1, 1, BF16, (far_other, 0)))
    gate_got = theirs(h_two, d_fca)
    own_part = whole_product(nt, fc_lefts, fc_rights, 0, 1, F32, (far_own, 0))
    up_got = theirs(h_two, d_fcb)
    out_far_other, out_far_own = far_product(nn, [hidden], [w2])

    def middle_back(own_part, near):
        d_h2 = own_part + near.astype(F32)
        ln2_normed, ln2_scale = env.ln2
        d_middle = cot_share.astype(F32) + norm_back(d_h2, ln2_normed, ln2_scale, ln2_gain)
        return d_middle.astype(BF16), d_middle, jnp.sum(d_h2 * ln2_normed, axis=0)

    d_mid_low, d_middle, g_ln2 = step(middle_back, own_part, near)
    d_mid_y, d_mid_c = over_y(d_mid_low), over_core(d_mid_low)
    fc_gate_mine = ours(h_two, d_fca, gate_got)
    out_near = whole_product(nn, [hidden], [w2], 1, 1, BF16, (out_far_other, 0))
    out_own = whole_product(nn, [hidden], [w2], 0, 1, F32, (out_far_own, 0), (middle, 0))
    d_mid_y, out_near, up_got = step(lambda *a: a, d_mid_y, out_near, up_got)
    d_mid_cy = over_core(d_mid_y)
    out_near = over_y(out_near)
    down_begun = begin_finish(down_mine)
    fc_up_mine = ours(h_two, d_fcb, up_got)

    def gate_back(share, y, c, cy):
        d_branch = stack_rows(share, y, c, cy)
        return sum_of_products(nt, [d_branch], [wo], 0, 4 * share_rows, BF16), d_branch

    d_gated, d_branch = step(gate_back, d_mid_low, d_mid_y, d_mid_c, d_mid_cy)
    down_beside, d_gated = tie(down_begun[1], d_gated)
    kq, values, state_in = shaped(env.kq), shaped(env.v), env.state

    def retained_back(d_gated, kq):
        return per_head(
            norm_back_kernel,
            scalars,
            [
                (shaped(d_gated), ROWS),
                (shaped(gate_pre), ROWS),
                (env.retained, ROWS),
                (kq, ROWS),
                (gains, GAINS),
            ],
            [(rows_type, ROWS), (rows_type, ROWS), (gain_type, STATES), (state_type, STATES)],
        )

    d_gate, d_retained, g_norm, leaving = step(retained_back, d_gated, kq)
    d_gate = flat(d_gate)
    g_norm = jnp.sum(g_norm, axis=0).reshape(v_half)
    state_grad = lax.ppermute(leaving, CONTEXT, DOWN_X)
    out_mine = chip_rows(gated, d_branch)
    gg_theirs = step(lambda a, b: quarter_product(a, b, 1 - x_at), h_one, d_gate)
    state_grad, gg_theirs = tie(state_grad, gg_theirs)
    gg_got = over_x(gg_theirs)

    def pair_back(d_retained, state_grad):
        return per_head(
            backward_kernel,
            scalars,
            [
                (kq, ROWS),
                (values, ROWS),
                (d_retained, ROWS),
                (state_in, STATES),
                (state_grad, STATES),
            ],
            [(kq_type, ROWS), (rows_type, ROWS)],
        )

    g_down = end_finish([False], down_begun[0], down_beside)
    dkq_low, dv_low = step(pair_back, d_retained, state_grad)
    dkq_low, dv_low = flat(dkq_low), flat(dv_low)
    v_got = theirs(h_one, dv_low)
    kq_got = theirs(h_one, dkq_low)
    h1_lefts, h1_rights = (dkq_low, dv_low, d_gate), (wkq, wv, wg)
    output = step(lambda a, b: (a + b.astype(F32)).astype(BF16), out_own, out_near)
    fc_gate_mine, gg_got = tie(fc_gate_mine, gg_got)
    gg_mine = ours(h_one, d_gate, gg_got)
    far_other, far_own = far_product(nt, h1_lefts, h1_rights)
    v_mine = ours(h_one, dv_low, v_got)
    near = over_y(whole_product(nt, h1_lefts, h1_rights, 1, 1, BF16, (far_other, 0)))
    own_part = whole_product(nt, h1_lefts, h1_rights, 0, 1, F32, (far_own, 0))
    fc_begun = begin_finish(fc_gate_mine, fc_up_mine)
    kq_mine = ours(h_one, dkq_low, kq_got)

    def tokens_back(own_part, near):
        d_h1 = own_part + near.astype(F32)
        ln1_normed, ln1_scale = env.ln1
        grad = d_middle + norm_back(d_h1, ln1_normed, ln1_scale, ln1_gain)
        return grad, jnp.sum(d_h1 * ln1_normed, axis=0)

    grad_tokens, g_ln1 = step(tokens_back, own_part, near)
    rest_begun = begin_finish(out_mine, gg_mine, v_mine)
    g_fc = end_finish([True, True], *fc_begun)
    kq_begun = begin_finish(kq_mine)
    g_rest = end_finish([False, True, True], *rest_begun)
    g_kq = end_finish([True], *kq_begun)
    sides = quarters(g_kq, 0)
    g_key = jnp.concatenate([side[:, :qk_width] for side in sides], axis=1).astype(F32)
    g_query = jnp.concatenate([side[:, qk_width:] for side in sides], axis=1).astype(F32)

    norm_size = lax.axis_size(TENSOR) * norm_gain.shape[0]
    norm_all = lax.dynamic_update_slice_in_dim(
        jnp.zeros((norm_size,), F32), g_norm, (2 * y_at + core) * v_half, 0
    )
    gain_sums = jnp.concatenate([g_ln1, g_ln2, norm_all])
    for axis in (TENSOR, FSDP, CONTEXT):
        gain_sums = butterfly(gain_sums, axis)
    g_ln1, g_ln2 = gain_sums[:width], gain_sums[width : 2 * width]
    g_norm = lax.dynamic_slice_in_dim(
        gain_sums, 2 * width + y_at * norm_gain.shape[0], norm_gain.shape[0]
    )
    return (
        output.reshape(tokens.shape),
        grad_tokens.reshape(tokens.shape),
        g_ln1,
        g_query,
        g_key,
        shard(g_rest, 2, False),
        shard(g_rest, 1, False),
        g_norm,
        shard(g_rest, 0, True),
        g_ln2,
        shard(g_fc, 0, False),
        shard(g_fc, 1, False),
        shard(g_down, 0, True),
    )


def body(tensor_size, *arrays):
    heads_here = arrays[2].shape[0]
    paired = tensor_size == 2 and heads_here % 2 == 0 and lax.axis_size(CONTEXT) == 4
    paired = paired and lax.axis_size(FSDP) == 4
    return (paired_body if paired else general_body)(*arrays)


def solution(mesh):
    in_specs = (
        P(FSDP, (CONTEXT, TENSOR), None),
        P(FSDP, None),
        P(TENSOR),
        P(),
        P(FSDP, TENSOR),
        P(FSDP, TENSOR),
        P(FSDP, TENSOR),
        P(FSDP, TENSOR),
        P(TENSOR),
        P(TENSOR, FSDP),
        P(),
        P(FSDP, TENSOR),
        P(FSDP, TENSOR),
        P(TENSOR, FSDP),
        P(FSDP, (CONTEXT, TENSOR), None),
    )
    out_specs = (
        P(FSDP, (CONTEXT, TENSOR), None),
        P(FSDP, (CONTEXT, TENSOR), None),
        P(),
        P(FSDP, TENSOR),
        P(FSDP, TENSOR),
        P(FSDP, TENSOR),
        P(FSDP, TENSOR),
        P(TENSOR),
        P(TENSOR, FSDP),
        P(),
        P(FSDP, TENSOR),
        P(FSDP, TENSOR),
        P(TENSOR, FSDP),
    )
    return jax.shard_map(partial(body, mesh.shape[TENSOR]), mesh=mesh, in_specs=in_specs, out_specs=out_specs, check_vma=False)
```

```python
from functools import partial
from types import SimpleNamespace

import jax
import jax.numpy as jnp
from jax import lax
from jax.experimental import pallas as pl
from jax.experimental.pallas import tpu as pltpu
from jax.sharding import PartitionSpec as P

FSDP, CONTEXT, TENSOR = "fsdp", "context", "tensor"

careful = partial(jnp.einsum, precision=lax.Precision.HIGH)


def entering(part, axis, combine, identity):
    place = lax.axis_index(axis)
    gathered = jax.tree.map(lambda a: lax.all_gather(a, axis), part)
    state = jax.tree.map(lambda a, e: jnp.zeros_like(a) + jnp.asarray(e, a.dtype), part, identity)

    def one(step, state):
        return combine(
            state, jax.tree.map(lambda a: lax.dynamic_index_in_dim(a, step, 0, False), gathered)
        )

    return lax.fori_loop(0, place, one, state)


def carried_in(value, axis, combine, identity):
    count, place = (lax.axis_size(axis), lax.axis_index(axis))
    everything = jax.tree.map(
        lambda part, kind: lax.all_gather(part.astype(kind), axis),
        value,
        jax.tree.map(lambda a: jnp.bfloat16 if a.dtype == jnp.float32 else a.dtype, value),
    )
    start = jax.tree.map(
        lambda part, zero: jnp.broadcast_to(jnp.asarray(zero, part.dtype), part.shape),
        value,
        identity,
    )

    def step(k, before):
        at = count - 1 - k
        reached = at > place
        new = combine(
            before, jax.tree.map(lambda part, own: part[at].astype(own.dtype), everything, value)
        )
        return jax.tree.map(lambda a, b: jnp.where(reached, a, b), new, before)

    return lax.fori_loop(0, count, step, start)


def norm_rows(values, gain_vec, epsilon=1e-05):
    centred = values - jnp.mean(values, axis=-1, keepdims=True)
    scale = lax.rsqrt(jnp.mean(centred * centred, axis=-1, keepdims=True) + epsilon)
    normed = centred * scale
    return (normed * gain_vec, normed, scale)


def norm_back(grad_in, normed, scale, gain_vec):
    d_normed = grad_in * gain_vec
    first_mean = jnp.mean(d_normed, axis=-1, keepdims=True)
    second_mean = jnp.mean(d_normed * normed, axis=-1, keepdims=True)
    return scale * (d_normed - first_mean - normed * second_mean)


def swish_slope(values):
    sigma = jax.nn.sigmoid(values)
    return sigma * (1.0 + values * (1.0 - sigma))


def compose(earlier, latter):
    return (earlier[0] * latter[0], latter[0][:, :, None, None] * earlier[1] + latter[1])


def share_gather(piece):
    return lax.all_gather(piece, TENSOR, axis=1, tiled=True)


def branch_sum(terms):
    return lax.psum_scatter(terms, TENSOR, scatter_dimension=1, tiled=True)


def input_sum(terms):
    return lax.psum_scatter(
        terms.astype(jnp.bfloat16), TENSOR, scatter_dimension=1, tiled=True
    ).astype(jnp.float32)


def mixer_fetch(w_query, w_key, w_value, w_gate, w_out):
    return (
        lax.all_gather(w_query, FSDP, axis=0, tiled=True),
        lax.all_gather(w_key, FSDP, axis=0, tiled=True),
        lax.all_gather(w_value, FSDP, axis=0, tiled=True),
        lax.all_gather(w_gate, FSDP, axis=0, tiled=True),
        lax.all_gather(w_out, FSDP, axis=1, tiled=True),
    )


def mlp_fetch(w_fc_gate, w_fc_up, w_fc_down):
    return (
        lax.all_gather(w_fc_gate, FSDP, axis=0, tiled=True),
        lax.all_gather(w_fc_up, FSDP, axis=0, tiled=True),
        lax.all_gather(w_fc_down, FSDP, axis=1, tiled=True),
    )


def product(form, left, right):
    return jnp.einsum(form, left, right, preferred_element_type=jnp.float32)


def general_body(
    tokens,
    segments,
    forget,
    ln1_gain,
    w_query,
    w_key,
    w_value,
    w_gate,
    norm_gain,
    w_out,
    ln2_gain,
    w_fc_gate,
    w_fc_up,
    w_fc_down,
    cotangent,
):
    heads_here = forget.shape[0]
    qk_width = w_query.shape[1] // heads_here
    v_width = w_value.shape[1] // heads_here
    v_local = heads_here * v_width
    gain_heads = norm_gain.reshape(heads_here, v_width)
    x_share = tokens.astype(jnp.float32)
    h1_share, ln1_normed, ln1_scale = norm_rows(x_share, ln1_gain)
    h_one = share_gather(h1_share.astype(jnp.bfloat16))
    wq_all, wk_all, wv_all, wg_all, wo_all = mixer_fetch(w_query, w_key, w_value, w_gate, w_out)
    seq_count, stretch_len = (h_one.shape[0], h_one.shape[1])
    query = product("btd,dq->btq", h_one, wq_all).astype(jnp.bfloat16)
    keys = product("btd,dq->btq", h_one, wk_all).astype(jnp.bfloat16)
    values = product("btd,dv->btv", h_one, wv_all).astype(jnp.bfloat16)
    gate_pre = product("btd,dv->btv", h_one, wg_all)
    query_heads = query.reshape(seq_count, stretch_len, heads_here, qk_width)
    keys_heads = keys.reshape(seq_count, stretch_len, heads_here, qk_width)
    query_full = query_heads.astype(jnp.float32) * 0.0625
    keys_full = keys_heads.astype(jnp.float32)
    values_full = values.astype(jnp.float32).reshape(seq_count, stretch_len, heads_here, v_width)
    log_keep = jnp.log(1.0 - forget)
    ctx_place = lax.axis_index(CONTEXT)
    seg_stretch = lax.dynamic_slice_in_dim(segments, ctx_place * stretch_len, stretch_len, 1)
    seg_prev = lax.dynamic_slice_in_dim(segments, jnp.maximum(ctx_place * stretch_len - 1, 0), 1, 1)
    live_mask = (seg_stretch == seg_prev).astype(jnp.float32)
    steps_idx = jnp.arange(stretch_len, dtype=jnp.float32)
    step_gap = jnp.maximum(steps_idx[:, None] - steps_idx[None, :], 0.0)
    causal = steps_idx[:, None] >= steps_idx[None, :]
    same_doc = (seg_stretch[:, :, None] == seg_stretch[:, None, :]) & causal[None]
    weights_mask = jnp.where(
        same_doc[:, None], jnp.exp(step_gap[None] * log_keep[:, None, None])[None], 0.0
    )
    inflow = live_mask[:, :, None] * jnp.exp((steps_idx[:, None] + 1.0) * log_keep[None, :])[None]
    outflow = (seg_stretch == seg_stretch[:, -1:]).astype(jnp.float32)[:, :, None] * jnp.exp(
        (stretch_len - 1.0 - steps_idx)[:, None] * log_keep[None, :]
    )[None]
    carry_decay = live_mask[:, -1:] * jnp.exp(stretch_len * log_keep)[None, :]
    update = careful("bshd,bsh,bshe->bhde", keys_full, outflow, values_full)
    identity = (jnp.ones_like(carry_decay), jnp.zeros_like(update))
    state_in = entering((carry_decay, update), CONTEXT, compose, identity)[1]
    scores = product("bthd,bshd->bhts", query_heads, keys_heads) * 0.0625 * weights_mask
    retained = careful("bhts,bshe->bthe", scores, values_full)
    retained = retained + inflow[..., None] * careful("bthd,bhde->bthe", query_full, state_in)
    normed_out, gn_normed, gn_scale = norm_rows(retained, gain_heads, 0.01)
    norm_flat = normed_out.reshape(seq_count, stretch_len, v_local)
    gate_act = jax.nn.silu(gate_pre)
    gated = (gate_act * norm_flat).astype(jnp.bfloat16)
    middle = x_share + branch_sum(product("btv,vd->btd", gated, wo_all))
    h2_share, ln2_normed, ln2_scale = norm_rows(middle, ln2_gain)
    h_two = share_gather(h2_share.astype(jnp.bfloat16))
    w1_all, w3_all, w2_all = mlp_fetch(w_fc_gate, w_fc_up, w_fc_down)
    fc_a = product("btd,df->btf", h_two, w1_all)
    fc_b = product("btd,df->btf", h_two, w3_all)
    silu_a = jax.nn.silu(fc_a)
    hidden = (silu_a * fc_b).astype(jnp.bfloat16)
    output = (middle + branch_sum(product("btf,fd->btd", hidden, w2_all))).astype(jnp.bfloat16)
    wq_all, wk_all, wv_all, wg_all, wo_all = mixer_fetch(w_query, w_key, w_value, w_gate, w_out)
    w1_all, w3_all, w2_all = mlp_fetch(w_fc_gate, w_fc_up, w_fc_down)
    cot_full = share_gather(cotangent)
    d_hidden = product("btd,fd->btf", cot_full, w2_all)
    g_down = product("btf,btd->fd", hidden, cot_full)
    d_fca = (d_hidden * fc_b * swish_slope(fc_a)).astype(jnp.bfloat16)
    d_fcb = (d_hidden * silu_a).astype(jnp.bfloat16)
    g_fc_gate = product("btd,btf->df", h_two, d_fca)
    g_fc_up = product("btd,btf->df", h_two, d_fcb)
    d_h2 = input_sum(product("btf,df->btd", d_fca, w1_all) + product("btf,df->btd", d_fcb, w3_all))
    d_middle = cotangent.astype(jnp.float32) + norm_back(d_h2, ln2_normed, ln2_scale, ln2_gain)
    g_ln2 = jnp.sum(d_h2 * ln2_normed, axis=(0, 1))
    d_branch = share_gather(d_middle.astype(jnp.bfloat16))
    d_gated = product("btd,vd->btv", d_branch, wo_all)
    g_out = product("btv,btd->vd", gated, d_branch)
    d_gate = (d_gated * norm_flat * swish_slope(gate_pre)).astype(jnp.bfloat16)
    d_normed = (d_gated * gate_act).reshape(seq_count, stretch_len, heads_here, v_width)
    g_norm = jnp.sum(d_normed * gn_normed, axis=(0, 1)).reshape(v_local)
    d_retained = norm_back(d_normed, gn_normed, gn_scale, gain_heads)
    d_scores = careful("bthe,bshe->bhts", d_retained, values_full) * weights_mask
    d_values = careful("bhts,bthe->bshe", scores, d_retained)
    d_query = careful("bhts,bshd->bthd", d_scores, keys_full)
    d_query = d_query + inflow[..., None] * careful("bthe,bhde->bthd", d_retained, state_in)
    d_keys = careful("bhts,bthd->bshd", d_scores, query_full)
    leaving = careful("bthd,bth,bthe->bhde", query_full, inflow, d_retained)
    state_grad = carried_in((carry_decay, leaving), CONTEXT, compose, identity)[1]
    d_keys = d_keys + outflow[..., None] * careful("bshe,bhde->bshd", values_full, state_grad)
    d_values = d_values + outflow[..., None] * careful("bshd,bhde->bshe", keys_full, state_grad)
    dq_low = (
        (d_query * 0.0625)
        .reshape(seq_count, stretch_len, heads_here * qk_width)
        .astype(jnp.bfloat16)
    )
    dk_low = d_keys.reshape(seq_count, stretch_len, heads_here * qk_width).astype(jnp.bfloat16)
    dv_low = d_values.reshape(seq_count, stretch_len, v_local).astype(jnp.bfloat16)
    g_query = product("btd,btq->dq", h_one, dq_low)
    g_key = product("btd,btq->dq", h_one, dk_low)
    g_value = product("btd,btv->dv", h_one, dv_low)
    g_gate = product("btd,btv->dv", h_one, d_gate)
    d_h1 = product("btq,dq->btd", dq_low, wq_all) + product("btq,dq->btd", dk_low, wk_all)
    d_h1 = d_h1 + product("btv,dv->btd", dv_low, wv_all) + product("btv,dv->btd", d_gate, wg_all)
    d_h1 = input_sum(d_h1)
    grad_tokens = d_middle + norm_back(d_h1, ln1_normed, ln1_scale, ln1_gain)
    g_ln1 = jnp.sum(d_h1 * ln1_normed, axis=(0, 1))
    tensor_place = lax.axis_index(TENSOR)
    norm_full = lax.dynamic_update_slice(
        jnp.zeros((v_local * lax.axis_size(TENSOR),), jnp.float32),
        g_norm,
        (tensor_place * v_local,),
    )
    g_ln1, g_ln2, norm_full = lax.psum((g_ln1, g_ln2, norm_full), (FSDP, CONTEXT, TENSOR))
    g_norm = lax.dynamic_slice_in_dim(norm_full, tensor_place * v_local, v_local)
    weight_grads = (g_query, g_key, g_value, g_gate, g_out, g_fc_gate, g_fc_up, g_down)
    summed = (
        lax.psum(weight_grads[0].astype(jnp.bfloat16), CONTEXT).astype(jnp.float32),
        lax.psum(weight_grads[1].astype(jnp.bfloat16), CONTEXT).astype(jnp.float32),
        lax.psum(weight_grads[2].astype(jnp.bfloat16), CONTEXT).astype(jnp.float32),
        lax.psum(weight_grads[3].astype(jnp.bfloat16), CONTEXT).astype(jnp.float32),
        lax.psum(weight_grads[4].astype(jnp.bfloat16), CONTEXT).astype(jnp.float32),
        lax.psum(weight_grads[5].astype(jnp.bfloat16), CONTEXT).astype(jnp.float32),
        lax.psum(weight_grads[6].astype(jnp.bfloat16), CONTEXT).astype(jnp.float32),
        lax.psum(weight_grads[7].astype(jnp.bfloat16), CONTEXT).astype(jnp.float32),
    )
    shards = (
        lax.psum_scatter(
            summed[0].astype(jnp.bfloat16), FSDP, scatter_dimension=0, tiled=True
        ).astype(jnp.float32),
        lax.psum_scatter(
            summed[1].astype(jnp.bfloat16), FSDP, scatter_dimension=0, tiled=True
        ).astype(jnp.float32),
        lax.psum_scatter(
            summed[2].astype(jnp.bfloat16), FSDP, scatter_dimension=0, tiled=True
        ).astype(jnp.float32),
        lax.psum_scatter(
            summed[3].astype(jnp.bfloat16), FSDP, scatter_dimension=0, tiled=True
        ).astype(jnp.float32),
        lax.psum_scatter(
            summed[4].astype(jnp.bfloat16), FSDP, scatter_dimension=1, tiled=True
        ).astype(jnp.float32),
        lax.psum_scatter(
            summed[5].astype(jnp.bfloat16), FSDP, scatter_dimension=0, tiled=True
        ).astype(jnp.float32),
        lax.psum_scatter(
            summed[6].astype(jnp.bfloat16), FSDP, scatter_dimension=0, tiled=True
        ).astype(jnp.float32),
        lax.psum_scatter(
            summed[7].astype(jnp.bfloat16), FSDP, scatter_dimension=1, tiled=True
        ).astype(jnp.float32),
    )
    return (
        output,
        grad_tokens,
        g_ln1,
        shards[0],
        shards[1],
        shards[2],
        shards[3],
        g_norm,
        shards[4],
        g_ln2,
        shards[5],
        shards[6],
        shards[7],
    )


F32 = jnp.float32
BF16 = jnp.bfloat16
BOTH_X = [(0, 2), (2, 0), (1, 3), (3, 1)]
UP_X = [(0, 2), (1, 3)]
DOWN_X = [(2, 0), (3, 1)]
CORES = [(0, 1), (1, 0), (2, 3), (3, 2)]
UP_Z = [[(0, 1), (1, 2), (2, 3)], [(1, 2), (2, 3)]]
DOWN_Z = [[(3, 2), (2, 1), (1, 0)], [(2, 1), (1, 0)]]
LAST_Z = [(2, 3), (1, 0)]
SCALE = 0.0625
ROWS, GAINS, STATES = range(3)


def cost(flops):
    return pl.CostEstimate(flops=3 * flops // 5, transcendentals=0, bytes_accessed=0)


COPYING = 2 << 30
DOWN_Z = [[(3, 2), (2, 1), (1, 0)], [(2, 1), (1, 0)], [(1, 0)]]


def over_x(value):
    return lax.ppermute(value, CONTEXT, BOTH_X)


def over_core(value):
    return lax.ppermute(value, CONTEXT, CORES)


def over_y(value):
    return lax.ppermute(value, TENSOR, [(0, 1), (1, 0)])


def tie(*values):
    return lax.optimization_barrier(values)


def butterfly(value, axis):
    size = lax.axis_size(axis)
    step = 1
    while step < size:
        value = value + lax.ppermute(value, axis, [(i, i ^ step) for i in range(size)])
        step *= 2
    return value


def quarter_of(weight, dim, index):
    size = weight.shape[dim] // 4
    return lax.dynamic_slice_in_dim(weight, index * size, size, dim)


def assemble_kernel(spot_ref, *refs):
    at = pl.program_id(0)
    for index, block in enumerate(refs[:8]):

        @pl.when(at == index)
        def _(block=block):
            refs[8][...] = block[...]


def assemble(blocks, spots, by_rows, size):
    shape = (2 * size, 4 * size) if by_rows else (4 * size, 2 * size)

    def spot(at, spots_ref):
        z_from, x_from = spots_ref[at], spots_ref[8 + at]
        return (x_from, z_from) if by_rows else (z_from, x_from)

    return pl.pallas_call(
        assemble_kernel,
        out_shape=jax.ShapeDtypeStruct(shape, BF16),
        grid_spec=pltpu.PrefetchScalarGridSpec(
            num_scalar_prefetch=1,
            grid=(8,),
            in_specs=[
                pl.BlockSpec((size, size), lambda at, spots_ref, row=row: (row, 0))
                for _, row in blocks
            ],
            out_specs=pl.BlockSpec((size, size), spot),
        ),
        compiler_params=pltpu.CompilerParams(vmem_limit_bytes=32 << 20),
        cost_estimate=cost(COPYING),
    )(spots, *(array for array, _ in blocks))


def sum_kernel(product, count, outs, *refs):
    lefts, rights, extras = refs[:count], refs[count : 2 * count], refs[2 * count : -outs]
    total = product(lefts[0][...], rights[0][...])
    for left, right in zip(lefts[1:], rights[1:]):
        total = total + product(left[...], right[...])
    for extra in extras:
        total = total + extra[...].astype(F32)
    size = total.shape[0] // outs
    for index, out_ref in enumerate(refs[-outs:]):
        out_ref[...] = total[index * size : (index + 1) * size].astype(out_ref.dtype)


def sum_of_products(product, lefts, rights, first, rows, kind, extras=(), outs=1, weight=1):
    by_columns = product is nn
    width = rights[0].shape[1 if by_columns else 0]
    block, tile = min(1024, rows), min(512, width)
    if outs > 1:
        block = rows

    def right_spec(right):
        if by_columns:
            return pl.BlockSpec((right.shape[0], tile), lambda n, m: (0, n))
        return pl.BlockSpec((tile, right.shape[1]), lambda n, m: (n, 0))

    def tile_spec(from_row, size):
        return pl.BlockSpec((size, tile), lambda n, m: (from_row // size + m, n))

    out_shape = [jax.ShapeDtypeStruct((rows // outs, width), kind)] * outs
    result = pl.pallas_call(
        partial(sum_kernel, product, len(lefts), outs),
        grid=(width // tile, rows // block),
        out_shape=out_shape,
        in_specs=[
            pl.BlockSpec((block, left.shape[1]), lambda n, m: (first // block + m, 0))
            for left in lefts
        ]
        + [right_spec(right) for right in rights]
        + [tile_spec(from_row, block) for _, from_row in extras],
        out_specs=[tile_spec(0, block // outs)] * outs,
        compiler_params=pltpu.CompilerParams(vmem_limit_bytes=60 << 20),
        cost_estimate=cost(2 * weight * rows * width * sum(left.shape[1] for left in lefts)),
    )(*lefts, *rights, *(array for array, _ in extras))
    return result[0] if outs == 1 else result


def quarter_kernel(spots_ref, left, right, *rest):
    total = tn(left[...], right[...])
    for extra in rest[:-1]:
        total = total + extra[...].astype(F32)
    rest[-1][...] = total.astype(BF16)


def quarter_product(left, right, index, extras=(), weight=1):
    tokens, width = left.shape
    size, block = right.shape[1] // 2, min(1024, width)
    return pl.pallas_call(
        quarter_kernel,
        out_shape=jax.ShapeDtypeStruct((width, size), BF16),
        grid_spec=pltpu.PrefetchScalarGridSpec(
            num_scalar_prefetch=1,
            grid=(width // block,),
            in_specs=[
                pl.BlockSpec((tokens, block), lambda m, at: (0, m)),
                pl.BlockSpec((tokens, size), lambda m, at: (0, at[0])),
            ]
            + [pl.BlockSpec((block, size), lambda m, at: (m, 0)) for _ in extras],
            out_specs=pl.BlockSpec((block, size), lambda m, at: (m, 0)),
        ),
        compiler_params=pltpu.CompilerParams(vmem_limit_bytes=60 << 20),
        cost_estimate=cost(2 * weight * tokens * width * size),
    )(index.reshape(1).astype(jnp.int32), left, right, *extras)


def split_kernel(left, right, out):
    out[0] = tn(left[...], right[...]).astype(BF16)


def split_product(left, right, count):
    tokens, rows = left.shape
    size = right.shape[1] // count
    return pl.pallas_call(
        split_kernel,
        grid=(count,),
        out_shape=jax.ShapeDtypeStruct((count, rows, size), BF16),
        in_specs=[
            pl.BlockSpec((tokens, rows), lambda n: (0, 0)),
            pl.BlockSpec((tokens, size), lambda n: (0, n)),
        ],
        out_specs=pl.BlockSpec((1, rows, size), lambda n: (n, 0, 0)),
        compiler_params=pltpu.CompilerParams(vmem_limit_bytes=60 << 20),
        cost_estimate=cost(2 * tokens * rows * size * count),
    )(left, right)


def unit_kernel(h_ref, w1_ref, w3_ref, d_hidden_ref, hidden_ref, d_a_ref, d_b_ref):
    fc_a, fc_b = nn(h_ref[...], w1_ref[...]), nn(h_ref[...], w3_ref[...])
    d_hidden = d_hidden_ref[...].astype(F32)
    sigma = jax.nn.sigmoid(fc_a)
    silu_a = fc_a * sigma
    hidden_ref[...] = (silu_a * fc_b).astype(BF16)
    d_a_ref[...] = (d_hidden * fc_b * (sigma * (1.0 + fc_a * (1.0 - sigma)))).astype(BF16)
    d_b_ref[...] = (d_hidden * silu_a).astype(BF16)


def hidden_units(h_two, w1, w3, d_hidden):
    rows, width = h_two.shape
    count = w1.shape[1]
    block, tile = min(512, rows), min(512, count)
    weight = pl.BlockSpec((width, tile), lambda n, m: (0, n))
    spot = pl.BlockSpec((block, tile), lambda n, m: (m, n))
    return pl.pallas_call(
        unit_kernel,
        grid=(count // tile, rows // block),
        out_shape=[jax.ShapeDtypeStruct((rows, count), BF16)] * 3,
        in_specs=[pl.BlockSpec((block, width), lambda n, m: (m, 0)), weight, weight, spot],
        out_specs=[spot] * 3,
        compiler_params=pltpu.CompilerParams(vmem_limit_bytes=60 << 20),
        cost_estimate=cost(4 * rows * width * count),
    )(h_two, w1, w3, d_hidden)


def stack_kernel(*refs):
    count = len(refs) - 4
    shares, out_ref, held, sems_in, sems_out = refs[:count], *refs[count:]
    rows = shares[0].shape[0]
    ins, outs = [], []
    for index, share in enumerate(shares):
        ins.append(pltpu.make_async_copy(share, held.at[index], sems_in.at[index]))
        spot = out_ref.at[pl.ds(index * rows, rows)]
        outs.append(pltpu.make_async_copy(held.at[index], spot, sems_out.at[index]))
    for copy in ins:
        copy.start()
    for copy, onward in zip(ins, outs):
        copy.wait()
        onward.start()
    for onward in outs:
        onward.wait()


def stack_rows(*shares):
    rows, width = shares[0].shape
    count = len(shares)
    return pl.pallas_call(
        stack_kernel,
        out_shape=jax.ShapeDtypeStruct((count * rows, width), shares[0].dtype),
        in_specs=[pl.BlockSpec(memory_space=pl.ANY)] * count,
        out_specs=pl.BlockSpec(memory_space=pl.ANY),
        scratch_shapes=[
            pltpu.VMEM((count, rows, width), shares[0].dtype),
            pltpu.SemaphoreType.DMA((count,)),
            pltpu.SemaphoreType.DMA((count,)),
        ],
        compiler_params=pltpu.CompilerParams(vmem_limit_bytes=48 << 20),
        cost_estimate=cost(2 * COPYING),
    )(*shares)


def nn(left, right):
    return lax.dot_general(left, right, (((1,), (0,)), ((), ())), preferred_element_type=F32)


def nt(left, right):
    return lax.dot_general(left, right, (((1,), (1,)), ((), ())), preferred_element_type=F32)


def tn(left, right):
    return lax.dot_general(left, right, (((0,), (0,)), ((), ())), preferred_element_type=F32)


def where_is(whole, chunk, piece_len):
    share_len = piece_len // 2
    spots = []
    for shape, dim in (((piece_len, 1), 0), ((1, piece_len), 1)):
        at = lax.broadcasted_iota(jnp.int32, shape, dim) + whole[2] * share_len
        spots.append(jnp.where(at >= piece_len, at - piece_len, at))
    start = whole[0] * (2 * piece_len) + chunk * piece_len
    return spots[0], spots[1], start


def document(whole, spot):
    seq = pl.program_id(0)
    first, second = whole[3 + 2 * seq], whole[4 + 2 * seq]
    return jnp.where(spot >= second, 2, jnp.where(spot >= first, 1, 0))


def fade(gap, log_keep):
    return jnp.exp(jnp.maximum(gap, 0).astype(F32) * log_keep)


def piece_terms(whole, log_keep, chunk, piece_len):
    rows, cols, start = where_is(whole, chunk, piece_len)
    doc_rows, doc_cols = document(whole, start + rows), document(whole, start + cols)
    before, last = document(whole, start - 1), document(whole, start + piece_len - 1)
    within = jnp.where(
        (rows >= cols) & (doc_rows == doc_cols), fade(rows - cols, log_keep) * SCALE, 0.0
    )
    inflow = jnp.where(doc_rows == before, fade(rows + 1, log_keep) * SCALE, 0.0)
    outflow = jnp.where(doc_rows == last, fade(piece_len - 1 - rows, log_keep), 0.0)
    whole_gap = jnp.full((1, 1), piece_len, jnp.int32)
    over = jnp.where(before == last, fade(whole_gap, log_keep), 0.0)
    return within, inflow, outflow, over


def piece_of(ref, whole, chunk):
    group = lax.rem(chunk + whole[1], 2) * 2
    value = ref[pl.ds(group, 2), 0]
    return value.reshape(value.shape[0] * value.shape[1], value.shape[2])


def put_piece(ref, whole, chunk, value):
    group = lax.rem(chunk + whole[1], 2) * 2
    ref[pl.ds(group, 2), 0] = value.astype(ref.dtype).reshape(2, value.shape[0] // 2, value.shape[1])


def split_kq(ref, whole, chunk):
    both = piece_of(ref, whole, chunk)
    width = both.shape[1] // 2
    return both[:, :width], both[:, width:]


def update_kernel(whole, keeps, kq_ref, v_ref, out_ref):
    log_keep = keeps[pl.program_id(1)]
    piece_len = 2 * kq_ref.shape[2]
    total = jnp.zeros(out_ref.shape[2:], F32)
    for chunk in range(2):
        rows, _, start = where_is(whole, chunk, piece_len)
        last = document(whole, whole[0] * (2 * piece_len) + 2 * piece_len - 1)
        gap = (2 - chunk) * piece_len - 1 - rows
        weight = jnp.where(document(whole, start + rows) == last, fade(gap, log_keep), 0.0)
        keys, _ = split_kq(kq_ref, whole, chunk)
        values = piece_of(v_ref, whole, chunk)
        total = total + tn((keys.astype(F32) * weight).astype(BF16), values)
    out_ref[0, 0] = total.astype(BF16)


def next_state(state, keys, values, outflow, over):
    return over * state + tn((keys.astype(F32) * outflow).astype(BF16), values)


def forward_kernel(
    whole, keeps, kq_ref, v_ref, gate_ref, state_ref, gain_ref, gated_ref, retained_ref
):
    log_keep = keeps[pl.program_id(1)]
    piece_len = 2 * kq_ref.shape[2]
    state = state_ref[0, 0].astype(F32)
    for chunk in range(2):
        within, inflow, outflow, over = piece_terms(whole, log_keep, chunk, piece_len)
        keys, query = split_kq(kq_ref, whole, chunk)
        values = piece_of(v_ref, whole, chunk)
        scores = (nt(query, keys) * within).astype(BF16)
        retained = nn(scores, values) + inflow * nn(query, state.astype(BF16))
        if chunk == 0:
            state = next_state(state, keys, values, outflow, over)
        put_piece(retained_ref, whole, chunk, retained)
        normed, _, _ = norm_rows(retained, gain_ref[0], 0.01)
        gate = piece_of(gate_ref, whole, chunk).astype(F32)
        put_piece(gated_ref, whole, chunk, gate * jax.nn.sigmoid(gate) * normed)


def norm_back_kernel(
    whole,
    keeps,
    d_gated_ref,
    gate_ref,
    retained_ref,
    kq_ref,
    gain_ref,
    d_gate_ref,
    d_retained_ref,
    d_gain_ref,
    leaving_ref,
):
    log_keep = keeps[pl.program_id(1)]
    piece_len = 2 * kq_ref.shape[2]
    total = jnp.zeros(leaving_ref.shape[2:], F32)
    gain = gain_ref[0]
    d_gain = jnp.zeros(gain.shape, F32)
    for chunk in range(2):
        rows, _, start = where_is(whole, chunk, piece_len)
        before = document(whole, whole[0] * (2 * piece_len) - 1)
        gap = chunk * piece_len + rows + 1
        weight = jnp.where(
            document(whole, start + rows) == before, fade(gap, log_keep) * SCALE, 0.0
        )
        _, query = split_kq(kq_ref, whole, chunk)
        retained = piece_of(retained_ref, whole, chunk).astype(F32)
        normed, unit, scale = norm_rows(retained, gain, 0.01)
        gate = piece_of(gate_ref, whole, chunk).astype(F32)
        d_gated = piece_of(d_gated_ref, whole, chunk).astype(F32)
        sigma = jax.nn.sigmoid(gate)
        put_piece(
            d_gate_ref, whole, chunk, d_gated * normed * sigma * (1.0 + gate * (1.0 - sigma))
        )
        d_normed = d_gated * gate * sigma
        d_gain = d_gain + jnp.sum(d_normed * unit, axis=0, keepdims=True)
        d_retained = norm_back(d_normed, unit, scale, gain)
        put_piece(d_retained_ref, whole, chunk, d_retained)
        total = total + tn(query, (d_retained * weight).astype(BF16))
    d_gain_ref[0, 0] = d_gain
    leaving_ref[0, 0] = total.astype(BF16)


def backward_kernel(
    whole, keeps, kq_ref, v_ref, d_retained_ref, state_ref, d_state_ref, d_kq_ref, d_v_ref
):
    log_keep = keeps[pl.program_id(1)]
    piece_len = 2 * kq_ref.shape[2]
    terms = [piece_terms(whole, log_keep, chunk, piece_len) for chunk in range(2)]
    state = state_ref[0, 0].astype(F32)
    keys, _ = split_kq(kq_ref, whole, 0)
    _, _, outflow, over = terms[0]
    states = [state, next_state(state, keys, piece_of(v_ref, whole, 0), outflow, over)]
    d_state = d_state_ref[0, 0].astype(F32)
    for chunk in (1, 0):
        within, inflow, outflow, over = terms[chunk]
        keys, query = split_kq(kq_ref, whole, chunk)
        values = piece_of(v_ref, whole, chunk)
        d_ret = piece_of(d_retained_ref, whole, chunk)
        state_low, d_state_low = states[chunk].astype(BF16), d_state.astype(BF16)
        scores = (nt(query, keys) * within).astype(BF16)
        d_scores = (nt(d_ret, values) * within).astype(BF16)
        d_values = tn(scores, d_ret) + outflow * nn(keys, d_state_low)
        put_piece(d_v_ref, whole, chunk, d_values)
        d_query = nn(d_scores, keys) + inflow * nt(d_ret, state_low)
        d_keys = tn(d_scores, query) + outflow * nt(values, d_state_low)
        put_piece(d_kq_ref, whole, chunk, jnp.concatenate([d_keys, d_query], axis=1))
        if chunk == 1:
            entering = tn(query, (d_ret.astype(F32) * inflow).astype(BF16))
            d_state = over * d_state + entering


def per_head(kernel, scalars, blocks, outs, flops=12 << 30):
    def spec(array, kind):
        if kind == ROWS:
            width = array.shape[3] // heads
            return pl.BlockSpec((4, 1, array.shape[2], width), lambda b, h, *_: (0, b, 0, h))
        if kind == GAINS:
            return pl.BlockSpec((1, *array.shape[1:]), lambda b, h, *_: (h, 0, 0))
        return pl.BlockSpec((1, 1, *array.shape[2:]), lambda b, h, *_: (b, h, 0, 0))

    heads = scalars[1].shape[0]
    seq_count = (scalars[0].shape[0] - 3) // 2
    return pl.pallas_call(
        kernel,
        out_shape=[a for a, _ in outs],
        grid_spec=pltpu.PrefetchScalarGridSpec(
            num_scalar_prefetch=2,
            grid=(seq_count, heads),
            in_specs=[spec(*block) for block in blocks],
            out_specs=[spec(*out) for out in outs],
        ),
        compiler_params=pltpu.CompilerParams(vmem_limit_bytes=56 << 20),
        cost_estimate=cost(flops),
    )(*scalars, *(a for a, _ in blocks))


def both_quarters(mine, across, first, dim):
    return jnp.concatenate(
        [jnp.where(first, mine, across), jnp.where(first, across, mine)], axis=dim
    )


def paired_body(
    tokens,
    segments,
    forget,
    ln1_gain,
    w_query,
    w_key,
    w_value,
    w_gate,
    norm_gain,
    w_out,
    ln2_gain,
    w_fc_gate,
    w_fc_up,
    w_fc_down,
    cotangent,
):
    place = lax.axis_index(CONTEXT)
    x_at, core, y_at = place // 2, place % 2, lax.axis_index(TENSOR)
    z_at = lax.axis_index(FSDP)
    heads = forget.shape[0] // 2
    qk_width = w_query.shape[1] // forget.shape[0]
    v_width = w_value.shape[1] // forget.shape[0]
    width = tokens.shape[2]
    seq_count, share_len = tokens.shape[0], tokens.shape[1]
    share_rows = seq_count * share_len
    piece_len = 2 * share_len
    chip_len = 2 * piece_len
    v_half = heads * v_width
    forget_half = lax.dynamic_slice_in_dim(forget, core * heads, heads)
    gain_half = lax.dynamic_slice_in_dim(norm_gain, core * v_half, v_half)

    def part(array, first, last):
        return array[first * share_rows : last * share_rows]

    def unit(x_index):
        q = core * 2 + x_index
        key_query = [quarter_of(w_key, 1, q), quarter_of(w_query, 1, q)]
        return [
            jnp.concatenate(key_query, axis=1),
            quarter_of(w_value, 1, q),
            quarter_of(w_gate, 1, q),
            quarter_of(w_out, 0, q),
            quarter_of(w_fc_down, 0, q),
            quarter_of(w_fc_gate, 1, q),
            quarter_of(w_fc_up, 1, q),
        ]

    KQ, V, G, O, W2, W1, W3 = range(7)
    by_rows = [False, False, False, True, True, False, False]
    own, sibling = unit(x_at), unit(1 - x_at)
    size = own[0].shape[0]
    z_last = lax.axis_size(FSDP) - 1
    z_count = z_last + 1
    s_one = jnp.where(z_at == 0, 1, z_at - 1)
    s_three = jnp.where(z_at == z_last, 0, jnp.where(z_at == 1, 2, z_last))
    z_spots = [z_at, s_one, z_at ^ 2, s_three]
    spots = jnp.stack(z_spots + z_spots + [x_at] * 4 + [1 - x_at] * 4).astype(jnp.int32)
    groups = [[KQ, V], [G, O], [W2, W1, W3]]
    slots, across = [[], [], []], [[], [], []]

    def weight(index):
        at, row = next((i, g.index(index)) for i, g in enumerate(groups) if index in g)
        blocks = [(own[index], 0)] + [(array, row) for array in slots[at]]
        blocks += [(sibling[index], 0)] + [(array, row) for array in across[at]]
        return assemble(blocks, spots, by_rows[index], size)

    env = SimpleNamespace()
    firsts = jnp.sum((segments == 0).astype(jnp.int32), axis=1)
    seconds = jnp.sum((segments <= 1).astype(jnp.int32), axis=1)
    starts = jnp.stack([firsts, seconds], axis=1).reshape(-1)
    whole = jnp.concatenate([jnp.stack([x_at, core, y_at]).astype(jnp.int32), starts])
    scalars = (whole, jnp.log(1.0 - forget_half))
    gains = gain_half.reshape(heads, 1, v_width)
    state_type = jax.ShapeDtypeStruct((seq_count, heads, qk_width, v_width), BF16)
    rows_type = jax.ShapeDtypeStruct((4, seq_count, share_len, v_half), BF16)
    kq_type = jax.ShapeDtypeStruct((4, seq_count, share_len, 2 * heads * qk_width), BF16)
    gain_type = jax.ShapeDtypeStruct((seq_count, heads, 1, v_width), F32)

    def shaped(rows_in):
        return rows_in.reshape(4, seq_count, share_len, -1)

    def flat(rows_in):
        return rows_in.reshape(4 * share_rows, -1)

    x_share = tokens.reshape(share_rows, width).astype(F32)
    cot_share = cotangent.reshape(share_rows, width)

    def work_norm():
        h1, ln1_normed, ln1_scale = norm_rows(x_share, ln1_gain)
        env.ln1 = (ln1_normed, ln1_scale)
        env.h = h1.astype(BF16)
        env.hy = over_y(env.h)
        return [env.h]

    def work_core():
        env.hc, env.hcy = over_core(env.h), over_core(env.hy)
        env.cy = over_y(cot_share)
        return []

    def work_rows():
        env.h_one = stack_rows(env.h, env.hy, env.hc, env.hcy)
        return [env.h_one]

    def work_kq():
        env.wkq = weight(KQ)
        env.kq = sum_of_products(nn, [env.h_one], [env.wkq], 0, 4 * share_rows, BF16)
        return [env.kq]

    def work_v():
        env.wv = weight(V)
        env.v = sum_of_products(nn, [env.h_one], [env.wv], 0, 4 * share_rows, BF16)
        return [env.v]

    def work_state():
        (update,) = per_head(
            update_kernel,
            scalars,
            [(shaped(env.kq), ROWS), (shaped(env.v), ROWS)],
            [(state_type, STATES)],
            4 << 30,
        )
        env.state = lax.ppermute(update, CONTEXT, UP_X)
        env.cc, env.ccy = over_core(cot_share), over_core(env.cy)
        return [update]

    def work_gate():
        env.wg = weight(G)
        env.gate = sum_of_products(nn, [env.h_one], [env.wg], 0, 4 * share_rows, BF16)
        return [env.gate]

    def work_retained():
        gated, env.retained = per_head(
            forward_kernel,
            scalars,
            [
                (shaped(env.kq), ROWS),
                (shaped(env.v), ROWS),
                (shaped(env.gate), ROWS),
                (env.state, STATES),
                (gains, GAINS),
            ],
            [(rows_type, ROWS), (rows_type, ROWS)],
        )
        env.gated = flat(gated)
        return [env.gated]

    def work_out_far():
        env.wo = weight(O)
        own, other = sum_of_products(
            nn, [env.gated], [env.wo], 2 * share_rows, 2 * share_rows, BF16, (), 2
        )
        env.far_other, env.far_own = over_core(other), over_core(own)
        return [other]

    def work_out_near():
        near = sum_of_products(
            nn, [env.gated], [env.wo], share_rows, share_rows, BF16, [(env.far_other, 0)]
        )
        env.near = over_y(near)
        return [near]

    def work_out_own():
        extras = [(env.far_own, 0), (tokens.reshape(share_rows, width), 0)]
        env.own = sum_of_products(nn, [env.gated], [env.wo], 0, share_rows, F32, extras)
        return [env.own]

    def work_cot():
        env.cot = stack_rows(cot_share, env.cy, env.cc, env.ccy)
        return [env.cot]

    def work_d_hidden():
        env.w2 = weight(W2)
        env.d_hidden = sum_of_products(nt, [env.cot], [env.w2], 0, 4 * share_rows, BF16)
        return [env.d_hidden]

    def work_middle():
        env.middle = env.own + env.near.astype(F32)
        h2, ln2_normed, ln2_scale = norm_rows(env.middle, ln2_gain)
        env.ln2 = (ln2_normed, ln2_scale)
        env.h2 = h2.astype(BF16)
        env.h2y, env.h2c = over_y(env.h2), over_core(env.h2)
        return [env.h2]

    def work_up():
        env.w1 = weight(W1)
        return [env.w1]

    def work_h2():
        env.w3 = weight(W3)
        env.h2y, env.d_hidden, env.w1, env.w3 = tie(env.h2y, env.d_hidden, env.w1, env.w3)
        env.h2cy = over_core(env.h2y)
        return [env.w3]

    plan = [
        [work_norm],
        [],
        [work_core],
        [work_rows],
        [work_kq],
        [work_v, work_state],
        [work_cot, work_gate],
        [work_retained, work_out_far],
        [work_out_near, work_out_own],
        [work_middle],
        [work_d_hidden, work_up, work_h2],
    ]
    stacks = [jnp.concatenate([own[index] for index in group], axis=0) for group in groups]
    up = down = kept = to_send = None
    for tick, works in enumerate(plan):
        at, hop = divmod(tick, 3)
        moving = at < len(groups)
        sent, to_send = to_send, None
        if sent is not None:
            slots[sent[0]].append(sent[1])
            across[sent[0]].append(over_x(sent[1]))
        if moving and hop < 2:
            up = stacks[at] if hop == 0 else up
            down = stacks[at] if hop == 0 else down
            got = [lax.ppermute(up, FSDP, UP_Z[hop]), lax.ppermute(down, FSDP, DOWN_Z[hop])]
        elif moving:
            got = [lax.ppermute(slots[at][1], FSDP, LAST_Z)]
        held = []
        for work in works:
            held += work()
        if not moving:
            continue
        names = [n for n in ("h_one", "kq", "gate", "gated", "cot") if hasattr(env, n)]
        held = held + ([across[sent[0]][-1]] if sent is not None else [])
        ahead = stacks[at + 1 : at + 2] if hop == 2 else []
        tied = list(tie(*got, *[getattr(env, n) for n in names], *ahead, *held))
        got = [tied.pop(0) for _ in got]
        for n in names:
            setattr(env, n, tied.pop(0))
        if hasattr(env, "far_other"):
            env.far_other = tie(env.far_other, *got)[0]
        if ahead:
            stacks[at + 1] = tied.pop(0)
        if hop == 0:
            up, down = kept = got
            to_send = (at, jnp.where(z_at > 0, up, down))
        elif hop == 1:
            up, down = got
            to_send = (at, jnp.where(z_at >= 2, up, down))
        else:
            ends = (z_at == 0) | (z_at == z_last)
            to_send = (at, jnp.where(ends, got[0], kept[1]))

    h_one, gated, gate_pre = env.h_one, env.gated, env.gate
    wkq, wv, wg, wo, w1, w2, w3 = env.wkq, env.wv, env.wg, env.wo, env.w1, env.w2, env.w3
    cot_full, d_hidden, middle = env.cot, env.d_hidden, env.middle

    token = [h_one]

    def step(run, *args):
        *args, _ = tie(*args, token[0])
        out = run(*args)
        token[0] = out[0] if isinstance(out, (tuple, list)) else out
        return out

    def far_product(product, lefts, rights, weight=1):
        def run(*arrays):
            return sum_of_products(
                product, arrays, rights, 2 * share_rows, 2 * share_rows, BF16, (), 2, weight
            )

        own, other = step(run, *lefts)
        return over_core(other), over_core(own)

    def whole_product(product, lefts, rights, first, rows, kind, *extras, weight=1):
        count = len(lefts)

        def run(*arrays):
            added = [(a, row) for a, (_, row) in zip(arrays[count:], extras)]
            return sum_of_products(
                product,
                arrays[:count],
                rights,
                first * share_rows,
                rows * share_rows,
                kind,
                added,
                1,
                weight,
            )

        return step(run, *lefts, *(a for a, _ in extras))

    def theirs(left, right):
        return over_x(step(lambda a, b: quarter_product(a, b, 1 - x_at), left, right))

    def ours(left, right, got):
        total = step(lambda a, b, c: quarter_product(a, b, x_at, [c]), left, right, got)
        return lax.psum_scatter(total, FSDP, scatter_dimension=0, tiled=True)

    def chip_rows(left, right):
        total = step(lambda a, b: split_product(a, b, z_count), left, right)
        return lax.psum_scatter(total, FSDP, scatter_dimension=0, tiled=False)

    def begin_finish(*mine):
        mine = step(lambda *a: jnp.concatenate(a, axis=0), *mine)
        return mine, over_x(mine)

    def end_finish(firsts, mine, beside):
        def join(mine, beside):
            blocks, row = [], 0
            for x_summed in firsts:
                count = 1 if x_summed else 2
                one, other = (a[row * size : (row + count) * size] for a in (mine, beside))
                if x_summed:
                    blocks += [jnp.where(x_at == 0, one, other), jnp.where(x_at == 0, other, one)]
                else:
                    blocks.append((one.astype(F32) + other.astype(F32)).astype(BF16))
                row += count
            return jnp.concatenate(blocks, axis=0)

        both = step(join, mine, beside)
        return both, over_core(both)

    def quarters(pair, at):
        both, other = pair
        mine, theirs = (a[2 * at * size : (2 * at + 2) * size] for a in (both, other))
        first, second = jnp.where(core == 0, mine, theirs), jnp.where(core == 0, theirs, mine)
        return [first[:size], first[size:], second[:size], second[size:]]

    def shard(pair, at, rows):
        return jnp.concatenate(quarters(pair, at), axis=1 - int(rows)).astype(F32)

    h_two = stack_rows(env.h2, env.h2y, env.h2c, env.h2cy)
    hidden, d_fca, d_fcb = step(hidden_units, h_two, w1, w3, d_hidden)

    fc_lefts, fc_rights = (d_fca, d_fcb), (w1, w3)
    far_other, far_own = far_product(nt, fc_lefts, fc_rights)
    near = over_y(whole_product(nt, fc_lefts, fc_rights, 1, 1, BF16, (far_other, 0)))
    down_mine = chip_rows(hidden, cot_full)
    gate_got = theirs(h_two, d_fca)
    own_part = whole_product(nt, fc_lefts, fc_rights, 0, 1, F32, (far_own, 0))
    up_got = theirs(h_two, d_fcb)
    out_far_other, out_far_own = far_product(nn, [hidden], [w2])

    def middle_back(own_part, near):
        d_h2 = own_part + near.astype(F32)
        ln2_normed, ln2_scale = env.ln2
        d_middle = cot_share.astype(F32) + norm_back(d_h2, ln2_normed, ln2_scale, ln2_gain)
        return d_middle.astype(BF16), d_middle, jnp.sum(d_h2 * ln2_normed, axis=0)

    d_mid_low, d_middle, g_ln2 = step(middle_back, own_part, near)
    d_mid_y, d_mid_c = over_y(d_mid_low), over_core(d_mid_low)
    fc_gate_mine = ours(h_two, d_fca, gate_got)
    out_near = whole_product(nn, [hidden], [w2], 1, 1, BF16, (out_far_other, 0))
    out_own = whole_product(nn, [hidden], [w2], 0, 1, F32, (out_far_own, 0), (middle, 0))
    d_mid_y, out_near, up_got = step(lambda *a: a, d_mid_y, out_near, up_got)
    d_mid_cy = over_core(d_mid_y)
    out_near = over_y(out_near)
    down_begun = begin_finish(down_mine)
    fc_up_mine = ours(h_two, d_fcb, up_got)

    def gate_back(share, y, c, cy):
        d_branch = stack_rows(share, y, c, cy)
        return sum_of_products(nt, [d_branch], [wo], 0, 4 * share_rows, BF16), d_branch

    d_gated, d_branch = step(gate_back, d_mid_low, d_mid_y, d_mid_c, d_mid_cy)
    down_beside, d_gated = tie(down_begun[1], d_gated)
    kq, values, state_in = shaped(env.kq), shaped(env.v), env.state

    def retained_back(d_gated, kq):
        return per_head(
            norm_back_kernel,
            scalars,
            [
                (shaped(d_gated), ROWS),
                (shaped(gate_pre), ROWS),
                (env.retained, ROWS),
                (kq, ROWS),
                (gains, GAINS),
            ],
            [(rows_type, ROWS), (rows_type, ROWS), (gain_type, STATES), (state_type, STATES)],
        )

    d_gate, d_retained, g_norm, leaving = step(retained_back, d_gated, kq)
    d_gate = flat(d_gate)
    g_norm = jnp.sum(g_norm, axis=0).reshape(v_half)
    state_grad = lax.ppermute(leaving, CONTEXT, DOWN_X)
    out_mine = chip_rows(gated, d_branch)
    gg_theirs = step(lambda a, b: quarter_product(a, b, 1 - x_at, (), 0), h_one, d_gate)
    state_grad, gg_theirs = tie(state_grad, gg_theirs)
    gg_got = over_x(gg_theirs)

    def pair_back(d_retained, state_grad):
        return per_head(
            backward_kernel,
            scalars,
            [
                (kq, ROWS),
                (values, ROWS),
                (d_retained, ROWS),
                (state_in, STATES),
                (state_grad, STATES),
            ],
            [(kq_type, ROWS), (rows_type, ROWS)],
        )

    g_down = end_finish([False], down_begun[0], down_beside)
    dkq_low, dv_low = step(pair_back, d_retained, state_grad)
    dkq_low, dv_low = flat(dkq_low), flat(dv_low)
    v_got = theirs(h_one, dv_low)
    kq_got = theirs(h_one, dkq_low)
    h1_lefts, h1_rights = (dkq_low, dv_low, d_gate), (wkq, wv, wg)
    output = step(lambda a, b: (a + b.astype(F32)).astype(BF16), out_own, out_near)
    fc_gate_mine, gg_got = tie(fc_gate_mine, gg_got)
    gg_mine = ours(h_one, d_gate, gg_got)
    far_other, far_own = far_product(nt, h1_lefts, h1_rights, 0)
    v_mine = ours(h_one, dv_low, v_got)
    near = over_y(whole_product(nt, h1_lefts, h1_rights, 1, 1, BF16, (far_other, 0), weight=0))
    own_part = whole_product(nt, h1_lefts, h1_rights, 0, 1, F32, (far_own, 0), weight=0)
    fc_begun = begin_finish(fc_gate_mine, fc_up_mine)
    out_mine, kq_got = tie(out_mine, kq_got)
    kq_mine = ours(h_one, dkq_low, kq_got)

    def tokens_back(own_part, near):
        d_h1 = own_part + near.astype(F32)
        ln1_normed, ln1_scale = env.ln1
        grad = d_middle + norm_back(d_h1, ln1_normed, ln1_scale, ln1_gain)
        return grad, jnp.sum(d_h1 * ln1_normed, axis=0)

    grad_tokens, g_ln1 = step(tokens_back, own_part, near)
    out_begun = begin_finish(out_mine, gg_mine)
    g_fc = end_finish([True, True], *fc_begun)
    v_begun = begin_finish(v_mine)
    kq_begun = begin_finish(kq_mine)
    g_out = end_finish([False, True], *out_begun)
    g_value = end_finish([True], *v_begun)
    g_kq = end_finish([True], *kq_begun)
    sides = quarters(g_kq, 0)
    g_key = jnp.concatenate([side[:, :qk_width] for side in sides], axis=1).astype(F32)
    g_query = jnp.concatenate([side[:, qk_width:] for side in sides], axis=1).astype(F32)

    norm_size = lax.axis_size(TENSOR) * norm_gain.shape[0]
    norm_all = lax.dynamic_update_slice_in_dim(
        jnp.zeros((norm_size,), F32), g_norm, (2 * y_at + core) * v_half, 0
    )
    gain_sums = jnp.concatenate([g_ln1, g_ln2, norm_all])
    for axis in (TENSOR, FSDP, CONTEXT):
        gain_sums = butterfly(gain_sums, axis)
    g_ln1, g_ln2 = gain_sums[:width], gain_sums[width : 2 * width]
    g_norm = lax.dynamic_slice_in_dim(
        gain_sums, 2 * width + y_at * norm_gain.shape[0], norm_gain.shape[0]
    )
    return (
        output.reshape(tokens.shape),
        grad_tokens.reshape(tokens.shape),
        g_ln1,
        g_query,
        g_key,
        shard(g_value, 0, False),
        shard(g_out, 1, False),
        g_norm,
        shard(g_out, 0, True),
        g_ln2,
        shard(g_fc, 0, False),
        shard(g_fc, 1, False),
        shard(g_down, 0, True),
    )


def body(tensor_size, *arrays):
    heads_here = arrays[2].shape[0]
    paired = tensor_size == 2 and heads_here % 2 == 0 and lax.axis_size(CONTEXT) == 4
    paired = paired and lax.axis_size(FSDP) == 4
    return (paired_body if paired else general_body)(*arrays)


def solution(mesh):
    in_specs = (
        P(FSDP, (CONTEXT, TENSOR), None),
        P(FSDP, None),
        P(TENSOR),
        P(),
        P(FSDP, TENSOR),
        P(FSDP, TENSOR),
        P(FSDP, TENSOR),
        P(FSDP, TENSOR),
        P(TENSOR),
        P(TENSOR, FSDP),
        P(),
        P(FSDP, TENSOR),
        P(FSDP, TENSOR),
        P(TENSOR, FSDP),
        P(FSDP, (CONTEXT, TENSOR), None),
    )
    out_specs = (
        P(FSDP, (CONTEXT, TENSOR), None),
        P(FSDP, (CONTEXT, TENSOR), None),
        P(),
        P(FSDP, TENSOR),
        P(FSDP, TENSOR),
        P(FSDP, TENSOR),
        P(FSDP, TENSOR),
        P(TENSOR),
        P(TENSOR, FSDP),
        P(),
        P(FSDP, TENSOR),
        P(FSDP, TENSOR),
        P(TENSOR, FSDP),
    )
    return jax.shard_map(partial(body, mesh.shape[TENSOR]), mesh=mesh, in_specs=in_specs, out_specs=out_specs, check_vma=False)
```

```python
from functools import partial
from types import SimpleNamespace

import jax
import jax.numpy as jnp
from jax import lax
from jax.experimental import pallas as pl
from jax.experimental.pallas import tpu as pltpu
from jax.sharding import PartitionSpec as P

FSDP, CONTEXT, TENSOR = "fsdp", "context", "tensor"

careful = partial(jnp.einsum, precision=lax.Precision.HIGH)


def entering(part, axis, combine, identity):
    place = lax.axis_index(axis)
    gathered = jax.tree.map(lambda a: lax.all_gather(a, axis), part)
    state = jax.tree.map(lambda a, e: jnp.zeros_like(a) + jnp.asarray(e, a.dtype), part, identity)

    def one(step, state):
        return combine(
            state, jax.tree.map(lambda a: lax.dynamic_index_in_dim(a, step, 0, False), gathered)
        )

    return lax.fori_loop(0, place, one, state)


def carried_in(value, axis, combine, identity):
    count, place = (lax.axis_size(axis), lax.axis_index(axis))
    everything = jax.tree.map(
        lambda part, kind: lax.all_gather(part.astype(kind), axis),
        value,
        jax.tree.map(lambda a: jnp.bfloat16 if a.dtype == jnp.float32 else a.dtype, value),
    )
    start = jax.tree.map(
        lambda part, zero: jnp.broadcast_to(jnp.asarray(zero, part.dtype), part.shape),
        value,
        identity,
    )

    def step(k, before):
        at = count - 1 - k
        reached = at > place
        new = combine(
            before, jax.tree.map(lambda part, own: part[at].astype(own.dtype), everything, value)
        )
        return jax.tree.map(lambda a, b: jnp.where(reached, a, b), new, before)

    return lax.fori_loop(0, count, step, start)


def norm_rows(values, gain_vec, epsilon=1e-05):
    centred = values - jnp.mean(values, axis=-1, keepdims=True)
    scale = lax.rsqrt(jnp.mean(centred * centred, axis=-1, keepdims=True) + epsilon)
    normed = centred * scale
    return (normed * gain_vec, normed, scale)


def norm_back(grad_in, normed, scale, gain_vec):
    d_normed = grad_in * gain_vec
    first_mean = jnp.mean(d_normed, axis=-1, keepdims=True)
    second_mean = jnp.mean(d_normed * normed, axis=-1, keepdims=True)
    return scale * (d_normed - first_mean - normed * second_mean)


def swish_slope(values):
    sigma = jax.nn.sigmoid(values)
    return sigma * (1.0 + values * (1.0 - sigma))


def compose(earlier, latter):
    return (earlier[0] * latter[0], latter[0][:, :, None, None] * earlier[1] + latter[1])


def share_gather(piece):
    return lax.all_gather(piece, TENSOR, axis=1, tiled=True)


def branch_sum(terms):
    return lax.psum_scatter(terms, TENSOR, scatter_dimension=1, tiled=True)


def input_sum(terms):
    return lax.psum_scatter(
        terms.astype(jnp.bfloat16), TENSOR, scatter_dimension=1, tiled=True
    ).astype(jnp.float32)


def mixer_fetch(w_query, w_key, w_value, w_gate, w_out):
    return (
        lax.all_gather(w_query, FSDP, axis=0, tiled=True),
        lax.all_gather(w_key, FSDP, axis=0, tiled=True),
        lax.all_gather(w_value, FSDP, axis=0, tiled=True),
        lax.all_gather(w_gate, FSDP, axis=0, tiled=True),
        lax.all_gather(w_out, FSDP, axis=1, tiled=True),
    )


def mlp_fetch(w_fc_gate, w_fc_up, w_fc_down):
    return (
        lax.all_gather(w_fc_gate, FSDP, axis=0, tiled=True),
        lax.all_gather(w_fc_up, FSDP, axis=0, tiled=True),
        lax.all_gather(w_fc_down, FSDP, axis=1, tiled=True),
    )


def product(form, left, right):
    return jnp.einsum(form, left, right, preferred_element_type=jnp.float32)


def general_body(
    tokens,
    segments,
    forget,
    ln1_gain,
    w_query,
    w_key,
    w_value,
    w_gate,
    norm_gain,
    w_out,
    ln2_gain,
    w_fc_gate,
    w_fc_up,
    w_fc_down,
    cotangent,
):
    heads_here = forget.shape[0]
    qk_width = w_query.shape[1] // heads_here
    v_width = w_value.shape[1] // heads_here
    v_local = heads_here * v_width
    gain_heads = norm_gain.reshape(heads_here, v_width)
    x_share = tokens.astype(jnp.float32)
    h1_share, ln1_normed, ln1_scale = norm_rows(x_share, ln1_gain)
    h_one = share_gather(h1_share.astype(jnp.bfloat16))
    wq_all, wk_all, wv_all, wg_all, wo_all = mixer_fetch(w_query, w_key, w_value, w_gate, w_out)
    seq_count, stretch_len = (h_one.shape[0], h_one.shape[1])
    query = product("btd,dq->btq", h_one, wq_all).astype(jnp.bfloat16)
    keys = product("btd,dq->btq", h_one, wk_all).astype(jnp.bfloat16)
    values = product("btd,dv->btv", h_one, wv_all).astype(jnp.bfloat16)
    gate_pre = product("btd,dv->btv", h_one, wg_all)
    query_heads = query.reshape(seq_count, stretch_len, heads_here, qk_width)
    keys_heads = keys.reshape(seq_count, stretch_len, heads_here, qk_width)
    query_full = query_heads.astype(jnp.float32) * 0.0625
    keys_full = keys_heads.astype(jnp.float32)
    values_full = values.astype(jnp.float32).reshape(seq_count, stretch_len, heads_here, v_width)
    log_keep = jnp.log(1.0 - forget)
    ctx_place = lax.axis_index(CONTEXT)
    seg_stretch = lax.dynamic_slice_in_dim(segments, ctx_place * stretch_len, stretch_len, 1)
    seg_prev = lax.dynamic_slice_in_dim(segments, jnp.maximum(ctx_place * stretch_len - 1, 0), 1, 1)
    live_mask = (seg_stretch == seg_prev).astype(jnp.float32)
    steps_idx = jnp.arange(stretch_len, dtype=jnp.float32)
    step_gap = jnp.maximum(steps_idx[:, None] - steps_idx[None, :], 0.0)
    causal = steps_idx[:, None] >= steps_idx[None, :]
    same_doc = (seg_stretch[:, :, None] == seg_stretch[:, None, :]) & causal[None]
    weights_mask = jnp.where(
        same_doc[:, None], jnp.exp(step_gap[None] * log_keep[:, None, None])[None], 0.0
    )
    inflow = live_mask[:, :, None] * jnp.exp((steps_idx[:, None] + 1.0) * log_keep[None, :])[None]
    outflow = (seg_stretch == seg_stretch[:, -1:]).astype(jnp.float32)[:, :, None] * jnp.exp(
        (stretch_len - 1.0 - steps_idx)[:, None] * log_keep[None, :]
    )[None]
    carry_decay = live_mask[:, -1:] * jnp.exp(stretch_len * log_keep)[None, :]
    update = careful("bshd,bsh,bshe->bhde", keys_full, outflow, values_full)
    identity = (jnp.ones_like(carry_decay), jnp.zeros_like(update))
    state_in = entering((carry_decay, update), CONTEXT, compose, identity)[1]
    scores = product("bthd,bshd->bhts", query_heads, keys_heads) * 0.0625 * weights_mask
    retained = careful("bhts,bshe->bthe", scores, values_full)
    retained = retained + inflow[..., None] * careful("bthd,bhde->bthe", query_full, state_in)
    normed_out, gn_normed, gn_scale = norm_rows(retained, gain_heads, 0.01)
    norm_flat = normed_out.reshape(seq_count, stretch_len, v_local)
    gate_act = jax.nn.silu(gate_pre)
    gated = (gate_act * norm_flat).astype(jnp.bfloat16)
    middle = x_share + branch_sum(product("btv,vd->btd", gated, wo_all))
    h2_share, ln2_normed, ln2_scale = norm_rows(middle, ln2_gain)
    h_two = share_gather(h2_share.astype(jnp.bfloat16))
    w1_all, w3_all, w2_all = mlp_fetch(w_fc_gate, w_fc_up, w_fc_down)
    fc_a = product("btd,df->btf", h_two, w1_all)
    fc_b = product("btd,df->btf", h_two, w3_all)
    silu_a = jax.nn.silu(fc_a)
    hidden = (silu_a * fc_b).astype(jnp.bfloat16)
    output = (middle + branch_sum(product("btf,fd->btd", hidden, w2_all))).astype(jnp.bfloat16)
    wq_all, wk_all, wv_all, wg_all, wo_all = mixer_fetch(w_query, w_key, w_value, w_gate, w_out)
    w1_all, w3_all, w2_all = mlp_fetch(w_fc_gate, w_fc_up, w_fc_down)
    cot_full = share_gather(cotangent)
    d_hidden = product("btd,fd->btf", cot_full, w2_all)
    g_down = product("btf,btd->fd", hidden, cot_full)
    d_fca = (d_hidden * fc_b * swish_slope(fc_a)).astype(jnp.bfloat16)
    d_fcb = (d_hidden * silu_a).astype(jnp.bfloat16)
    g_fc_gate = product("btd,btf->df", h_two, d_fca)
    g_fc_up = product("btd,btf->df", h_two, d_fcb)
    d_h2 = input_sum(product("btf,df->btd", d_fca, w1_all) + product("btf,df->btd", d_fcb, w3_all))
    d_middle = cotangent.astype(jnp.float32) + norm_back(d_h2, ln2_normed, ln2_scale, ln2_gain)
    g_ln2 = jnp.sum(d_h2 * ln2_normed, axis=(0, 1))
    d_branch = share_gather(d_middle.astype(jnp.bfloat16))
    d_gated = product("btd,vd->btv", d_branch, wo_all)
    g_out = product("btv,btd->vd", gated, d_branch)
    d_gate = (d_gated * norm_flat * swish_slope(gate_pre)).astype(jnp.bfloat16)
    d_normed = (d_gated * gate_act).reshape(seq_count, stretch_len, heads_here, v_width)
    g_norm = jnp.sum(d_normed * gn_normed, axis=(0, 1)).reshape(v_local)
    d_retained = norm_back(d_normed, gn_normed, gn_scale, gain_heads)
    d_scores = careful("bthe,bshe->bhts", d_retained, values_full) * weights_mask
    d_values = careful("bhts,bthe->bshe", scores, d_retained)
    d_query = careful("bhts,bshd->bthd", d_scores, keys_full)
    d_query = d_query + inflow[..., None] * careful("bthe,bhde->bthd", d_retained, state_in)
    d_keys = careful("bhts,bthd->bshd", d_scores, query_full)
    leaving = careful("bthd,bth,bthe->bhde", query_full, inflow, d_retained)
    state_grad = carried_in((carry_decay, leaving), CONTEXT, compose, identity)[1]
    d_keys = d_keys + outflow[..., None] * careful("bshe,bhde->bshd", values_full, state_grad)
    d_values = d_values + outflow[..., None] * careful("bshd,bhde->bshe", keys_full, state_grad)
    dq_low = (
        (d_query * 0.0625)
        .reshape(seq_count, stretch_len, heads_here * qk_width)
        .astype(jnp.bfloat16)
    )
    dk_low = d_keys.reshape(seq_count, stretch_len, heads_here * qk_width).astype(jnp.bfloat16)
    dv_low = d_values.reshape(seq_count, stretch_len, v_local).astype(jnp.bfloat16)
    g_query = product("btd,btq->dq", h_one, dq_low)
    g_key = product("btd,btq->dq", h_one, dk_low)
    g_value = product("btd,btv->dv", h_one, dv_low)
    g_gate = product("btd,btv->dv", h_one, d_gate)
    d_h1 = product("btq,dq->btd", dq_low, wq_all) + product("btq,dq->btd", dk_low, wk_all)
    d_h1 = d_h1 + product("btv,dv->btd", dv_low, wv_all) + product("btv,dv->btd", d_gate, wg_all)
    d_h1 = input_sum(d_h1)
    grad_tokens = d_middle + norm_back(d_h1, ln1_normed, ln1_scale, ln1_gain)
    g_ln1 = jnp.sum(d_h1 * ln1_normed, axis=(0, 1))
    tensor_place = lax.axis_index(TENSOR)
    norm_full = lax.dynamic_update_slice(
        jnp.zeros((v_local * lax.axis_size(TENSOR),), jnp.float32),
        g_norm,
        (tensor_place * v_local,),
    )
    g_ln1, g_ln2, norm_full = lax.psum((g_ln1, g_ln2, norm_full), (FSDP, CONTEXT, TENSOR))
    g_norm = lax.dynamic_slice_in_dim(norm_full, tensor_place * v_local, v_local)
    weight_grads = (g_query, g_key, g_value, g_gate, g_out, g_fc_gate, g_fc_up, g_down)
    summed = (
        lax.psum(weight_grads[0].astype(jnp.bfloat16), CONTEXT).astype(jnp.float32),
        lax.psum(weight_grads[1].astype(jnp.bfloat16), CONTEXT).astype(jnp.float32),
        lax.psum(weight_grads[2].astype(jnp.bfloat16), CONTEXT).astype(jnp.float32),
        lax.psum(weight_grads[3].astype(jnp.bfloat16), CONTEXT).astype(jnp.float32),
        lax.psum(weight_grads[4].astype(jnp.bfloat16), CONTEXT).astype(jnp.float32),
        lax.psum(weight_grads[5].astype(jnp.bfloat16), CONTEXT).astype(jnp.float32),
        lax.psum(weight_grads[6].astype(jnp.bfloat16), CONTEXT).astype(jnp.float32),
        lax.psum(weight_grads[7].astype(jnp.bfloat16), CONTEXT).astype(jnp.float32),
    )
    shards = (
        lax.psum_scatter(
            summed[0].astype(jnp.bfloat16), FSDP, scatter_dimension=0, tiled=True
        ).astype(jnp.float32),
        lax.psum_scatter(
            summed[1].astype(jnp.bfloat16), FSDP, scatter_dimension=0, tiled=True
        ).astype(jnp.float32),
        lax.psum_scatter(
            summed[2].astype(jnp.bfloat16), FSDP, scatter_dimension=0, tiled=True
        ).astype(jnp.float32),
        lax.psum_scatter(
            summed[3].astype(jnp.bfloat16), FSDP, scatter_dimension=0, tiled=True
        ).astype(jnp.float32),
        lax.psum_scatter(
            summed[4].astype(jnp.bfloat16), FSDP, scatter_dimension=1, tiled=True
        ).astype(jnp.float32),
        lax.psum_scatter(
            summed[5].astype(jnp.bfloat16), FSDP, scatter_dimension=0, tiled=True
        ).astype(jnp.float32),
        lax.psum_scatter(
            summed[6].astype(jnp.bfloat16), FSDP, scatter_dimension=0, tiled=True
        ).astype(jnp.float32),
        lax.psum_scatter(
            summed[7].astype(jnp.bfloat16), FSDP, scatter_dimension=1, tiled=True
        ).astype(jnp.float32),
    )
    return (
        output,
        grad_tokens,
        g_ln1,
        shards[0],
        shards[1],
        shards[2],
        shards[3],
        g_norm,
        shards[4],
        g_ln2,
        shards[5],
        shards[6],
        shards[7],
    )


F32 = jnp.float32
BF16 = jnp.bfloat16
BOTH_X = [(0, 2), (2, 0), (1, 3), (3, 1)]
UP_X = [(0, 2), (1, 3)]
DOWN_X = [(2, 0), (3, 1)]
CORES = [(0, 1), (1, 0), (2, 3), (3, 2)]
UP_Z = [[(0, 1), (1, 2), (2, 3)], [(1, 2), (2, 3)]]
DOWN_Z = [[(3, 2), (2, 1), (1, 0)], [(2, 1), (1, 0)]]
LAST_Z = [(2, 3), (1, 0)]
SCALE = 0.0625
ROWS, GAINS, STATES = range(3)


def cost(flops):
    return pl.CostEstimate(flops=3 * flops // 5, transcendentals=0, bytes_accessed=0)


COPYING = 2 << 30
DOWN_Z = [[(3, 2), (2, 1), (1, 0)], [(2, 1), (1, 0)], [(1, 0)]]


def over_x(value):
    return lax.ppermute(value, CONTEXT, BOTH_X)


def over_core(value):
    return lax.ppermute(value, CONTEXT, CORES)


def over_y(value):
    return lax.ppermute(value, TENSOR, [(0, 1), (1, 0)])


def tie(*values):
    return lax.optimization_barrier(values)


def butterfly(value, axis):
    size = lax.axis_size(axis)
    step = 1
    while step < size:
        value = value + lax.ppermute(value, axis, [(i, i ^ step) for i in range(size)])
        step *= 2
    return value


def quarter_of(weight, dim, index):
    size = weight.shape[dim] // 4
    return lax.dynamic_slice_in_dim(weight, index * size, size, dim)


def assemble_kernel(spot_ref, *refs):
    at = pl.program_id(0)
    for index, block in enumerate(refs[:8]):

        @pl.when(at == index)
        def _(block=block):
            refs[8][...] = block[...]


def assemble(blocks, spots, by_rows, size):
    shape = (2 * size, 4 * size) if by_rows else (4 * size, 2 * size)

    def spot(at, spots_ref):
        z_from, x_from = spots_ref[at], spots_ref[8 + at]
        return (x_from, z_from) if by_rows else (z_from, x_from)

    return pl.pallas_call(
        assemble_kernel,
        out_shape=jax.ShapeDtypeStruct(shape, BF16),
        grid_spec=pltpu.PrefetchScalarGridSpec(
            num_scalar_prefetch=1,
            grid=(8,),
            in_specs=[
                pl.BlockSpec((size, size), lambda at, spots_ref, row=row: (row, 0))
                for _, row in blocks
            ],
            out_specs=pl.BlockSpec((size, size), spot),
        ),
        compiler_params=pltpu.CompilerParams(vmem_limit_bytes=32 << 20),
        cost_estimate=cost(COPYING),
    )(spots, *(array for array, _ in blocks))


def sum_kernel(product, count, outs, *refs):
    lefts, rights, extras = refs[:count], refs[count : 2 * count], refs[2 * count : -outs]
    total = product(lefts[0][...], rights[0][...])
    for left, right in zip(lefts[1:], rights[1:]):
        total = total + product(left[...], right[...])
    for extra in extras:
        total = total + extra[...].astype(F32)
    size = total.shape[0] // outs
    for index, out_ref in enumerate(refs[-outs:]):
        out_ref[...] = total[index * size : (index + 1) * size].astype(out_ref.dtype)


def sum_of_products(product, lefts, rights, first, rows, kind, extras=(), outs=1, weight=1):
    by_columns = product is nn
    width = rights[0].shape[1 if by_columns else 0]
    block, tile = min(1024, rows), min(512, width)
    if outs > 1:
        block = rows

    def right_spec(right):
        if by_columns:
            return pl.BlockSpec((right.shape[0], tile), lambda n, m: (0, n))
        return pl.BlockSpec((tile, right.shape[1]), lambda n, m: (n, 0))

    def tile_spec(from_row, size):
        return pl.BlockSpec((size, tile), lambda n, m: (from_row // size + m, n))

    out_shape = [jax.ShapeDtypeStruct((rows // outs, width), kind)] * outs
    result = pl.pallas_call(
        partial(sum_kernel, product, len(lefts), outs),
        grid=(width // tile, rows // block),
        out_shape=out_shape,
        in_specs=[
            pl.BlockSpec((block, left.shape[1]), lambda n, m: (first // block + m, 0))
            for left in lefts
        ]
        + [right_spec(right) for right in rights]
        + [tile_spec(from_row, block) for _, from_row in extras],
        out_specs=[tile_spec(0, block // outs)] * outs,
        compiler_params=pltpu.CompilerParams(vmem_limit_bytes=60 << 20),
        cost_estimate=cost(2 * weight * rows * width * sum(left.shape[1] for left in lefts)),
    )(*lefts, *rights, *(array for array, _ in extras))
    return result[0] if outs == 1 else result


def quarter_kernel(spots_ref, left, right, *rest):
    total = tn(left[...], right[...])
    for extra in rest[:-1]:
        total = total + extra[...].astype(F32)
    rest[-1][...] = total.astype(BF16)


def quarter_product(left, right, index, extras=(), weight=1):
    tokens, width = left.shape
    size, block = right.shape[1] // 2, min(1024, width)
    return pl.pallas_call(
        quarter_kernel,
        out_shape=jax.ShapeDtypeStruct((width, size), BF16),
        grid_spec=pltpu.PrefetchScalarGridSpec(
            num_scalar_prefetch=1,
            grid=(width // block,),
            in_specs=[
                pl.BlockSpec((tokens, block), lambda m, at: (0, m)),
                pl.BlockSpec((tokens, size), lambda m, at: (0, at[0])),
            ]
            + [pl.BlockSpec((block, size), lambda m, at: (m, 0)) for _ in extras],
            out_specs=pl.BlockSpec((block, size), lambda m, at: (m, 0)),
        ),
        compiler_params=pltpu.CompilerParams(vmem_limit_bytes=60 << 20),
        cost_estimate=cost(2 * weight * tokens * width * size),
    )(index.reshape(1).astype(jnp.int32), left, right, *extras)


def plain_kernel(left, right, out):
    out[...] = tn(left[...], right[...]).astype(BF16)


def plain_product(left, right):
    tokens, rows = left.shape
    columns = right.shape[1]
    block = min(1024, rows)
    return pl.pallas_call(
        plain_kernel,
        grid=(rows // block,),
        out_shape=jax.ShapeDtypeStruct((rows, columns), BF16),
        in_specs=[
            pl.BlockSpec((tokens, block), lambda m: (0, m)),
            pl.BlockSpec((tokens, columns), lambda m: (0, 0)),
        ],
        out_specs=pl.BlockSpec((block, columns), lambda m: (m, 0)),
        compiler_params=pltpu.CompilerParams(vmem_limit_bytes=60 << 20),
        cost_estimate=cost(2 * tokens * rows * columns),
    )(left, right)


def split_kernel(left, right, out):
    out[0] = tn(left[...], right[...]).astype(BF16)


def split_product(left, right, count):
    tokens, rows = left.shape
    size = right.shape[1] // count
    return pl.pallas_call(
        split_kernel,
        grid=(count,),
        out_shape=jax.ShapeDtypeStruct((count, rows, size), BF16),
        in_specs=[
            pl.BlockSpec((tokens, rows), lambda n: (0, 0)),
            pl.BlockSpec((tokens, size), lambda n: (0, n)),
        ],
        out_specs=pl.BlockSpec((1, rows, size), lambda n: (n, 0, 0)),
        compiler_params=pltpu.CompilerParams(vmem_limit_bytes=60 << 20),
        cost_estimate=cost(2 * tokens * rows * size * count),
    )(left, right)


def unit_kernel(h_ref, w1_ref, w3_ref, d_hidden_ref, hidden_ref, d_a_ref, d_b_ref):
    fc_a, fc_b = nn(h_ref[...], w1_ref[...]), nn(h_ref[...], w3_ref[...])
    d_hidden = d_hidden_ref[...].astype(F32)
    sigma = jax.nn.sigmoid(fc_a)
    silu_a = fc_a * sigma
    hidden_ref[...] = (silu_a * fc_b).astype(BF16)
    d_a_ref[...] = (d_hidden * fc_b * (sigma * (1.0 + fc_a * (1.0 - sigma)))).astype(BF16)
    d_b_ref[...] = (d_hidden * silu_a).astype(BF16)


def hidden_units(h_two, w1, w3, d_hidden):
    rows, width = h_two.shape
    count = w1.shape[1]
    block, tile = min(512, rows), min(512, count)
    weight = pl.BlockSpec((width, tile), lambda n, m: (0, n))
    spot = pl.BlockSpec((block, tile), lambda n, m: (m, n))
    return pl.pallas_call(
        unit_kernel,
        grid=(count // tile, rows // block),
        out_shape=[jax.ShapeDtypeStruct((rows, count), BF16)] * 3,
        in_specs=[pl.BlockSpec((block, width), lambda n, m: (m, 0)), weight, weight, spot],
        out_specs=[spot] * 3,
        compiler_params=pltpu.CompilerParams(vmem_limit_bytes=60 << 20),
        cost_estimate=cost(4 * rows * width * count),
    )(h_two, w1, w3, d_hidden)


def stack_kernel(*refs):
    count = len(refs) - 4
    shares, out_ref, held, sems_in, sems_out = refs[:count], *refs[count:]
    rows = shares[0].shape[0]
    ins, outs = [], []
    for index, share in enumerate(shares):
        ins.append(pltpu.make_async_copy(share, held.at[index], sems_in.at[index]))
        spot = out_ref.at[pl.ds(index * rows, rows)]
        outs.append(pltpu.make_async_copy(held.at[index], spot, sems_out.at[index]))
    for copy in ins:
        copy.start()
    for copy, onward in zip(ins, outs):
        copy.wait()
        onward.start()
    for onward in outs:
        onward.wait()


def stack_rows(*shares):
    rows, width = shares[0].shape
    count = len(shares)
    return pl.pallas_call(
        stack_kernel,
        out_shape=jax.ShapeDtypeStruct((count * rows, width), shares[0].dtype),
        in_specs=[pl.BlockSpec(memory_space=pl.ANY)] * count,
        out_specs=pl.BlockSpec(memory_space=pl.ANY),
        scratch_shapes=[
            pltpu.VMEM((count, rows, width), shares[0].dtype),
            pltpu.SemaphoreType.DMA((count,)),
            pltpu.SemaphoreType.DMA((count,)),
        ],
        compiler_params=pltpu.CompilerParams(vmem_limit_bytes=48 << 20),
        cost_estimate=cost(2 * COPYING),
    )(*shares)


def nn(left, right):
    return lax.dot_general(left, right, (((1,), (0,)), ((), ())), preferred_element_type=F32)


def nt(left, right):
    return lax.dot_general(left, right, (((1,), (1,)), ((), ())), preferred_element_type=F32)


def tn(left, right):
    return lax.dot_general(left, right, (((0,), (0,)), ((), ())), preferred_element_type=F32)


def where_is(whole, chunk, piece_len):
    share_len = piece_len // 2
    spots = []
    for shape, dim in (((piece_len, 1), 0), ((1, piece_len), 1)):
        at = lax.broadcasted_iota(jnp.int32, shape, dim) + whole[2] * share_len
        spots.append(jnp.where(at >= piece_len, at - piece_len, at))
    start = whole[0] * (2 * piece_len) + chunk * piece_len
    return spots[0], spots[1], start


def document(whole, spot):
    seq = pl.program_id(0)
    first, second = whole[3 + 2 * seq], whole[4 + 2 * seq]
    return jnp.where(spot >= second, 2, jnp.where(spot >= first, 1, 0))


def fade(gap, log_keep):
    return jnp.exp(jnp.maximum(gap, 0).astype(F32) * log_keep)


def piece_terms(whole, log_keep, chunk, piece_len):
    rows, cols, start = where_is(whole, chunk, piece_len)
    doc_rows, doc_cols = document(whole, start + rows), document(whole, start + cols)
    before, last = document(whole, start - 1), document(whole, start + piece_len - 1)
    within = jnp.where(
        (rows >= cols) & (doc_rows == doc_cols), fade(rows - cols, log_keep) * SCALE, 0.0
    )
    inflow = jnp.where(doc_rows == before, fade(rows + 1, log_keep) * SCALE, 0.0)
    outflow = jnp.where(doc_rows == last, fade(piece_len - 1 - rows, log_keep), 0.0)
    whole_gap = jnp.full((1, 1), piece_len, jnp.int32)
    over = jnp.where(before == last, fade(whole_gap, log_keep), 0.0)
    return within, inflow, outflow, over


def piece_of(ref, whole, chunk):
    group = lax.rem(chunk + whole[1], 2) * 2
    value = ref[pl.ds(group, 2), 0]
    return value.reshape(value.shape[0] * value.shape[1], value.shape[2])


def put_piece(ref, whole, chunk, value):
    group = lax.rem(chunk + whole[1], 2) * 2
    ref[pl.ds(group, 2), 0] = value.astype(ref.dtype).reshape(2, value.shape[0] // 2, value.shape[1])


def split_kq(ref, whole, chunk):
    both = piece_of(ref, whole, chunk)
    width = both.shape[1] // 2
    return both[:, :width], both[:, width:]


def update_kernel(whole, keeps, kq_ref, v_ref, out_ref):
    log_keep = keeps[pl.program_id(1)]
    piece_len = 2 * kq_ref.shape[2]
    total = jnp.zeros(out_ref.shape[2:], F32)
    for chunk in range(2):
        rows, _, start = where_is(whole, chunk, piece_len)
        last = document(whole, whole[0] * (2 * piece_len) + 2 * piece_len - 1)
        gap = (2 - chunk) * piece_len - 1 - rows
        weight = jnp.where(document(whole, start + rows) == last, fade(gap, log_keep), 0.0)
        keys, _ = split_kq(kq_ref, whole, chunk)
        values = piece_of(v_ref, whole, chunk)
        total = total + tn((keys.astype(F32) * weight).astype(BF16), values)
    out_ref[0, 0] = total.astype(BF16)


def next_state(state, keys, values, outflow, over):
    return over * state + tn((keys.astype(F32) * outflow).astype(BF16), values)


def forward_kernel(
    whole, keeps, kq_ref, v_ref, gate_ref, state_ref, gain_ref, gated_ref, retained_ref
):
    log_keep = keeps[pl.program_id(1)]
    piece_len = 2 * kq_ref.shape[2]
    state = state_ref[0, 0].astype(F32)
    for chunk in range(2):
        within, inflow, outflow, over = piece_terms(whole, log_keep, chunk, piece_len)
        keys, query = split_kq(kq_ref, whole, chunk)
        values = piece_of(v_ref, whole, chunk)
        scores = (nt(query, keys) * within).astype(BF16)
        retained = nn(scores, values) + inflow * nn(query, state.astype(BF16))
        if chunk == 0:
            state = next_state(state, keys, values, outflow, over)
        put_piece(retained_ref, whole, chunk, retained)
        normed, _, _ = norm_rows(retained, gain_ref[0], 0.01)
        gate = piece_of(gate_ref, whole, chunk).astype(F32)
        put_piece(gated_ref, whole, chunk, gate * jax.nn.sigmoid(gate) * normed)


def norm_back_kernel(
    whole,
    keeps,
    d_gated_ref,
    gate_ref,
    retained_ref,
    kq_ref,
    gain_ref,
    d_gate_ref,
    d_retained_ref,
    d_gain_ref,
    leaving_ref,
):
    log_keep = keeps[pl.program_id(1)]
    piece_len = 2 * kq_ref.shape[2]
    total = jnp.zeros(leaving_ref.shape[2:], F32)
    gain = gain_ref[0]
    d_gain = jnp.zeros(gain.shape, F32)
    for chunk in range(2):
        rows, _, start = where_is(whole, chunk, piece_len)
        before = document(whole, whole[0] * (2 * piece_len) - 1)
        gap = chunk * piece_len + rows + 1
        weight = jnp.where(
            document(whole, start + rows) == before, fade(gap, log_keep) * SCALE, 0.0
        )
        _, query = split_kq(kq_ref, whole, chunk)
        retained = piece_of(retained_ref, whole, chunk).astype(F32)
        normed, unit, scale = norm_rows(retained, gain, 0.01)
        gate = piece_of(gate_ref, whole, chunk).astype(F32)
        d_gated = piece_of(d_gated_ref, whole, chunk).astype(F32)
        sigma = jax.nn.sigmoid(gate)
        put_piece(
            d_gate_ref, whole, chunk, d_gated * normed * sigma * (1.0 + gate * (1.0 - sigma))
        )
        d_normed = d_gated * gate * sigma
        d_gain = d_gain + jnp.sum(d_normed * unit, axis=0, keepdims=True)
        d_retained = norm_back(d_normed, unit, scale, gain)
        put_piece(d_retained_ref, whole, chunk, d_retained)
        total = total + tn(query, (d_retained * weight).astype(BF16))
    d_gain_ref[0, 0] = d_gain
    leaving_ref[0, 0] = total.astype(BF16)


def backward_kernel(
    whole, keeps, kq_ref, v_ref, d_retained_ref, state_ref, d_state_ref, d_kq_ref, d_v_ref
):
    log_keep = keeps[pl.program_id(1)]
    piece_len = 2 * kq_ref.shape[2]
    terms = [piece_terms(whole, log_keep, chunk, piece_len) for chunk in range(2)]
    state = state_ref[0, 0].astype(F32)
    keys, _ = split_kq(kq_ref, whole, 0)
    _, _, outflow, over = terms[0]
    states = [state, next_state(state, keys, piece_of(v_ref, whole, 0), outflow, over)]
    d_state = d_state_ref[0, 0].astype(F32)
    for chunk in (1, 0):
        within, inflow, outflow, over = terms[chunk]
        keys, query = split_kq(kq_ref, whole, chunk)
        values = piece_of(v_ref, whole, chunk)
        d_ret = piece_of(d_retained_ref, whole, chunk)
        state_low, d_state_low = states[chunk].astype(BF16), d_state.astype(BF16)
        scores = (nt(query, keys) * within).astype(BF16)
        d_scores = (nt(d_ret, values) * within).astype(BF16)
        d_values = tn(scores, d_ret) + outflow * nn(keys, d_state_low)
        put_piece(d_v_ref, whole, chunk, d_values)
        d_query = nn(d_scores, keys) + inflow * nt(d_ret, state_low)
        d_keys = tn(d_scores, query) + outflow * nt(values, d_state_low)
        put_piece(d_kq_ref, whole, chunk, jnp.concatenate([d_keys, d_query], axis=1))
        if chunk == 1:
            entering = tn(query, (d_ret.astype(F32) * inflow).astype(BF16))
            d_state = over * d_state + entering


def per_head(kernel, scalars, blocks, outs, flops=12 << 30):
    def spec(array, kind):
        if kind == ROWS:
            width = array.shape[3] // heads
            return pl.BlockSpec((4, 1, array.shape[2], width), lambda b, h, *_: (0, b, 0, h))
        if kind == GAINS:
            return pl.BlockSpec((1, *array.shape[1:]), lambda b, h, *_: (h, 0, 0))
        return pl.BlockSpec((1, 1, *array.shape[2:]), lambda b, h, *_: (b, h, 0, 0))

    heads = scalars[1].shape[0]
    seq_count = (scalars[0].shape[0] - 3) // 2
    return pl.pallas_call(
        kernel,
        out_shape=[a for a, _ in outs],
        grid_spec=pltpu.PrefetchScalarGridSpec(
            num_scalar_prefetch=2,
            grid=(seq_count, heads),
            in_specs=[spec(*block) for block in blocks],
            out_specs=[spec(*out) for out in outs],
        ),
        compiler_params=pltpu.CompilerParams(vmem_limit_bytes=56 << 20),
        cost_estimate=cost(flops),
    )(*scalars, *(a for a, _ in blocks))


def both_quarters(mine, across, first, dim):
    return jnp.concatenate(
        [jnp.where(first, mine, across), jnp.where(first, across, mine)], axis=dim
    )


def paired_body(
    tokens,
    segments,
    forget,
    ln1_gain,
    w_query,
    w_key,
    w_value,
    w_gate,
    norm_gain,
    w_out,
    ln2_gain,
    w_fc_gate,
    w_fc_up,
    w_fc_down,
    cotangent,
):
    place = lax.axis_index(CONTEXT)
    x_at, core, y_at = place // 2, place % 2, lax.axis_index(TENSOR)
    z_at = lax.axis_index(FSDP)
    heads = forget.shape[0] // 2
    qk_width = w_query.shape[1] // forget.shape[0]
    v_width = w_value.shape[1] // forget.shape[0]
    width = tokens.shape[2]
    seq_count, share_len = tokens.shape[0], tokens.shape[1]
    share_rows = seq_count * share_len
    piece_len = 2 * share_len
    chip_len = 2 * piece_len
    v_half = heads * v_width
    forget_half = lax.dynamic_slice_in_dim(forget, core * heads, heads)
    gain_half = lax.dynamic_slice_in_dim(norm_gain, core * v_half, v_half)

    def part(array, first, last):
        return array[first * share_rows : last * share_rows]

    def unit(x_index):
        q = core * 2 + x_index
        key_query = [quarter_of(w_key, 1, q), quarter_of(w_query, 1, q)]
        return [
            jnp.concatenate(key_query, axis=1),
            quarter_of(w_value, 1, q),
            quarter_of(w_gate, 1, q),
            quarter_of(w_out, 0, q),
            quarter_of(w_fc_down, 0, q),
            quarter_of(w_fc_gate, 1, q),
            quarter_of(w_fc_up, 1, q),
        ]

    KQ, V, G, O, W2, W1, W3 = range(7)
    by_rows = [False, False, False, True, True, False, False]
    own, sibling = unit(x_at), unit(1 - x_at)
    size = own[0].shape[0]
    z_last = lax.axis_size(FSDP) - 1
    z_count = z_last + 1
    s_one = jnp.where(z_at == 0, 1, z_at - 1)
    s_three = jnp.where(z_at == z_last, 0, jnp.where(z_at == 1, 2, z_last))
    z_spots = [z_at, s_one, z_at ^ 2, s_three]
    spots = jnp.stack(z_spots + z_spots + [x_at] * 4 + [1 - x_at] * 4).astype(jnp.int32)
    groups = [[KQ, V], [G, O], [W2, W1, W3]]
    slots, across = [[], [], []], [[], [], []]

    def weight(index):
        at, row = next((i, g.index(index)) for i, g in enumerate(groups) if index in g)
        blocks = [(own[index], 0)] + [(array, row) for array in slots[at]]
        blocks += [(sibling[index], 0)] + [(array, row) for array in across[at]]
        return assemble(blocks, spots, by_rows[index], size)

    env = SimpleNamespace()
    firsts = jnp.sum((segments == 0).astype(jnp.int32), axis=1)
    seconds = jnp.sum((segments <= 1).astype(jnp.int32), axis=1)
    starts = jnp.stack([firsts, seconds], axis=1).reshape(-1)
    whole = jnp.concatenate([jnp.stack([x_at, core, y_at]).astype(jnp.int32), starts])
    scalars = (whole, jnp.log(1.0 - forget_half))
    gains = gain_half.reshape(heads, 1, v_width)
    state_type = jax.ShapeDtypeStruct((seq_count, heads, qk_width, v_width), BF16)
    rows_type = jax.ShapeDtypeStruct((4, seq_count, share_len, v_half), BF16)
    kq_type = jax.ShapeDtypeStruct((4, seq_count, share_len, 2 * heads * qk_width), BF16)
    gain_type = jax.ShapeDtypeStruct((seq_count, heads, 1, v_width), F32)

    def shaped(rows_in):
        return rows_in.reshape(4, seq_count, share_len, -1)

    def flat(rows_in):
        return rows_in.reshape(4 * share_rows, -1)

    x_share = tokens.reshape(share_rows, width).astype(F32)
    cot_share = cotangent.reshape(share_rows, width)

    def work_norm():
        h1, ln1_normed, ln1_scale = norm_rows(x_share, ln1_gain)
        env.ln1 = (ln1_normed, ln1_scale)
        env.h = h1.astype(BF16)
        env.hy = over_y(env.h)
        return [env.h]

    def work_core():
        env.hc, env.hcy = over_core(env.h), over_core(env.hy)
        env.cy = over_y(cot_share)
        return []

    def work_rows():
        env.h_one = stack_rows(env.h, env.hy, env.hc, env.hcy)
        return [env.h_one]

    def work_kq():
        env.wkq = weight(KQ)
        env.kq = sum_of_products(nn, [env.h_one], [env.wkq], 0, 4 * share_rows, BF16)
        return [env.kq]

    def work_v():
        env.wv = weight(V)
        env.v = sum_of_products(nn, [env.h_one], [env.wv], 0, 4 * share_rows, BF16)
        return [env.v]

    def work_state():
        (update,) = per_head(
            update_kernel,
            scalars,
            [(shaped(env.kq), ROWS), (shaped(env.v), ROWS)],
            [(state_type, STATES)],
            4 << 30,
        )
        env.state = lax.ppermute(update, CONTEXT, UP_X)
        env.cc, env.ccy = over_core(cot_share), over_core(env.cy)
        return [update]

    def work_gate():
        env.wg = weight(G)
        env.gate = sum_of_products(nn, [env.h_one], [env.wg], 0, 4 * share_rows, BF16)
        return [env.gate]

    def work_retained():
        gated, env.retained = per_head(
            forward_kernel,
            scalars,
            [
                (shaped(env.kq), ROWS),
                (shaped(env.v), ROWS),
                (shaped(env.gate), ROWS),
                (env.state, STATES),
                (gains, GAINS),
            ],
            [(rows_type, ROWS), (rows_type, ROWS)],
        )
        env.gated = flat(gated)
        return [env.gated]

    def work_out_far():
        env.wo = weight(O)
        own, other = sum_of_products(
            nn, [env.gated], [env.wo], 2 * share_rows, 2 * share_rows, BF16, (), 2
        )
        env.far_other, env.far_own = over_core(other), over_core(own)
        return [other]

    def work_out_near():
        near = sum_of_products(
            nn, [env.gated], [env.wo], share_rows, share_rows, BF16, [(env.far_other, 0)]
        )
        env.near = over_y(near)
        return [near]

    def work_out_own():
        extras = [(env.far_own, 0), (tokens.reshape(share_rows, width), 0)]
        env.own = sum_of_products(nn, [env.gated], [env.wo], 0, share_rows, F32, extras)
        return [env.own]

    def work_cot():
        env.cot = stack_rows(cot_share, env.cy, env.cc, env.ccy)
        return [env.cot]

    def work_d_hidden():
        env.w2 = weight(W2)
        env.d_hidden = sum_of_products(nt, [env.cot], [env.w2], 0, 4 * share_rows, BF16)
        return [env.d_hidden]

    def work_middle():
        env.middle = env.own + env.near.astype(F32)
        h2, ln2_normed, ln2_scale = norm_rows(env.middle, ln2_gain)
        env.ln2 = (ln2_normed, ln2_scale)
        env.h2 = h2.astype(BF16)
        env.h2y, env.h2c = over_y(env.h2), over_core(env.h2)
        return [env.h2]

    def work_up():
        env.w1 = weight(W1)
        return [env.w1]

    def work_h2():
        env.w3 = weight(W3)
        env.h2y, env.d_hidden, env.w1, env.w3 = tie(env.h2y, env.d_hidden, env.w1, env.w3)
        env.h2cy = over_core(env.h2y)
        return [env.w3]

    plan = [
        [work_norm],
        [],
        [work_core],
        [work_rows],
        [work_kq],
        [work_v, work_state],
        [work_cot, work_gate],
        [work_retained, work_out_far],
        [work_out_near, work_out_own],
        [work_middle],
        [work_d_hidden, work_up, work_h2],
    ]
    stacks = [jnp.concatenate([own[index] for index in group], axis=0) for group in groups]
    up = down = kept = to_send = None
    for tick, works in enumerate(plan):
        at, hop = divmod(tick, 3)
        moving = at < len(groups)
        sent, to_send = to_send, None
        if sent is not None:
            slots[sent[0]].append(sent[1])
            across[sent[0]].append(over_x(sent[1]))
        if moving and hop < 2:
            up = stacks[at] if hop == 0 else up
            down = stacks[at] if hop == 0 else down
            got = [lax.ppermute(up, FSDP, UP_Z[hop]), lax.ppermute(down, FSDP, DOWN_Z[hop])]
        elif moving:
            got = [lax.ppermute(slots[at][1], FSDP, LAST_Z)]
        held = []
        for work in works:
            held += work()
        if not moving:
            continue
        names = [n for n in ("h_one", "kq", "gate", "gated", "cot") if hasattr(env, n)]
        held = held + ([across[sent[0]][-1]] if sent is not None else [])
        ahead = stacks[at + 1 : at + 2] if hop == 2 else []
        tied = list(tie(*got, *[getattr(env, n) for n in names], *ahead, *held))
        got = [tied.pop(0) for _ in got]
        for n in names:
            setattr(env, n, tied.pop(0))
        if hasattr(env, "far_other"):
            env.far_other = tie(env.far_other, *got)[0]
        if ahead:
            stacks[at + 1] = tied.pop(0)
        if hop == 0:
            up, down = kept = got
            to_send = (at, jnp.where(z_at > 0, up, down))
        elif hop == 1:
            up, down = got
            to_send = (at, jnp.where(z_at >= 2, up, down))
        else:
            ends = (z_at == 0) | (z_at == z_last)
            to_send = (at, jnp.where(ends, got[0], kept[1]))

    h_one, gated, gate_pre = env.h_one, env.gated, env.gate
    wkq, wv, wg, wo, w1, w2, w3 = env.wkq, env.wv, env.wg, env.wo, env.w1, env.w2, env.w3
    cot_full, d_hidden, middle = env.cot, env.d_hidden, env.middle

    token = [h_one]

    def step(run, *args):
        *args, _ = tie(*args, token[0])
        out = run(*args)
        token[0] = out[0] if isinstance(out, (tuple, list)) else out
        return out

    def far_product(product, lefts, rights, weight=1):
        def run(*arrays):
            return sum_of_products(
                product, arrays, rights, 2 * share_rows, 2 * share_rows, BF16, (), 2, weight
            )

        own, other = step(run, *lefts)
        return over_core(other), over_core(own)

    def whole_product(product, lefts, rights, first, rows, kind, *extras, weight=1):
        count = len(lefts)

        def run(*arrays):
            added = [(a, row) for a, (_, row) in zip(arrays[count:], extras)]
            return sum_of_products(
                product,
                arrays[:count],
                rights,
                first * share_rows,
                rows * share_rows,
                kind,
                added,
                1,
                weight,
            )

        return step(run, *lefts, *(a for a, _ in extras))

    def theirs(left, right):
        return over_x(step(lambda a, b: quarter_product(a, b, 1 - x_at), left, right))

    def ours(left, right, got):
        total = step(lambda a, b, c: quarter_product(a, b, x_at, [c]), left, right, got)
        return lax.psum_scatter(total, FSDP, scatter_dimension=0, tiled=True)

    def chip_rows(left, right):
        total = step(lambda a, b: split_product(a, b, z_count), left, right)
        return lax.psum_scatter(total, FSDP, scatter_dimension=0, tiled=False)

    def chip_columns(left, right):
        total = step(plain_product, left, right)
        mine = lax.psum_scatter(total, FSDP, scatter_dimension=0, tiled=True)
        return jnp.concatenate(jnp.split(mine, 2, axis=1), axis=0)

    def begin_finish(*mine):
        mine = step(lambda *a: jnp.concatenate(a, axis=0), *mine)
        return mine, over_x(mine)

    def end_finish(firsts, mine, beside):
        def join(mine, beside):
            blocks, row = [], 0
            for x_summed in firsts:
                count = 1 if x_summed else 2
                one, other = (a[row * size : (row + count) * size] for a in (mine, beside))
                if x_summed:
                    blocks += [jnp.where(x_at == 0, one, other), jnp.where(x_at == 0, other, one)]
                else:
                    blocks.append((one.astype(F32) + other.astype(F32)).astype(BF16))
                row += count
            return jnp.concatenate(blocks, axis=0)

        both = step(join, mine, beside)
        return both, over_core(both)

    def quarters(pair, at):
        both, other = pair
        mine, theirs = (a[2 * at * size : (2 * at + 2) * size] for a in (both, other))
        first, second = jnp.where(core == 0, mine, theirs), jnp.where(core == 0, theirs, mine)
        return [first[:size], first[size:], second[:size], second[size:]]

    def shard(pair, at, rows):
        return jnp.concatenate(quarters(pair, at), axis=1 - int(rows)).astype(F32)

    h_two = stack_rows(env.h2, env.h2y, env.h2c, env.h2cy)
    hidden, d_fca, d_fcb = step(hidden_units, h_two, w1, w3, d_hidden)

    fc_lefts, fc_rights = (d_fca, d_fcb), (w1, w3)
    far_other, far_own = far_product(nt, fc_lefts, fc_rights)
    down_mine = chip_rows(hidden, cot_full)
    near = over_y(whole_product(nt, fc_lefts, fc_rights, 1, 1, BF16, (far_other, 0)))
    gate_got = theirs(h_two, d_fca)
    own_part = whole_product(nt, fc_lefts, fc_rights, 0, 1, F32, (far_own, 0))
    up_got = theirs(h_two, d_fcb)
    out_far_other, out_far_own = far_product(nn, [hidden], [w2])

    def middle_back(own_part, near):
        d_h2 = own_part + near.astype(F32)
        ln2_normed, ln2_scale = env.ln2
        d_middle = cot_share.astype(F32) + norm_back(d_h2, ln2_normed, ln2_scale, ln2_gain)
        return d_middle.astype(BF16), d_middle, jnp.sum(d_h2 * ln2_normed, axis=0)

    d_mid_low, d_middle, g_ln2 = step(middle_back, own_part, near)
    d_mid_y, d_mid_c = over_y(d_mid_low), over_core(d_mid_low)
    fc_gate_mine = ours(h_two, d_fca, gate_got)
    out_near = whole_product(nn, [hidden], [w2], 1, 1, BF16, (out_far_other, 0))
    out_own = whole_product(nn, [hidden], [w2], 0, 1, F32, (out_far_own, 0), (middle, 0))
    d_mid_y, out_near, up_got = step(lambda *a: a, d_mid_y, out_near, up_got)
    d_mid_cy = over_core(d_mid_y)
    out_near = over_y(out_near)
    down_begun = begin_finish(down_mine)
    fc_up_mine = ours(h_two, d_fcb, up_got)

    def gate_back(share, y, c, cy):
        d_branch = stack_rows(share, y, c, cy)
        return sum_of_products(nt, [d_branch], [wo], 0, 4 * share_rows, BF16), d_branch

    d_gated, d_branch = step(gate_back, d_mid_low, d_mid_y, d_mid_c, d_mid_cy)
    down_beside, d_gated = tie(down_begun[1], d_gated)
    kq, values, state_in = shaped(env.kq), shaped(env.v), env.state

    def retained_back(d_gated, kq):
        return per_head(
            norm_back_kernel,
            scalars,
            [
                (shaped(d_gated), ROWS),
                (shaped(gate_pre), ROWS),
                (env.retained, ROWS),
                (kq, ROWS),
                (gains, GAINS),
            ],
            [(rows_type, ROWS), (rows_type, ROWS), (gain_type, STATES), (state_type, STATES)],
        )

    d_gate, d_retained, g_norm, leaving = step(retained_back, d_gated, kq)
    d_gate = flat(d_gate)
    g_norm = jnp.sum(g_norm, axis=0).reshape(v_half)
    state_grad = lax.ppermute(leaving, CONTEXT, DOWN_X)
    out_mine = chip_rows(gated, d_branch)

    def pair_back(d_retained, state_grad):
        return per_head(
            backward_kernel,
            scalars,
            [
                (kq, ROWS),
                (values, ROWS),
                (d_retained, ROWS),
                (state_in, STATES),
                (state_grad, STATES),
            ],
            [(kq_type, ROWS), (rows_type, ROWS)],
        )

    g_down = end_finish([False], down_begun[0], down_beside)
    dkq_low, dv_low = step(pair_back, d_retained, state_grad)
    dkq_low, dv_low = flat(dkq_low), flat(dv_low)
    gg_mine = chip_columns(h_one, d_gate)
    v_got = theirs(h_one, dv_low)
    kq_got = theirs(h_one, dkq_low)
    h1_lefts, h1_rights = (dkq_low, dv_low, d_gate), (wkq, wv, wg)
    output = step(lambda a, b: (a + b.astype(F32)).astype(BF16), out_own, out_near)
    far_other, far_own = far_product(nt, h1_lefts, h1_rights)
    fc_gate_mine, v_got = tie(fc_gate_mine, v_got)
    v_mine = ours(h_one, dv_low, v_got)
    near = over_y(whole_product(nt, h1_lefts, h1_rights, 1, 1, BF16, (far_other, 0)))
    own_part = whole_product(nt, h1_lefts, h1_rights, 0, 1, F32, (far_own, 0))
    fc_begun = begin_finish(fc_gate_mine, fc_up_mine)
    out_mine, kq_got = tie(out_mine, kq_got)
    kq_mine = ours(h_one, dkq_low, kq_got)

    def tokens_back(own_part, near):
        d_h1 = own_part + near.astype(F32)
        ln1_normed, ln1_scale = env.ln1
        grad = d_middle + norm_back(d_h1, ln1_normed, ln1_scale, ln1_gain)
        return grad, jnp.sum(d_h1 * ln1_normed, axis=0)

    grad_tokens, g_ln1 = step(tokens_back, own_part, near)
    norm_size = lax.axis_size(TENSOR) * norm_gain.shape[0]
    norm_all = lax.dynamic_update_slice_in_dim(
        jnp.zeros((norm_size,), F32), g_norm, (2 * y_at + core) * v_half, 0
    )
    gain_sums = jnp.concatenate([g_ln1, g_ln2, norm_all])
    gain_sums = gain_sums + over_x(gain_sums)
    out_mine, gain_sums = tie(out_mine, gain_sums)
    out_begun = begin_finish(out_mine, gg_mine)
    g_fc = end_finish([True, True], *fc_begun)
    v_begun = begin_finish(v_mine)
    kq_begun = begin_finish(kq_mine)
    gain_sums = gain_sums + over_core(gain_sums)
    gain_sums = butterfly(butterfly(gain_sums, TENSOR), FSDP)
    g_out = end_finish([False, False], *out_begun)
    g_value = end_finish([True], *v_begun)
    g_kq = end_finish([True], *kq_begun)
    sides = quarters(g_kq, 0)
    g_key = jnp.concatenate([side[:, :qk_width] for side in sides], axis=1).astype(F32)
    g_query = jnp.concatenate([side[:, qk_width:] for side in sides], axis=1).astype(F32)

    g_ln1, g_ln2 = gain_sums[:width], gain_sums[width : 2 * width]
    g_norm = lax.dynamic_slice_in_dim(
        gain_sums, 2 * width + y_at * norm_gain.shape[0], norm_gain.shape[0]
    )
    return (
        output.reshape(tokens.shape),
        grad_tokens.reshape(tokens.shape),
        g_ln1,
        g_query,
        g_key,
        shard(g_value, 0, False),
        shard(g_out, 1, False),
        g_norm,
        shard(g_out, 0, True),
        g_ln2,
        shard(g_fc, 0, False),
        shard(g_fc, 1, False),
        shard(g_down, 0, True),
    )


def body(tensor_size, *arrays):
    heads_here = arrays[2].shape[0]
    paired = tensor_size == 2 and heads_here % 2 == 0 and lax.axis_size(CONTEXT) == 4
    paired = paired and lax.axis_size(FSDP) == 4
    return (paired_body if paired else general_body)(*arrays)


def solution(mesh):
    in_specs = (
        P(FSDP, (CONTEXT, TENSOR), None),
        P(FSDP, None),
        P(TENSOR),
        P(),
        P(FSDP, TENSOR),
        P(FSDP, TENSOR),
        P(FSDP, TENSOR),
        P(FSDP, TENSOR),
        P(TENSOR),
        P(TENSOR, FSDP),
        P(),
        P(FSDP, TENSOR),
        P(FSDP, TENSOR),
        P(TENSOR, FSDP),
        P(FSDP, (CONTEXT, TENSOR), None),
    )
    out_specs = (
        P(FSDP, (CONTEXT, TENSOR), None),
        P(FSDP, (CONTEXT, TENSOR), None),
        P(),
        P(FSDP, TENSOR),
        P(FSDP, TENSOR),
        P(FSDP, TENSOR),
        P(FSDP, TENSOR),
        P(TENSOR),
        P(TENSOR, FSDP),
        P(),
        P(FSDP, TENSOR),
        P(FSDP, TENSOR),
        P(TENSOR, FSDP),
    )
    return jax.shard_map(partial(body, mesh.shape[TENSOR]), mesh=mesh, in_specs=in_specs, out_specs=out_specs, check_vma=False)
```

```python
from functools import partial
from types import SimpleNamespace

import jax
import jax.numpy as jnp
from jax import lax
from jax.experimental import pallas as pl
from jax.experimental.pallas import tpu as pltpu
from jax.sharding import PartitionSpec as P

FSDP, CONTEXT, TENSOR = "fsdp", "context", "tensor"

careful = partial(jnp.einsum, precision=lax.Precision.HIGH)


def entering(part, axis, combine, identity):
    place = lax.axis_index(axis)
    gathered = jax.tree.map(lambda a: lax.all_gather(a, axis), part)
    state = jax.tree.map(lambda a, e: jnp.zeros_like(a) + jnp.asarray(e, a.dtype), part, identity)

    def one(step, state):
        return combine(
            state, jax.tree.map(lambda a: lax.dynamic_index_in_dim(a, step, 0, False), gathered)
        )

    return lax.fori_loop(0, place, one, state)


def carried_in(value, axis, combine, identity):
    count, place = (lax.axis_size(axis), lax.axis_index(axis))
    everything = jax.tree.map(
        lambda part, kind: lax.all_gather(part.astype(kind), axis),
        value,
        jax.tree.map(lambda a: jnp.bfloat16 if a.dtype == jnp.float32 else a.dtype, value),
    )
    start = jax.tree.map(
        lambda part, zero: jnp.broadcast_to(jnp.asarray(zero, part.dtype), part.shape),
        value,
        identity,
    )

    def step(k, before):
        at = count - 1 - k
        reached = at > place
        new = combine(
            before, jax.tree.map(lambda part, own: part[at].astype(own.dtype), everything, value)
        )
        return jax.tree.map(lambda a, b: jnp.where(reached, a, b), new, before)

    return lax.fori_loop(0, count, step, start)


def norm_rows(values, gain_vec, epsilon=1e-05):
    centred = values - jnp.mean(values, axis=-1, keepdims=True)
    scale = lax.rsqrt(jnp.mean(centred * centred, axis=-1, keepdims=True) + epsilon)
    normed = centred * scale
    return (normed * gain_vec, normed, scale)


def norm_back(grad_in, normed, scale, gain_vec):
    d_normed = grad_in * gain_vec
    first_mean = jnp.mean(d_normed, axis=-1, keepdims=True)
    second_mean = jnp.mean(d_normed * normed, axis=-1, keepdims=True)
    return scale * (d_normed - first_mean - normed * second_mean)


def swish_slope(values):
    sigma = jax.nn.sigmoid(values)
    return sigma * (1.0 + values * (1.0 - sigma))


def compose(earlier, latter):
    return (earlier[0] * latter[0], latter[0][:, :, None, None] * earlier[1] + latter[1])


def share_gather(piece):
    return lax.all_gather(piece, TENSOR, axis=1, tiled=True)


def branch_sum(terms):
    return lax.psum_scatter(terms, TENSOR, scatter_dimension=1, tiled=True)


def input_sum(terms):
    return lax.psum_scatter(
        terms.astype(jnp.bfloat16), TENSOR, scatter_dimension=1, tiled=True
    ).astype(jnp.float32)


def mixer_fetch(w_query, w_key, w_value, w_gate, w_out):
    return (
        lax.all_gather(w_query, FSDP, axis=0, tiled=True),
        lax.all_gather(w_key, FSDP, axis=0, tiled=True),
        lax.all_gather(w_value, FSDP, axis=0, tiled=True),
        lax.all_gather(w_gate, FSDP, axis=0, tiled=True),
        lax.all_gather(w_out, FSDP, axis=1, tiled=True),
    )


def mlp_fetch(w_fc_gate, w_fc_up, w_fc_down):
    return (
        lax.all_gather(w_fc_gate, FSDP, axis=0, tiled=True),
        lax.all_gather(w_fc_up, FSDP, axis=0, tiled=True),
        lax.all_gather(w_fc_down, FSDP, axis=1, tiled=True),
    )


def product(form, left, right):
    return jnp.einsum(form, left, right, preferred_element_type=jnp.float32)


def general_body(
    tokens,
    segments,
    forget,
    ln1_gain,
    w_query,
    w_key,
    w_value,
    w_gate,
    norm_gain,
    w_out,
    ln2_gain,
    w_fc_gate,
    w_fc_up,
    w_fc_down,
    cotangent,
):
    heads_here = forget.shape[0]
    qk_width = w_query.shape[1] // heads_here
    v_width = w_value.shape[1] // heads_here
    v_local = heads_here * v_width
    gain_heads = norm_gain.reshape(heads_here, v_width)
    x_share = tokens.astype(jnp.float32)
    h1_share, ln1_normed, ln1_scale = norm_rows(x_share, ln1_gain)
    h_one = share_gather(h1_share.astype(jnp.bfloat16))
    wq_all, wk_all, wv_all, wg_all, wo_all = mixer_fetch(w_query, w_key, w_value, w_gate, w_out)
    seq_count, stretch_len = (h_one.shape[0], h_one.shape[1])
    query = product("btd,dq->btq", h_one, wq_all).astype(jnp.bfloat16)
    keys = product("btd,dq->btq", h_one, wk_all).astype(jnp.bfloat16)
    values = product("btd,dv->btv", h_one, wv_all).astype(jnp.bfloat16)
    gate_pre = product("btd,dv->btv", h_one, wg_all)
    query_heads = query.reshape(seq_count, stretch_len, heads_here, qk_width)
    keys_heads = keys.reshape(seq_count, stretch_len, heads_here, qk_width)
    query_full = query_heads.astype(jnp.float32) * 0.0625
    keys_full = keys_heads.astype(jnp.float32)
    values_full = values.astype(jnp.float32).reshape(seq_count, stretch_len, heads_here, v_width)
    log_keep = jnp.log(1.0 - forget)
    ctx_place = lax.axis_index(CONTEXT)
    seg_stretch = lax.dynamic_slice_in_dim(segments, ctx_place * stretch_len, stretch_len, 1)
    seg_prev = lax.dynamic_slice_in_dim(segments, jnp.maximum(ctx_place * stretch_len - 1, 0), 1, 1)
    live_mask = (seg_stretch == seg_prev).astype(jnp.float32)
    steps_idx = jnp.arange(stretch_len, dtype=jnp.float32)
    step_gap = jnp.maximum(steps_idx[:, None] - steps_idx[None, :], 0.0)
    causal = steps_idx[:, None] >= steps_idx[None, :]
    same_doc = (seg_stretch[:, :, None] == seg_stretch[:, None, :]) & causal[None]
    weights_mask = jnp.where(
        same_doc[:, None], jnp.exp(step_gap[None] * log_keep[:, None, None])[None], 0.0
    )
    inflow = live_mask[:, :, None] * jnp.exp((steps_idx[:, None] + 1.0) * log_keep[None, :])[None]
    outflow = (seg_stretch == seg_stretch[:, -1:]).astype(jnp.float32)[:, :, None] * jnp.exp(
        (stretch_len - 1.0 - steps_idx)[:, None] * log_keep[None, :]
    )[None]
    carry_decay = live_mask[:, -1:] * jnp.exp(stretch_len * log_keep)[None, :]
    update = careful("bshd,bsh,bshe->bhde", keys_full, outflow, values_full)
    identity = (jnp.ones_like(carry_decay), jnp.zeros_like(update))
    state_in = entering((carry_decay, update), CONTEXT, compose, identity)[1]
    scores = product("bthd,bshd->bhts", query_heads, keys_heads) * 0.0625 * weights_mask
    retained = careful("bhts,bshe->bthe", scores, values_full)
    retained = retained + inflow[..., None] * careful("bthd,bhde->bthe", query_full, state_in)
    normed_out, gn_normed, gn_scale = norm_rows(retained, gain_heads, 0.01)
    norm_flat = normed_out.reshape(seq_count, stretch_len, v_local)
    gate_act = jax.nn.silu(gate_pre)
    gated = (gate_act * norm_flat).astype(jnp.bfloat16)
    middle = x_share + branch_sum(product("btv,vd->btd", gated, wo_all))
    h2_share, ln2_normed, ln2_scale = norm_rows(middle, ln2_gain)
    h_two = share_gather(h2_share.astype(jnp.bfloat16))
    w1_all, w3_all, w2_all = mlp_fetch(w_fc_gate, w_fc_up, w_fc_down)
    fc_a = product("btd,df->btf", h_two, w1_all)
    fc_b = product("btd,df->btf", h_two, w3_all)
    silu_a = jax.nn.silu(fc_a)
    hidden = (silu_a * fc_b).astype(jnp.bfloat16)
    output = (middle + branch_sum(product("btf,fd->btd", hidden, w2_all))).astype(jnp.bfloat16)
    wq_all, wk_all, wv_all, wg_all, wo_all = mixer_fetch(w_query, w_key, w_value, w_gate, w_out)
    w1_all, w3_all, w2_all = mlp_fetch(w_fc_gate, w_fc_up, w_fc_down)
    cot_full = share_gather(cotangent)
    d_hidden = product("btd,fd->btf", cot_full, w2_all)
    g_down = product("btf,btd->fd", hidden, cot_full)
    d_fca = (d_hidden * fc_b * swish_slope(fc_a)).astype(jnp.bfloat16)
    d_fcb = (d_hidden * silu_a).astype(jnp.bfloat16)
    g_fc_gate = product("btd,btf->df", h_two, d_fca)
    g_fc_up = product("btd,btf->df", h_two, d_fcb)
    d_h2 = input_sum(product("btf,df->btd", d_fca, w1_all) + product("btf,df->btd", d_fcb, w3_all))
    d_middle = cotangent.astype(jnp.float32) + norm_back(d_h2, ln2_normed, ln2_scale, ln2_gain)
    g_ln2 = jnp.sum(d_h2 * ln2_normed, axis=(0, 1))
    d_branch = share_gather(d_middle.astype(jnp.bfloat16))
    d_gated = product("btd,vd->btv", d_branch, wo_all)
    g_out = product("btv,btd->vd", gated, d_branch)
    d_gate = (d_gated * norm_flat * swish_slope(gate_pre)).astype(jnp.bfloat16)
    d_normed = (d_gated * gate_act).reshape(seq_count, stretch_len, heads_here, v_width)
    g_norm = jnp.sum(d_normed * gn_normed, axis=(0, 1)).reshape(v_local)
    d_retained = norm_back(d_normed, gn_normed, gn_scale, gain_heads)
    d_scores = careful("bthe,bshe->bhts", d_retained, values_full) * weights_mask
    d_values = careful("bhts,bthe->bshe", scores, d_retained)
    d_query = careful("bhts,bshd->bthd", d_scores, keys_full)
    d_query = d_query + inflow[..., None] * careful("bthe,bhde->bthd", d_retained, state_in)
    d_keys = careful("bhts,bthd->bshd", d_scores, query_full)
    leaving = careful("bthd,bth,bthe->bhde", query_full, inflow, d_retained)
    state_grad = carried_in((carry_decay, leaving), CONTEXT, compose, identity)[1]
    d_keys = d_keys + outflow[..., None] * careful("bshe,bhde->bshd", values_full, state_grad)
    d_values = d_values + outflow[..., None] * careful("bshd,bhde->bshe", keys_full, state_grad)
    dq_low = (
        (d_query * 0.0625)
        .reshape(seq_count, stretch_len, heads_here * qk_width)
        .astype(jnp.bfloat16)
    )
    dk_low = d_keys.reshape(seq_count, stretch_len, heads_here * qk_width).astype(jnp.bfloat16)
    dv_low = d_values.reshape(seq_count, stretch_len, v_local).astype(jnp.bfloat16)
    g_query = product("btd,btq->dq", h_one, dq_low)
    g_key = product("btd,btq->dq", h_one, dk_low)
    g_value = product("btd,btv->dv", h_one, dv_low)
    g_gate = product("btd,btv->dv", h_one, d_gate)
    d_h1 = product("btq,dq->btd", dq_low, wq_all) + product("btq,dq->btd", dk_low, wk_all)
    d_h1 = d_h1 + product("btv,dv->btd", dv_low, wv_all) + product("btv,dv->btd", d_gate, wg_all)
    d_h1 = input_sum(d_h1)
    grad_tokens = d_middle + norm_back(d_h1, ln1_normed, ln1_scale, ln1_gain)
    g_ln1 = jnp.sum(d_h1 * ln1_normed, axis=(0, 1))
    tensor_place = lax.axis_index(TENSOR)
    norm_full = lax.dynamic_update_slice(
        jnp.zeros((v_local * lax.axis_size(TENSOR),), jnp.float32),
        g_norm,
        (tensor_place * v_local,),
    )
    g_ln1, g_ln2, norm_full = lax.psum((g_ln1, g_ln2, norm_full), (FSDP, CONTEXT, TENSOR))
    g_norm = lax.dynamic_slice_in_dim(norm_full, tensor_place * v_local, v_local)
    weight_grads = (g_query, g_key, g_value, g_gate, g_out, g_fc_gate, g_fc_up, g_down)
    summed = (
        lax.psum(weight_grads[0].astype(jnp.bfloat16), CONTEXT).astype(jnp.float32),
        lax.psum(weight_grads[1].astype(jnp.bfloat16), CONTEXT).astype(jnp.float32),
        lax.psum(weight_grads[2].astype(jnp.bfloat16), CONTEXT).astype(jnp.float32),
        lax.psum(weight_grads[3].astype(jnp.bfloat16), CONTEXT).astype(jnp.float32),
        lax.psum(weight_grads[4].astype(jnp.bfloat16), CONTEXT).astype(jnp.float32),
        lax.psum(weight_grads[5].astype(jnp.bfloat16), CONTEXT).astype(jnp.float32),
        lax.psum(weight_grads[6].astype(jnp.bfloat16), CONTEXT).astype(jnp.float32),
        lax.psum(weight_grads[7].astype(jnp.bfloat16), CONTEXT).astype(jnp.float32),
    )
    shards = (
        lax.psum_scatter(
            summed[0].astype(jnp.bfloat16), FSDP, scatter_dimension=0, tiled=True
        ).astype(jnp.float32),
        lax.psum_scatter(
            summed[1].astype(jnp.bfloat16), FSDP, scatter_dimension=0, tiled=True
        ).astype(jnp.float32),
        lax.psum_scatter(
            summed[2].astype(jnp.bfloat16), FSDP, scatter_dimension=0, tiled=True
        ).astype(jnp.float32),
        lax.psum_scatter(
            summed[3].astype(jnp.bfloat16), FSDP, scatter_dimension=0, tiled=True
        ).astype(jnp.float32),
        lax.psum_scatter(
            summed[4].astype(jnp.bfloat16), FSDP, scatter_dimension=1, tiled=True
        ).astype(jnp.float32),
        lax.psum_scatter(
            summed[5].astype(jnp.bfloat16), FSDP, scatter_dimension=0, tiled=True
        ).astype(jnp.float32),
        lax.psum_scatter(
            summed[6].astype(jnp.bfloat16), FSDP, scatter_dimension=0, tiled=True
        ).astype(jnp.float32),
        lax.psum_scatter(
            summed[7].astype(jnp.bfloat16), FSDP, scatter_dimension=1, tiled=True
        ).astype(jnp.float32),
    )
    return (
        output,
        grad_tokens,
        g_ln1,
        shards[0],
        shards[1],
        shards[2],
        shards[3],
        g_norm,
        shards[4],
        g_ln2,
        shards[5],
        shards[6],
        shards[7],
    )


F32 = jnp.float32
BF16 = jnp.bfloat16
BOTH_X = [(0, 2), (2, 0), (1, 3), (3, 1)]
UP_X = [(0, 2), (1, 3)]
DOWN_X = [(2, 0), (3, 1)]
CORES = [(0, 1), (1, 0), (2, 3), (3, 2)]
UP_Z = [[(0, 1), (1, 2), (2, 3)], [(1, 2), (2, 3)]]
DOWN_Z = [[(3, 2), (2, 1), (1, 0)], [(2, 1), (1, 0)]]
LAST_Z = [(2, 3), (1, 0)]
SCALE = 0.0625
ROWS, GAINS, STATES = range(3)


def cost(flops):
    return pl.CostEstimate(flops=3 * flops // 5, transcendentals=0, bytes_accessed=0)


COPYING = 2 << 30
DOWN_Z = [[(3, 2), (2, 1), (1, 0)], [(2, 1), (1, 0)], [(1, 0)]]


def over_x(value):
    return lax.ppermute(value, CONTEXT, BOTH_X)


def over_core(value):
    return lax.ppermute(value, CONTEXT, CORES)


def over_y(value):
    return lax.ppermute(value, TENSOR, [(0, 1), (1, 0)])


def tie(*values):
    return lax.optimization_barrier(values)


def butterfly(value, axis):
    size = lax.axis_size(axis)
    step = 1
    while step < size:
        value = value + lax.ppermute(value, axis, [(i, i ^ step) for i in range(size)])
        step *= 2
    return value


def quarter_of(weight, dim, index):
    size = weight.shape[dim] // 4
    return lax.dynamic_slice_in_dim(weight, index * size, size, dim)


def assemble_kernel(spot_ref, *refs):
    at = pl.program_id(0)
    for index, block in enumerate(refs[:8]):

        @pl.when(at == index)
        def _(block=block):
            refs[8][...] = block[...]


def assemble(blocks, spots, by_rows, size):
    shape = (2 * size, 4 * size) if by_rows else (4 * size, 2 * size)

    def spot(at, spots_ref):
        z_from, x_from = spots_ref[at], spots_ref[8 + at]
        return (x_from, z_from) if by_rows else (z_from, x_from)

    return pl.pallas_call(
        assemble_kernel,
        out_shape=jax.ShapeDtypeStruct(shape, BF16),
        grid_spec=pltpu.PrefetchScalarGridSpec(
            num_scalar_prefetch=1,
            grid=(8,),
            in_specs=[
                pl.BlockSpec((size, size), lambda at, spots_ref, row=row: (row, 0))
                for _, row in blocks
            ],
            out_specs=pl.BlockSpec((size, size), spot),
        ),
        compiler_params=pltpu.CompilerParams(vmem_limit_bytes=32 << 20),
        cost_estimate=cost(COPYING),
    )(spots, *(array for array, _ in blocks))


def sum_kernel(product, count, outs, *refs):
    lefts, rights, extras = refs[:count], refs[count : 2 * count], refs[2 * count : -outs]
    total = product(lefts[0][...], rights[0][...])
    for left, right in zip(lefts[1:], rights[1:]):
        total = total + product(left[...], right[...])
    for extra in extras:
        total = total + extra[...].astype(F32)
    size = total.shape[0] // outs
    for index, out_ref in enumerate(refs[-outs:]):
        out_ref[...] = total[index * size : (index + 1) * size].astype(out_ref.dtype)


def sum_of_products(product, lefts, rights, first, rows, kind, extras=(), outs=1, weight=1):
    by_columns = product is nn
    width = rights[0].shape[1 if by_columns else 0]
    block, tile = min(1024, rows), min(512, width)
    if outs > 1:
        block = rows

    def right_spec(right):
        if by_columns:
            return pl.BlockSpec((right.shape[0], tile), lambda n, m: (0, n))
        return pl.BlockSpec((tile, right.shape[1]), lambda n, m: (n, 0))

    def tile_spec(from_row, size):
        return pl.BlockSpec((size, tile), lambda n, m: (from_row // size + m, n))

    out_shape = [jax.ShapeDtypeStruct((rows // outs, width), kind)] * outs
    result = pl.pallas_call(
        partial(sum_kernel, product, len(lefts), outs),
        grid=(width // tile, rows // block),
        out_shape=out_shape,
        in_specs=[
            pl.BlockSpec((block, left.shape[1]), lambda n, m: (first // block + m, 0))
            for left in lefts
        ]
        + [right_spec(right) for right in rights]
        + [tile_spec(from_row, block) for _, from_row in extras],
        out_specs=[tile_spec(0, block // outs)] * outs,
        compiler_params=pltpu.CompilerParams(vmem_limit_bytes=60 << 20),
        cost_estimate=cost(2 * weight * rows * width * sum(left.shape[1] for left in lefts)),
    )(*lefts, *rights, *(array for array, _ in extras))
    return result[0] if outs == 1 else result


def quarter_kernel(spots_ref, left, right, *rest):
    total = tn(left[...], right[...])
    for extra in rest[:-1]:
        total = total + extra[...].astype(F32)
    rest[-1][...] = total.astype(BF16)


def quarter_product(left, right, index, extras=(), weight=1):
    tokens, width = left.shape
    size, block = right.shape[1] // 2, min(1024, width)
    return pl.pallas_call(
        quarter_kernel,
        out_shape=jax.ShapeDtypeStruct((width, size), BF16),
        grid_spec=pltpu.PrefetchScalarGridSpec(
            num_scalar_prefetch=1,
            grid=(width // block,),
            in_specs=[
                pl.BlockSpec((tokens, block), lambda m, at: (0, m)),
                pl.BlockSpec((tokens, size), lambda m, at: (0, at[0])),
            ]
            + [pl.BlockSpec((block, size), lambda m, at: (m, 0)) for _ in extras],
            out_specs=pl.BlockSpec((block, size), lambda m, at: (m, 0)),
        ),
        compiler_params=pltpu.CompilerParams(vmem_limit_bytes=60 << 20),
        cost_estimate=cost(2 * weight * tokens * width * size),
    )(index.reshape(1).astype(jnp.int32), left, right, *extras)


def plain_kernel(left, right, out):
    out[...] = tn(left[...], right[...]).astype(BF16)


def plain_product(left, right):
    tokens, rows = left.shape
    columns = right.shape[1]
    block = min(1024, rows)
    return pl.pallas_call(
        plain_kernel,
        grid=(rows // block,),
        out_shape=jax.ShapeDtypeStruct((rows, columns), BF16),
        in_specs=[
            pl.BlockSpec((tokens, block), lambda m: (0, m)),
            pl.BlockSpec((tokens, columns), lambda m: (0, 0)),
        ],
        out_specs=pl.BlockSpec((block, columns), lambda m: (m, 0)),
        compiler_params=pltpu.CompilerParams(vmem_limit_bytes=60 << 20),
        cost_estimate=cost(2 * tokens * rows * columns),
    )(left, right)


def split_kernel(left, right, out):
    out[0] = tn(left[...], right[...]).astype(BF16)


def split_product(left, right, count):
    tokens, rows = left.shape
    size = right.shape[1] // count
    return pl.pallas_call(
        split_kernel,
        grid=(count,),
        out_shape=jax.ShapeDtypeStruct((count, rows, size), BF16),
        in_specs=[
            pl.BlockSpec((tokens, rows), lambda n: (0, 0)),
            pl.BlockSpec((tokens, size), lambda n: (0, n)),
        ],
        out_specs=pl.BlockSpec((1, rows, size), lambda n: (n, 0, 0)),
        compiler_params=pltpu.CompilerParams(vmem_limit_bytes=60 << 20),
        cost_estimate=cost(2 * tokens * rows * size * count),
    )(left, right)


def unit_kernel(h_ref, w1_ref, w3_ref, d_hidden_ref, hidden_ref, d_a_ref, d_b_ref):
    fc_a, fc_b = nn(h_ref[...], w1_ref[...]), nn(h_ref[...], w3_ref[...])
    d_hidden = d_hidden_ref[...].astype(F32)
    sigma = jax.nn.sigmoid(fc_a)
    silu_a = fc_a * sigma
    hidden_ref[...] = (silu_a * fc_b).astype(BF16)
    d_a_ref[...] = (d_hidden * fc_b * (sigma * (1.0 + fc_a * (1.0 - sigma)))).astype(BF16)
    d_b_ref[...] = (d_hidden * silu_a).astype(BF16)


def hidden_units(h_two, w1, w3, d_hidden):
    rows, width = h_two.shape
    count = w1.shape[1]
    block, tile = min(512, rows), min(512, count)
    weight = pl.BlockSpec((width, tile), lambda n, m: (0, n))
    spot = pl.BlockSpec((block, tile), lambda n, m: (m, n))
    return pl.pallas_call(
        unit_kernel,
        grid=(count // tile, rows // block),
        out_shape=[jax.ShapeDtypeStruct((rows, count), BF16)] * 3,
        in_specs=[pl.BlockSpec((block, width), lambda n, m: (m, 0)), weight, weight, spot],
        out_specs=[spot] * 3,
        compiler_params=pltpu.CompilerParams(vmem_limit_bytes=60 << 20),
        cost_estimate=cost(4 * rows * width * count),
    )(h_two, w1, w3, d_hidden)


def stack_kernel(*refs):
    count = len(refs) - 4
    shares, out_ref, held, sems_in, sems_out = refs[:count], *refs[count:]
    rows = shares[0].shape[0]
    ins, outs = [], []
    for index, share in enumerate(shares):
        ins.append(pltpu.make_async_copy(share, held.at[index], sems_in.at[index]))
        spot = out_ref.at[pl.ds(index * rows, rows)]
        outs.append(pltpu.make_async_copy(held.at[index], spot, sems_out.at[index]))
    for copy in ins:
        copy.start()
    for copy, onward in zip(ins, outs):
        copy.wait()
        onward.start()
    for onward in outs:
        onward.wait()


def stack_rows(*shares):
    rows, width = shares[0].shape
    count = len(shares)
    return pl.pallas_call(
        stack_kernel,
        out_shape=jax.ShapeDtypeStruct((count * rows, width), shares[0].dtype),
        in_specs=[pl.BlockSpec(memory_space=pl.ANY)] * count,
        out_specs=pl.BlockSpec(memory_space=pl.ANY),
        scratch_shapes=[
            pltpu.VMEM((count, rows, width), shares[0].dtype),
            pltpu.SemaphoreType.DMA((count,)),
            pltpu.SemaphoreType.DMA((count,)),
        ],
        compiler_params=pltpu.CompilerParams(vmem_limit_bytes=48 << 20),
        cost_estimate=cost(2 * COPYING),
    )(*shares)


def nn(left, right):
    return lax.dot_general(left, right, (((1,), (0,)), ((), ())), preferred_element_type=F32)


def nt(left, right):
    return lax.dot_general(left, right, (((1,), (1,)), ((), ())), preferred_element_type=F32)


def tn(left, right):
    return lax.dot_general(left, right, (((0,), (0,)), ((), ())), preferred_element_type=F32)


def where_is(whole, chunk, piece_len):
    share_len = piece_len // 2
    spots = []
    for shape, dim in (((piece_len, 1), 0), ((1, piece_len), 1)):
        at = lax.broadcasted_iota(jnp.int32, shape, dim) + whole[2] * share_len
        spots.append(jnp.where(at >= piece_len, at - piece_len, at))
    start = whole[0] * (2 * piece_len) + chunk * piece_len
    return spots[0], spots[1], start


def document(whole, spot):
    seq = pl.program_id(0)
    first, second = whole[3 + 2 * seq], whole[4 + 2 * seq]
    return jnp.where(spot >= second, 2, jnp.where(spot >= first, 1, 0))


def fade(gap, log_keep):
    return jnp.exp(jnp.maximum(gap, 0).astype(F32) * log_keep)


def piece_terms(whole, log_keep, chunk, piece_len):
    rows, cols, start = where_is(whole, chunk, piece_len)
    doc_rows, doc_cols = document(whole, start + rows), document(whole, start + cols)
    before, last = document(whole, start - 1), document(whole, start + piece_len - 1)
    within = jnp.where(
        (rows >= cols) & (doc_rows == doc_cols), fade(rows - cols, log_keep) * SCALE, 0.0
    )
    inflow = jnp.where(doc_rows == before, fade(rows + 1, log_keep) * SCALE, 0.0)
    outflow = jnp.where(doc_rows == last, fade(piece_len - 1 - rows, log_keep), 0.0)
    whole_gap = jnp.full((1, 1), piece_len, jnp.int32)
    over = jnp.where(before == last, fade(whole_gap, log_keep), 0.0)
    return within, inflow, outflow, over


def piece_of(ref, whole, chunk):
    group = lax.rem(chunk + whole[1], 2) * 2
    value = ref[pl.ds(group, 2), 0]
    return value.reshape(value.shape[0] * value.shape[1], value.shape[2])


def put_piece(ref, whole, chunk, value):
    group = lax.rem(chunk + whole[1], 2) * 2
    ref[pl.ds(group, 2), 0] = value.astype(ref.dtype).reshape(2, value.shape[0] // 2, value.shape[1])


def split_kq(ref, whole, chunk):
    both = piece_of(ref, whole, chunk)
    width = both.shape[1] // 2
    return both[:, :width], both[:, width:]


def update_kernel(whole, keeps, kq_ref, v_ref, out_ref):
    log_keep = keeps[pl.program_id(1)]
    piece_len = 2 * kq_ref.shape[2]
    total = jnp.zeros(out_ref.shape[2:], F32)
    for chunk in range(2):
        rows, _, start = where_is(whole, chunk, piece_len)
        last = document(whole, whole[0] * (2 * piece_len) + 2 * piece_len - 1)
        gap = (2 - chunk) * piece_len - 1 - rows
        weight = jnp.where(document(whole, start + rows) == last, fade(gap, log_keep), 0.0)
        keys, _ = split_kq(kq_ref, whole, chunk)
        values = piece_of(v_ref, whole, chunk)
        total = total + tn((keys.astype(F32) * weight).astype(BF16), values)
    out_ref[0, 0] = total.astype(BF16)


def next_state(state, keys, values, outflow, over):
    return over * state + tn((keys.astype(F32) * outflow).astype(BF16), values)


def forward_kernel(
    whole, keeps, kq_ref, v_ref, gate_ref, state_ref, gain_ref, gated_ref, retained_ref
):
    log_keep = keeps[pl.program_id(1)]
    piece_len = 2 * kq_ref.shape[2]
    state = state_ref[0, 0].astype(F32)
    for chunk in range(2):
        within, inflow, outflow, over = piece_terms(whole, log_keep, chunk, piece_len)
        keys, query = split_kq(kq_ref, whole, chunk)
        values = piece_of(v_ref, whole, chunk)
        scores = (nt(query, keys) * within).astype(BF16)
        retained = nn(scores, values) + inflow * nn(query, state.astype(BF16))
        if chunk == 0:
            state = next_state(state, keys, values, outflow, over)
        put_piece(retained_ref, whole, chunk, retained)
        normed, _, _ = norm_rows(retained, gain_ref[0], 0.01)
        gate = piece_of(gate_ref, whole, chunk).astype(F32)
        put_piece(gated_ref, whole, chunk, gate * jax.nn.sigmoid(gate) * normed)


def norm_back_kernel(
    whole,
    keeps,
    d_gated_ref,
    gate_ref,
    retained_ref,
    kq_ref,
    gain_ref,
    d_gate_ref,
    d_retained_ref,
    d_gain_ref,
    leaving_ref,
):
    log_keep = keeps[pl.program_id(1)]
    piece_len = 2 * kq_ref.shape[2]
    total = jnp.zeros(leaving_ref.shape[2:], F32)
    gain = gain_ref[0]
    d_gain = jnp.zeros(gain.shape, F32)
    for chunk in range(2):
        rows, _, start = where_is(whole, chunk, piece_len)
        before = document(whole, whole[0] * (2 * piece_len) - 1)
        gap = chunk * piece_len + rows + 1
        weight = jnp.where(
            document(whole, start + rows) == before, fade(gap, log_keep) * SCALE, 0.0
        )
        _, query = split_kq(kq_ref, whole, chunk)
        retained = piece_of(retained_ref, whole, chunk).astype(F32)
        normed, unit, scale = norm_rows(retained, gain, 0.01)
        gate = piece_of(gate_ref, whole, chunk).astype(F32)
        d_gated = piece_of(d_gated_ref, whole, chunk).astype(F32)
        sigma = jax.nn.sigmoid(gate)
        put_piece(
            d_gate_ref, whole, chunk, d_gated * normed * sigma * (1.0 + gate * (1.0 - sigma))
        )
        d_normed = d_gated * gate * sigma
        d_gain = d_gain + jnp.sum(d_normed * unit, axis=0, keepdims=True)
        d_retained = norm_back(d_normed, unit, scale, gain)
        put_piece(d_retained_ref, whole, chunk, d_retained)
        total = total + tn(query, (d_retained * weight).astype(BF16))
    d_gain_ref[0, 0] = d_gain
    leaving_ref[0, 0] = total.astype(BF16)


def backward_kernel(
    whole, keeps, kq_ref, v_ref, d_retained_ref, state_ref, d_state_ref, d_kq_ref, d_v_ref
):
    log_keep = keeps[pl.program_id(1)]
    piece_len = 2 * kq_ref.shape[2]
    terms = [piece_terms(whole, log_keep, chunk, piece_len) for chunk in range(2)]
    state = state_ref[0, 0].astype(F32)
    keys, _ = split_kq(kq_ref, whole, 0)
    _, _, outflow, over = terms[0]
    states = [state, next_state(state, keys, piece_of(v_ref, whole, 0), outflow, over)]
    d_state = d_state_ref[0, 0].astype(F32)
    for chunk in (1, 0):
        within, inflow, outflow, over = terms[chunk]
        keys, query = split_kq(kq_ref, whole, chunk)
        values = piece_of(v_ref, whole, chunk)
        d_ret = piece_of(d_retained_ref, whole, chunk)
        state_low, d_state_low = states[chunk].astype(BF16), d_state.astype(BF16)
        scores = (nt(query, keys) * within).astype(BF16)
        d_scores = (nt(d_ret, values) * within).astype(BF16)
        d_values = tn(scores, d_ret) + outflow * nn(keys, d_state_low)
        put_piece(d_v_ref, whole, chunk, d_values)
        d_query = nn(d_scores, keys) + inflow * nt(d_ret, state_low)
        d_keys = tn(d_scores, query) + outflow * nt(values, d_state_low)
        put_piece(d_kq_ref, whole, chunk, jnp.concatenate([d_keys, d_query], axis=1))
        if chunk == 1:
            entering = tn(query, (d_ret.astype(F32) * inflow).astype(BF16))
            d_state = over * d_state + entering


def per_head(kernel, scalars, blocks, outs, flops=12 << 30):
    def spec(array, kind):
        if kind == ROWS:
            width = array.shape[3] // heads
            return pl.BlockSpec((4, 1, array.shape[2], width), lambda b, h, *_: (0, b, 0, h))
        if kind == GAINS:
            return pl.BlockSpec((1, *array.shape[1:]), lambda b, h, *_: (h, 0, 0))
        return pl.BlockSpec((1, 1, *array.shape[2:]), lambda b, h, *_: (b, h, 0, 0))

    heads = scalars[1].shape[0]
    seq_count = (scalars[0].shape[0] - 3) // 2
    return pl.pallas_call(
        kernel,
        out_shape=[a for a, _ in outs],
        grid_spec=pltpu.PrefetchScalarGridSpec(
            num_scalar_prefetch=2,
            grid=(seq_count, heads),
            in_specs=[spec(*block) for block in blocks],
            out_specs=[spec(*out) for out in outs],
        ),
        compiler_params=pltpu.CompilerParams(vmem_limit_bytes=56 << 20),
        cost_estimate=cost(flops),
    )(*scalars, *(a for a, _ in blocks))


def both_quarters(mine, across, first, dim):
    return jnp.concatenate(
        [jnp.where(first, mine, across), jnp.where(first, across, mine)], axis=dim
    )


def paired_body(
    tokens,
    segments,
    forget,
    ln1_gain,
    w_query,
    w_key,
    w_value,
    w_gate,
    norm_gain,
    w_out,
    ln2_gain,
    w_fc_gate,
    w_fc_up,
    w_fc_down,
    cotangent,
):
    place = lax.axis_index(CONTEXT)
    x_at, core, y_at = place // 2, place % 2, lax.axis_index(TENSOR)
    z_at = lax.axis_index(FSDP)
    heads = forget.shape[0] // 2
    qk_width = w_query.shape[1] // forget.shape[0]
    v_width = w_value.shape[1] // forget.shape[0]
    width = tokens.shape[2]
    seq_count, share_len = tokens.shape[0], tokens.shape[1]
    share_rows = seq_count * share_len
    piece_len = 2 * share_len
    chip_len = 2 * piece_len
    v_half = heads * v_width
    forget_half = lax.dynamic_slice_in_dim(forget, core * heads, heads)
    gain_half = lax.dynamic_slice_in_dim(norm_gain, core * v_half, v_half)

    def part(array, first, last):
        return array[first * share_rows : last * share_rows]

    def unit(x_index):
        q = core * 2 + x_index
        key_query = [quarter_of(w_key, 1, q), quarter_of(w_query, 1, q)]
        return [
            jnp.concatenate(key_query, axis=1),
            quarter_of(w_value, 1, q),
            quarter_of(w_gate, 1, q),
            quarter_of(w_out, 0, q),
            quarter_of(w_fc_down, 0, q),
            quarter_of(w_fc_gate, 1, q),
            quarter_of(w_fc_up, 1, q),
        ]

    KQ, V, G, O, W2, W1, W3 = range(7)
    by_rows = [False, False, False, True, True, False, False]
    own, sibling = unit(x_at), unit(1 - x_at)
    size = own[0].shape[0]
    z_last = lax.axis_size(FSDP) - 1
    z_count = z_last + 1
    s_one = jnp.where(z_at == 0, 1, z_at - 1)
    s_three = jnp.where(z_at == z_last, 0, jnp.where(z_at == 1, 2, z_last))
    z_spots = [z_at, s_one, z_at ^ 2, s_three]
    spots = jnp.stack(z_spots + z_spots + [x_at] * 4 + [1 - x_at] * 4).astype(jnp.int32)
    groups = [[KQ, V], [G, O], [W2, W1, W3]]
    slots, across = [[], [], []], [[], [], []]

    def weight(index):
        at, row = next((i, g.index(index)) for i, g in enumerate(groups) if index in g)
        blocks = [(own[index], 0)] + [(array, row) for array in slots[at]]
        blocks += [(sibling[index], 0)] + [(array, row) for array in across[at]]
        return assemble(blocks, spots, by_rows[index], size)

    env = SimpleNamespace()
    firsts = jnp.sum((segments == 0).astype(jnp.int32), axis=1)
    seconds = jnp.sum((segments <= 1).astype(jnp.int32), axis=1)
    starts = jnp.stack([firsts, seconds], axis=1).reshape(-1)
    whole = jnp.concatenate([jnp.stack([x_at, core, y_at]).astype(jnp.int32), starts])
    scalars = (whole, jnp.log(1.0 - forget_half))
    gains = gain_half.reshape(heads, 1, v_width)
    state_type = jax.ShapeDtypeStruct((seq_count, heads, qk_width, v_width), BF16)
    rows_type = jax.ShapeDtypeStruct((4, seq_count, share_len, v_half), BF16)
    kq_type = jax.ShapeDtypeStruct((4, seq_count, share_len, 2 * heads * qk_width), BF16)
    gain_type = jax.ShapeDtypeStruct((seq_count, heads, 1, v_width), F32)

    def shaped(rows_in):
        return rows_in.reshape(4, seq_count, share_len, -1)

    def flat(rows_in):
        return rows_in.reshape(4 * share_rows, -1)

    x_share = tokens.reshape(share_rows, width).astype(F32)
    cot_share = cotangent.reshape(share_rows, width)

    def work_norm():
        h1, ln1_normed, ln1_scale = norm_rows(x_share, ln1_gain)
        env.ln1 = (ln1_normed, ln1_scale)
        env.h = h1.astype(BF16)
        env.hy = over_y(env.h)
        return [env.h]

    def work_core():
        env.hc, env.hcy = over_core(env.h), over_core(env.hy)
        env.cy = over_y(cot_share)
        return []

    def work_rows():
        env.h_one = stack_rows(env.h, env.hy, env.hc, env.hcy)
        return [env.h_one]

    def work_kq():
        env.wkq = weight(KQ)
        env.kq = sum_of_products(nn, [env.h_one], [env.wkq], 0, 4 * share_rows, BF16)
        return [env.kq]

    def work_v():
        env.wv = weight(V)
        env.v = sum_of_products(nn, [env.h_one], [env.wv], 0, 4 * share_rows, BF16)
        return [env.v]

    def work_state():
        (update,) = per_head(
            update_kernel,
            scalars,
            [(shaped(env.kq), ROWS), (shaped(env.v), ROWS)],
            [(state_type, STATES)],
            4 << 30,
        )
        env.state = lax.ppermute(update, CONTEXT, UP_X)
        env.cc, env.ccy = over_core(cot_share), over_core(env.cy)
        return [update]

    def work_gate():
        env.wg = weight(G)
        env.gate = sum_of_products(nn, [env.h_one], [env.wg], 0, 4 * share_rows, BF16)
        return [env.gate]

    def work_retained():
        gated, env.retained = per_head(
            forward_kernel,
            scalars,
            [
                (shaped(env.kq), ROWS),
                (shaped(env.v), ROWS),
                (shaped(env.gate), ROWS),
                (env.state, STATES),
                (gains, GAINS),
            ],
            [(rows_type, ROWS), (rows_type, ROWS)],
        )
        env.gated = flat(gated)
        return [env.gated]

    def work_out_far():
        env.wo = weight(O)
        own, other = sum_of_products(
            nn, [env.gated], [env.wo], 2 * share_rows, 2 * share_rows, BF16, (), 2
        )
        env.far_other, env.far_own = over_core(other), over_core(own)
        return [other]

    def work_out_near():
        near = sum_of_products(
            nn, [env.gated], [env.wo], share_rows, share_rows, BF16, [(env.far_other, 0)]
        )
        env.near = over_y(near)
        return [near]

    def work_out_own():
        extras = [(env.far_own, 0), (tokens.reshape(share_rows, width), 0)]
        env.own = sum_of_products(nn, [env.gated], [env.wo], 0, share_rows, F32, extras)
        return [env.own]

    def work_cot():
        env.cot = stack_rows(cot_share, env.cy, env.cc, env.ccy)
        return [env.cot]

    def work_d_hidden():
        env.w2 = weight(W2)
        env.d_hidden = sum_of_products(nt, [env.cot], [env.w2], 0, 4 * share_rows, BF16)
        return [env.d_hidden]

    def work_middle():
        env.middle = env.own + env.near.astype(F32)
        h2, ln2_normed, ln2_scale = norm_rows(env.middle, ln2_gain)
        env.ln2 = (ln2_normed, ln2_scale)
        env.h2 = h2.astype(BF16)
        env.h2y, env.h2c = over_y(env.h2), over_core(env.h2)
        return [env.h2]

    def work_up():
        env.w1 = weight(W1)
        return [env.w1]

    def work_h2():
        env.w3 = weight(W3)
        env.h2y, env.d_hidden, env.w1, env.w3 = tie(env.h2y, env.d_hidden, env.w1, env.w3)
        env.h2cy = over_core(env.h2y)
        return [env.w3]

    plan = [
        [work_norm],
        [],
        [work_core],
        [work_rows],
        [work_kq],
        [work_v, work_state],
        [work_cot, work_gate],
        [work_retained, work_out_far],
        [work_out_near, work_out_own],
        [work_middle],
        [work_d_hidden, work_up, work_h2],
    ]
    stacks = [jnp.concatenate([own[index] for index in group], axis=0) for group in groups]
    up = down = kept = to_send = None
    for tick, works in enumerate(plan):
        at, hop = divmod(tick, 3)
        moving = at < len(groups)
        sent, to_send = to_send, None
        if sent is not None:
            slots[sent[0]].append(sent[1])
            across[sent[0]].append(over_x(sent[1]))
        if moving and hop < 2:
            up = stacks[at] if hop == 0 else up
            down = stacks[at] if hop == 0 else down
            got = [lax.ppermute(up, FSDP, UP_Z[hop]), lax.ppermute(down, FSDP, DOWN_Z[hop])]
        elif moving:
            got = [lax.ppermute(slots[at][1], FSDP, LAST_Z)]
        held = []
        for work in works:
            held += work()
        if not moving:
            continue
        names = [n for n in ("h_one", "kq", "gate", "gated", "cot") if hasattr(env, n)]
        held = held + ([across[sent[0]][-1]] if sent is not None else [])
        ahead = stacks[at + 1 : at + 2] if hop == 2 else []
        tied = list(tie(*got, *[getattr(env, n) for n in names], *ahead, *held))
        got = [tied.pop(0) for _ in got]
        for n in names:
            setattr(env, n, tied.pop(0))
        if hasattr(env, "far_other"):
            env.far_other = tie(env.far_other, *got)[0]
        if ahead:
            stacks[at + 1] = tied.pop(0)
        if hop == 0:
            up, down = kept = got
            to_send = (at, jnp.where(z_at > 0, up, down))
        elif hop == 1:
            up, down = got
            to_send = (at, jnp.where(z_at >= 2, up, down))
        else:
            ends = (z_at == 0) | (z_at == z_last)
            to_send = (at, jnp.where(ends, got[0], kept[1]))

    h_one, gated, gate_pre = env.h_one, env.gated, env.gate
    wkq, wv, wg, wo, w1, w2, w3 = env.wkq, env.wv, env.wg, env.wo, env.w1, env.w2, env.w3
    cot_full, d_hidden, middle = env.cot, env.d_hidden, env.middle

    token = [h_one]

    def step(run, *args):
        *args, _ = tie(*args, token[0])
        out = run(*args)
        token[0] = out[0] if isinstance(out, (tuple, list)) else out
        return out

    def far_product(product, lefts, rights, weight=1):
        def run(*arrays):
            return sum_of_products(
                product, arrays, rights, 2 * share_rows, 2 * share_rows, BF16, (), 2, weight
            )

        own, other = step(run, *lefts)
        return over_core(other), over_core(own)

    def whole_product(product, lefts, rights, first, rows, kind, *extras, weight=1):
        count = len(lefts)

        def run(*arrays):
            added = [(a, row) for a, (_, row) in zip(arrays[count:], extras)]
            return sum_of_products(
                product,
                arrays[:count],
                rights,
                first * share_rows,
                rows * share_rows,
                kind,
                added,
                1,
                weight,
            )

        return step(run, *lefts, *(a for a, _ in extras))

    def theirs(left, right):
        return over_x(step(lambda a, b: quarter_product(a, b, 1 - x_at), left, right))

    def ours(left, right, got):
        total = step(lambda a, b, c: quarter_product(a, b, x_at, [c]), left, right, got)
        return lax.psum_scatter(total, FSDP, scatter_dimension=0, tiled=True)

    def chip_rows(left, right):
        total = step(lambda a, b: split_product(a, b, z_count), left, right)
        return lax.psum_scatter(total, FSDP, scatter_dimension=0, tiled=False)

    def chip_columns(left, right):
        total = step(plain_product, left, right)
        mine = lax.psum_scatter(total, FSDP, scatter_dimension=0, tiled=True)
        return jnp.concatenate(jnp.split(mine, 2, axis=1), axis=0)

    def begin_finish(*mine):
        mine = step(lambda *a: jnp.concatenate(a, axis=0), *mine)
        return mine, over_x(mine)

    def end_finish(firsts, mine, beside):
        def join(mine, beside):
            blocks, row = [], 0
            for x_summed in firsts:
                count = 1 if x_summed else 2
                one, other = (a[row * size : (row + count) * size] for a in (mine, beside))
                if x_summed:
                    blocks += [jnp.where(x_at == 0, one, other), jnp.where(x_at == 0, other, one)]
                else:
                    blocks.append((one.astype(F32) + other.astype(F32)).astype(BF16))
                row += count
            return jnp.concatenate(blocks, axis=0)

        both = step(join, mine, beside)
        return both, over_core(both)

    def quarters(pair, at):
        both, other = pair
        mine, theirs = (a[2 * at * size : (2 * at + 2) * size] for a in (both, other))
        first, second = jnp.where(core == 0, mine, theirs), jnp.where(core == 0, theirs, mine)
        return [first[:size], first[size:], second[:size], second[size:]]

    def shard(pair, at, rows):
        return jnp.concatenate(quarters(pair, at), axis=1 - int(rows)).astype(F32)

    h_two = stack_rows(env.h2, env.h2y, env.h2c, env.h2cy)
    hidden, d_fca, d_fcb = step(hidden_units, h_two, w1, w3, d_hidden)

    fc_lefts, fc_rights = (d_fca, d_fcb), (w1, w3)
    far_other, far_own = far_product(nt, fc_lefts, fc_rights)
    down_mine = chip_rows(hidden, cot_full)
    near = over_y(whole_product(nt, fc_lefts, fc_rights, 1, 1, BF16, (far_other, 0)))
    gate_got = theirs(h_two, d_fca)
    own_part = whole_product(nt, fc_lefts, fc_rights, 0, 1, F32, (far_own, 0))
    up_got = theirs(h_two, d_fcb)
    out_far_other, out_far_own = far_product(nn, [hidden], [w2])

    def middle_back(own_part, near):
        d_h2 = own_part + near.astype(F32)
        ln2_normed, ln2_scale = env.ln2
        d_middle = cot_share.astype(F32) + norm_back(d_h2, ln2_normed, ln2_scale, ln2_gain)
        return d_middle.astype(BF16), d_middle, jnp.sum(d_h2 * ln2_normed, axis=0)

    d_mid_low, d_middle, g_ln2 = step(middle_back, own_part, near)
    d_mid_y, d_mid_c = over_y(d_mid_low), over_core(d_mid_low)
    fc_gate_mine = ours(h_two, d_fca, gate_got)
    out_near = whole_product(nn, [hidden], [w2], 1, 1, BF16, (out_far_other, 0))
    out_own = whole_product(nn, [hidden], [w2], 0, 1, F32, (out_far_own, 0), (middle, 0))
    d_mid_y, out_near, up_got = step(lambda *a: a, d_mid_y, out_near, up_got)
    d_mid_cy = over_core(d_mid_y)
    out_near = over_y(out_near)
    down_begun = begin_finish(down_mine)
    fc_up_mine = ours(h_two, d_fcb, up_got)

    def gate_back(share, y, c, cy):
        d_branch = stack_rows(share, y, c, cy)
        return sum_of_products(nt, [d_branch], [wo], 0, 4 * share_rows, BF16), d_branch

    d_gated, d_branch = step(gate_back, d_mid_low, d_mid_y, d_mid_c, d_mid_cy)
    down_beside, d_gated = tie(down_begun[1], d_gated)
    kq, values, state_in = shaped(env.kq), shaped(env.v), env.state

    def retained_back(d_gated, kq):
        return per_head(
            norm_back_kernel,
            scalars,
            [
                (shaped(d_gated), ROWS),
                (shaped(gate_pre), ROWS),
                (env.retained, ROWS),
                (kq, ROWS),
                (gains, GAINS),
            ],
            [(rows_type, ROWS), (rows_type, ROWS), (gain_type, STATES), (state_type, STATES)],
        )

    d_gate, d_retained, g_norm, leaving = step(retained_back, d_gated, kq)
    d_gate = flat(d_gate)
    g_norm = jnp.sum(g_norm, axis=0).reshape(v_half)
    state_grad = lax.ppermute(leaving, CONTEXT, DOWN_X)
    out_mine = chip_rows(gated, d_branch)

    def pair_back(d_retained, state_grad):
        return per_head(
            backward_kernel,
            scalars,
            [
                (kq, ROWS),
                (values, ROWS),
                (d_retained, ROWS),
                (state_in, STATES),
                (state_grad, STATES),
            ],
            [(kq_type, ROWS), (rows_type, ROWS)],
        )

    g_down = end_finish([False], down_begun[0], down_beside)
    dkq_low, dv_low = step(pair_back, d_retained, state_grad)
    dkq_low, dv_low = flat(dkq_low), flat(dv_low)
    gg_mine = chip_columns(h_one, d_gate)
    v_got = theirs(h_one, dv_low)
    kq_got = theirs(h_one, dkq_low)
    h1_lefts, h1_rights = (dkq_low, dv_low, d_gate), (wkq, wv, wg)
    far_other, far_own = far_product(nt, h1_lefts, h1_rights)
    v_mine = ours(h_one, dv_low, v_got)
    output = step(lambda a, b: (a + b.astype(F32)).astype(BF16), out_own, out_near)
    near = over_y(whole_product(nt, h1_lefts, h1_rights, 1, 1, BF16, (far_other, 0)))
    own_part = whole_product(nt, h1_lefts, h1_rights, 0, 1, F32, (far_own, 0))
    fc_begun = begin_finish(fc_gate_mine)
    out_mine, kq_got = tie(out_mine, kq_got)
    kq_mine = ours(h_one, dkq_low, kq_got)
    up_begun = begin_finish(fc_up_mine)

    def tokens_back(own_part, near):
        d_h1 = own_part + near.astype(F32)
        ln1_normed, ln1_scale = env.ln1
        grad = d_middle + norm_back(d_h1, ln1_normed, ln1_scale, ln1_gain)
        return grad, jnp.sum(d_h1 * ln1_normed, axis=0)

    grad_tokens, g_ln1 = step(tokens_back, own_part, near)
    norm_size = lax.axis_size(TENSOR) * norm_gain.shape[0]
    norm_all = lax.dynamic_update_slice_in_dim(
        jnp.zeros((norm_size,), F32), g_norm, (2 * y_at + core) * v_half, 0
    )
    gain_sums = jnp.concatenate([g_ln1, g_ln2, norm_all])
    gain_sums = gain_sums + over_x(gain_sums)
    out_mine, gain_sums = tie(out_mine, gain_sums)
    out_begun = begin_finish(out_mine, gg_mine)
    g_fc = end_finish([True], *fc_begun)
    g_up = end_finish([True], *up_begun)
    v_begun = begin_finish(v_mine)
    kq_begun = begin_finish(kq_mine)
    gain_sums = tie(gain_sums, kq_begun[0])[0]
    gain_sums = gain_sums + over_core(gain_sums)
    gain_sums = butterfly(butterfly(gain_sums, TENSOR), FSDP)
    g_out = end_finish([False, False], *out_begun)
    g_value = end_finish([True], *v_begun)
    g_kq = end_finish([True], *kq_begun)
    sides = quarters(g_kq, 0)
    g_key = jnp.concatenate([side[:, :qk_width] for side in sides], axis=1).astype(F32)
    g_query = jnp.concatenate([side[:, qk_width:] for side in sides], axis=1).astype(F32)

    g_ln1, g_ln2 = gain_sums[:width], gain_sums[width : 2 * width]
    g_norm = lax.dynamic_slice_in_dim(
        gain_sums, 2 * width + y_at * norm_gain.shape[0], norm_gain.shape[0]
    )
    return (
        output.reshape(tokens.shape),
        grad_tokens.reshape(tokens.shape),
        g_ln1,
        g_query,
        g_key,
        shard(g_value, 0, False),
        shard(g_out, 1, False),
        g_norm,
        shard(g_out, 0, True),
        g_ln2,
        shard(g_fc, 0, False),
        shard(g_up, 0, False),
        shard(g_down, 0, True),
    )


def body(tensor_size, *arrays):
    heads_here = arrays[2].shape[0]
    paired = tensor_size == 2 and heads_here % 2 == 0 and lax.axis_size(CONTEXT) == 4
    paired = paired and lax.axis_size(FSDP) == 4
    return (paired_body if paired else general_body)(*arrays)


def solution(mesh):
    in_specs = (
        P(FSDP, (CONTEXT, TENSOR), None),
        P(FSDP, None),
        P(TENSOR),
        P(),
        P(FSDP, TENSOR),
        P(FSDP, TENSOR),
        P(FSDP, TENSOR),
        P(FSDP, TENSOR),
        P(TENSOR),
        P(TENSOR, FSDP),
        P(),
        P(FSDP, TENSOR),
        P(FSDP, TENSOR),
        P(TENSOR, FSDP),
        P(FSDP, (CONTEXT, TENSOR), None),
    )
    out_specs = (
        P(FSDP, (CONTEXT, TENSOR), None),
        P(FSDP, (CONTEXT, TENSOR), None),
        P(),
        P(FSDP, TENSOR),
        P(FSDP, TENSOR),
        P(FSDP, TENSOR),
        P(FSDP, TENSOR),
        P(TENSOR),
        P(TENSOR, FSDP),
        P(),
        P(FSDP, TENSOR),
        P(FSDP, TENSOR),
        P(TENSOR, FSDP),
    )
    return jax.shard_map(partial(body, mesh.shape[TENSOR]), mesh=mesh, in_specs=in_specs, out_specs=out_specs, check_vma=False)
```
